32 devices in a mesh: branch: 1, dap: 32 (over z, y, x, core).
Axes of the slice: x: 2, y: 2, z: 4, core: 2. Of those that a mesh axis runs over, the one named last changes fastest.
Arguments:
- alignment: bfloat16 [256, 256, 256], P('dap'), may hold values from -24 to 24
- pair_rep: bfloat16 [256, 256, 128], P('dap', 'branch'), may hold values from -6 to 6
- align_mask: int32 [256, 256], replicated, may hold values from 0 to 1, as said below
- residue_mask: int32 [256], replicated, may hold values from 0 to 1, as said below
- bias_weight: bfloat16 [128, 8], replicated, may hold values from -1 to 1
- row_proj_weight: bfloat16 [4, 256, 256], P(None, None, 'branch'), may hold values from -0.375 to 0.375
- row_out_weight: bfloat16 [256, 256], replicated, may hold values from -1 to 1
- column_proj_weight: bfloat16 [4, 256, 256], P(None, None, 'branch'), may hold values from -0.375 to 0.375
- column_out_weight: bfloat16 [256, 256], replicated, may hold values from -1 to 1
- outer_factor_weight: bfloat16 [256, 64], replicated, may hold values from -0.375 to 0.375
- outer_out: bfloat16 [1024, 128], replicated, may hold values from -0.375 to 0.375
Outputs:
- updated_alignment: bfloat16 [256, 256, 256], P(None, 'dap')
- pair_out: bfloat16 [256, 256, 128], P('dap', 'branch')
The draws below stay inside these ranges and needn't reach their ends.
Inputs may be any that keep to these rules, and one draw needn't show every extreme that they name: `align_mask`: the first alignment is all ones; in every other alignment the ones form one contiguous run of residues that is never empty. `residue_mask`: ones on a leading run of residues and zeros after it; both values occur.
All inputs are finite; a program needn't handle non-finite values.
Results may differ from the reference program's by a relative error of at most 0.0085.
Values may be sent and summed in bfloat16 or wider, within the bound.
No kernel may reach another device: no remote copies, remote signals or barrier semaphores. Data moves between devices by JAX's collectives and lax.ppermute only.
A program may use at most 128 MiB of HBM per device.

```python
import math
import jax
import jax.numpy as jnp
from jax import lax

ALIGN_CHANNELS = 256
PAIR_DIM = 128
ATTN_HEAD_COUNT = 8
HEAD_CHANNELS = 32
FACTOR_CHANNELS = 32
SEQUENCE_COUNT = 256
RESIDUE_COUNT = 256


def draw_alignment(key, part):
    random_keys = jax.random.split(key, 2)
    shared_setup = jax.random.normal(random_keys[0], (RESIDUE_COUNT, ALIGN_CHANNELS), jnp.float32)
    random_noise = jax.random.normal(random_keys[1], (SEQUENCE_COUNT, RESIDUE_COUNT, ALIGN_CHANNELS), jnp.float32)
    values = 0.8 * shared_setup[None, :, :] + random_noise
    return jnp.clip(values, -24.0, 24.0).astype(jnp.bfloat16)


def draw_align_mask(key, part):
    random_keys = jax.random.split(jax.random.fold_in(key, 11), 2)
    least = max(RESIDUE_COUNT // 4, 1)
    first = jax.random.randint(random_keys[0], (SEQUENCE_COUNT, 1), 0, RESIDUE_COUNT - least + 1)
    length = jax.random.randint(random_keys[1], (SEQUENCE_COUNT, 1), least, RESIDUE_COUNT + 1 - first)
    position = jnp.arange(RESIDUE_COUNT, dtype=jnp.int32)[None, :]
    live = jnp.logical_and(position >= first, position < first + length)
    leading = jnp.arange(SEQUENCE_COUNT, dtype=jnp.int32)[:, None] == 0
    return jnp.logical_or(live, leading).astype(jnp.int32)


def draw_residue_mask(key, part):
    length = jax.random.randint(jax.random.fold_in(key, 23), (), RESIDUE_COUNT // 2, RESIDUE_COUNT)
    return (jnp.arange(RESIDUE_COUNT, dtype=jnp.int32) < length).astype(jnp.int32)


def block_scale(own_key, shape, cuts, low, top_value):
    level = 1.0
    for dim, parts in cuts:
        draws = jax.random.uniform(jax.random.fold_in(jax.random.fold_in(own_key, 6), dim), (parts,), jnp.float32, low / len(cuts), top_value / len(cuts))
        level = level * jnp.repeat(jnp.exp(draws), shape[dim] // parts).reshape((-1,) + (1,) * (len(shape) - 1 - dim))
    return level


def gaussian(rng, shape, scale, most, cuts=(), kind=jnp.bfloat16):
    drawn = scale * jax.random.normal(rng, shape, jnp.float32)
    if cuts:
        drawn = drawn * block_scale(rng, shape, cuts, -0.22, 0.18)
    return jnp.clip(drawn, -most, most).astype(kind)


def setup_inputs(seed: int = 0) -> dict:
    key_of = jax.random.split(jax.random.key(seed), 12)
    alignment = draw_alignment(jax.random.fold_in(key_of[11], 71), 0)
    pair_rep = gaussian(key_of[1], (RESIDUE_COUNT, RESIDUE_COUNT, PAIR_DIM), 1.0, 6.0, ((0, 32),))
    align_mask = draw_align_mask(jax.random.fold_in(key_of[11], 71), 0)
    residue_mask = draw_residue_mask(jax.random.fold_in(key_of[11], 71), 0)
    bias_weight = gaussian(key_of[4], (PAIR_DIM, ATTN_HEAD_COUNT), (PAIR_DIM // 4) ** -0.5, 1.0)
    row_proj_weight = gaussian(key_of[5], (4, ALIGN_CHANNELS, ATTN_HEAD_COUNT * HEAD_CHANNELS), ALIGN_CHANNELS ** -0.5, 0.375)
    row_out_weight = gaussian(key_of[6], (ATTN_HEAD_COUNT * HEAD_CHANNELS, ALIGN_CHANNELS), HEAD_CHANNELS ** -0.5, 1.0)
    column_proj_weight = gaussian(key_of[7], (4, ALIGN_CHANNELS, ATTN_HEAD_COUNT * HEAD_CHANNELS), ALIGN_CHANNELS ** -0.5, 0.375)
    column_out_weight = gaussian(key_of[8], (ATTN_HEAD_COUNT * HEAD_CHANNELS, ALIGN_CHANNELS), HEAD_CHANNELS ** -0.5, 1.0)
    outer_factor_weight = gaussian(key_of[9], (ALIGN_CHANNELS, 2 * FACTOR_CHANNELS), ALIGN_CHANNELS ** -0.5, 0.375)
    outer_out = gaussian(key_of[10], (FACTOR_CHANNELS * FACTOR_CHANNELS, PAIR_DIM), (FACTOR_CHANNELS * FACTOR_CHANNELS // 4) ** -0.5, 0.375)
    return dict(alignment=alignment, pair_rep=pair_rep, align_mask=align_mask, residue_mask=residue_mask, bias_weight=bias_weight, row_proj_weight=row_proj_weight, row_out_weight=row_out_weight, column_proj_weight=column_proj_weight, column_out_weight=column_out_weight, outer_factor_weight=outer_factor_weight, outer_out=outer_out)


norm_eps = 1e-05
count_eps = 0.001

def layer_normalize(values):
    centre = lax.optimization_barrier(jnp.mean(values, axis=-1, keepdims=True))
    centred = values - centre
    spread = lax.optimization_barrier(jnp.mean(centred * centred, axis=-1, keepdims=True))
    return centred * lax.rsqrt(spread + norm_eps)

def attend_heads(inputs, key_mask, proj_weight, out_weight, score_bias):
    normed = layer_normalize(inputs.astype(jnp.float32)).astype(jnp.bfloat16)

    def attend_one(operands):
        current, normed_row, mask_row = operands
        length = current.shape[0]
        projected = jnp.einsum('lc,kcd->kld', normed_row.astype(jnp.float32), proj_weight.astype(jnp.float32))
        triple = lax.optimization_barrier(projected[:3].astype(jnp.bfloat16)).astype(jnp.float32)
        queries = triple[0].reshape(length, ATTN_HEAD_COUNT, HEAD_CHANNELS)
        key_rows = triple[1].reshape(length, ATTN_HEAD_COUNT, HEAD_CHANNELS)
        value_rows = triple[2].reshape(length, ATTN_HEAD_COUNT, HEAD_CHANNELS)
        scores = jnp.einsum('ihd,jhd->hij', queries, key_rows) / math.sqrt(HEAD_CHANNELS)
        if score_bias is not None:
            scores = scores + score_bias.astype(jnp.float32)
        raised = jnp.exp(scores) * mask_row[None, None, :]
        weights = raised / lax.optimization_barrier(jnp.sum(raised, axis=-1, keepdims=True))
        weights = lax.optimization_barrier(weights.astype(jnp.bfloat16)).astype(jnp.float32)
        attended_rows = jnp.einsum('hij,jhd->ihd', weights, value_rows).reshape(length, ATTN_HEAD_COUNT * HEAD_CHANNELS)
        gating = jax.nn.sigmoid(projected[3])
        heads_out = (attended_rows * gating).astype(jnp.bfloat16)
        update = jnp.dot(heads_out, out_weight, preferred_element_type=jnp.float32)
        return (current.astype(jnp.float32) + update).astype(jnp.bfloat16)
    return lax.map(attend_one, (inputs, normed, key_mask))

def reference(alignment, pair_rep, align_mask, residue_mask, bias_weight, row_proj_weight, row_out_weight, column_proj_weight, column_out_weight, outer_factor_weight, outer_out):
    float_mask = align_mask.astype(jnp.float32)
    res_float = residue_mask.astype(jnp.float32)
    pair_normed = layer_normalize(pair_rep.astype(jnp.float32)).astype(jnp.bfloat16)
    pair_score_bias = jnp.einsum('ijc,ch->hij', pair_normed.astype(jnp.float32), bias_weight.astype(jnp.float32)).astype(jnp.bfloat16)
    row_alignment = attend_heads(alignment, float_mask, row_proj_weight, row_out_weight, pair_score_bias)
    transposed_rows = jnp.swapaxes(row_alignment, 0, 1)
    column_alignment = attend_heads(transposed_rows, jnp.swapaxes(float_mask, 0, 1), column_proj_weight, column_out_weight, None)
    updated_alignment = jnp.swapaxes(column_alignment, 0, 1)
    outer_mean_normed = layer_normalize(updated_alignment.astype(jnp.float32)).astype(jnp.bfloat16)
    factor_pairs = jnp.einsum('src,ce->sre', outer_mean_normed.astype(jnp.float32), outer_factor_weight.astype(jnp.float32))
    factor_pairs = (factor_pairs * float_mask[:, :, None]).astype(jnp.bfloat16)
    left_side = factor_pairs[:, :, :FACTOR_CHANNELS]
    right_side = factor_pairs[:, :, FACTOR_CHANNELS:].astype(jnp.float32)
    counts = jnp.dot(float_mask.T, float_mask, preferred_element_type=jnp.float32, precision=lax.Precision.HIGHEST)
    outer_weight = outer_out.astype(jnp.float32)

    def outer_row(operands):
        left_row, count_row, pair_row, live_one = operands
        outer = jnp.einsum('sc,sje->jce', left_row.astype(jnp.float32), right_side)
        outer = outer.reshape(right_side.shape[1], FACTOR_CHANNELS * FACTOR_CHANNELS)
        update = jnp.dot(outer, outer_weight, precision=lax.Precision.HIGHEST)
        update = update / (count_row[:, None] + count_eps) * (live_one * res_float)[:, None]
        return (pair_row.astype(jnp.float32) + update).astype(jnp.bfloat16)
    pair_out = lax.map(outer_row, (jnp.swapaxes(left_side, 0, 1), counts, pair_rep, res_float))
    return (updated_alignment, pair_out)
```

```python
import functools
import math

import jax
import jax.numpy as jnp
from jax import lax
from jax.experimental import pallas as pl
from jax.experimental.pallas import tpu as pltpu
from jax.sharding import PartitionSpec as P

ATTN_HEAD_COUNT = 8
HEAD_CHANNELS = 32
FACTOR_CHANNELS = 32


norm_eps = 1e-05
count_eps = 0.001


def layer_normalize(values):
    centre = jnp.mean(values, axis=-1, keepdims=True)
    centred = values - centre
    spread = jnp.mean(centred * centred, axis=-1, keepdims=True)
    return centred * lax.rsqrt(spread + norm_eps)


def attend_heads(inputs, key_mask, proj_weight, out_weight, score_bias):
    batch = inputs.shape[0]
    length = inputs.shape[1]
    local_width = proj_weight.shape[2]
    local_heads = local_width // HEAD_CHANNELS
    normed = layer_normalize(inputs.astype(jnp.float32)).astype(jnp.bfloat16)
    projected = jnp.einsum("blc,kcd->kbld", normed, proj_weight, preferred_element_type=jnp.float32)
    triple = (
        projected[:3].astype(jnp.bfloat16).reshape(3, batch, length, local_heads, HEAD_CHANNELS)
    )
    gating = jax.nn.sigmoid(projected[3])

    def attend_one(operands):
        queries, key_rows, value_rows, mask_row = operands
        scores = jnp.einsum(
            "ihd,jhd->hij", queries, key_rows, preferred_element_type=jnp.float32
        ) / math.sqrt(HEAD_CHANNELS)
        if score_bias is not None:
            scores = scores + score_bias.astype(jnp.float32)
        raised = jnp.exp(scores) * mask_row[None, None, :]
        weights = (raised / jnp.sum(raised, axis=-1, keepdims=True)).astype(jnp.bfloat16)
        return jnp.einsum("hij,jhd->ihd", weights, value_rows, preferred_element_type=jnp.float32)

    attended_rows = lax.map(attend_one, (triple[0], triple[1], triple[2], key_mask))
    heads_out = (attended_rows.reshape(batch, length, local_width) * gating).astype(jnp.bfloat16)
    gathered = lax.all_gather(heads_out, "branch", axis=2, tiled=True)
    update = jnp.einsum("blf,fc->blc", gathered, out_weight, preferred_element_type=jnp.float32)
    return (inputs.astype(jnp.float32) + update).astype(jnp.bfloat16)


def per_device_general(
    alignment,
    pair_rep,
    align_mask,
    residue_mask,
    bias_weight,
    row_proj_weight,
    row_out_weight,
    column_proj_weight,
    column_out_weight,
    outer_factor_weight,
    outer_out,
):
    branch_count = lax.axis_size("branch")
    dap_count = lax.axis_size("dap")
    branch_index = lax.axis_index("branch")
    dap_index = lax.axis_index("dap")
    seq_dev = alignment.shape[0]
    res_dev = pair_rep.shape[0]
    quarter = pair_rep.shape[1]
    total_seqs = align_mask.shape[0]
    local_heads = ATTN_HEAD_COUNT // branch_count
    float_mask = align_mask.astype(jnp.float32)
    res_float = residue_mask.astype(jnp.float32)
    pair_normed = layer_normalize(pair_rep.astype(jnp.float32)).astype(jnp.bfloat16)
    bias_block = jnp.einsum(
        "ijc,ch->hij", pair_normed, bias_weight, preferred_element_type=jnp.float32
    ).astype(jnp.bfloat16)
    bias_wide = lax.all_gather(bias_block, "branch", axis=2, tiled=True)
    bias_full = lax.all_gather(bias_wide, "dap", axis=1, tiled=True)
    pair_score_bias = lax.dynamic_slice_in_dim(
        bias_full, branch_index * local_heads, local_heads, 0
    )
    sequence_row_mask = lax.dynamic_slice_in_dim(float_mask, dap_index * seq_dev, seq_dev, 0)
    row_alignment = attend_heads(
        alignment, sequence_row_mask, row_proj_weight, row_out_weight, pair_score_bias
    )
    send_mask = sequence_row_mask.astype(jnp.bfloat16)
    blocked_rows = row_alignment.reshape(seq_dev, dap_count, res_dev, row_alignment.shape[2])
    blocked_mask = send_mask.reshape(seq_dev, dap_count, res_dev)
    moved_rows = lax.all_to_all(blocked_rows, "dap", split_axis=1, concat_axis=0, tiled=True)
    moved_mask = lax.all_to_all(blocked_mask, "dap", split_axis=1, concat_axis=0, tiled=True)
    seq_total = moved_rows.shape[0]
    items = moved_rows.shape[2]
    flat_rows = moved_rows.reshape(seq_total, items, moved_rows.shape[3])
    flat_mask = moved_mask.reshape(seq_total, items)
    transposed_rows = jnp.swapaxes(flat_rows, 0, 1)
    key_mask = jnp.swapaxes(flat_mask, 0, 1).astype(jnp.float32)
    attended_rows = attend_heads(
        transposed_rows, key_mask, column_proj_weight, column_out_weight, None
    )
    column_alignment = jnp.swapaxes(attended_rows, 0, 1)
    outer_mean_normed = layer_normalize(column_alignment.astype(jnp.float32)).astype(jnp.bfloat16)
    projected = jnp.einsum(
        "src,ce->sre", outer_mean_normed, outer_factor_weight, preferred_element_type=jnp.float32
    )
    factor_pairs = (projected * flat_mask.astype(jnp.float32)[:, :, None]).astype(jnp.bfloat16)
    column_alignment, factor_pairs = (column_alignment, factor_pairs)
    blocked_out = column_alignment.reshape(seq_total, 1, items, column_alignment.shape[2])
    blocked_factors = factor_pairs.reshape(seq_total, 1, items, factor_pairs.shape[2])
    updated_alignment = blocked_out.reshape(total_seqs, res_dev, blocked_out.shape[3])
    factor_pairs = blocked_factors.reshape(total_seqs, res_dev, blocked_factors.shape[3])
    left_side = factor_pairs[:, :, :FACTOR_CHANNELS]
    right_local = factor_pairs[:, :, FACTOR_CHANNELS:]
    col_start = branch_index * quarter
    row_start = dap_index * res_dev
    mask_rows = lax.dynamic_slice_in_dim(align_mask, row_start, res_dev, 1).astype(jnp.bfloat16)
    mask_cols = lax.dynamic_slice_in_dim(align_mask, col_start, quarter, 1).astype(jnp.bfloat16)
    counts = jnp.einsum("si,sj->ij", mask_rows, mask_cols, preferred_element_type=jnp.float32)
    live_rows = lax.dynamic_slice_in_dim(res_float, row_start, res_dev, 0)
    live_cols = lax.dynamic_slice_in_dim(res_float, col_start, quarter, 0)
    outer_weight = outer_out.astype(jnp.float32)
    right_all = lax.all_gather(right_local, "dap", axis=1, tiled=True)
    right_mine = lax.dynamic_slice_in_dim(right_all, col_start, quarter, 1)
    outer_sums = jnp.einsum(
        "sic,sje->ijce", left_side, right_mine, preferred_element_type=jnp.float32
    )
    outer_sums = outer_sums.reshape(res_dev, quarter, FACTOR_CHANNELS * FACTOR_CHANNELS)
    update = jnp.einsum("ijf,fz->ijz", outer_sums, outer_weight, precision=lax.Precision.HIGHEST)
    live = live_rows[:, None] * live_cols[None, :]
    update = update / (counts[:, :, None] + count_eps) * live[:, :, None]
    pair_out = (pair_rep.astype(jnp.float32) + update).astype(jnp.bfloat16)
    return (updated_alignment, pair_out)


LANES = 128
LOG2E = math.log2(math.e)
VALUE_SCALE = 1.0 / 128.0
BF16 = jnp.bfloat16
F32 = jnp.float32
MIB = 1024 * 1024


def nt_dot(a, b):
    return lax.dot_general(a, b, (((1,), (1,)), ((), ())), preferred_element_type=F32)


def nn_dot(a, b):
    return jnp.dot(a, b, preferred_element_type=F32)


def full_spec(shape):
    zeros = (0,) * len(shape)
    return pl.BlockSpec(shape, lambda *_: zeros)


def params(mib):
    return pltpu.CompilerParams(vmem_limit_bytes=mib * MIB)


def tiled_scratch(rows, cols):
    return pltpu.VMEM((cols // LANES, rows, LANES), F32)


def store_strided(held, first, stride, values):
    rows = values.shape[0]
    for t in range(held.shape[0]):
        held[t, pl.ds(first, rows, stride=stride), :] = values[:, t * LANES : (t + 1) * LANES]


def load_strided(held, first, stride, rows):
    parts = [held[t, pl.ds(first, rows, stride=stride), :] for t in range(held.shape[0])]
    return jnp.concatenate(parts, axis=1)


def joined_tiles(held):
    return jnp.concatenate([held[t] for t in range(held.shape[0])], axis=1)


def head_lanes(length):
    lane = lax.broadcasted_iota(jnp.int32, (length, LANES), 1) // HEAD_CHANNELS
    return [
        jnp.where(lane == t, 1.0, 0.0).astype(BF16) for t in range(LANES // HEAD_CHANNELS)
    ]


def attend_block(query, key, value, live, lanes, bias_of):
    pieces = []
    per_tile = LANES // HEAD_CHANNELS
    for tile in range(query.shape[1] // LANES):
        cut = slice(tile * LANES, (tile + 1) * LANES)
        query_t, key_t = query[:, cut], key[:, cut]
        value_t = value[:, cut] * live
        total = None
        for t in range(per_tile):
            scores = nt_dot(query_t * lanes[t], key_t)
            if bias_of is not None:
                scores = scores + bias_of(tile * per_tile + t)
            raised = jnp.exp2(scores).astype(BF16)
            side = jnp.concatenate([value_t * lanes[t], live * lanes[t]], axis=1)
            part = nn_dot(raised, side)
            total = part if total is None else total + part
        pieces.append(total[:, :LANES] / total[:, LANES:])
    return jnp.concatenate(pieces, axis=1)


def project(normed, weight_ref):
    scale = LOG2E / math.sqrt(HEAD_CHANNELS)
    query = (nn_dot(normed, weight_ref[0]) * scale).astype(BF16)
    key = nn_dot(normed, weight_ref[1]).astype(BF16)
    value = (nn_dot(normed, weight_ref[2]) * VALUE_SCALE).astype(BF16)
    gate = jax.nn.sigmoid(nn_dot(normed, weight_ref[3])) * (1.0 / VALUE_SCALE)
    return query, key, value, gate


def bias_kernel(pair_ref, weight_ref, out_ref, held):
    rows, cols, width = pair_ref.shape
    normed = layer_normalize(pair_ref[...].astype(F32)).astype(BF16).reshape(rows * cols, width)
    bias = nt_dot(weight_ref[...], normed)[:ATTN_HEAD_COUNT] * LOG2E
    for i in range(rows):
        store_strided(held, i, rows, bias[:, i * cols : (i + 1) * cols])
    out_ref[...] = joined_tiles(held).astype(BF16)


def pair_bias_block(pair_rep, bias_weight):
    rows, cols, width = pair_rep.shape
    weight = jnp.pad(bias_weight.T, ((0, 16 - ATTN_HEAD_COUNT), (0, 0)))
    out = jax.ShapeDtypeStruct((ATTN_HEAD_COUNT * rows, cols), BF16)
    return pl.pallas_call(
        bias_kernel,
        out_shape=out,
        scratch_shapes=[tiled_scratch(*out.shape)],
        compiler_params=params(32),
        name="pair_bias",
    )(pair_rep, weight)


def row_project_kernel(x_ref, weight_ref, q_ref, k_ref, v_ref, g_ref):
    for s in range(x_ref.shape[0]):
        normed = layer_normalize(x_ref[s].astype(F32)).astype(BF16)
        q_ref[s], k_ref[s], v_ref[s], g_ref[s] = project(normed, weight_ref)


def row_project(alignment, weight):
    seqs, length, width = alignment.shape
    step = 2
    block = pl.BlockSpec((step, length, width), lambda i: (i, 0, 0))
    small = jax.ShapeDtypeStruct(alignment.shape, BF16)
    return pl.pallas_call(
        row_project_kernel,
        grid=(seqs // step,),
        in_specs=[block, full_spec(weight.shape)],
        out_specs=[block] * 4,
        out_shape=[small, small, small, jax.ShapeDtypeStruct(alignment.shape, F32)],
        compiler_params=params(48),
        name="row_project",
    )(alignment, weight)


def row_attend_kernel(group, step, me_ref, x_ref, q_ref, k_ref, v_ref, g_ref, live_ref, out_w_ref, *rest):
    bias_refs, out_ref, bias_all = rest[:group], rest[group], rest[group + 1]
    heads, length, _ = bias_all.shape
    outer = bias_refs[0].shape[0]

    @pl.when(pl.program_id(0) == 0)
    def _():
        here = me_ref[0]
        for k in range(group):
            for z in range(outer):
                rows = bias_refs[k].shape[1] // heads
                owner = here ^ (z * group + k)
                at = pl.ds(pl.multiple_of(owner * rows, rows), rows)
                block = bias_refs[k][z].astype(F32).reshape(heads, rows, length)
                bias_all[:, at, :] = block

    lanes = head_lanes(length)
    results = []
    for s in range(step):
        heads_out = attend_block(
            q_ref[s], k_ref[s], v_ref[s], live_ref[s], lanes, lambda h: bias_all[h]
        )
        heads_out = (heads_out * g_ref[s]).astype(BF16)
        total = x_ref[s].astype(F32) + nn_dot(heads_out, out_w_ref[...])
        parts, rows = out_ref.shape[0], out_ref.shape[1]
        results.append(total.reshape(parts, 1, rows // step, total.shape[1]))
    joined = jnp.concatenate(results, axis=1)
    out_ref[...] = joined.reshape(out_ref.shape).astype(BF16)


def row_attend(me, alignment, projected, live, out_weight, bias_parts, dap_count):
    seqs, length, width = alignment.shape
    rows = length // dap_count
    step = 2
    block = pl.BlockSpec((step, length, width), lambda i: (i, 0, 0))
    return pl.pallas_call(
        functools.partial(row_attend_kernel, len(bias_parts), step),
        grid=(seqs // step,),
        in_specs=[pl.BlockSpec(memory_space=pltpu.SMEM)]
        + [block] * 5
        + [pl.BlockSpec((step, length, LANES), lambda i: (i, 0, 0)), full_spec(out_weight.shape)]
        + [full_spec(b.shape) for b in bias_parts],
        out_specs=pl.BlockSpec((dap_count, step * rows, width), lambda i: (0, i, 0)),
        out_shape=jax.ShapeDtypeStruct((dap_count, seqs * rows, width), BF16),
        scratch_shapes=[pltpu.VMEM((ATTN_HEAD_COUNT, length, length), F32)],
        compiler_params=params(56),
        name="row_attend",
    )(me, alignment, *projected, live, out_weight, *bias_parts)


def column_kernel(
    items, x_ref, live_ref, mask_ref, weight_ref, out_w_ref, factor_ref,
    out_ref, left_ref, right_ref, held, right_held,
):
    step = pl.program_id(0)
    total_rows = held.shape[1]
    length = total_rows // items

    @pl.when(step == 0)
    def _():
        for t in range(held.shape[0]):
            part = x_ref[:, :, t * LANES : (t + 1) * LANES].astype(F32)
            held[t] = part.reshape(total_rows, LANES)

    lanes = head_lanes(length)
    current = load_strided(held, step, items, length)
    normed = layer_normalize(current).astype(BF16)
    query, key, value, gate = project(normed, weight_ref)
    heads_out = attend_block(query, key, value, live_ref[0], lanes, None)
    heads_out = (heads_out * gate).astype(BF16)
    updated = (current + nn_dot(heads_out, out_w_ref[...])).astype(BF16).astype(F32)
    store_strided(held, step, items, updated)
    normed = layer_normalize(updated).astype(BF16)
    factors = nt_dot(factor_ref[...], normed) * mask_ref[pl.ds(step, 1), :]
    left_at = pl.ds(pl.multiple_of(step * FACTOR_CHANNELS, FACTOR_CHANNELS), FACTOR_CHANNELS)
    left_ref[left_at, :] = factors[:FACTOR_CHANNELS].astype(BF16)
    store_strided(right_held, step, items, factors[FACTOR_CHANNELS:])

    @pl.when(step == items - 1)
    def _():
        for t in range(held.shape[0]):
            part = held[t].reshape(out_ref.shape[:2] + (LANES,))
            out_ref[:, :, t * LANES : (t + 1) * LANES] = part.astype(BF16)
        right_ref[...] = joined_tiles(right_held).astype(BF16)


def column_attend(moved, live, mask_rows, weight, out_weight, factor_weight, items):
    width = moved.shape[2]
    total_rows = moved.shape[0] * moved.shape[1]
    length = total_rows // items
    factor_t = factor_weight.T
    side = jax.ShapeDtypeStruct((items * FACTOR_CHANNELS, length), BF16)
    out = jax.ShapeDtypeStruct((length, items, width), BF16)
    return pl.pallas_call(
        functools.partial(column_kernel, items),
        grid=(items,),
        in_specs=[
            full_spec(moved.shape),
            pl.BlockSpec((1, length, LANES), lambda i: (i, 0, 0)),
            full_spec(mask_rows.shape),
            full_spec(weight.shape),
            full_spec(out_weight.shape),
            full_spec(factor_t.shape),
        ],
        out_specs=[full_spec(out.shape), full_spec(side.shape), full_spec(side.shape)],
        out_shape=[out, side, side],
        scratch_shapes=[tiled_scratch(total_rows, width), tiled_scratch(*side.shape)],
        compiler_params=params(56),
        name="column_attend",
    )(moved, live, mask_rows, weight, out_weight, factor_t)


def outer_kernel(group, outer, items, *refs):
    lefts, rights = refs[:group], refs[group : group + outer]
    weight_ref = refs[group + outer]
    outs = refs[group + outer + 1 : 2 * group + outer + 1]
    held = refs[-1]
    feat = FACTOR_CHANNELS
    quad = LANES // feat
    tiles = items * feat // LANES
    cols = outer * items
    right = jnp.concatenate([r[...] for r in rights], axis=0)
    for k in range(group):
        sums = nt_dot(right, lefts[k][...])
        sums = sums.reshape(outer, feat, items, sums.shape[1])
        sums = jnp.transpose(sums, (1, 0, 2, 3)).reshape(feat, cols, sums.shape[3]).astype(BF16)
        for t in range(tiles):
            at = slice((k * tiles + t) * cols, (k * tiles + t + 1) * cols)
            for e in range(feat):
                held[at, e * LANES : (e + 1) * LANES] = sums[e, :, t * LANES : (t + 1) * LANES]
    update = nn_dot(held[...], weight_ref[...])
    width = update.shape[1] // quad
    for k in range(group):
        for t in range(tiles):
            rows = update[(k * tiles + t) * cols : (k * tiles + t + 1) * cols]
            for i in range(quad):
                outs[k][t * quad + i] = rows[:, i * width : (i + 1) * width].astype(BF16)


def outer_product(lefts, rights, weight, items):
    group, outer = len(lefts), len(rights)
    cols = outer * items
    width = weight.shape[1] * FACTOR_CHANNELS // LANES
    out = jax.ShapeDtypeStruct((items, cols, width), BF16)
    tiles = items * FACTOR_CHANNELS // LANES
    return pl.pallas_call(
        functools.partial(outer_kernel, group, outer, items),
        out_shape=[out] * group,
        scratch_shapes=[pltpu.VMEM((group * tiles * cols, weight.shape[0]), BF16)],
        compiler_params=params(56),
        name="outer_product",
    )(*lefts, *rights, weight)


def finish_kernel(group, outer, items, me_ref, pair_ref, scale_ref, *refs):
    parts, out_ref = refs[:group], refs[group]
    here = me_ref[0]
    odd = (here & 1) == 1
    for pairing in range(group // 2):
        for i in range(items):
            first = parts[2 * pairing][i].astype(F32)
            second = parts[2 * pairing + 1][i].astype(F32)
            low = jnp.where(odd, second, first)
            high = jnp.where(odd, first, second)
            for z in range(outer):
                owner = here ^ (z * group + 2 * pairing)
                start = pl.multiple_of((owner >> 1) * (2 * items), 2 * items)
                at = pl.ds(start, 2 * items)
                cut = slice(z * items, (z + 1) * items)
                update = jnp.concatenate([low[cut], high[cut]], axis=0)
                update = update * scale_ref[at, i : i + 1]
                out_ref[i, at, :] = (pair_ref[i, at, :].astype(F32) + update).astype(BF16)


def finish(me, pair_rep, scale, parts, outer):
    items = pair_rep.shape[0]
    return pl.pallas_call(
        functools.partial(finish_kernel, len(parts), outer, items),
        in_specs=[pl.BlockSpec(memory_space=pltpu.SMEM), full_spec(pair_rep.shape), full_spec(scale.shape)]
        + [full_spec(p.shape) for p in parts],
        out_specs=full_spec(pair_rep.shape),
        out_shape=jax.ShapeDtypeStruct(pair_rep.shape, BF16),
        compiler_params=params(48),
        name="finish",
    )(me, pair_rep, scale, *parts)


def exchange(block, count, offset):
    pairs = [(i, i ^ offset) for i in range(count)]
    return lax.ppermute(block, "dap", pairs)


def per_device_fast(
    alignment,
    pair_rep,
    align_mask,
    residue_mask,
    bias_weight,
    row_proj_weight,
    row_out_weight,
    column_proj_weight,
    column_out_weight,
    outer_factor_weight,
    outer_out,
):
    dap_count = lax.axis_size("dap")
    group = inner_size(dap_count)
    outer = dap_count // group
    dap_index = lax.axis_index("dap")
    me = jnp.reshape(dap_index, (1,)).astype(jnp.int32)
    seq_dev = alignment.shape[0]
    items = pair_rep.shape[0]
    width = alignment.shape[2]
    total_seqs, total_res = align_mask.shape

    bias = pair_bias_block(pair_rep, bias_weight)
    column = [bias] + [exchange(bias, dap_count, z * group) for z in range(1, outer)]
    projected = row_project(alignment, row_proj_weight)
    column = jnp.stack(column)
    bias_parts = [column] + [exchange(column, dap_count, k) for k in range(1, group)]

    mask = align_mask.astype(F32)
    own_seqs = lax.dynamic_slice_in_dim(align_mask, dap_index * seq_dev, seq_dev, 0)
    own_res = lax.dynamic_slice_in_dim(align_mask, dap_index * items, items, 1)
    row_live = jnp.broadcast_to(own_seqs.astype(BF16)[:, :, None], (seq_dev, total_res, LANES))
    col_live = jnp.broadcast_to(own_res.T.astype(BF16)[:, :, None], (items, total_seqs, LANES))
    counts = jnp.einsum(
        "si,sj->ji", own_res.astype(BF16), mask.astype(BF16), preferred_element_type=F32
    )
    res_float = residue_mask.astype(F32)
    live_rows = lax.dynamic_slice_in_dim(res_float, dap_index * items, items, 0)
    scale = live_rows[None, :] * res_float[:, None] / (counts + count_eps)

    quad = LANES // FACTOR_CHANNELS
    weight = outer_out.reshape(FACTOR_CHANNELS, FACTOR_CHANNELS, -1).swapaxes(0, 1)
    spread = jnp.eye(quad, dtype=BF16)[None, :, None, :, None] * weight[:, None, :, None, :]
    spread = spread.reshape(FACTOR_CHANNELS * LANES, quad * weight.shape[2])

    row_out = row_attend(me, alignment, projected, row_live, row_out_weight, bias_parts, dap_count)
    moved = lax.all_to_all(row_out, "dap", split_axis=0, concat_axis=0, tiled=True)
    updated, left, right = column_attend(
        moved,
        col_live,
        own_res.T.astype(F32),
        column_proj_weight,
        column_out_weight,
        outer_factor_weight,
        items,
    )
    rights = [right] + [exchange(right, dap_count, z * group) for z in range(1, outer)]
    lefts = [left] + [exchange(left, dap_count, k) for k in range(1, group)]
    parts = outer_product(lefts, rights, spread, items)
    parts = [parts[0]] + [exchange(parts[k], dap_count, k) for k in range(1, group)]
    pair_out = finish(me, pair_rep, scale, parts, outer)
    return updated, pair_out


def inner_size(count):
    size = 1
    while 2 * size * size < count * 2 and count % (2 * size) == 0:
        size *= 2
    return size


def solution(mesh):
    placed = (
        P("dap", None, None),
        P("dap", "branch", None),
        P(),
        P(),
        P(),
        P(None, None, "branch"),
        P(),
        P(None, None, "branch"),
        P(),
        P(),
        P(),
    )
    count = mesh.shape["dap"]
    whole_heads = mesh.shape["branch"] == 1 and count & (count - 1) == 0

    def per_device(*operands):
        alignment, pair_rep = operands[0], operands[1]
        tile = 8
        fits = whole_heads and alignment.shape[0] == tile and pair_rep.shape[0] == tile
        return (per_device_fast if fits else per_device_general)(*operands)

    return jax.shard_map(
        per_device,
        mesh=mesh,
        in_specs=placed,
        out_specs=(P(None, "dap", None), P("dap", "branch", None)),
        check_vma=False,
    )
```

```python
import functools
import math

import jax
import jax.numpy as jnp
from jax import lax
from jax.experimental import pallas as pl
from jax.experimental.pallas import tpu as pltpu
from jax.sharding import PartitionSpec as P

ATTN_HEAD_COUNT = 8
HEAD_CHANNELS = 32
FACTOR_CHANNELS = 32


norm_eps = 1e-05
count_eps = 0.001


def layer_normalize(values):
    centre = jnp.mean(values, axis=-1, keepdims=True)
    centred = values - centre
    spread = jnp.mean(centred * centred, axis=-1, keepdims=True)
    return centred * lax.rsqrt(spread + norm_eps)


def attend_heads(inputs, key_mask, proj_weight, out_weight, score_bias):
    batch = inputs.shape[0]
    length = inputs.shape[1]
    local_width = proj_weight.shape[2]
    local_heads = local_width // HEAD_CHANNELS
    normed = layer_normalize(inputs.astype(jnp.float32)).astype(jnp.bfloat16)
    projected = jnp.einsum("blc,kcd->kbld", normed, proj_weight, preferred_element_type=jnp.float32)
    triple = (
        projected[:3].astype(jnp.bfloat16).reshape(3, batch, length, local_heads, HEAD_CHANNELS)
    )
    gating = jax.nn.sigmoid(projected[3])

    def attend_one(operands):
        queries, key_rows, value_rows, mask_row = operands
        scores = jnp.einsum(
            "ihd,jhd->hij", queries, key_rows, preferred_element_type=jnp.float32
        ) / math.sqrt(HEAD_CHANNELS)
        if score_bias is not None:
            scores = scores + score_bias.astype(jnp.float32)
        raised = jnp.exp(scores) * mask_row[None, None, :]
        weights = (raised / jnp.sum(raised, axis=-1, keepdims=True)).astype(jnp.bfloat16)
        return jnp.einsum("hij,jhd->ihd", weights, value_rows, preferred_element_type=jnp.float32)

    attended_rows = lax.map(attend_one, (triple[0], triple[1], triple[2], key_mask))
    heads_out = (attended_rows.reshape(batch, length, local_width) * gating).astype(jnp.bfloat16)
    gathered = lax.all_gather(heads_out, "branch", axis=2, tiled=True)
    update = jnp.einsum("blf,fc->blc", gathered, out_weight, preferred_element_type=jnp.float32)
    return (inputs.astype(jnp.float32) + update).astype(jnp.bfloat16)


def per_device_general(
    alignment,
    pair_rep,
    align_mask,
    residue_mask,
    bias_weight,
    row_proj_weight,
    row_out_weight,
    column_proj_weight,
    column_out_weight,
    outer_factor_weight,
    outer_out,
):
    branch_count = lax.axis_size("branch")
    dap_count = lax.axis_size("dap")
    branch_index = lax.axis_index("branch")
    dap_index = lax.axis_index("dap")
    seq_dev = alignment.shape[0]
    res_dev = pair_rep.shape[0]
    quarter = pair_rep.shape[1]
    total_seqs = align_mask.shape[0]
    local_heads = ATTN_HEAD_COUNT // branch_count
    float_mask = align_mask.astype(jnp.float32)
    res_float = residue_mask.astype(jnp.float32)
    pair_normed = layer_normalize(pair_rep.astype(jnp.float32)).astype(jnp.bfloat16)
    bias_block = jnp.einsum(
        "ijc,ch->hij", pair_normed, bias_weight, preferred_element_type=jnp.float32
    ).astype(jnp.bfloat16)
    bias_wide = lax.all_gather(bias_block, "branch", axis=2, tiled=True)
    bias_full = lax.all_gather(bias_wide, "dap", axis=1, tiled=True)
    pair_score_bias = lax.dynamic_slice_in_dim(
        bias_full, branch_index * local_heads, local_heads, 0
    )
    sequence_row_mask = lax.dynamic_slice_in_dim(float_mask, dap_index * seq_dev, seq_dev, 0)
    row_alignment = attend_heads(
        alignment, sequence_row_mask, row_proj_weight, row_out_weight, pair_score_bias
    )
    send_mask = sequence_row_mask.astype(jnp.bfloat16)
    blocked_rows = row_alignment.reshape(seq_dev, dap_count, res_dev, row_alignment.shape[2])
    blocked_mask = send_mask.reshape(seq_dev, dap_count, res_dev)
    moved_rows = lax.all_to_all(blocked_rows, "dap", split_axis=1, concat_axis=0, tiled=True)
    moved_mask = lax.all_to_all(blocked_mask, "dap", split_axis=1, concat_axis=0, tiled=True)
    seq_total = moved_rows.shape[0]
    items = moved_rows.shape[2]
    flat_rows = moved_rows.reshape(seq_total, items, moved_rows.shape[3])
    flat_mask = moved_mask.reshape(seq_total, items)
    transposed_rows = jnp.swapaxes(flat_rows, 0, 1)
    key_mask = jnp.swapaxes(flat_mask, 0, 1).astype(jnp.float32)
    attended_rows = attend_heads(
        transposed_rows, key_mask, column_proj_weight, column_out_weight, None
    )
    column_alignment = jnp.swapaxes(attended_rows, 0, 1)
    outer_mean_normed = layer_normalize(column_alignment.astype(jnp.float32)).astype(jnp.bfloat16)
    projected = jnp.einsum(
        "src,ce->sre", outer_mean_normed, outer_factor_weight, preferred_element_type=jnp.float32
    )
    factor_pairs = (projected * flat_mask.astype(jnp.float32)[:, :, None]).astype(jnp.bfloat16)
    column_alignment, factor_pairs = (column_alignment, factor_pairs)
    blocked_out = column_alignment.reshape(seq_total, 1, items, column_alignment.shape[2])
    blocked_factors = factor_pairs.reshape(seq_total, 1, items, factor_pairs.shape[2])
    updated_alignment = blocked_out.reshape(total_seqs, res_dev, blocked_out.shape[3])
    factor_pairs = blocked_factors.reshape(total_seqs, res_dev, blocked_factors.shape[3])
    left_side = factor_pairs[:, :, :FACTOR_CHANNELS]
    right_local = factor_pairs[:, :, FACTOR_CHANNELS:]
    col_start = branch_index * quarter
    row_start = dap_index * res_dev
    mask_rows = lax.dynamic_slice_in_dim(align_mask, row_start, res_dev, 1).astype(jnp.bfloat16)
    mask_cols = lax.dynamic_slice_in_dim(align_mask, col_start, quarter, 1).astype(jnp.bfloat16)
    counts = jnp.einsum("si,sj->ij", mask_rows, mask_cols, preferred_element_type=jnp.float32)
    live_rows = lax.dynamic_slice_in_dim(res_float, row_start, res_dev, 0)
    live_cols = lax.dynamic_slice_in_dim(res_float, col_start, quarter, 0)
    outer_weight = outer_out.astype(jnp.float32)
    right_all = lax.all_gather(right_local, "dap", axis=1, tiled=True)
    right_mine = lax.dynamic_slice_in_dim(right_all, col_start, quarter, 1)
    outer_sums = jnp.einsum(
        "sic,sje->ijce", left_side, right_mine, preferred_element_type=jnp.float32
    )
    outer_sums = outer_sums.reshape(res_dev, quarter, FACTOR_CHANNELS * FACTOR_CHANNELS)
    update = jnp.einsum("ijf,fz->ijz", outer_sums, outer_weight, precision=lax.Precision.HIGHEST)
    live = live_rows[:, None] * live_cols[None, :]
    update = update / (counts[:, :, None] + count_eps) * live[:, :, None]
    pair_out = (pair_rep.astype(jnp.float32) + update).astype(jnp.bfloat16)
    return (updated_alignment, pair_out)


LANES = 128
LOG2E = math.log2(math.e)
VALUE_SCALE = 1.0 / 128.0
BF16 = jnp.bfloat16
F32 = jnp.float32
MIB = 1024 * 1024


def nt_dot(a, b):
    return lax.dot_general(a, b, (((1,), (1,)), ((), ())), preferred_element_type=F32)


def nn_dot(a, b):
    return jnp.dot(a, b, preferred_element_type=F32)


def full_spec(shape):
    zeros = (0,) * len(shape)
    return pl.BlockSpec(shape, lambda *_: zeros)


def params(mib):
    return pltpu.CompilerParams(vmem_limit_bytes=mib * MIB)


def tiled_scratch(rows, cols):
    return pltpu.VMEM((cols // LANES, rows, LANES), F32)


def store_strided(held, first, stride, values):
    rows = values.shape[0]
    for t in range(held.shape[0]):
        held[t, pl.ds(first, rows, stride=stride), :] = values[:, t * LANES : (t + 1) * LANES]


def load_strided(held, first, stride, rows):
    parts = [held[t, pl.ds(first, rows, stride=stride), :] for t in range(held.shape[0])]
    return jnp.concatenate(parts, axis=1)


def joined_tiles(held):
    return jnp.concatenate([held[t] for t in range(held.shape[0])], axis=1)


def head_lanes(length):
    lane = lax.broadcasted_iota(jnp.int32, (length, LANES), 1) // HEAD_CHANNELS
    return [
        jnp.where(lane == t, 1.0, 0.0).astype(BF16) for t in range(LANES // HEAD_CHANNELS)
    ]


def attend_block(query, key, value, live, lanes, bias_of):
    pieces = []
    per_tile = LANES // HEAD_CHANNELS
    length = query.shape[0]
    for tile in range(query.shape[1] // LANES):
        cut = slice(tile * LANES, (tile + 1) * LANES)
        query_t, key_t = query[:, cut], key[:, cut]
        value_t = value[:, cut] * live
        if bias_of is None:
            all_scores = [nt_dot(query_t * lanes[t], key_t) for t in range(per_tile)]
        else:
            stacked = jnp.concatenate([query_t * lanes[t] for t in range(per_tile)], axis=0)
            stacked = nt_dot(stacked, key_t)
            all_scores = [
                stacked[t * length : (t + 1) * length] + bias_of(tile * per_tile + t)
                for t in range(per_tile)
            ]
        raised = [jnp.exp2(scores).astype(BF16) for scores in all_scores]
        sides = [
            jnp.concatenate([value_t * lanes[t], live * lanes[t]], axis=1) for t in range(per_tile)
        ]
        if bias_of is None:
            total = sum(nn_dot(r, s) for r, s in zip(raised, sides))
        else:
            total = nn_dot(jnp.concatenate(raised, axis=1), jnp.concatenate(sides, axis=0))
        pieces.append(total[:, :LANES] / total[:, LANES:])
    return jnp.concatenate(pieces, axis=1)


def project(normed, weight_ref):
    scale = LOG2E / math.sqrt(HEAD_CHANNELS)
    query = (nn_dot(normed, weight_ref[0]) * scale).astype(BF16)
    key = nn_dot(normed, weight_ref[1]).astype(BF16)
    value = (nn_dot(normed, weight_ref[2]) * VALUE_SCALE).astype(BF16)
    gate = jax.nn.sigmoid(nn_dot(normed, weight_ref[3])) * (1.0 / VALUE_SCALE)
    return query, key, value, gate


def bias_kernel(pair_ref, weight_ref, out_ref, held):
    rows, cols, width = pair_ref.shape
    normed = layer_normalize(pair_ref[...].astype(F32)).astype(BF16).reshape(rows * cols, width)
    bias = nt_dot(weight_ref[...], normed)[:ATTN_HEAD_COUNT] * LOG2E
    for i in range(rows):
        store_strided(held, i, rows, bias[:, i * cols : (i + 1) * cols])
    out_ref[...] = joined_tiles(held).astype(BF16)


def pair_bias_block(pair_rep, bias_weight):
    rows, cols, width = pair_rep.shape
    weight = jnp.pad(bias_weight.T, ((0, 16 - ATTN_HEAD_COUNT), (0, 0)))
    out = jax.ShapeDtypeStruct((ATTN_HEAD_COUNT * rows, cols), BF16)
    return pl.pallas_call(
        bias_kernel,
        out_shape=out,
        scratch_shapes=[tiled_scratch(*out.shape)],
        compiler_params=params(12),
        name="pair_bias",
    )(pair_rep, weight)


def row_project_kernel(x_ref, weight_ref, q_ref, k_ref, v_ref, g_ref):
    for s in range(x_ref.shape[0]):
        normed = layer_normalize(x_ref[s].astype(F32)).astype(BF16)
        q_ref[s], k_ref[s], v_ref[s], g_ref[s] = project(normed, weight_ref)


def row_project(alignment, weight):
    seqs, length, width = alignment.shape
    step = 2
    block = pl.BlockSpec((step, length, width), lambda i: (i, 0, 0))
    small = jax.ShapeDtypeStruct(alignment.shape, BF16)
    return pl.pallas_call(
        row_project_kernel,
        grid=(seqs // step,),
        in_specs=[block, full_spec(weight.shape)],
        out_specs=[block] * 4,
        out_shape=[small, small, small, jax.ShapeDtypeStruct(alignment.shape, F32)],
        compiler_params=params(24),
        name="row_project",
    )(alignment, weight)


def row_attend_kernel(step, x_ref, q_ref, k_ref, v_ref, g_ref, live_ref, out_w_ref, bias_ref, out_ref, bias_all):
    heads, length, _ = bias_all.shape
    group, outer, block_rows, _ = bias_ref.shape
    rows = block_rows // heads

    @pl.when(pl.program_id(0) == 0)
    def _():
        for k in range(group):
            for z in range(outer):
                owner = z * group + k
                block = bias_ref[k, z].astype(F32).reshape(heads, rows, length)
                bias_all[:, owner * rows : (owner + 1) * rows, :] = block

    lanes = head_lanes(length)
    results = []
    for s in range(step):
        heads_out = attend_block(
            q_ref[s], k_ref[s], v_ref[s], live_ref[s], lanes, lambda h: bias_all[h]
        )
        heads_out = (heads_out * g_ref[s]).astype(BF16)
        total = x_ref[s].astype(F32) + nn_dot(heads_out, out_w_ref[...])
        parts, rows = out_ref.shape[0], out_ref.shape[1]
        results.append(total.reshape(parts, 1, rows // step, total.shape[1]))
    joined = jnp.concatenate(results, axis=1)
    out_ref[...] = joined.reshape(out_ref.shape).astype(BF16)


def row_attend(alignment, projected, live, out_weight, bias, dap_count):
    seqs, length, width = alignment.shape
    rows = length // dap_count
    step = 2
    block = pl.BlockSpec((step, length, width), lambda i: (i, 0, 0))
    return pl.pallas_call(
        functools.partial(row_attend_kernel, step),
        grid=(seqs // step,),
        in_specs=[block] * 5
        + [pl.BlockSpec((step, length, LANES), lambda i: (i, 0, 0)), full_spec(out_weight.shape)]
        + [full_spec(bias.shape)],
        out_specs=pl.BlockSpec((dap_count, step * rows, width), lambda i: (0, i, 0)),
        out_shape=jax.ShapeDtypeStruct((dap_count, seqs * rows, width), BF16),
        scratch_shapes=[pltpu.VMEM((ATTN_HEAD_COUNT, length, length), F32)],
        compiler_params=params(28),
        name="row_attend",
    )(alignment, *projected, live, out_weight, bias)


def column_kernel(
    items, each, x_ref, live_ref, mask_ref, weight_ref, out_w_ref, factor_ref,
    out_ref, left_ref, right_ref, held, left_held, right_held,
):
    step = pl.program_id(0)
    total_rows = held.shape[1]
    length = total_rows // items

    @pl.when(step == 0)
    def _():
        for t in range(held.shape[0]):
            part = x_ref[:, :, t * LANES : (t + 1) * LANES].astype(F32)
            held[t] = part.reshape(total_rows, LANES)

    lanes = head_lanes(length)
    for n in range(each):
        item = step * each + n
        current = load_strided(held, item, items, length)
        normed = layer_normalize(current).astype(BF16)
        query, key, value, gate = project(normed, weight_ref)
        heads_out = attend_block(query, key, value, live_ref[n], lanes, None)
        heads_out = (heads_out * gate).astype(BF16)
        updated = (current + nn_dot(heads_out, out_w_ref[...])).astype(BF16).astype(F32)
        store_strided(held, item, items, updated)
        normed = layer_normalize(updated).astype(BF16)
        factors = nt_dot(factor_ref[...], normed) * mask_ref[pl.ds(item, 1), :]
        left_at = pl.ds(pl.multiple_of(item * FACTOR_CHANNELS, FACTOR_CHANNELS), FACTOR_CHANNELS)
        left_held[left_at, :] = factors[:FACTOR_CHANNELS].astype(BF16)
        store_strided(right_held, item, items, factors[FACTOR_CHANNELS:])

    @pl.when(step == items // each - 1)
    def _():
        for t in range(held.shape[0]):
            part = held[t].reshape(out_ref.shape[:2] + (LANES,))
            out_ref[:, :, t * LANES : (t + 1) * LANES] = part.astype(BF16)
        right = joined_tiles(right_held).astype(BF16)
        for k in range(right_ref.shape[0]):
            right_ref[k] = right
        for k in range(left_ref.shape[0]):
            left_ref[k] = left_held[...]


def column_attend(moved, live, mask_rows, weight, out_weight, factor_weight, items, group, outer):
    width = moved.shape[2]
    total_rows = moved.shape[0] * moved.shape[1]
    length = total_rows // items
    factor_t = factor_weight.T
    each = 2
    side = (items * FACTOR_CHANNELS, length)
    left = jax.ShapeDtypeStruct((group,) + side, BF16)
    right = jax.ShapeDtypeStruct((outer,) + side, BF16)
    out = jax.ShapeDtypeStruct((length, items, width), BF16)
    return pl.pallas_call(
        functools.partial(column_kernel, items, each),
        grid=(items // each,),
        in_specs=[
            full_spec(moved.shape),
            pl.BlockSpec((each, length, LANES), lambda i: (i, 0, 0)),
            full_spec(mask_rows.shape),
            full_spec(weight.shape),
            full_spec(out_weight.shape),
            full_spec(factor_t.shape),
        ],
        out_specs=[full_spec(out.shape), full_spec(left.shape), full_spec(right.shape)],
        out_shape=[out, left, right],
        scratch_shapes=[tiled_scratch(total_rows, width), pltpu.VMEM(side, BF16), tiled_scratch(*side)],
        compiler_params=params(28),
        name="column_attend",
    )(moved, live, mask_rows, weight, out_weight, factor_t)


def spread_kernel(weight_ref, out_ref):
    feat = weight_ref.shape[1]
    width = weight_ref.shape[2]
    out_ref[...] = jnp.zeros_like(out_ref)
    for e in range(weight_ref.shape[0]):
        for i in range(LANES // feat):
            start = e * LANES + i * feat
            out_ref[start : start + feat, i * width : (i + 1) * width] = weight_ref[e]


def spread_weight(outer_out):
    weight = outer_out.reshape(FACTOR_CHANNELS, FACTOR_CHANNELS, -1).swapaxes(0, 1)
    quad = LANES // FACTOR_CHANNELS
    out = jax.ShapeDtypeStruct((FACTOR_CHANNELS * LANES, quad * weight.shape[2]), BF16)
    return pl.pallas_call(
        spread_kernel, out_shape=out, compiler_params=params(12), name="spread_weight"
    )(weight)


def outer_kernel(items, left_ref, right_ref, weight_ref, out_ref, held):
    group, outer = left_ref.shape[0], right_ref.shape[0]
    feat = FACTOR_CHANNELS
    quad = LANES // feat
    tiles = items * feat // LANES
    cols = outer * items
    right = right_ref[...].reshape(outer * right_ref.shape[1], right_ref.shape[2])
    for k in range(group):
        sums = nt_dot(right, left_ref[k])
        sums = sums.reshape(outer, feat, items, sums.shape[1])
        sums = jnp.transpose(sums, (1, 0, 2, 3)).reshape(feat, cols, sums.shape[3]).astype(BF16)
        for t in range(tiles):
            at = slice((k * tiles + t) * cols, (k * tiles + t + 1) * cols)
            for e in range(feat):
                held[at, e * LANES : (e + 1) * LANES] = sums[e, :, t * LANES : (t + 1) * LANES]
    update = nn_dot(held[...], weight_ref[...])
    width = update.shape[1] // quad
    for k in range(group):
        for t in range(tiles):
            rows = update[(k * tiles + t) * cols : (k * tiles + t + 1) * cols]
            for i in range(quad):
                out_ref[k, t * quad + i] = rows[:, i * width : (i + 1) * width].astype(BF16)


def outer_product(lefts, rights, weight, items):
    group, outer = lefts.shape[0], rights.shape[0]
    cols = outer * items
    width = weight.shape[1] * FACTOR_CHANNELS // LANES
    tiles = items * FACTOR_CHANNELS // LANES
    return pl.pallas_call(
        functools.partial(outer_kernel, items),
        out_shape=jax.ShapeDtypeStruct((group, items, cols, width), BF16),
        scratch_shapes=[pltpu.VMEM((group * tiles * cols, weight.shape[0]), BF16)],
        compiler_params=params(28),
        name="outer_product",
    )(lefts, rights, weight)


def finish_kernel(pair_ref, scale_ref, parts_ref, out_ref):
    group, items, cols, width = parts_ref.shape
    outer = cols // items
    for pairing in range(group // 2):
        for i in range(items):
            low = parts_ref[2 * pairing, i].astype(F32).reshape(outer, 1, items, width)
            high = parts_ref[2 * pairing + 1, i].astype(F32).reshape(outer, 1, items, width)
            both = jnp.concatenate([low, high], axis=1).reshape(outer, 2 * items, width)
            for z in range(outer):
                start = (z * group + 2 * pairing) * items
                at = slice(start, start + 2 * items)
                update = both[z] * scale_ref[at, i : i + 1]
                out_ref[i, at, :] = (pair_ref[i, at, :].astype(F32) + update).astype(BF16)


def finish(pair_rep, scale, parts):
    return pl.pallas_call(
        finish_kernel,
        out_shape=jax.ShapeDtypeStruct(pair_rep.shape, BF16),
        compiler_params=params(16),
        name="finish",
    )(pair_rep, scale, parts)


def per_device_fast(
    alignment,
    pair_rep,
    align_mask,
    residue_mask,
    bias_weight,
    row_proj_weight,
    row_out_weight,
    column_proj_weight,
    column_out_weight,
    outer_factor_weight,
    outer_out,
):
    dap_count = lax.axis_size("dap")
    group = inner_size(dap_count)
    outer = dap_count // group
    dap_index = lax.axis_index("dap")
    plane = [[z * group + k for k in range(group)] for z in range(outer)]
    line = [[z * group + k for z in range(outer)] for k in range(group)]
    seq_dev = alignment.shape[0]
    items = pair_rep.shape[0]
    width = alignment.shape[2]
    total_seqs, total_res = align_mask.shape

    bias = pair_bias_block(pair_rep, bias_weight)
    bias = lax.all_gather(bias, "dap", axis_index_groups=line)
    projected = row_project(alignment, row_proj_weight)
    bias = lax.all_gather(bias, "dap", axis_index_groups=plane)

    mask = align_mask.astype(F32)
    own_seqs = lax.dynamic_slice_in_dim(align_mask, dap_index * seq_dev, seq_dev, 0)
    own_res = lax.dynamic_slice_in_dim(align_mask, dap_index * items, items, 1)
    row_live = jnp.broadcast_to(own_seqs.astype(BF16)[:, :, None], (seq_dev, total_res, LANES))
    col_live = jnp.broadcast_to(own_res.T.astype(BF16)[:, :, None], (items, total_seqs, LANES))
    counts = jnp.einsum(
        "si,sj->ji", own_res.astype(BF16), mask.astype(BF16), preferred_element_type=F32
    )
    res_float = residue_mask.astype(F32)
    live_rows = lax.dynamic_slice_in_dim(res_float, dap_index * items, items, 0)
    scale = live_rows[None, :] * res_float[:, None] / (counts + count_eps)

    spread = spread_weight(outer_out)
    spread, scale, col_live = lax.optimization_barrier((spread, scale, col_live))

    row_out = row_attend(alignment, projected, row_live, row_out_weight, bias, dap_count)
    moved = lax.all_to_all(row_out, "dap", split_axis=0, concat_axis=0, tiled=True)
    updated, left, right = column_attend(
        moved,
        col_live,
        own_res.T.astype(F32),
        column_proj_weight,
        column_out_weight,
        outer_factor_weight,
        items,
        group,
        outer,
    )
    rights = grouped_exchange(right, line)
    lefts = grouped_exchange(left, plane)
    parts = grouped_exchange(outer_product(lefts, rights, spread, items), plane)
    pair_out = finish(pair_rep, scale, parts)
    return updated, pair_out


def grouped_exchange(blocks, groups):
    return lax.all_to_all(
        blocks, "dap", split_axis=0, concat_axis=0, tiled=True, axis_index_groups=groups
    )


def inner_size(count):
    size = 1
    while 2 * size * size < count * 2 and count % (2 * size) == 0:
        size *= 2
    return size


def solution(mesh):
    placed = (
        P("dap", None, None),
        P("dap", "branch", None),
        P(),
        P(),
        P(),
        P(None, None, "branch"),
        P(),
        P(None, None, "branch"),
        P(),
        P(),
        P(),
    )
    count = mesh.shape["dap"]
    whole_heads = mesh.shape["branch"] == 1 and count & (count - 1) == 0

    def per_device(*operands):
        alignment, pair_rep = operands[0], operands[1]
        tile = 8
        fits = whole_heads and alignment.shape[0] == tile and pair_rep.shape[0] == tile
        return (per_device_fast if fits else per_device_general)(*operands)

    return jax.shard_map(
        per_device,
        mesh=mesh,
        in_specs=placed,
        out_specs=(P(None, "dap", None), P("dap", "branch", None)),
        check_vma=False,
    )
```

```python
import functools
import math

import jax
import jax.numpy as jnp
from jax import lax
from jax.experimental import pallas as pl
from jax.experimental.pallas import tpu as pltpu
from jax.sharding import PartitionSpec as P

ATTN_HEAD_COUNT = 8
HEAD_CHANNELS = 32
FACTOR_CHANNELS = 32


norm_eps = 1e-05
count_eps = 0.001


def layer_normalize(values):
    centre = jnp.mean(values, axis=-1, keepdims=True)
    centred = values - centre
    spread = jnp.mean(centred * centred, axis=-1, keepdims=True)
    return centred * lax.rsqrt(spread + norm_eps)


def attend_heads(inputs, key_mask, proj_weight, out_weight, score_bias):
    batch = inputs.shape[0]
    length = inputs.shape[1]
    local_width = proj_weight.shape[2]
    local_heads = local_width // HEAD_CHANNELS
    normed = layer_normalize(inputs.astype(jnp.float32)).astype(jnp.bfloat16)
    projected = jnp.einsum("blc,kcd->kbld", normed, proj_weight, preferred_element_type=jnp.float32)
    triple = (
        projected[:3].astype(jnp.bfloat16).reshape(3, batch, length, local_heads, HEAD_CHANNELS)
    )
    gating = jax.nn.sigmoid(projected[3])

    def attend_one(operands):
        queries, key_rows, value_rows, mask_row = operands
        scores = jnp.einsum(
            "ihd,jhd->hij", queries, key_rows, preferred_element_type=jnp.float32
        ) / math.sqrt(HEAD_CHANNELS)
        if score_bias is not None:
            scores = scores + score_bias.astype(jnp.float32)
        raised = jnp.exp(scores) * mask_row[None, None, :]
        weights = (raised / jnp.sum(raised, axis=-1, keepdims=True)).astype(jnp.bfloat16)
        return jnp.einsum("hij,jhd->ihd", weights, value_rows, preferred_element_type=jnp.float32)

    attended_rows = lax.map(attend_one, (triple[0], triple[1], triple[2], key_mask))
    heads_out = (attended_rows.reshape(batch, length, local_width) * gating).astype(jnp.bfloat16)
    gathered = lax.all_gather(heads_out, "branch", axis=2, tiled=True)
    update = jnp.einsum("blf,fc->blc", gathered, out_weight, preferred_element_type=jnp.float32)
    return (inputs.astype(jnp.float32) + update).astype(jnp.bfloat16)


def per_device_general(
    alignment,
    pair_rep,
    align_mask,
    residue_mask,
    bias_weight,
    row_proj_weight,
    row_out_weight,
    column_proj_weight,
    column_out_weight,
    outer_factor_weight,
    outer_out,
):
    branch_count = lax.axis_size("branch")
    dap_count = lax.axis_size("dap")
    branch_index = lax.axis_index("branch")
    dap_index = lax.axis_index("dap")
    seq_dev = alignment.shape[0]
    res_dev = pair_rep.shape[0]
    quarter = pair_rep.shape[1]
    total_seqs = align_mask.shape[0]
    local_heads = ATTN_HEAD_COUNT // branch_count
    float_mask = align_mask.astype(jnp.float32)
    res_float = residue_mask.astype(jnp.float32)
    pair_normed = layer_normalize(pair_rep.astype(jnp.float32)).astype(jnp.bfloat16)
    bias_block = jnp.einsum(
        "ijc,ch->hij", pair_normed, bias_weight, preferred_element_type=jnp.float32
    ).astype(jnp.bfloat16)
    bias_wide = lax.all_gather(bias_block, "branch", axis=2, tiled=True)
    bias_full = lax.all_gather(bias_wide, "dap", axis=1, tiled=True)
    pair_score_bias = lax.dynamic_slice_in_dim(
        bias_full, branch_index * local_heads, local_heads, 0
    )
    sequence_row_mask = lax.dynamic_slice_in_dim(float_mask, dap_index * seq_dev, seq_dev, 0)
    row_alignment = attend_heads(
        alignment, sequence_row_mask, row_proj_weight, row_out_weight, pair_score_bias
    )
    send_mask = sequence_row_mask.astype(jnp.bfloat16)
    blocked_rows = row_alignment.reshape(seq_dev, dap_count, res_dev, row_alignment.shape[2])
    blocked_mask = send_mask.reshape(seq_dev, dap_count, res_dev)
    moved_rows = lax.all_to_all(blocked_rows, "dap", split_axis=1, concat_axis=0, tiled=True)
    moved_mask = lax.all_to_all(blocked_mask, "dap", split_axis=1, concat_axis=0, tiled=True)
    seq_total = moved_rows.shape[0]
    items = moved_rows.shape[2]
    flat_rows = moved_rows.reshape(seq_total, items, moved_rows.shape[3])
    flat_mask = moved_mask.reshape(seq_total, items)
    transposed_rows = jnp.swapaxes(flat_rows, 0, 1)
    key_mask = jnp.swapaxes(flat_mask, 0, 1).astype(jnp.float32)
    attended_rows = attend_heads(
        transposed_rows, key_mask, column_proj_weight, column_out_weight, None
    )
    column_alignment = jnp.swapaxes(attended_rows, 0, 1)
    outer_mean_normed = layer_normalize(column_alignment.astype(jnp.float32)).astype(jnp.bfloat16)
    projected = jnp.einsum(
        "src,ce->sre", outer_mean_normed, outer_factor_weight, preferred_element_type=jnp.float32
    )
    factor_pairs = (projected * flat_mask.astype(jnp.float32)[:, :, None]).astype(jnp.bfloat16)
    column_alignment, factor_pairs = (column_alignment, factor_pairs)
    blocked_out = column_alignment.reshape(seq_total, 1, items, column_alignment.shape[2])
    blocked_factors = factor_pairs.reshape(seq_total, 1, items, factor_pairs.shape[2])
    updated_alignment = blocked_out.reshape(total_seqs, res_dev, blocked_out.shape[3])
    factor_pairs = blocked_factors.reshape(total_seqs, res_dev, blocked_factors.shape[3])
    left_side = factor_pairs[:, :, :FACTOR_CHANNELS]
    right_local = factor_pairs[:, :, FACTOR_CHANNELS:]
    col_start = branch_index * quarter
    row_start = dap_index * res_dev
    mask_rows = lax.dynamic_slice_in_dim(align_mask, row_start, res_dev, 1).astype(jnp.bfloat16)
    mask_cols = lax.dynamic_slice_in_dim(align_mask, col_start, quarter, 1).astype(jnp.bfloat16)
    counts = jnp.einsum("si,sj->ij", mask_rows, mask_cols, preferred_element_type=jnp.float32)
    live_rows = lax.dynamic_slice_in_dim(res_float, row_start, res_dev, 0)
    live_cols = lax.dynamic_slice_in_dim(res_float, col_start, quarter, 0)
    outer_weight = outer_out.astype(jnp.float32)
    right_all = lax.all_gather(right_local, "dap", axis=1, tiled=True)
    right_mine = lax.dynamic_slice_in_dim(right_all, col_start, quarter, 1)
    outer_sums = jnp.einsum(
        "sic,sje->ijce", left_side, right_mine, preferred_element_type=jnp.float32
    )
    outer_sums = outer_sums.reshape(res_dev, quarter, FACTOR_CHANNELS * FACTOR_CHANNELS)
    update = jnp.einsum("ijf,fz->ijz", outer_sums, outer_weight, precision=lax.Precision.HIGHEST)
    live = live_rows[:, None] * live_cols[None, :]
    update = update / (counts[:, :, None] + count_eps) * live[:, :, None]
    pair_out = (pair_rep.astype(jnp.float32) + update).astype(jnp.bfloat16)
    return (updated_alignment, pair_out)


LANES = 128
LOG2E = math.log2(math.e)
VALUE_SCALE = 1.0 / 128.0
BF16 = jnp.bfloat16
F32 = jnp.float32
MIB = 1024 * 1024


def nt_dot(a, b):
    return lax.dot_general(a, b, (((1,), (1,)), ((), ())), preferred_element_type=F32)


def nn_dot(a, b):
    return jnp.dot(a, b, preferred_element_type=F32)


def full_spec(shape):
    zeros = (0,) * len(shape)
    return pl.BlockSpec(shape, lambda *_: zeros)


def params(mib):
    return pltpu.CompilerParams(vmem_limit_bytes=mib * MIB)


def tiled_scratch(rows, cols):
    return pltpu.VMEM((cols // LANES, rows, LANES), F32)


def store_strided(held, first, stride, values):
    rows = values.shape[0]
    for t in range(held.shape[0]):
        held[t, pl.ds(first, rows, stride=stride), :] = values[:, t * LANES : (t + 1) * LANES]


def load_strided(held, first, stride, rows):
    parts = [held[t, pl.ds(first, rows, stride=stride), :] for t in range(held.shape[0])]
    return jnp.concatenate(parts, axis=1)


def joined_tiles(held):
    return jnp.concatenate([held[t] for t in range(held.shape[0])], axis=1)


def head_lanes(length):
    lane = lax.broadcasted_iota(jnp.int32, (length, LANES), 1) // HEAD_CHANNELS
    return [
        jnp.where(lane == t, 1.0, 0.0).astype(BF16) for t in range(LANES // HEAD_CHANNELS)
    ]


def attend_block(query, key, value, live, lanes, bias_of):
    pieces = []
    per_tile = LANES // HEAD_CHANNELS
    rows = query.shape[0]
    for tile in range(query.shape[1] // LANES):
        cut = slice(tile * LANES, (tile + 1) * LANES)
        query_t, key_t = query[:, cut], key[:, cut]
        value_t = value[:, cut] * live
        stacked = jnp.concatenate([query_t * lanes[t][:rows] for t in range(per_tile)], axis=0)
        stacked = nt_dot(stacked, key_t)
        raised, sides = [], []
        for t in range(per_tile):
            scores = stacked[t * rows : (t + 1) * rows]
            if bias_of is not None:
                scores = scores + bias_of(tile * per_tile + t)
            raised.append(jnp.exp2(scores).astype(BF16))
            sides.append(jnp.concatenate([value_t * lanes[t], live * lanes[t]], axis=1))
        total = nn_dot(jnp.concatenate(raised, axis=1), jnp.concatenate(sides, axis=0))
        pieces.append(total[:, :LANES] / total[:, LANES:])
    return jnp.concatenate(pieces, axis=1)


def project(normed, weight_ref):
    scale = LOG2E / math.sqrt(HEAD_CHANNELS)
    query = (nn_dot(normed, weight_ref[0]) * scale).astype(BF16)
    key = nn_dot(normed, weight_ref[1]).astype(BF16)
    value = (nn_dot(normed, weight_ref[2]) * VALUE_SCALE).astype(BF16)
    gate = jax.nn.sigmoid(nn_dot(normed, weight_ref[3])) * (1.0 / VALUE_SCALE)
    return query, key, value, gate


def regrouped(held, values, parts):
    items = values.shape[0] // parts
    for t in range(held.shape[0]):
        held[t] = values[:, t * LANES : (t + 1) * LANES]
    return jnp.concatenate([load_strided(held, r, items, parts) for r in range(items)], axis=0)


def bias_kernel(parts, pair_ref, weight_ref, out_ref, held, column):
    rows, cols, width = pair_ref.shape
    normed = layer_normalize(pair_ref[...].astype(F32))
    ordered = [regrouped(column.at[i], normed[i], parts) for i in range(rows)]
    normed = jnp.concatenate(ordered, axis=0).astype(BF16)
    bias = nt_dot(weight_ref[...], normed) * LOG2E
    for i in range(rows):
        store_strided(held, i, rows, bias[:, i * cols : (i + 1) * cols])
    out_ref[...] = joined_tiles(held).astype(BF16)


def pair_bias_block(pair_rep, bias_weight, parts):
    rows, cols, width = pair_rep.shape
    out = jax.ShapeDtypeStruct((ATTN_HEAD_COUNT * rows, cols), BF16)
    return pl.pallas_call(
        functools.partial(bias_kernel, parts),
        out_shape=out,
        scratch_shapes=[tiled_scratch(*out.shape), pltpu.VMEM((rows, 1, cols, width), F32)],
        compiler_params=params(16),
        name="pair_bias",
    )(pair_rep, bias_weight.T)


def row_project_kernel(parts, x_ref, weight_ref, x_out, q_ref, k_ref, v_ref, g_ref, held):
    for s in range(x_ref.shape[0]):
        ordered = regrouped(held.at[s], x_ref[s].astype(F32), parts)
        x_out[s] = ordered.astype(BF16)
        normed = layer_normalize(ordered).astype(BF16)
        q_ref[s], k_ref[s], v_ref[s], g_ref[s] = project(normed, weight_ref)


def row_project(alignment, weight, parts):
    seqs, length, width = alignment.shape
    step = 2
    block = pl.BlockSpec((step, length, width), lambda i: (i, 0, 0))
    small = jax.ShapeDtypeStruct(alignment.shape, BF16)
    return pl.pallas_call(
        functools.partial(row_project_kernel, parts),
        grid=(seqs // step,),
        in_specs=[block, full_spec(weight.shape)],
        out_specs=[block] * 5,
        out_shape=[small] * 4 + [jax.ShapeDtypeStruct(alignment.shape, F32)],
        scratch_shapes=[pltpu.VMEM((step, width // LANES, length, LANES), F32)],
        compiler_params=params(24),
        name="row_project",
    )(alignment, weight)


def row_attend_kernel(
    plan, step, half, me_ref, x_ref, q_ref, k_ref, v_ref, g_ref, live_ref, out_w_ref, *rest
):
    bias_refs, out_ref, bias_all, held = rest[: len(plan)], rest[-3], rest[-2], rest[-1]
    heads, rows, length = ATTN_HEAD_COUNT, q_ref.shape[1], k_ref.shape[1]
    parts, block_rows = out_ref.shape[0], out_ref.shape[1]
    items = rows // parts
    at = pl.program_id(0)

    @pl.when(at == 0)
    def _():
        for bias_ref, offsets in zip(bias_refs, plan):
            for z, offset in enumerate(offsets):
                owner = me_ref[0] ^ offset
                block = bias_ref[z].astype(F32).reshape(heads, -1, length)
                own = block.shape[1]
                for h in range(heads):
                    for t in range(bias_all.shape[0]):
                        to = pl.ds(h * length + owner, own, stride=parts)
                        bias_all[t, to, :] = block[h, :, t * LANES : (t + 1) * LANES]

    def bias_of(h):
        start = h * length + half * rows
        return jnp.concatenate(
            [bias_all[t, start : start + rows, :] for t in range(bias_all.shape[0])], axis=1
        )

    lanes = head_lanes(length)
    for s in range(step):
        heads_out = attend_block(q_ref[s], k_ref[s], v_ref[s], live_ref[s], lanes, bias_of)
        heads_out = (heads_out * g_ref[s]).astype(BF16)
        total = x_ref[s].astype(F32) + nn_dot(heads_out, out_w_ref[...])
        for r in range(items):
            first = (at * step + s) * items + r
            store_strided(held, first, block_rows, total[r * parts : (r + 1) * parts])

    @pl.when(at == pl.num_programs(0) - 1)
    def _():
        out_ref[...] = joined_tiles(held).reshape(out_ref.shape).astype(BF16)


def row_attend(me, projected, live, out_weight, bias_parts, plan, dap_count, half, halves):
    x_rows, query, key, value, gate = projected
    seqs, length, width = x_rows.shape
    rows = length // halves
    step = 2
    block = pl.BlockSpec((step, length, width), lambda i: (i, 0, 0))
    part = pl.BlockSpec((step, rows, width), lambda i: (i, half, 0))
    out = (dap_count, seqs * rows // dap_count, width)
    return pl.pallas_call(
        functools.partial(row_attend_kernel, plan, step, half),
        grid=(seqs // step,),
        in_specs=[pl.BlockSpec(memory_space=pltpu.SMEM), part, part, block, block, part]
        + [pl.BlockSpec((step, length, LANES), lambda i: (i, 0, 0)), full_spec(out_weight.shape)]
        + [full_spec(b.shape) for b in bias_parts],
        out_specs=full_spec(out),
        out_shape=jax.ShapeDtypeStruct(out, BF16),
        scratch_shapes=[
            tiled_scratch(ATTN_HEAD_COUNT * length, length),
            tiled_scratch(seqs * rows, width),
        ],
        compiler_params=params(28),
        name="row_attend",
    )(me, x_rows, query, key, value, gate, live, out_weight, *bias_parts)


def column_kernel(
    first, items, each, x_ref, live_ref, mask_ref, weight_ref, out_w_ref, factor_ref, *rest
):
    before, rest = rest[:-7], rest[-7:]
    out_ref, left_ref, right_ref, x_held, held, left_held, right_held = rest
    step = pl.program_id(0)
    length = out_ref.shape[0]
    here = x_held.shape[1] // length

    @pl.when(step == 0)
    def _():
        for t in range(held.shape[0]):
            cut = slice(t * LANES, (t + 1) * LANES)
            x_held[t] = x_ref[:, :, cut].astype(F32).reshape(x_held.shape[1:])
            if before:
                held[t] = before[0][:, :, cut].astype(F32).reshape(held.shape[1:])
                right_held[t] = before[2][:, cut].astype(F32)
        if before:
            left_held[...] = before[1][...]

    lanes = head_lanes(length)
    for n in range(each):
        inner = step * each + n
        item = inner + first
        current = load_strided(x_held, inner, here, length)
        normed = layer_normalize(current).astype(BF16)
        query, key, value, gate = project(normed, weight_ref)
        heads_out = attend_block(query, key, value, live_ref[n], lanes, None)
        heads_out = (heads_out * gate).astype(BF16)
        updated = (current + nn_dot(heads_out, out_w_ref[...])).astype(BF16).astype(F32)
        store_strided(held, item, items, updated)
        normed = layer_normalize(updated).astype(BF16)
        factors = nt_dot(factor_ref[...], normed) * mask_ref[pl.ds(item, 1), :]
        left_at = pl.ds(pl.multiple_of(item * FACTOR_CHANNELS, FACTOR_CHANNELS), FACTOR_CHANNELS)
        left_held[left_at, :] = factors[:FACTOR_CHANNELS].astype(BF16)
        store_strided(right_held, item, items, factors[FACTOR_CHANNELS:])

    @pl.when(step == pl.num_programs(0) - 1)
    def _():
        for t in range(held.shape[0]):
            part = held[t].reshape(out_ref.shape[:2] + (LANES,))
            out_ref[:, :, t * LANES : (t + 1) * LANES] = part.astype(BF16)
        right_ref[...] = joined_tiles(right_held).astype(BF16)
        left_ref[...] = left_held[...]


def column_attend(moved, live, mask_rows, weight, out_weight, factor_t, half, halves, before):
    width = moved.shape[2]
    items = mask_rows.shape[0]
    here = items // halves
    rows = moved.shape[0] * moved.shape[1]
    length = rows // here
    each = 2
    start = half * here
    side = (items * FACTOR_CHANNELS, length)
    outs = [jax.ShapeDtypeStruct((length, items, width), BF16)]
    outs += [jax.ShapeDtypeStruct(side, BF16)] * 2
    return pl.pallas_call(
        functools.partial(column_kernel, start, items, each),
        grid=(here // each,),
        in_specs=[
            full_spec(moved.shape),
            pl.BlockSpec((each, length, LANES), lambda i: (i + start // each, 0, 0)),
            full_spec(mask_rows.shape),
            full_spec(weight.shape),
            full_spec(out_weight.shape),
            full_spec(factor_t.shape),
        ]
        + [full_spec(b.shape) for b in before],
        out_specs=[full_spec(o.shape) for o in outs],
        out_shape=outs,
        scratch_shapes=[
            tiled_scratch(rows, width),
            tiled_scratch(length * items, width),
            pltpu.VMEM(side, BF16),
            tiled_scratch(*side),
        ],
        compiler_params=params(28),
        name="column_attend",
    )(moved, live, mask_rows, weight, out_weight, factor_t, *before)


def outer_kernel(group, outer, items, *refs):
    lefts, rights = refs[:group], refs[group : group + outer]
    weight_ref = refs[group + outer]
    outs = refs[group + outer + 1 : -3]
    weight_rows, weight, held = refs[-3:]
    feat = FACTOR_CHANNELS
    quad = LANES // feat
    tiles = items * feat // LANES
    cols = outer * items
    width = weight_ref.shape[1]

    weight_rows[...] = weight_ref[...].astype(F32)
    weight[...] = jnp.zeros_like(weight)
    for e in range(feat):
        block = weight_rows[pl.ds(e, feat, stride=feat), :].astype(BF16)
        for i in range(quad):
            start = e * LANES + i * feat
            weight[start : start + feat, i * width : (i + 1) * width] = block

    right = jnp.concatenate([r[...] for r in rights], axis=0)
    for k in range(group):
        sums = nt_dot(right, lefts[k][...])
        sums = sums.reshape(outer, feat, items, sums.shape[1])
        sums = jnp.transpose(sums, (1, 0, 2, 3)).reshape(feat, cols, sums.shape[3]).astype(BF16)
        for t in range(tiles):
            at = slice((k * tiles + t) * cols, (k * tiles + t + 1) * cols)
            for e in range(feat):
                held[at, e * LANES : (e + 1) * LANES] = sums[e, :, t * LANES : (t + 1) * LANES]
    update = nn_dot(held[...], weight[...])
    for k in range(group):
        for t in range(tiles):
            rows = update[(k * tiles + t) * cols : (k * tiles + t + 1) * cols]
            for i in range(quad):
                outs[k][t * quad + i] = rows[:, i * width : (i + 1) * width].astype(BF16)


def outer_product(lefts, rights, weight, items):
    group, outer = len(lefts), len(rights)
    cols = outer * items
    tiles = items * FACTOR_CHANNELS // LANES
    depth = FACTOR_CHANNELS * LANES
    width = weight.shape[1]
    return pl.pallas_call(
        functools.partial(outer_kernel, group, outer, items),
        out_shape=[jax.ShapeDtypeStruct((items, cols, width), BF16)] * group,
        scratch_shapes=[
            pltpu.VMEM(weight.shape, F32),
            pltpu.VMEM((depth, LANES // FACTOR_CHANNELS * width), BF16),
            pltpu.VMEM((group * tiles * cols, depth), BF16),
        ],
        compiler_params=params(28),
        name="outer_product",
    )(*lefts, *rights, weight)


def finish_kernel(offsets, line, me_ref, pair_ref, scale_ref, *refs):
    parts, out_ref = refs[:-1], refs[-1]
    here = me_ref[0]
    items, cols, width = parts[0].shape
    outer = cols // items
    odd = (here & 1) == 1
    for k, offset in enumerate(offsets):
        for i in range(items):
            both = parts[k][i].astype(F32).reshape(outer // 2, 2, items, width)
            low, high = both[:, 0:1], both[:, 1:2]
            both = jnp.concatenate([jnp.where(odd, high, low), jnp.where(odd, low, high)], axis=1)
            both = both.reshape(outer // 2, 2 * items, width)
            for z in range(outer // 2):
                owner = here ^ (offset | line[z])
                start = pl.multiple_of((owner >> 1) * (2 * items), 2 * items)
                at = pl.ds(start, 2 * items)
                update = both[z] * scale_ref[at, i : i + 1]
                out_ref[i, at, :] = (pair_ref[i, at, :].astype(F32) + update).astype(BF16)


def finish(me, pair_rep, scale, parts, offsets, line):
    vmem = pl.BlockSpec(memory_space=pltpu.VMEM)
    return pl.pallas_call(
        functools.partial(finish_kernel, offsets, line),
        in_specs=[pl.BlockSpec(memory_space=pltpu.SMEM)] + [vmem] * (2 + len(parts)),
        out_specs=vmem,
        out_shape=jax.ShapeDtypeStruct(pair_rep.shape, BF16),
        compiler_params=params(16),
        name="finish",
    )(me, pair_rep, scale, *parts)


def exchange(block, count, offset):
    if offset == 0:
        return block
    return lax.ppermute(block, "dap", [(i, i ^ offset) for i in range(count)])


def per_device_fast(
    alignment,
    pair_rep,
    align_mask,
    residue_mask,
    bias_weight,
    row_proj_weight,
    row_out_weight,
    column_proj_weight,
    column_out_weight,
    outer_factor_weight,
    outer_out,
):
    count = lax.axis_size("dap")
    dap_index = lax.axis_index("dap")
    me = jnp.reshape(dap_index, (1,)).astype(jnp.int32)
    plane, line = offset_groups(count)
    seq_dev = alignment.shape[0]
    items = pair_rep.shape[0]
    total_seqs, total_res = align_mask.shape
    halves = 2

    bias = pair_bias_block(pair_rep, bias_weight, count)
    bias = jnp.stack([exchange(bias, count, z) for z in line])
    bias_parts = [exchange(bias, count, k) for k in plane]
    plan = [[k | z for z in line] for k in plane]
    bias_parts += [exchange(part, count, 1) for part in bias_parts]
    plan += [[offset | 1 for offset in offsets] for offsets in plan]
    projected = row_project(alignment, row_proj_weight, count)

    own_seqs = lax.dynamic_slice_in_dim(align_mask, dap_index * seq_dev, seq_dev, 0)
    own_seqs = own_seqs.astype(BF16).reshape(seq_dev, count, items).swapaxes(1, 2)
    own_res = lax.dynamic_slice_in_dim(align_mask, dap_index * items, items, 1)
    row_live = own_seqs.reshape(seq_dev, total_res)[:, :, None]
    row_live = jnp.broadcast_to(row_live, (seq_dev, total_res, LANES))
    col_live = jnp.broadcast_to(own_res.T.astype(BF16)[:, :, None], (items, total_seqs, LANES))
    counts = jnp.einsum(
        "si,sj->ji", own_res.astype(BF16), align_mask.astype(BF16), preferred_element_type=F32
    )
    res_float = residue_mask.astype(F32)
    live_rows = lax.dynamic_slice_in_dim(res_float, dap_index * items, items, 0)
    scale = live_rows[None, :] * res_float[:, None] / (counts + count_eps)
    mask_rows = own_res.T.astype(F32)

    moved = []
    for half in range(halves):
        rows = row_attend(
            me, projected, row_live, row_out_weight, bias_parts, plan, count, half, halves
        )
        moved.append(lax.all_to_all(rows, "dap", split_axis=0, concat_axis=0, tiled=True))
    done = ()
    for half in range(halves):
        done = column_attend(
            moved[half],
            col_live,
            mask_rows,
            column_proj_weight,
            column_out_weight,
            outer_factor_weight.T,
            half,
            halves,
            done,
        )
    updated, left, right = done
    rights = [exchange(right, count, z) for z in line]
    rights = [part for own in rights for part in (own, exchange(own, count, 1))]
    lefts = [exchange(left, count, k) for k in plane]
    parts = outer_product(lefts, rights, outer_out, items)
    parts = [exchange(part, count, k) for part, k in zip(parts, plane)]
    pair_out = finish(me, pair_rep, scale, parts, plane, line)
    return updated, pair_out


def offset_groups(count):
    bits = count.bit_length() - 1
    near = (bits - 1) // 2
    plane = [k << 1 for k in range(1 << near)]
    line = [z << (1 + near) for z in range(1 << (bits - 1 - near))]
    return plane, line


def solution(mesh):
    placed = (
        P("dap", None, None),
        P("dap", "branch", None),
        P(),
        P(),
        P(),
        P(None, None, "branch"),
        P(),
        P(None, None, "branch"),
        P(),
        P(),
        P(),
    )
    count = mesh.shape["dap"]
    whole_heads = mesh.shape["branch"] == 1 and count & (count - 1) == 0

    def per_device(*operands):
        alignment, pair_rep = operands[0], operands[1]
        tile = 8
        fits = whole_heads and alignment.shape[0] == tile and pair_rep.shape[0] == tile
        return (per_device_fast if fits else per_device_general)(*operands)

    return jax.shard_map(
        per_device,
        mesh=mesh,
        in_specs=placed,
        out_specs=(P(None, "dap", None), P("dap", "branch", None)),
        check_vma=False,
    )
```

```python
import functools
import math

import jax
import jax.numpy as jnp
from jax import lax
from jax.experimental import pallas as pl
from jax.experimental.pallas import tpu as pltpu
from jax.sharding import PartitionSpec as P

ATTN_HEAD_COUNT = 8
HEAD_CHANNELS = 32
FACTOR_CHANNELS = 32


norm_eps = 1e-05
count_eps = 0.001


def layer_normalize(values):
    centre = jnp.mean(values, axis=-1, keepdims=True)
    centred = values - centre
    spread = jnp.mean(centred * centred, axis=-1, keepdims=True)
    return centred * lax.rsqrt(spread + norm_eps)


def attend_heads(inputs, key_mask, proj_weight, out_weight, score_bias):
    batch = inputs.shape[0]
    length = inputs.shape[1]
    local_width = proj_weight.shape[2]
    local_heads = local_width // HEAD_CHANNELS
    normed = layer_normalize(inputs.astype(jnp.float32)).astype(jnp.bfloat16)
    projected = jnp.einsum("blc,kcd->kbld", normed, proj_weight, preferred_element_type=jnp.float32)
    triple = (
        projected[:3].astype(jnp.bfloat16).reshape(3, batch, length, local_heads, HEAD_CHANNELS)
    )
    gating = jax.nn.sigmoid(projected[3])

    def attend_one(operands):
        queries, key_rows, value_rows, mask_row = operands
        scores = jnp.einsum(
            "ihd,jhd->hij", queries, key_rows, preferred_element_type=jnp.float32
        ) / math.sqrt(HEAD_CHANNELS)
        if score_bias is not None:
            scores = scores + score_bias.astype(jnp.float32)
        raised = jnp.exp(scores) * mask_row[None, None, :]
        weights = (raised / jnp.sum(raised, axis=-1, keepdims=True)).astype(jnp.bfloat16)
        return jnp.einsum("hij,jhd->ihd", weights, value_rows, preferred_element_type=jnp.float32)

    attended_rows = lax.map(attend_one, (triple[0], triple[1], triple[2], key_mask))
    heads_out = (attended_rows.reshape(batch, length, local_width) * gating).astype(jnp.bfloat16)
    gathered = lax.all_gather(heads_out, "branch", axis=2, tiled=True)
    update = jnp.einsum("blf,fc->blc", gathered, out_weight, preferred_element_type=jnp.float32)
    return (inputs.astype(jnp.float32) + update).astype(jnp.bfloat16)


def per_device_general(
    alignment,
    pair_rep,
    align_mask,
    residue_mask,
    bias_weight,
    row_proj_weight,
    row_out_weight,
    column_proj_weight,
    column_out_weight,
    outer_factor_weight,
    outer_out,
):
    branch_count = lax.axis_size("branch")
    dap_count = lax.axis_size("dap")
    branch_index = lax.axis_index("branch")
    dap_index = lax.axis_index("dap")
    seq_dev = alignment.shape[0]
    res_dev = pair_rep.shape[0]
    quarter = pair_rep.shape[1]
    total_seqs = align_mask.shape[0]
    local_heads = ATTN_HEAD_COUNT // branch_count
    float_mask = align_mask.astype(jnp.float32)
    res_float = residue_mask.astype(jnp.float32)
    pair_normed = layer_normalize(pair_rep.astype(jnp.float32)).astype(jnp.bfloat16)
    bias_block = jnp.einsum(
        "ijc,ch->hij", pair_normed, bias_weight, preferred_element_type=jnp.float32
    ).astype(jnp.bfloat16)
    bias_wide = lax.all_gather(bias_block, "branch", axis=2, tiled=True)
    bias_full = lax.all_gather(bias_wide, "dap", axis=1, tiled=True)
    pair_score_bias = lax.dynamic_slice_in_dim(
        bias_full, branch_index * local_heads, local_heads, 0
    )
    sequence_row_mask = lax.dynamic_slice_in_dim(float_mask, dap_index * seq_dev, seq_dev, 0)
    row_alignment = attend_heads(
        alignment, sequence_row_mask, row_proj_weight, row_out_weight, pair_score_bias
    )
    send_mask = sequence_row_mask.astype(jnp.bfloat16)
    blocked_rows = row_alignment.reshape(seq_dev, dap_count, res_dev, row_alignment.shape[2])
    blocked_mask = send_mask.reshape(seq_dev, dap_count, res_dev)
    moved_rows = lax.all_to_all(blocked_rows, "dap", split_axis=1, concat_axis=0, tiled=True)
    moved_mask = lax.all_to_all(blocked_mask, "dap", split_axis=1, concat_axis=0, tiled=True)
    seq_total = moved_rows.shape[0]
    items = moved_rows.shape[2]
    flat_rows = moved_rows.reshape(seq_total, items, moved_rows.shape[3])
    flat_mask = moved_mask.reshape(seq_total, items)
    transposed_rows = jnp.swapaxes(flat_rows, 0, 1)
    key_mask = jnp.swapaxes(flat_mask, 0, 1).astype(jnp.float32)
    attended_rows = attend_heads(
        transposed_rows, key_mask, column_proj_weight, column_out_weight, None
    )
    column_alignment = jnp.swapaxes(attended_rows, 0, 1)
    outer_mean_normed = layer_normalize(column_alignment.astype(jnp.float32)).astype(jnp.bfloat16)
    projected = jnp.einsum(
        "src,ce->sre", outer_mean_normed, outer_factor_weight, preferred_element_type=jnp.float32
    )
    factor_pairs = (projected * flat_mask.astype(jnp.float32)[:, :, None]).astype(jnp.bfloat16)
    column_alignment, factor_pairs = (column_alignment, factor_pairs)
    blocked_out = column_alignment.reshape(seq_total, 1, items, column_alignment.shape[2])
    blocked_factors = factor_pairs.reshape(seq_total, 1, items, factor_pairs.shape[2])
    updated_alignment = blocked_out.reshape(total_seqs, res_dev, blocked_out.shape[3])
    factor_pairs = blocked_factors.reshape(total_seqs, res_dev, blocked_factors.shape[3])
    left_side = factor_pairs[:, :, :FACTOR_CHANNELS]
    right_local = factor_pairs[:, :, FACTOR_CHANNELS:]
    col_start = branch_index * quarter
    row_start = dap_index * res_dev
    mask_rows = lax.dynamic_slice_in_dim(align_mask, row_start, res_dev, 1).astype(jnp.bfloat16)
    mask_cols = lax.dynamic_slice_in_dim(align_mask, col_start, quarter, 1).astype(jnp.bfloat16)
    counts = jnp.einsum("si,sj->ij", mask_rows, mask_cols, preferred_element_type=jnp.float32)
    live_rows = lax.dynamic_slice_in_dim(res_float, row_start, res_dev, 0)
    live_cols = lax.dynamic_slice_in_dim(res_float, col_start, quarter, 0)
    outer_weight = outer_out.astype(jnp.float32)
    right_all = lax.all_gather(right_local, "dap", axis=1, tiled=True)
    right_mine = lax.dynamic_slice_in_dim(right_all, col_start, quarter, 1)
    outer_sums = jnp.einsum(
        "sic,sje->ijce", left_side, right_mine, preferred_element_type=jnp.float32
    )
    outer_sums = outer_sums.reshape(res_dev, quarter, FACTOR_CHANNELS * FACTOR_CHANNELS)
    update = jnp.einsum("ijf,fz->ijz", outer_sums, outer_weight, precision=lax.Precision.HIGHEST)
    live = live_rows[:, None] * live_cols[None, :]
    update = update / (counts[:, :, None] + count_eps) * live[:, :, None]
    pair_out = (pair_rep.astype(jnp.float32) + update).astype(jnp.bfloat16)
    return (updated_alignment, pair_out)


LANES = 128
LOG2E = math.log2(math.e)
VALUE_SCALE = 1.0 / 128.0
BF16 = jnp.bfloat16
F32 = jnp.float32
MIB = 1024 * 1024


def nt_dot(a, b):
    return lax.dot_general(a, b, (((1,), (1,)), ((), ())), preferred_element_type=F32)


def nn_dot(a, b):
    return jnp.dot(a, b, preferred_element_type=F32)


def full_spec(shape):
    zeros = (0,) * len(shape)
    return pl.BlockSpec(shape, lambda *_: zeros)


def params(mib):
    return pltpu.CompilerParams(vmem_limit_bytes=mib * MIB)


def tiled_scratch(rows, cols):
    return pltpu.VMEM((cols // LANES, rows, LANES), F32)


def store_strided(held, first, stride, values):
    rows = values.shape[0]
    for t in range(held.shape[0]):
        held[t, pl.ds(first, rows, stride=stride), :] = values[:, t * LANES : (t + 1) * LANES]


def load_strided(held, first, stride, rows):
    parts = [held[t, pl.ds(first, rows, stride=stride), :] for t in range(held.shape[0])]
    return jnp.concatenate(parts, axis=1)


def joined_tiles(held):
    return jnp.concatenate([held[t] for t in range(held.shape[0])], axis=1)


def in_hbm(*arrays):
    return [pltpu.with_memory_space_constraint(a, pltpu.HBM) for a in arrays]


def head_lanes(length):
    lane = lax.broadcasted_iota(jnp.int32, (length, LANES), 1) // HEAD_CHANNELS
    return [
        jnp.where(lane == t, 1.0, 0.0).astype(BF16) for t in range(LANES // HEAD_CHANNELS)
    ]


def attend_block(query, key, value, live, lanes, bias_of):
    pieces = []
    per_tile = LANES // HEAD_CHANNELS
    rows = query.shape[0]
    for tile in range(query.shape[1] // LANES):
        cut = slice(tile * LANES, (tile + 1) * LANES)
        query_t, key_t = query[:, cut], key[:, cut]
        value_t = value[:, cut] * live
        stacked = jnp.concatenate([query_t * lanes[t][:rows] for t in range(per_tile)], axis=0)
        stacked = nt_dot(stacked, key_t)
        raised, sides = [], []
        for t in range(per_tile):
            scores = stacked[t * rows : (t + 1) * rows]
            if bias_of is not None:
                scores = scores + bias_of(tile * per_tile + t)
            raised.append(jnp.exp2(scores).astype(BF16))
            sides.append(jnp.concatenate([value_t * lanes[t], live * lanes[t]], axis=1))
        total = nn_dot(jnp.concatenate(raised, axis=1), jnp.concatenate(sides, axis=0))
        pieces.append(total[:, :LANES] / total[:, LANES:])
    return jnp.concatenate(pieces, axis=1)


def project(normed, weight_ref):
    scale = LOG2E / math.sqrt(HEAD_CHANNELS)
    query = (nn_dot(normed, weight_ref[0]) * scale).astype(BF16)
    key = nn_dot(normed, weight_ref[1]).astype(BF16)
    value = (nn_dot(normed, weight_ref[2]) * VALUE_SCALE).astype(BF16)
    gate = jax.nn.sigmoid(nn_dot(normed, weight_ref[3])) * (1.0 / VALUE_SCALE)
    return query, key, value, gate


def bias_kernel(pair_ref, weight_ref, out_ref, held):
    rows, cols, width = pair_ref.shape
    total = out_ref.shape[0] // ATTN_HEAD_COUNT
    step = pl.program_id(0)
    normed = layer_normalize(pair_ref[...].astype(F32)).astype(BF16).reshape(rows * cols, width)
    bias = nt_dot(weight_ref[...], normed) * LOG2E
    for i in range(rows):
        store_strided(held, step * rows + i, total, bias[:, i * cols : (i + 1) * cols])

    @pl.when(step == pl.num_programs(0) - 1)
    def _():
        out_ref[...] = joined_tiles(held).astype(BF16)


def pair_bias_block(pair_rep, bias_weight):
    rows, cols, width = pair_rep.shape
    out = jax.ShapeDtypeStruct((ATTN_HEAD_COUNT * rows, cols), BF16)
    step = 2
    weight = bias_weight.T
    return pl.pallas_call(
        bias_kernel,
        grid=(rows // step,),
        in_specs=[
            pl.BlockSpec((step, cols, width), lambda i: (i, 0, 0)),
            full_spec(weight.shape),
        ],
        out_specs=full_spec(out.shape),
        out_shape=out,
        scratch_shapes=[tiled_scratch(*out.shape)],
        compiler_params=params(16),
        name="pair_bias",
    )(*in_hbm(pair_rep, weight))


def order_kernel(plan, me_ref, *refs):
    parts, out_ref = refs[:-1], refs[-1]
    for part, offsets in zip(parts, plan):
        for z, offset in enumerate(offsets):
            out_ref[me_ref[0] ^ offset] = part[z]


def order_blocks(me, parts, plan):
    vmem = pl.BlockSpec(memory_space=pltpu.VMEM)
    shape = (len(parts) * parts[0].shape[0],) + parts[0].shape[1:]
    return pl.pallas_call(
        functools.partial(order_kernel, plan),
        grid=(1,),
        in_specs=[pl.BlockSpec(memory_space=pltpu.SMEM)] + [vmem] * len(parts),
        out_specs=full_spec(shape),
        out_shape=pltpu.HBM(shape, BF16),
        compiler_params=params(8),
        name="order_blocks",
    )(me, *parts)


def row_project_kernel(x_ref, weight_ref, q_ref, k_ref, v_ref, g_ref):
    for s in range(x_ref.shape[0]):
        normed = layer_normalize(x_ref[s].astype(F32)).astype(BF16)
        q_ref[s], k_ref[s], v_ref[s], g_ref[s] = project(normed, weight_ref)


def row_project(alignment, weight):
    seqs, length, width = alignment.shape
    step = 2
    block = pl.BlockSpec((step, length, width), lambda i: (i, 0, 0))
    return pl.pallas_call(
        row_project_kernel,
        grid=(seqs // step,),
        in_specs=[block, full_spec(weight.shape)],
        out_specs=[block] * 4,
        out_shape=[pltpu.HBM(alignment.shape, BF16)] * 3 + [pltpu.HBM(alignment.shape, F32)],
        compiler_params=params(24),
        name="row_project",
    )(*in_hbm(alignment, weight))


def row_attend_kernel(
    halves, x_ref, q_ref, k_ref, v_ref, g_ref, live_ref, out_w_ref, bias_ref, *rest
):
    outs, bias_all = rest[:-1], rest[-1]
    heads, length, _ = bias_all.shape
    parts = bias_ref.shape[0]

    @pl.when(pl.program_id(0) == 0)
    def _():
        for owner in range(parts):
            block = bias_ref[owner].astype(F32).reshape(heads, -1, length)
            rows = block.shape[1]
            bias_all[:, owner * rows : (owner + 1) * rows, :] = block

    lanes = head_lanes(length)
    results = []
    for s in range(halves):
        heads_out = attend_block(
            q_ref[s], k_ref[s], v_ref[s], live_ref[s], lanes, lambda h: bias_all[h]
        )
        heads_out = (heads_out * g_ref[s]).astype(BF16)
        results.append(x_ref[s].astype(F32) + nn_dot(heads_out, out_w_ref[...]))
    items = length // parts
    first, second = (r.reshape(parts, items, -1) for r in results)
    rolled_first = pltpu.roll(first, items // 2, 1)
    rolled_second = pltpu.roll(second, items // 2, 1)
    low = lax.broadcasted_iota(jnp.int32, first.shape, 1) < items // 2
    outs[0][:, 0] = jnp.where(low, first, rolled_second).astype(BF16)
    outs[1][:, 0] = jnp.where(low, rolled_first, second).astype(BF16)


def row_attend(alignment, projected, live, out_weight, bias, halves):
    seqs, length, width = alignment.shape
    parts = bias.shape[0]
    items = length // parts
    step = halves
    block = pl.BlockSpec((step, length, width), lambda i: (i, 0, 0))
    out = (parts, seqs // step, items, width)
    return pl.pallas_call(
        functools.partial(row_attend_kernel, halves),
        grid=(seqs // step,),
        in_specs=[block] * 5
        + [pl.BlockSpec((step, length, LANES), lambda i: (i, 0, 0)), full_spec(out_weight.shape)]
        + [full_spec(bias.shape)],
        out_specs=[pl.BlockSpec((parts, 1, items, width), lambda i: (0, i, 0, 0))] * halves,
        out_shape=[pltpu.HBM(out, BF16)] * halves,
        scratch_shapes=[pltpu.VMEM((ATTN_HEAD_COUNT, length, length), F32)],
        compiler_params=params(28),
        name="row_attend",
    )(*in_hbm(alignment, *projected, live, out_weight, bias))


def column_kernel(
    first, items, each, x_ref, live_ref, mask_ref, weight_ref, out_w_ref, factor_ref, *rest
):
    before, rest = rest[:-7], rest[-7:]
    out_ref, left_ref, right_ref, x_held, held, left_held, right_held = rest
    step = pl.program_id(0)
    length = out_ref.shape[0]
    here = x_held.shape[1] // length

    @pl.when(step == 0)
    def _():
        for t in range(held.shape[0]):
            cut = slice(t * LANES, (t + 1) * LANES)
            x_held[t] = x_ref[:, :, :, cut].astype(F32).reshape(x_held.shape[1:])
            if before:
                held[t] = before[0][:, :, cut].astype(F32).reshape(held.shape[1:])
                right_held[t] = before[2][:, cut].astype(F32)
        if before:
            left_held[...] = before[1][...]

    lanes = head_lanes(length)
    for n in range(each):
        inner = step * each + n
        item = inner + first
        current = load_strided(x_held, inner, here, length)
        normed = layer_normalize(current).astype(BF16)
        query, key, value, gate = project(normed, weight_ref)
        heads_out = attend_block(query, key, value, live_ref[n], lanes, None)
        heads_out = (heads_out * gate).astype(BF16)
        updated = (current + nn_dot(heads_out, out_w_ref[...])).astype(BF16).astype(F32)
        store_strided(held, item, items, updated)
        normed = layer_normalize(updated).astype(BF16)
        factors = nt_dot(factor_ref[...], normed) * mask_ref[pl.ds(item, 1), :]
        left_at = pl.ds(pl.multiple_of(item * FACTOR_CHANNELS, FACTOR_CHANNELS), FACTOR_CHANNELS)
        left_held[left_at, :] = factors[:FACTOR_CHANNELS].astype(BF16)
        store_strided(right_held, item, items, factors[FACTOR_CHANNELS:])

    @pl.when(step == pl.num_programs(0) - 1)
    def _():
        for t in range(held.shape[0]):
            part = held[t].reshape(out_ref.shape[:2] + (LANES,))
            out_ref[:, :, t * LANES : (t + 1) * LANES] = part.astype(BF16)
        right_ref[...] = joined_tiles(right_held).astype(BF16)
        left_ref[...] = left_held[...]


def column_attend(moved, live, mask_rows, weight, out_weight, factor_t, half, halves, before):
    width = moved.shape[-1]
    items = mask_rows.shape[0]
    here = items // halves
    rows = math.prod(moved.shape[:-1])
    length = rows // here
    each = 2
    start = half * here
    side = (items * FACTOR_CHANNELS, length)
    last = half == halves - 1
    outs = [pltpu.HBM((length, items, width), BF16)]
    outs += [jax.ShapeDtypeStruct(side, BF16) if last else pltpu.HBM(side, BF16)] * 2
    return pl.pallas_call(
        functools.partial(column_kernel, start, items, each),
        grid=(here // each,),
        in_specs=[
            full_spec(moved.shape),
            pl.BlockSpec((each, length, LANES), lambda i: (i + start // each, 0, 0)),
            full_spec(mask_rows.shape),
            full_spec(weight.shape),
            full_spec(out_weight.shape),
            full_spec(factor_t.shape),
        ]
        + [full_spec(b.shape) for b in before],
        out_specs=[full_spec(o.shape) for o in outs],
        out_shape=outs,
        scratch_shapes=[
            tiled_scratch(rows, width),
            tiled_scratch(length * items, width),
            pltpu.VMEM(side, BF16),
            tiled_scratch(*side),
        ],
        compiler_params=params(28),
        name="column_attend",
    )(moved, *in_hbm(live, mask_rows, weight, out_weight, factor_t, *before))


def outer_kernel(group, outer, items, *refs):
    lefts, rights = refs[:group], refs[group : group + outer]
    weight_ref = refs[group + outer]
    outs = refs[group + outer + 1 : -3]
    weight_rows, weight, held = refs[-3:]
    feat = FACTOR_CHANNELS
    quad = LANES // feat
    tiles = items * feat // LANES
    cols = outer * items
    width = weight_ref.shape[1]

    weight_rows[...] = weight_ref[...].astype(F32)
    weight[...] = jnp.zeros_like(weight)
    for e in range(feat):
        block = weight_rows[pl.ds(e, feat, stride=feat), :].astype(BF16)
        for i in range(quad):
            start = e * LANES + i * feat
            weight[start : start + feat, i * width : (i + 1) * width] = block

    right = jnp.concatenate([r[...] for r in rights], axis=0)
    for k in range(group):
        sums = nt_dot(right, lefts[k][...])
        sums = sums.reshape(outer, feat, items, sums.shape[1])
        sums = jnp.transpose(sums, (1, 0, 2, 3)).reshape(feat, cols, sums.shape[3]).astype(BF16)
        for t in range(tiles):
            at = slice((k * tiles + t) * cols, (k * tiles + t + 1) * cols)
            for e in range(feat):
                held[at, e * LANES : (e + 1) * LANES] = sums[e, :, t * LANES : (t + 1) * LANES]
    update = nn_dot(held[...], weight[...])
    for k in range(group):
        for t in range(tiles):
            rows = update[(k * tiles + t) * cols : (k * tiles + t + 1) * cols]
            for i in range(quad):
                outs[k][t * quad + i] = rows[:, i * width : (i + 1) * width].astype(BF16)


def outer_product(lefts, rights, weight, items):
    group, outer = len(lefts), len(rights)
    cols = outer * items
    tiles = items * FACTOR_CHANNELS // LANES
    depth = FACTOR_CHANNELS * LANES
    width = weight.shape[1]
    return pl.pallas_call(
        functools.partial(outer_kernel, group, outer, items),
        out_shape=[jax.ShapeDtypeStruct((items, cols, width), BF16)] * group,
        scratch_shapes=[
            pltpu.VMEM(weight.shape, F32),
            pltpu.VMEM((depth, LANES // FACTOR_CHANNELS * width), BF16),
            pltpu.VMEM((group * tiles * cols, depth), BF16),
        ],
        compiler_params=params(28),
        name="outer_product",
    )(*lefts, *rights, weight)


def finish_kernel(offsets, line, me_ref, pair_ref, scale_ref, *refs):
    parts, out_ref = refs[:-1], refs[-1]
    here = me_ref[0]
    items, cols, width = parts[0].shape
    outer = cols // items
    odd = (here & 1) == 1
    for k, offset in enumerate(offsets):
        for i in range(items):
            both = parts[k][i].astype(F32).reshape(outer // 2, 2, items, width)
            low, high = both[:, 0:1], both[:, 1:2]
            both = jnp.concatenate([jnp.where(odd, high, low), jnp.where(odd, low, high)], axis=1)
            both = both.reshape(outer // 2, 2 * items, width)
            for z in range(outer // 2):
                owner = here ^ (offset | line[z])
                start = pl.multiple_of((owner >> 1) * (2 * items), 2 * items)
                at = pl.ds(start, 2 * items)
                update = both[z] * scale_ref[at, i : i + 1]
                out_ref[i, at, :] = (pair_ref[i, at, :].astype(F32) + update).astype(BF16)


def finish(me, pair_rep, scale, parts, offsets, line):
    vmem = pl.BlockSpec(memory_space=pltpu.VMEM)
    return pl.pallas_call(
        functools.partial(finish_kernel, offsets, line),
        in_specs=[pl.BlockSpec(memory_space=pltpu.SMEM)] + [vmem] * (2 + len(parts)),
        out_specs=vmem,
        out_shape=jax.ShapeDtypeStruct(pair_rep.shape, BF16),
        compiler_params=params(16),
        name="finish",
    )(me, pair_rep, scale, *parts)


def exchange(block, count, offset):
    if offset == 0:
        return block
    return lax.ppermute(block, "dap", [(i, i ^ offset) for i in range(count)])


def per_device_fast(
    alignment,
    pair_rep,
    align_mask,
    residue_mask,
    bias_weight,
    row_proj_weight,
    row_out_weight,
    column_proj_weight,
    column_out_weight,
    outer_factor_weight,
    outer_out,
):
    count = lax.axis_size("dap")
    dap_index = lax.axis_index("dap")
    me = jnp.reshape(dap_index, (1,)).astype(jnp.int32)
    plane, line = offset_groups(count)
    seq_dev = alignment.shape[0]
    items = pair_rep.shape[0]
    total_seqs, total_res = align_mask.shape
    halves = 2

    projected = list(row_project(alignment, row_proj_weight))
    bias = pair_bias_block(pair_rep, bias_weight)
    column = jnp.stack([exchange(bias, count, z) for z in line])
    bias_parts = [exchange(column, count, k) for k in plane]
    *bias_parts, query = lax.optimization_barrier((*bias_parts, projected[0]))
    projected = [query] + projected[1:]
    plan = [[k | z for z in line] for k in plane]
    bias_parts += [exchange(part, count, 1) for part in bias_parts]
    plan += [[offset | 1 for offset in offsets] for offsets in plan]
    bias = order_blocks(me, bias_parts, plan)

    own_seqs = lax.dynamic_slice_in_dim(align_mask, dap_index * seq_dev, seq_dev, 0)
    own_res = lax.dynamic_slice_in_dim(align_mask, dap_index * items, items, 1)
    row_live = jnp.broadcast_to(own_seqs.astype(BF16)[:, :, None], (seq_dev, total_res, LANES))
    col_live = jnp.broadcast_to(own_res.T.astype(BF16)[:, :, None], (items, total_seqs, LANES))
    counts = jnp.einsum(
        "si,sj->ji", own_res.astype(BF16), align_mask.astype(BF16), preferred_element_type=F32
    )
    res_float = residue_mask.astype(F32)
    live_rows = lax.dynamic_slice_in_dim(res_float, dap_index * items, items, 0)
    scale = live_rows[None, :] * res_float[:, None] / (counts + count_eps)
    mask_rows = own_res.T.astype(F32)

    rows = row_attend(alignment, projected, row_live, row_out_weight, bias, halves)
    moved = [lax.all_to_all(r, "dap", split_axis=0, concat_axis=0, tiled=True) for r in rows]
    done = ()
    for half in range(halves):
        done = column_attend(
            moved[half],
            col_live,
            mask_rows,
            column_proj_weight,
            column_out_weight,
            outer_factor_weight.T,
            half,
            halves,
            done,
        )
    updated, left, right = done
    rights = [exchange(right, count, z) for z in line]
    rights = [part for own in rights for part in (own, exchange(own, count, 1))]
    lefts = [exchange(left, count, k) for k in plane]
    parts = outer_product(lefts, rights, outer_out, items)
    parts = [exchange(part, count, k) for part, k in zip(parts, plane)]
    pair_out = finish(me, pair_rep, scale, parts, plane, line)
    return updated, pair_out


def offset_groups(count):
    bits = count.bit_length() - 1
    near = (bits - 1) // 2
    plane = [k << 1 for k in range(1 << near)]
    line = [z << (1 + near) for z in range(1 << (bits - 1 - near))]
    return plane, line


def solution(mesh):
    placed = (
        P("dap", None, None),
        P("dap", "branch", None),
        P(),
        P(),
        P(),
        P(None, None, "branch"),
        P(),
        P(None, None, "branch"),
        P(),
        P(),
        P(),
    )
    count = mesh.shape["dap"]
    whole_heads = mesh.shape["branch"] == 1 and count & (count - 1) == 0

    def per_device(*operands):
        alignment, pair_rep = operands[0], operands[1]
        tile = 8
        fits = whole_heads and alignment.shape[0] == tile and pair_rep.shape[0] == tile
        return (per_device_fast if fits else per_device_general)(*operands)

    return jax.shard_map(
        per_device,
        mesh=mesh,
        in_specs=placed,
        out_specs=(P(None, "dap", None), P("dap", "branch", None)),
        check_vma=False,
    )
```

```python
import functools
import math

import jax
import jax.numpy as jnp
from jax import lax
from jax.experimental import pallas as pl
from jax.experimental.pallas import tpu as pltpu
from jax.sharding import PartitionSpec as P

ATTN_HEAD_COUNT = 8
HEAD_CHANNELS = 32
FACTOR_CHANNELS = 32


norm_eps = 1e-05
count_eps = 0.001


def layer_normalize(values):
    centre = jnp.mean(values, axis=-1, keepdims=True)
    centred = values - centre
    spread = jnp.mean(centred * centred, axis=-1, keepdims=True)
    return centred * lax.rsqrt(spread + norm_eps)


def attend_heads(inputs, key_mask, proj_weight, out_weight, score_bias):
    batch = inputs.shape[0]
    length = inputs.shape[1]
    local_width = proj_weight.shape[2]
    local_heads = local_width // HEAD_CHANNELS
    normed = layer_normalize(inputs.astype(jnp.float32)).astype(jnp.bfloat16)
    projected = jnp.einsum("blc,kcd->kbld", normed, proj_weight, preferred_element_type=jnp.float32)
    triple = (
        projected[:3].astype(jnp.bfloat16).reshape(3, batch, length, local_heads, HEAD_CHANNELS)
    )
    gating = jax.nn.sigmoid(projected[3])

    def attend_one(operands):
        queries, key_rows, value_rows, mask_row = operands
        scores = jnp.einsum(
            "ihd,jhd->hij", queries, key_rows, preferred_element_type=jnp.float32
        ) / math.sqrt(HEAD_CHANNELS)
        if score_bias is not None:
            scores = scores + score_bias.astype(jnp.float32)
        raised = jnp.exp(scores) * mask_row[None, None, :]
        weights = (raised / jnp.sum(raised, axis=-1, keepdims=True)).astype(jnp.bfloat16)
        return jnp.einsum("hij,jhd->ihd", weights, value_rows, preferred_element_type=jnp.float32)

    attended_rows = lax.map(attend_one, (triple[0], triple[1], triple[2], key_mask))
    heads_out = (attended_rows.reshape(batch, length, local_width) * gating).astype(jnp.bfloat16)
    gathered = lax.all_gather(heads_out, "branch", axis=2, tiled=True)
    update = jnp.einsum("blf,fc->blc", gathered, out_weight, preferred_element_type=jnp.float32)
    return (inputs.astype(jnp.float32) + update).astype(jnp.bfloat16)


def per_device_general(
    alignment,
    pair_rep,
    align_mask,
    residue_mask,
    bias_weight,
    row_proj_weight,
    row_out_weight,
    column_proj_weight,
    column_out_weight,
    outer_factor_weight,
    outer_out,
):
    branch_count = lax.axis_size("branch")
    dap_count = lax.axis_size("dap")
    branch_index = lax.axis_index("branch")
    dap_index = lax.axis_index("dap")
    seq_dev = alignment.shape[0]
    res_dev = pair_rep.shape[0]
    quarter = pair_rep.shape[1]
    total_seqs = align_mask.shape[0]
    local_heads = ATTN_HEAD_COUNT // branch_count
    float_mask = align_mask.astype(jnp.float32)
    res_float = residue_mask.astype(jnp.float32)
    pair_normed = layer_normalize(pair_rep.astype(jnp.float32)).astype(jnp.bfloat16)
    bias_block = jnp.einsum(
        "ijc,ch->hij", pair_normed, bias_weight, preferred_element_type=jnp.float32
    ).astype(jnp.bfloat16)
    bias_wide = lax.all_gather(bias_block, "branch", axis=2, tiled=True)
    bias_full = lax.all_gather(bias_wide, "dap", axis=1, tiled=True)
    pair_score_bias = lax.dynamic_slice_in_dim(
        bias_full, branch_index * local_heads, local_heads, 0
    )
    sequence_row_mask = lax.dynamic_slice_in_dim(float_mask, dap_index * seq_dev, seq_dev, 0)
    row_alignment = attend_heads(
        alignment, sequence_row_mask, row_proj_weight, row_out_weight, pair_score_bias
    )
    send_mask = sequence_row_mask.astype(jnp.bfloat16)
    blocked_rows = row_alignment.reshape(seq_dev, dap_count, res_dev, row_alignment.shape[2])
    blocked_mask = send_mask.reshape(seq_dev, dap_count, res_dev)
    moved_rows = lax.all_to_all(blocked_rows, "dap", split_axis=1, concat_axis=0, tiled=True)
    moved_mask = lax.all_to_all(blocked_mask, "dap", split_axis=1, concat_axis=0, tiled=True)
    seq_total = moved_rows.shape[0]
    items = moved_rows.shape[2]
    flat_rows = moved_rows.reshape(seq_total, items, moved_rows.shape[3])
    flat_mask = moved_mask.reshape(seq_total, items)
    transposed_rows = jnp.swapaxes(flat_rows, 0, 1)
    key_mask = jnp.swapaxes(flat_mask, 0, 1).astype(jnp.float32)
    attended_rows = attend_heads(
        transposed_rows, key_mask, column_proj_weight, column_out_weight, None
    )
    column_alignment = jnp.swapaxes(attended_rows, 0, 1)
    outer_mean_normed = layer_normalize(column_alignment.astype(jnp.float32)).astype(jnp.bfloat16)
    projected = jnp.einsum(
        "src,ce->sre", outer_mean_normed, outer_factor_weight, preferred_element_type=jnp.float32
    )
    factor_pairs = (projected * flat_mask.astype(jnp.float32)[:, :, None]).astype(jnp.bfloat16)
    column_alignment, factor_pairs = (column_alignment, factor_pairs)
    blocked_out = column_alignment.reshape(seq_total, 1, items, column_alignment.shape[2])
    blocked_factors = factor_pairs.reshape(seq_total, 1, items, factor_pairs.shape[2])
    updated_alignment = blocked_out.reshape(total_seqs, res_dev, blocked_out.shape[3])
    factor_pairs = blocked_factors.reshape(total_seqs, res_dev, blocked_factors.shape[3])
    left_side = factor_pairs[:, :, :FACTOR_CHANNELS]
    right_local = factor_pairs[:, :, FACTOR_CHANNELS:]
    col_start = branch_index * quarter
    row_start = dap_index * res_dev
    mask_rows = lax.dynamic_slice_in_dim(align_mask, row_start, res_dev, 1).astype(jnp.bfloat16)
    mask_cols = lax.dynamic_slice_in_dim(align_mask, col_start, quarter, 1).astype(jnp.bfloat16)
    counts = jnp.einsum("si,sj->ij", mask_rows, mask_cols, preferred_element_type=jnp.float32)
    live_rows = lax.dynamic_slice_in_dim(res_float, row_start, res_dev, 0)
    live_cols = lax.dynamic_slice_in_dim(res_float, col_start, quarter, 0)
    outer_weight = outer_out.astype(jnp.float32)
    right_all = lax.all_gather(right_local, "dap", axis=1, tiled=True)
    right_mine = lax.dynamic_slice_in_dim(right_all, col_start, quarter, 1)
    outer_sums = jnp.einsum(
        "sic,sje->ijce", left_side, right_mine, preferred_element_type=jnp.float32
    )
    outer_sums = outer_sums.reshape(res_dev, quarter, FACTOR_CHANNELS * FACTOR_CHANNELS)
    update = jnp.einsum("ijf,fz->ijz", outer_sums, outer_weight, precision=lax.Precision.HIGHEST)
    live = live_rows[:, None] * live_cols[None, :]
    update = update / (counts[:, :, None] + count_eps) * live[:, :, None]
    pair_out = (pair_rep.astype(jnp.float32) + update).astype(jnp.bfloat16)
    return (updated_alignment, pair_out)


LANES = 128
LOG2E = math.log2(math.e)
VALUE_SCALE = 1.0 / 128.0
BF16 = jnp.bfloat16
F32 = jnp.float32
MIB = 1024 * 1024


def nt_dot(a, b):
    return lax.dot_general(a, b, (((1,), (1,)), ((), ())), preferred_element_type=F32)


def nn_dot(a, b):
    return jnp.dot(a, b, preferred_element_type=F32)


def full_spec(shape):
    zeros = (0,) * len(shape)
    return pl.BlockSpec(shape, lambda *_: zeros)


def params(mib):
    return pltpu.CompilerParams(vmem_limit_bytes=mib * MIB)


def tiled_scratch(rows, cols):
    return pltpu.VMEM((cols // LANES, rows, LANES), F32)


def store_strided(held, first, stride, values):
    rows = values.shape[0]
    for t in range(held.shape[0]):
        held[t, pl.ds(first, rows, stride=stride), :] = values[:, t * LANES : (t + 1) * LANES]


def load_strided(held, first, stride, rows):
    parts = [held[t, pl.ds(first, rows, stride=stride), :] for t in range(held.shape[0])]
    return jnp.concatenate(parts, axis=1)


def joined_tiles(held):
    return jnp.concatenate([held[t] for t in range(held.shape[0])], axis=1)


def in_vmem(*arrays):
    return [pltpu.with_memory_space_constraint(a, pltpu.VMEM) for a in arrays]


def head_lanes(length):
    lane = lax.broadcasted_iota(jnp.int32, (length, LANES), 1) // HEAD_CHANNELS
    return [
        jnp.where(lane == t, 1.0, 0.0).astype(BF16) for t in range(LANES // HEAD_CHANNELS)
    ]


def attend_block(query, key, value, live, lanes, bias_of):
    pieces = []
    per_tile = LANES // HEAD_CHANNELS
    rows = query.shape[0]
    for tile in range(query.shape[1] // LANES):
        cut = slice(tile * LANES, (tile + 1) * LANES)
        query_t, key_t = query[:, cut], key[:, cut]
        value_t = value[:, cut] * live
        stacked = jnp.concatenate([query_t * lanes[t][:rows] for t in range(per_tile)], axis=0)
        stacked = nt_dot(stacked, key_t)
        raised, sides = [], []
        for t in range(per_tile):
            scores = stacked[t * rows : (t + 1) * rows]
            if bias_of is not None:
                scores = scores + bias_of(tile * per_tile + t)
            raised.append(jnp.exp2(scores).astype(BF16))
            sides.append(jnp.concatenate([value_t * lanes[t], live * lanes[t]], axis=1))
        total = nn_dot(jnp.concatenate(raised, axis=1), jnp.concatenate(sides, axis=0))
        pieces.append(total[:, :LANES] / total[:, LANES:])
    return jnp.concatenate(pieces, axis=1)


def project(normed, weight_ref):
    scale = LOG2E / math.sqrt(HEAD_CHANNELS)
    query = (nn_dot(normed, weight_ref[0]) * scale).astype(BF16)
    key = nn_dot(normed, weight_ref[1]).astype(BF16)
    value = (nn_dot(normed, weight_ref[2]) * VALUE_SCALE).astype(BF16)
    gate = jax.nn.sigmoid(nn_dot(normed, weight_ref[3])) * (1.0 / VALUE_SCALE)
    return query, key, value, gate


def bias_kernel(pair_ref, weight_ref, out_ref, held):
    rows, cols, width = pair_ref.shape
    normed = layer_normalize(pair_ref[...].astype(F32)).astype(BF16).reshape(rows * cols, width)
    bias = nt_dot(weight_ref[...], normed) * LOG2E
    for i in range(rows):
        store_strided(held, i, rows, bias[:, i * cols : (i + 1) * cols])
    out_ref[...] = joined_tiles(held).astype(BF16)


def pair_bias_block(pair_rep, bias_weight):
    rows, cols, width = pair_rep.shape
    out = jax.ShapeDtypeStruct((ATTN_HEAD_COUNT * rows, cols), BF16)
    weight = bias_weight.T
    pinned = [pltpu.with_memory_space_constraint(a, pltpu.HBM) for a in (pair_rep, weight)]
    return pl.pallas_call(
        bias_kernel,
        grid=(1,),
        in_specs=[full_spec(pair_rep.shape), full_spec(weight.shape)],
        out_specs=pl.BlockSpec(memory_space=pltpu.VMEM),
        out_shape=out,
        scratch_shapes=[tiled_scratch(*out.shape)],
        compiler_params=params(16),
        name="pair_bias",
    )(*pinned)


def row_project_kernel(x_ref, weight_ref, x_out, q_ref, k_ref, v_ref, g_ref):
    step = x_ref.shape[0]
    for s in range(step):
        at = pl.program_id(0) * step + s
        x_out[at] = x_ref[s]
        normed = layer_normalize(x_ref[s].astype(F32)).astype(BF16)
        q_ref[at], k_ref[at], v_ref[at], g_ref[at] = project(normed, weight_ref)


def row_project(alignment, weight):
    seqs, length, width = alignment.shape
    step = 2
    block = pl.BlockSpec((step, length, width), lambda i: (i, 0, 0))
    return pl.pallas_call(
        row_project_kernel,
        grid=(seqs // step,),
        in_specs=[block, full_spec(weight.shape)],
        out_specs=[pl.BlockSpec(memory_space=pltpu.VMEM)] * 5,
        out_shape=[pltpu.VMEM(alignment.shape, BF16)] * 4 + [pltpu.VMEM(alignment.shape, F32)],
        compiler_params=params(24),
        name="row_project",
    )(*[pltpu.with_memory_space_constraint(a, pltpu.HBM) for a in (alignment, weight)])


def row_attend_kernel(
    plan, step, me_ref, x_ref, q_ref, k_ref, v_ref, g_ref, live_ref, out_w_ref, *rest
):
    bias_refs, out_ref, bias_all = rest[: len(plan)], rest[-2], rest[-1]
    heads, length, _ = bias_all.shape

    @pl.when(pl.program_id(0) == 0)
    def _():
        for bias_ref, offsets in zip(bias_refs, plan):
            for z, offset in enumerate(offsets):
                block = bias_ref[z].astype(F32).reshape(heads, -1, length)
                rows = block.shape[1]
                owner = me_ref[0] ^ offset
                bias_all[:, pl.ds(pl.multiple_of(owner * rows, rows), rows), :] = block

    lanes = head_lanes(length)
    results = []
    parts, rows = out_ref.shape[0], out_ref.shape[1]
    for s in range(step):
        at = pl.program_id(0) * step + s
        heads_out = attend_block(
            q_ref[at], k_ref[at], v_ref[at], live_ref[at], lanes, lambda h: bias_all[h]
        )
        heads_out = (heads_out * g_ref[at]).astype(BF16)
        total = x_ref[at].astype(F32) + nn_dot(heads_out, out_w_ref[...])
        results.append(total.reshape(parts, 1, rows // step, total.shape[1]))
    joined = jnp.concatenate(results, axis=1)
    out_ref[...] = joined.reshape(out_ref.shape).astype(BF16)


def row_attend(me, projected, live, out_weight, bias_parts, plan, parts):
    seqs, length, width = projected[0].shape
    rows = length // parts
    step = 2
    vmem = pl.BlockSpec(memory_space=pltpu.VMEM)
    operands = in_vmem(*projected, live, out_weight, *bias_parts)
    return pl.pallas_call(
        functools.partial(row_attend_kernel, plan, step),
        grid=(seqs // step,),
        in_specs=[pl.BlockSpec(memory_space=pltpu.SMEM)] + [vmem] * len(operands),
        out_specs=pl.BlockSpec((parts, step * rows, width), lambda i: (0, i, 0)),
        out_shape=jax.ShapeDtypeStruct((parts, seqs * rows, width), BF16),
        scratch_shapes=[pltpu.VMEM((ATTN_HEAD_COUNT, length, length), F32)],
        compiler_params=params(24),
        name="row_attend",
    )(me, *operands)


def column_kernel(
    items, each, x_ref, live_ref, mask_ref, weight_ref, out_w_ref, factor_ref,
    out_ref, left_ref, right_ref, held, right_held,
):
    step = pl.program_id(0)
    total_rows = held.shape[1]
    length = total_rows // items

    @pl.when(step == 0)
    def _():
        for t in range(held.shape[0]):
            part = x_ref[:, :, t * LANES : (t + 1) * LANES].astype(F32)
            held[t] = part.reshape(total_rows, LANES)

    lanes = head_lanes(length)
    for n in range(each):
        item = step * each + n
        current = load_strided(held, item, items, length)
        normed = layer_normalize(current).astype(BF16)
        query, key, value, gate = project(normed, weight_ref)
        heads_out = attend_block(query, key, value, live_ref[n], lanes, None)
        heads_out = (heads_out * gate).astype(BF16)
        updated = (current + nn_dot(heads_out, out_w_ref[...])).astype(BF16).astype(F32)
        store_strided(held, item, items, updated)
        normed = layer_normalize(updated).astype(BF16)
        factors = nt_dot(factor_ref[...], normed) * mask_ref[pl.ds(item, 1), :]
        left_at = pl.ds(pl.multiple_of(item * FACTOR_CHANNELS, FACTOR_CHANNELS), FACTOR_CHANNELS)
        left_ref[left_at, :] = factors[:FACTOR_CHANNELS].astype(BF16)
        store_strided(right_held, item, items, factors[FACTOR_CHANNELS:])

    @pl.when(step == items // each - 1)
    def _():
        for t in range(held.shape[0]):
            part = held[t].reshape(out_ref.shape[:2] + (LANES,))
            out_ref[:, :, t * LANES : (t + 1) * LANES] = part.astype(BF16)
        right_ref[...] = joined_tiles(right_held).astype(BF16)


def column_attend(moved, live, mask_rows, weight, out_weight, factor_weight, items):
    width = moved.shape[2]
    total_rows = moved.shape[0] * moved.shape[1]
    length = total_rows // items
    factor_t = factor_weight.T
    each = 4
    side = (items * FACTOR_CHANNELS, length)
    left = right = jax.ShapeDtypeStruct(side, BF16)
    out = jax.ShapeDtypeStruct((length, items, width), BF16)
    return pl.pallas_call(
        functools.partial(column_kernel, items, each),
        grid=(items // each,),
        in_specs=[
            full_spec(moved.shape),
            pl.BlockSpec((each, length, LANES), lambda i: (i, 0, 0)),
            full_spec(mask_rows.shape),
            full_spec(weight.shape),
            full_spec(out_weight.shape),
            full_spec(factor_t.shape),
        ],
        out_specs=[full_spec(out.shape)] + [pl.BlockSpec(memory_space=pltpu.VMEM)] * 2,
        out_shape=[out, left, right],
        scratch_shapes=[tiled_scratch(total_rows, width), tiled_scratch(*side)],
        compiler_params=params(28),
        name="column_attend",
    )(moved, live, mask_rows, weight, out_weight, factor_t)


def outer_kernel(group, outer, items, *refs):
    lefts, rights = refs[:group], refs[group : group + outer]
    weight_ref = refs[group + outer]
    outs = refs[group + outer + 1 : -3]
    weight_rows, weight, held = refs[-3:]
    feat = FACTOR_CHANNELS
    quad = LANES // feat
    tiles = items * feat // LANES
    cols = outer * items
    width = weight_ref.shape[1]

    weight_rows[...] = weight_ref[...].astype(F32)
    weight[...] = jnp.zeros_like(weight)
    for e in range(feat):
        block = weight_rows[pl.ds(e, feat, stride=feat), :].astype(BF16)
        for i in range(quad):
            start = e * LANES + i * feat
            weight[start : start + feat, i * width : (i + 1) * width] = block

    right = jnp.concatenate([r[...] for r in rights], axis=0)
    for k in range(group):
        sums = nt_dot(right, lefts[k][...])
        sums = sums.reshape(outer, feat, items, sums.shape[1])
        sums = jnp.transpose(sums, (1, 0, 2, 3)).reshape(feat, cols, sums.shape[3]).astype(BF16)
        for t in range(tiles):
            at = slice((k * tiles + t) * cols, (k * tiles + t + 1) * cols)
            for e in range(feat):
                held[at, e * LANES : (e + 1) * LANES] = sums[e, :, t * LANES : (t + 1) * LANES]
    update = nn_dot(held[...], weight[...])
    for k in range(group):
        for t in range(tiles):
            rows = update[(k * tiles + t) * cols : (k * tiles + t + 1) * cols]
            for i in range(quad):
                outs[k][t * quad + i] = rows[:, i * width : (i + 1) * width].astype(BF16)


def outer_product(lefts, rights, weight, items):
    group, outer = len(lefts), len(rights)
    cols = outer * items
    tiles = items * FACTOR_CHANNELS // LANES
    depth = FACTOR_CHANNELS * LANES
    width = weight.shape[1]
    return pl.pallas_call(
        functools.partial(outer_kernel, group, outer, items),
        out_shape=[jax.ShapeDtypeStruct((items, cols, width), BF16)] * group,
        scratch_shapes=[
            pltpu.VMEM(weight.shape, F32),
            pltpu.VMEM((depth, LANES // FACTOR_CHANNELS * width), BF16),
            pltpu.VMEM((group * tiles * cols, depth), BF16),
        ],
        compiler_params=params(28),
        name="outer_product",
    )(*lefts, *rights, weight)


def finish_kernel(offsets, line, me_ref, pair_ref, scale_ref, *refs):
    parts, out_ref = refs[:-1], refs[-1]
    here = me_ref[0]
    items, cols, width = parts[0].shape
    outer = cols // items
    odd = (here & 1) == 1
    for k, offset in enumerate(offsets):
        for i in range(items):
            both = parts[k][i].astype(F32).reshape(outer // 2, 2, items, width)
            low, high = both[:, 0:1], both[:, 1:2]
            both = jnp.concatenate([jnp.where(odd, high, low), jnp.where(odd, low, high)], axis=1)
            both = both.reshape(outer // 2, 2 * items, width)
            for z in range(outer // 2):
                owner = here ^ (offset | line[z])
                start = pl.multiple_of((owner >> 1) * (2 * items), 2 * items)
                at = pl.ds(start, 2 * items)
                update = both[z] * scale_ref[at, i : i + 1]
                out_ref[i, at, :] = (pair_ref[i, at, :].astype(F32) + update).astype(BF16)


def finish(me, pair_rep, scale, parts, offsets, line):
    vmem = pl.BlockSpec(memory_space=pltpu.VMEM)
    return pl.pallas_call(
        functools.partial(finish_kernel, offsets, line),
        in_specs=[pl.BlockSpec(memory_space=pltpu.SMEM)] + [vmem] * (2 + len(parts)),
        out_specs=vmem,
        out_shape=jax.ShapeDtypeStruct(pair_rep.shape, BF16),
        compiler_params=params(16),
        name="finish",
    )(me, pair_rep, scale, *parts)


def exchange(block, count, offset):
    if offset == 0:
        return block
    return lax.ppermute(block, "dap", [(i, i ^ offset) for i in range(count)])


def per_device_fast(
    alignment,
    pair_rep,
    align_mask,
    residue_mask,
    bias_weight,
    row_proj_weight,
    row_out_weight,
    column_proj_weight,
    column_out_weight,
    outer_factor_weight,
    outer_out,
):
    count = lax.axis_size("dap")
    dap_index = lax.axis_index("dap")
    me = jnp.reshape(dap_index, (1,)).astype(jnp.int32)
    plane, line = offset_groups(count)
    seq_dev = alignment.shape[0]
    items = pair_rep.shape[0]
    total_seqs, total_res = align_mask.shape

    own_seqs = lax.dynamic_slice_in_dim(align_mask, dap_index * seq_dev, seq_dev, 0)
    own_res = lax.dynamic_slice_in_dim(align_mask, dap_index * items, items, 1)
    row_live = jnp.broadcast_to(own_seqs.astype(BF16)[:, :, None], (seq_dev, total_res, LANES))
    col_live = jnp.broadcast_to(own_res.T.astype(BF16)[:, :, None], (items, total_seqs, LANES))

    bias = pair_bias_block(pair_rep, bias_weight)
    projected = list(row_project(alignment, row_proj_weight))
    column = [exchange(bias, count, z) for z in line]
    *column, projected[0] = lax.optimization_barrier((*column, projected[0]))
    column = jnp.stack(column)
    bias_parts = [exchange(column, count, k) for k in plane]
    *bias_parts, row_live = lax.optimization_barrier((*bias_parts, row_live))
    plan = [[k | z for z in line] for k in plane]
    bias_parts += [exchange(part, count, 1) for part in bias_parts]
    plan += [[offset | 1 for offset in offsets] for offsets in plan]

    counts = jnp.einsum(
        "si,sj->ji", own_res.astype(BF16), align_mask.astype(BF16), preferred_element_type=F32
    )
    res_float = residue_mask.astype(F32)
    live_rows = lax.dynamic_slice_in_dim(res_float, dap_index * items, items, 0)
    scale = live_rows[None, :] * res_float[:, None] / (counts + count_eps)
    mask_rows = own_res.T.astype(F32)

    rows = row_attend(me, projected, row_live, row_out_weight, bias_parts, plan, count)
    moved = lax.all_to_all(rows, "dap", split_axis=0, concat_axis=0, tiled=True)
    updated, left, right = column_attend(
        moved,
        col_live,
        mask_rows,
        column_proj_weight,
        column_out_weight,
        outer_factor_weight,
        items,
    )
    rights = [exchange(right, count, z) for z in line]
    rights = [part for own in rights for part in (own, exchange(own, count, 1))]
    lefts = [exchange(left, count, k) for k in plane]
    parts = outer_product(lefts, rights, outer_out, items)
    parts = [exchange(part, count, k) for part, k in zip(parts, plane)]
    pair_out = finish(me, pair_rep, scale, parts, plane, line)
    return updated, pair_out


def offset_groups(count):
    bits = count.bit_length() - 1
    near = (bits - 1) // 2
    plane = [k << 1 for k in range(1 << near)]
    line = [z << (1 + near) for z in range(1 << (bits - 1 - near))]
    return plane, line


def solution(mesh):
    placed = (
        P("dap", None, None),
        P("dap", "branch", None),
        P(),
        P(),
        P(),
        P(None, None, "branch"),
        P(),
        P(None, None, "branch"),
        P(),
        P(),
        P(),
    )
    count = mesh.shape["dap"]
    whole_heads = mesh.shape["branch"] == 1 and count & (count - 1) == 0

    def per_device(*operands):
        alignment, pair_rep = operands[0], operands[1]
        tile = 8
        fits = whole_heads and alignment.shape[0] == tile and pair_rep.shape[0] == tile
        return (per_device_fast if fits else per_device_general)(*operands)

    return jax.shard_map(
        per_device,
        mesh=mesh,
        in_specs=placed,
        out_specs=(P(None, "dap", None), P("dap", "branch", None)),
        check_vma=False,
    )
```

```python
import functools
import math

import jax
import jax.numpy as jnp
from jax import lax
from jax.experimental import pallas as pl
from jax.experimental.pallas import tpu as pltpu
from jax.sharding import PartitionSpec as P

ATTN_HEAD_COUNT = 8
HEAD_CHANNELS = 32
FACTOR_CHANNELS = 32


norm_eps = 1e-05
count_eps = 0.001


def layer_normalize(values):
    centre = jnp.mean(values, axis=-1, keepdims=True)
    centred = values - centre
    spread = jnp.mean(centred * centred, axis=-1, keepdims=True)
    return centred * lax.rsqrt(spread + norm_eps)


def attend_heads(inputs, key_mask, proj_weight, out_weight, score_bias):
    batch = inputs.shape[0]
    length = inputs.shape[1]
    local_width = proj_weight.shape[2]
    local_heads = local_width // HEAD_CHANNELS
    normed = layer_normalize(inputs.astype(jnp.float32)).astype(jnp.bfloat16)
    projected = jnp.einsum("blc,kcd->kbld", normed, proj_weight, preferred_element_type=jnp.float32)
    triple = (
        projected[:3].astype(jnp.bfloat16).reshape(3, batch, length, local_heads, HEAD_CHANNELS)
    )
    gating = jax.nn.sigmoid(projected[3])

    def attend_one(operands):
        queries, key_rows, value_rows, mask_row = operands
        scores = jnp.einsum(
            "ihd,jhd->hij", queries, key_rows, preferred_element_type=jnp.float32
        ) / math.sqrt(HEAD_CHANNELS)
        if score_bias is not None:
            scores = scores + score_bias.astype(jnp.float32)
        raised = jnp.exp(scores) * mask_row[None, None, :]
        weights = (raised / jnp.sum(raised, axis=-1, keepdims=True)).astype(jnp.bfloat16)
        return jnp.einsum("hij,jhd->ihd", weights, value_rows, preferred_element_type=jnp.float32)

    attended_rows = lax.map(attend_one, (triple[0], triple[1], triple[2], key_mask))
    heads_out = (attended_rows.reshape(batch, length, local_width) * gating).astype(jnp.bfloat16)
    gathered = lax.all_gather(heads_out, "branch", axis=2, tiled=True)
    update = jnp.einsum("blf,fc->blc", gathered, out_weight, preferred_element_type=jnp.float32)
    return (inputs.astype(jnp.float32) + update).astype(jnp.bfloat16)


def per_device_general(
    alignment,
    pair_rep,
    align_mask,
    residue_mask,
    bias_weight,
    row_proj_weight,
    row_out_weight,
    column_proj_weight,
    column_out_weight,
    outer_factor_weight,
    outer_out,
):
    branch_count = lax.axis_size("branch")
    dap_count = lax.axis_size("dap")
    branch_index = lax.axis_index("branch")
    dap_index = lax.axis_index("dap")
    seq_dev = alignment.shape[0]
    res_dev = pair_rep.shape[0]
    quarter = pair_rep.shape[1]
    total_seqs = align_mask.shape[0]
    local_heads = ATTN_HEAD_COUNT // branch_count
    float_mask = align_mask.astype(jnp.float32)
    res_float = residue_mask.astype(jnp.float32)
    pair_normed = layer_normalize(pair_rep.astype(jnp.float32)).astype(jnp.bfloat16)
    bias_block = jnp.einsum(
        "ijc,ch->hij", pair_normed, bias_weight, preferred_element_type=jnp.float32
    ).astype(jnp.bfloat16)
    bias_wide = lax.all_gather(bias_block, "branch", axis=2, tiled=True)
    bias_full = lax.all_gather(bias_wide, "dap", axis=1, tiled=True)
    pair_score_bias = lax.dynamic_slice_in_dim(
        bias_full, branch_index * local_heads, local_heads, 0
    )
    sequence_row_mask = lax.dynamic_slice_in_dim(float_mask, dap_index * seq_dev, seq_dev, 0)
    row_alignment = attend_heads(
        alignment, sequence_row_mask, row_proj_weight, row_out_weight, pair_score_bias
    )
    send_mask = sequence_row_mask.astype(jnp.bfloat16)
    blocked_rows = row_alignment.reshape(seq_dev, dap_count, res_dev, row_alignment.shape[2])
    blocked_mask = send_mask.reshape(seq_dev, dap_count, res_dev)
    moved_rows = lax.all_to_all(blocked_rows, "dap", split_axis=1, concat_axis=0, tiled=True)
    moved_mask = lax.all_to_all(blocked_mask, "dap", split_axis=1, concat_axis=0, tiled=True)
    seq_total = moved_rows.shape[0]
    items = moved_rows.shape[2]
    flat_rows = moved_rows.reshape(seq_total, items, moved_rows.shape[3])
    flat_mask = moved_mask.reshape(seq_total, items)
    transposed_rows = jnp.swapaxes(flat_rows, 0, 1)
    key_mask = jnp.swapaxes(flat_mask, 0, 1).astype(jnp.float32)
    attended_rows = attend_heads(
        transposed_rows, key_mask, column_proj_weight, column_out_weight, None
    )
    column_alignment = jnp.swapaxes(attended_rows, 0, 1)
    outer_mean_normed = layer_normalize(column_alignment.astype(jnp.float32)).astype(jnp.bfloat16)
    projected = jnp.einsum(
        "src,ce->sre", outer_mean_normed, outer_factor_weight, preferred_element_type=jnp.float32
    )
    factor_pairs = (projected * flat_mask.astype(jnp.float32)[:, :, None]).astype(jnp.bfloat16)
    column_alignment, factor_pairs = (column_alignment, factor_pairs)
    blocked_out = column_alignment.reshape(seq_total, 1, items, column_alignment.shape[2])
    blocked_factors = factor_pairs.reshape(seq_total, 1, items, factor_pairs.shape[2])
    updated_alignment = blocked_out.reshape(total_seqs, res_dev, blocked_out.shape[3])
    factor_pairs = blocked_factors.reshape(total_seqs, res_dev, blocked_factors.shape[3])
    left_side = factor_pairs[:, :, :FACTOR_CHANNELS]
    right_local = factor_pairs[:, :, FACTOR_CHANNELS:]
    col_start = branch_index * quarter
    row_start = dap_index * res_dev
    mask_rows = lax.dynamic_slice_in_dim(align_mask, row_start, res_dev, 1).astype(jnp.bfloat16)
    mask_cols = lax.dynamic_slice_in_dim(align_mask, col_start, quarter, 1).astype(jnp.bfloat16)
    counts = jnp.einsum("si,sj->ij", mask_rows, mask_cols, preferred_element_type=jnp.float32)
    live_rows = lax.dynamic_slice_in_dim(res_float, row_start, res_dev, 0)
    live_cols = lax.dynamic_slice_in_dim(res_float, col_start, quarter, 0)
    outer_weight = outer_out.astype(jnp.float32)
    right_all = lax.all_gather(right_local, "dap", axis=1, tiled=True)
    right_mine = lax.dynamic_slice_in_dim(right_all, col_start, quarter, 1)
    outer_sums = jnp.einsum(
        "sic,sje->ijce", left_side, right_mine, preferred_element_type=jnp.float32
    )
    outer_sums = outer_sums.reshape(res_dev, quarter, FACTOR_CHANNELS * FACTOR_CHANNELS)
    update = jnp.einsum("ijf,fz->ijz", outer_sums, outer_weight, precision=lax.Precision.HIGHEST)
    live = live_rows[:, None] * live_cols[None, :]
    update = update / (counts[:, :, None] + count_eps) * live[:, :, None]
    pair_out = (pair_rep.astype(jnp.float32) + update).astype(jnp.bfloat16)
    return (updated_alignment, pair_out)


LANES = 128
LOG2E = math.log2(math.e)
LIVE_SCALE = 1.0 / 128.0
BF16 = jnp.bfloat16
F32 = jnp.float32
MIB = 1024 * 1024


def nt_dot(a, b):
    return lax.dot_general(a, b, (((1,), (1,)), ((), ())), preferred_element_type=F32)


def nn_dot(a, b):
    return jnp.dot(a, b, preferred_element_type=F32)


def full_spec(shape):
    zeros = (0,) * len(shape)
    return pl.BlockSpec(shape, lambda *_: zeros)


def params(mib):
    return pltpu.CompilerParams(vmem_limit_bytes=mib * MIB)


def tiled_scratch(rows, cols):
    return pltpu.VMEM((cols // LANES, rows, LANES), F32)


def store_strided(held, first, stride, values):
    rows = values.shape[0]
    for t in range(held.shape[0]):
        held[t, pl.ds(first, rows, stride=stride), :] = values[:, t * LANES : (t + 1) * LANES]


def load_strided(held, first, stride, rows):
    parts = [held[t, pl.ds(first, rows, stride=stride), :] for t in range(held.shape[0])]
    return jnp.concatenate(parts, axis=1)


def joined_tiles(held):
    return jnp.concatenate([held[t] for t in range(held.shape[0])], axis=1)


def in_hbm(*arrays):
    return [pltpu.with_memory_space_constraint(a, pltpu.HBM) for a in arrays]


def in_vmem(*arrays):
    return [pltpu.with_memory_space_constraint(a, pltpu.VMEM) for a in arrays]


def head_lanes(length):
    lane = lax.broadcasted_iota(jnp.int32, (length, LANES), 1) // HEAD_CHANNELS
    return [
        jnp.where(lane == t, 1.0, 0.0).astype(BF16) for t in range(LANES // HEAD_CHANNELS)
    ]


def quotient(top, below):
    guess = pl.reciprocal(below, approx=True)
    return top * (guess * (2.0 - below * guess))


def attend_block(query, key, value, live, lanes, bias_of):
    pieces = []
    per_tile = LANES // HEAD_CHANNELS
    rows = query.shape[0]
    for tile in range(query.shape[1] // LANES):
        cut = slice(tile * LANES, (tile + 1) * LANES)
        query_t, key_t = query[:, cut], key[:, cut]
        value_t = value[:, cut] * live
        stacked = jnp.concatenate([query_t * lanes[t][:rows] for t in range(per_tile)], axis=0)
        stacked = nt_dot(stacked, key_t)
        raised, sides = [], []
        for t in range(per_tile):
            scores = stacked[t * rows : (t + 1) * rows]
            if bias_of is not None:
                scores = scores + bias_of(tile * per_tile + t)
            raised.append(jnp.exp2(scores).astype(BF16))
            sides.append(jnp.concatenate([value_t * lanes[t], live * lanes[t]], axis=1))
        total = nn_dot(jnp.concatenate(raised, axis=1), jnp.concatenate(sides, axis=0))
        pieces.append(quotient(total[:, :LANES], total[:, LANES:]))
    return jnp.concatenate(pieces, axis=1)


def project(normed, weight_ref):
    scale = LOG2E / math.sqrt(HEAD_CHANNELS)
    query = (nn_dot(normed, weight_ref[0]) * scale).astype(BF16)
    key = nn_dot(normed, weight_ref[1]).astype(BF16)
    value = nn_dot(normed, weight_ref[2]).astype(BF16)
    gate = 0.5 * jnp.tanh(0.5 * nn_dot(normed, weight_ref[3])) + 0.5
    return query, key, value, gate


def bias_kernel(pair_ref, weight_ref, out_ref, held):
    rows, cols, width = pair_ref.shape
    normed = layer_normalize(pair_ref[...].astype(F32)).astype(BF16).reshape(rows * cols, width)
    bias = nt_dot(weight_ref[...], normed) * LOG2E
    for i in range(rows):
        store_strided(held, i, rows, bias[:, i * cols : (i + 1) * cols])
    out_ref[...] = joined_tiles(held).astype(BF16)


def pair_bias_block(pair_rep, bias_weight):
    rows, cols, width = pair_rep.shape
    out = jax.ShapeDtypeStruct((ATTN_HEAD_COUNT * rows, cols), BF16)
    weight = bias_weight.T
    return pl.pallas_call(
        bias_kernel,
        grid=(1,),
        in_specs=[full_spec(pair_rep.shape), full_spec(weight.shape)],
        out_specs=pl.BlockSpec(memory_space=pltpu.VMEM),
        out_shape=out,
        scratch_shapes=[tiled_scratch(*out.shape)],
        compiler_params=params(16),
        name="pair_bias",
    )(*in_hbm(pair_rep, weight))


def row_project_kernel(x_ref, weight_ref, q_ref, k_ref, v_ref, g_ref):
    for s in range(x_ref.shape[0]):
        normed = layer_normalize(x_ref[s].astype(F32)).astype(BF16)
        q_ref[s], k_ref[s], v_ref[s], g_ref[s] = project(normed, weight_ref)


def row_project(alignment, weight):
    seqs, length, width = alignment.shape
    step = 2
    block = pl.BlockSpec((step, length, width), lambda i: (i, 0, 0))
    return pl.pallas_call(
        row_project_kernel,
        grid=(seqs // step,),
        in_specs=[block, full_spec(weight.shape)],
        out_specs=[block] * 4,
        out_shape=[pltpu.HBM(alignment.shape, BF16)] * 3 + [pltpu.HBM(alignment.shape, F32)],
        compiler_params=params(24),
        name="row_project",
    )(*in_hbm(alignment, weight))


def row_attend_kernel(
    plan, step, me_ref, x_ref, q_ref, k_ref, v_ref, g_ref, live_ref, out_w_ref, *rest
):
    bias_refs, out_ref, bias_all = rest[: len(plan)], rest[-2], rest[-1]
    heads, length, _ = bias_all.shape

    @pl.when(pl.program_id(0) == 0)
    def _():
        for bias_ref, offsets in zip(bias_refs, plan):
            for z, offset in enumerate(offsets):
                block = bias_ref[z].astype(F32).reshape(heads, -1, length)
                rows = block.shape[1]
                owner = me_ref[0] ^ offset
                bias_all[:, pl.ds(pl.multiple_of(owner * rows, rows), rows), :] = block

    lanes = head_lanes(length)
    results = []
    parts, rows = out_ref.shape[0], out_ref.shape[1]
    for s in range(step):
        heads_out = attend_block(
            q_ref[s], k_ref[s], v_ref[s], live_ref[s], lanes, lambda h: bias_all[h]
        )
        heads_out = (heads_out * g_ref[s]).astype(BF16)
        total = x_ref[s].astype(F32) + nn_dot(heads_out, out_w_ref[...])
        results.append(total.reshape(parts, 1, rows // step, total.shape[1]))
    joined = jnp.concatenate(results, axis=1)
    out_ref[...] = joined.reshape(out_ref.shape).astype(BF16)


def row_attend(me, alignment, projected, live, out_weight, bias_parts, plan, parts):
    seqs, length, width = alignment.shape
    rows = length // parts
    step = 2
    vmem = pl.BlockSpec(memory_space=pltpu.VMEM)
    block = pl.BlockSpec((step, length, width), lambda i: (i, 0, 0))
    narrow = pl.BlockSpec((step, length, LANES), lambda i: (i, 0, 0))
    return pl.pallas_call(
        functools.partial(row_attend_kernel, plan, step),
        grid=(seqs // step,),
        in_specs=[pl.BlockSpec(memory_space=pltpu.SMEM)]
        + [block] * 5
        + [narrow, full_spec(out_weight.shape)]
        + [vmem] * len(bias_parts),
        out_specs=pl.BlockSpec((parts, step * rows, width), lambda i: (0, i, 0)),
        out_shape=jax.ShapeDtypeStruct((parts, seqs * rows, width), BF16),
        scratch_shapes=[pltpu.VMEM((ATTN_HEAD_COUNT, length, length), F32)],
        compiler_params=params(24),
        name="row_attend",
    )(me, *in_hbm(alignment, *projected, live, out_weight), *in_vmem(*bias_parts))


def column_kernel(
    items, each, x_ref, live_ref, mask_ref, weight_ref, out_w_ref, factor_ref,
    out_ref, left_ref, right_ref, held, right_held,
):
    step = pl.program_id(0)
    total_rows = held.shape[1]
    length = total_rows // items

    @pl.when(step == 0)
    def _():
        for t in range(held.shape[0]):
            part = x_ref[:, :, t * LANES : (t + 1) * LANES].astype(F32)
            held[t] = part.reshape(total_rows, LANES)

    lanes = head_lanes(length)
    for n in range(each):
        item = step * each + n
        current = load_strided(held, item, items, length)
        normed = layer_normalize(current).astype(BF16)
        query, key, value, gate = project(normed, weight_ref)
        live = live_ref[:, n : n + 1]
        for later in range(1, items // each):
            at = later * each + n
            live = jnp.where(step == later, live_ref[:, at : at + 1], live)
        live = jnp.broadcast_to(live * LIVE_SCALE, (length, LANES)).astype(BF16)
        heads_out = attend_block(query, key, value, live, lanes, None)
        heads_out = (heads_out * gate).astype(BF16)
        updated = (current + nn_dot(heads_out, out_w_ref[...])).astype(BF16).astype(F32)
        store_strided(held, item, items, updated)
        normed = layer_normalize(updated).astype(BF16)
        factors = nt_dot(factor_ref[...], normed) * mask_ref[pl.ds(item, 1), :]
        left_at = pl.ds(pl.multiple_of(item * FACTOR_CHANNELS, FACTOR_CHANNELS), FACTOR_CHANNELS)
        left_ref[left_at, :] = factors[:FACTOR_CHANNELS].astype(BF16)
        store_strided(right_held, item, items, factors[FACTOR_CHANNELS:])

    @pl.when(step == items // each - 1)
    def _():
        for t in range(held.shape[0]):
            part = held[t].reshape(out_ref.shape[:2] + (LANES,))
            out_ref[:, :, t * LANES : (t + 1) * LANES] = part.astype(BF16)
        right_ref[...] = joined_tiles(right_held).astype(BF16)


def column_attend(moved, live, mask_rows, weight, out_weight, factor_weight, items):
    width = moved.shape[2]
    total_rows = moved.shape[0] * moved.shape[1]
    length = total_rows // items
    factor_t = factor_weight.T
    each = 4
    side = (items * FACTOR_CHANNELS, length)
    left = right = jax.ShapeDtypeStruct(side, BF16)
    out = jax.ShapeDtypeStruct((length, items, width), BF16)
    return pl.pallas_call(
        functools.partial(column_kernel, items, each),
        grid=(items // each,),
        in_specs=[
            full_spec(moved.shape),
            full_spec(live.shape),
            full_spec(mask_rows.shape),
            full_spec(weight.shape),
            full_spec(out_weight.shape),
            full_spec(factor_t.shape),
        ],
        out_specs=[full_spec(out.shape)] + [pl.BlockSpec(memory_space=pltpu.VMEM)] * 2,
        out_shape=[out, left, right],
        scratch_shapes=[tiled_scratch(total_rows, width), tiled_scratch(*side)],
        compiler_params=params(28),
        name="column_attend",
    )(moved, live, mask_rows, weight, out_weight, factor_t)


def outer_kernel(group, outer, items, *refs):
    lefts, rights = refs[:group], refs[group : group + outer]
    weight_ref = refs[group + outer]
    outs = refs[group + outer + 1 : -3]
    weight_rows, weight, held = refs[-3:]
    feat = FACTOR_CHANNELS
    quad = LANES // feat
    tiles = items * feat // LANES
    cols = outer * items
    width = weight_ref.shape[1]

    weight_rows[...] = weight_ref[...].astype(F32)
    weight[...] = jnp.zeros_like(weight)
    for e in range(feat):
        block = weight_rows[pl.ds(e, feat, stride=feat), :].astype(BF16)
        for i in range(quad):
            start = e * LANES + i * feat
            weight[start : start + feat, i * width : (i + 1) * width] = block

    right = jnp.concatenate([r[...] for r in rights], axis=0)
    for k in range(group):
        sums = nt_dot(right, lefts[k][...])
        sums = sums.reshape(outer, feat, items, sums.shape[1])
        sums = jnp.transpose(sums, (1, 0, 2, 3)).reshape(feat, cols, sums.shape[3]).astype(BF16)
        for t in range(tiles):
            at = slice((k * tiles + t) * cols, (k * tiles + t + 1) * cols)
            for e in range(feat):
                held[at, e * LANES : (e + 1) * LANES] = sums[e, :, t * LANES : (t + 1) * LANES]
    update = nn_dot(held[...], weight[...])
    for k in range(group):
        for t in range(tiles):
            rows = update[(k * tiles + t) * cols : (k * tiles + t + 1) * cols]
            for i in range(quad):
                outs[k][t * quad + i] = rows[:, i * width : (i + 1) * width].astype(BF16)


def outer_product(lefts, rights, weight, items):
    group, outer = len(lefts), len(rights)
    cols = outer * items
    tiles = items * FACTOR_CHANNELS // LANES
    depth = FACTOR_CHANNELS * LANES
    width = weight.shape[1]
    return pl.pallas_call(
        functools.partial(outer_kernel, group, outer, items),
        out_shape=[jax.ShapeDtypeStruct((items, cols, width), BF16)] * group,
        scratch_shapes=[
            pltpu.VMEM(weight.shape, F32),
            pltpu.VMEM((depth, LANES // FACTOR_CHANNELS * width), BF16),
            pltpu.VMEM((group * tiles * cols, depth), BF16),
        ],
        compiler_params=params(28),
        name="outer_product",
    )(*lefts, *rights, weight)


def finish_kernel(offsets, line, me_ref, pair_ref, scale_ref, *refs):
    parts, out_ref = refs[:-1], refs[-1]
    here = me_ref[0]
    items, cols, width = parts[0].shape
    outer = cols // items
    odd = (here & 1) == 1
    for k, offset in enumerate(offsets):
        for i in range(items):
            both = parts[k][i].astype(F32).reshape(outer // 2, 2, items, width)
            low, high = both[:, 0:1], both[:, 1:2]
            both = jnp.concatenate([jnp.where(odd, high, low), jnp.where(odd, low, high)], axis=1)
            both = both.reshape(outer // 2, 2 * items, width)
            for z in range(outer // 2):
                owner = here ^ (offset | line[z])
                start = pl.multiple_of((owner >> 1) * (2 * items), 2 * items)
                at = pl.ds(start, 2 * items)
                update = both[z] * scale_ref[at, i : i + 1]
                out_ref[i, at, :] = (pair_ref[i, at, :].astype(F32) + update).astype(BF16)


def finish(me, pair_rep, scale, parts, offsets, line):
    vmem = pl.BlockSpec(memory_space=pltpu.VMEM)
    return pl.pallas_call(
        functools.partial(finish_kernel, offsets, line),
        in_specs=[pl.BlockSpec(memory_space=pltpu.SMEM)] + [vmem] * (2 + len(parts)),
        out_specs=vmem,
        out_shape=jax.ShapeDtypeStruct(pair_rep.shape, BF16),
        compiler_params=params(16),
        name="finish",
    )(me, pair_rep, scale, *parts)


def exchange(block, count, offset):
    if offset == 0:
        return block
    return lax.ppermute(block, "dap", [(i, i ^ offset) for i in range(count)])


def per_device_fast(
    alignment,
    pair_rep,
    align_mask,
    residue_mask,
    bias_weight,
    row_proj_weight,
    row_out_weight,
    column_proj_weight,
    column_out_weight,
    outer_factor_weight,
    outer_out,
):
    count = lax.axis_size("dap")
    dap_index = lax.axis_index("dap")
    me = jnp.reshape(dap_index, (1,)).astype(jnp.int32)
    plane, line = offset_groups(count)
    seq_dev = alignment.shape[0]
    items = pair_rep.shape[0]
    total_seqs, total_res = align_mask.shape

    own_seqs = lax.dynamic_slice_in_dim(align_mask, dap_index * seq_dev, seq_dev, 0)
    own_res = lax.dynamic_slice_in_dim(align_mask, dap_index * items, items, 1)
    row_live = (own_seqs.astype(F32) * LIVE_SCALE).astype(BF16)[:, :, None]
    row_live = jnp.broadcast_to(row_live, (seq_dev, total_res, LANES))
    col_live = own_res.astype(F32)

    bias = pair_bias_block(pair_rep, bias_weight)
    projected = list(row_project(alignment, row_proj_weight))
    column = [exchange(bias, count, z) for z in line]
    *column, projected[0] = lax.optimization_barrier((*column, projected[0]))
    column = jnp.stack(column)
    bias_parts = [exchange(column, count, k) for k in plane]
    *bias_parts, row_live = lax.optimization_barrier((*bias_parts, row_live))
    plan = [[k | z for z in line] for k in plane]
    bias_parts += [exchange(part, count, 1) for part in bias_parts]
    plan += [[offset | 1 for offset in offsets] for offsets in plan]

    counts = jnp.einsum(
        "si,sj->ji", own_res.astype(BF16), align_mask.astype(BF16), preferred_element_type=F32
    )
    res_float = residue_mask.astype(F32)
    live_rows = lax.dynamic_slice_in_dim(res_float, dap_index * items, items, 0)
    scale = live_rows[None, :] * res_float[:, None] / (counts + count_eps)
    mask_rows = own_res.T.astype(F32)

    rows = row_attend(
        me, alignment, projected, row_live, row_out_weight, bias_parts, plan, count
    )
    moved = lax.all_to_all(rows, "dap", split_axis=0, concat_axis=0, tiled=True)
    updated, left, right = column_attend(
        moved,
        col_live,
        mask_rows,
        column_proj_weight,
        column_out_weight,
        outer_factor_weight,
        items,
    )
    rights = [exchange(right, count, z) for z in line]
    rights = [part for own in rights for part in (own, exchange(own, count, 1))]
    lefts = [exchange(left, count, k) for k in plane]
    sent = outer_product(lefts[1:], rights, outer_out, items)
    parts = [exchange(part, count, k) for part, k in zip(sent, plane[1:])]
    own = outer_product([left], rights, outer_out, items)
    parts = list(own) + parts
    pair_out = finish(me, pair_rep, scale, parts, plane, line)
    return updated, pair_out


def offset_groups(count):
    bits = count.bit_length() - 1
    near = (bits - 1) // 2
    plane = [k << 1 for k in range(1 << near)]
    line = [z << (1 + near) for z in range(1 << (bits - 1 - near))]
    return plane, line


def solution(mesh):
    placed = (
        P("dap", None, None),
        P("dap", "branch", None),
        P(),
        P(),
        P(),
        P(None, None, "branch"),
        P(),
        P(None, None, "branch"),
        P(),
        P(),
        P(),
    )
    count = mesh.shape["dap"]
    whole_heads = mesh.shape["branch"] == 1 and count & (count - 1) == 0

    def per_device(*operands):
        alignment, pair_rep = operands[0], operands[1]
        tile = 8
        fits = whole_heads and alignment.shape[0] == tile and pair_rep.shape[0] == tile
        return (per_device_fast if fits else per_device_general)(*operands)

    return jax.shard_map(
        per_device,
        mesh=mesh,
        in_specs=placed,
        out_specs=(P(None, "dap", None), P("dap", "branch", None)),
        check_vma=False,
    )
```

```python
import functools
import math

import jax
import jax.numpy as jnp
from jax import lax
from jax.experimental import pallas as pl
from jax.experimental.pallas import tpu as pltpu
from jax.sharding import PartitionSpec as P

ATTN_HEAD_COUNT = 8
HEAD_CHANNELS = 32
FACTOR_CHANNELS = 32


norm_eps = 1e-05
count_eps = 0.001


def layer_normalize(values):
    centre = jnp.mean(values, axis=-1, keepdims=True)
    centred = values - centre
    spread = jnp.mean(centred * centred, axis=-1, keepdims=True)
    return centred * lax.rsqrt(spread + norm_eps)


def attend_heads(inputs, key_mask, proj_weight, out_weight, score_bias):
    batch = inputs.shape[0]
    length = inputs.shape[1]
    local_width = proj_weight.shape[2]
    local_heads = local_width // HEAD_CHANNELS
    normed = layer_normalize(inputs.astype(jnp.float32)).astype(jnp.bfloat16)
    projected = jnp.einsum("blc,kcd->kbld", normed, proj_weight, preferred_element_type=jnp.float32)
    triple = (
        projected[:3].astype(jnp.bfloat16).reshape(3, batch, length, local_heads, HEAD_CHANNELS)
    )
    gating = jax.nn.sigmoid(projected[3])

    def attend_one(operands):
        queries, key_rows, value_rows, mask_row = operands
        scores = jnp.einsum(
            "ihd,jhd->hij", queries, key_rows, preferred_element_type=jnp.float32
        ) / math.sqrt(HEAD_CHANNELS)
        if score_bias is not None:
            scores = scores + score_bias.astype(jnp.float32)
        raised = jnp.exp(scores) * mask_row[None, None, :]
        weights = (raised / jnp.sum(raised, axis=-1, keepdims=True)).astype(jnp.bfloat16)
        return jnp.einsum("hij,jhd->ihd", weights, value_rows, preferred_element_type=jnp.float32)

    attended_rows = lax.map(attend_one, (triple[0], triple[1], triple[2], key_mask))
    heads_out = (attended_rows.reshape(batch, length, local_width) * gating).astype(jnp.bfloat16)
    gathered = lax.all_gather(heads_out, "branch", axis=2, tiled=True)
    update = jnp.einsum("blf,fc->blc", gathered, out_weight, preferred_element_type=jnp.float32)
    return (inputs.astype(jnp.float32) + update).astype(jnp.bfloat16)


def per_device_general(
    alignment,
    pair_rep,
    align_mask,
    residue_mask,
    bias_weight,
    row_proj_weight,
    row_out_weight,
    column_proj_weight,
    column_out_weight,
    outer_factor_weight,
    outer_out,
):
    branch_count = lax.axis_size("branch")
    dap_count = lax.axis_size("dap")
    branch_index = lax.axis_index("branch")
    dap_index = lax.axis_index("dap")
    seq_dev = alignment.shape[0]
    res_dev = pair_rep.shape[0]
    quarter = pair_rep.shape[1]
    total_seqs = align_mask.shape[0]
    local_heads = ATTN_HEAD_COUNT // branch_count
    float_mask = align_mask.astype(jnp.float32)
    res_float = residue_mask.astype(jnp.float32)
    pair_normed = layer_normalize(pair_rep.astype(jnp.float32)).astype(jnp.bfloat16)
    bias_block = jnp.einsum(
        "ijc,ch->hij", pair_normed, bias_weight, preferred_element_type=jnp.float32
    ).astype(jnp.bfloat16)
    bias_wide = lax.all_gather(bias_block, "branch", axis=2, tiled=True)
    bias_full = lax.all_gather(bias_wide, "dap", axis=1, tiled=True)
    pair_score_bias = lax.dynamic_slice_in_dim(
        bias_full, branch_index * local_heads, local_heads, 0
    )
    sequence_row_mask = lax.dynamic_slice_in_dim(float_mask, dap_index * seq_dev, seq_dev, 0)
    row_alignment = attend_heads(
        alignment, sequence_row_mask, row_proj_weight, row_out_weight, pair_score_bias
    )
    send_mask = sequence_row_mask.astype(jnp.bfloat16)
    blocked_rows = row_alignment.reshape(seq_dev, dap_count, res_dev, row_alignment.shape[2])
    blocked_mask = send_mask.reshape(seq_dev, dap_count, res_dev)
    moved_rows = lax.all_to_all(blocked_rows, "dap", split_axis=1, concat_axis=0, tiled=True)
    moved_mask = lax.all_to_all(blocked_mask, "dap", split_axis=1, concat_axis=0, tiled=True)
    seq_total = moved_rows.shape[0]
    items = moved_rows.shape[2]
    flat_rows = moved_rows.reshape(seq_total, items, moved_rows.shape[3])
    flat_mask = moved_mask.reshape(seq_total, items)
    transposed_rows = jnp.swapaxes(flat_rows, 0, 1)
    key_mask = jnp.swapaxes(flat_mask, 0, 1).astype(jnp.float32)
    attended_rows = attend_heads(
        transposed_rows, key_mask, column_proj_weight, column_out_weight, None
    )
    column_alignment = jnp.swapaxes(attended_rows, 0, 1)
    outer_mean_normed = layer_normalize(column_alignment.astype(jnp.float32)).astype(jnp.bfloat16)
    projected = jnp.einsum(
        "src,ce->sre", outer_mean_normed, outer_factor_weight, preferred_element_type=jnp.float32
    )
    factor_pairs = (projected * flat_mask.astype(jnp.float32)[:, :, None]).astype(jnp.bfloat16)
    column_alignment, factor_pairs = (column_alignment, factor_pairs)
    blocked_out = column_alignment.reshape(seq_total, 1, items, column_alignment.shape[2])
    blocked_factors = factor_pairs.reshape(seq_total, 1, items, factor_pairs.shape[2])
    updated_alignment = blocked_out.reshape(total_seqs, res_dev, blocked_out.shape[3])
    factor_pairs = blocked_factors.reshape(total_seqs, res_dev, blocked_factors.shape[3])
    left_side = factor_pairs[:, :, :FACTOR_CHANNELS]
    right_local = factor_pairs[:, :, FACTOR_CHANNELS:]
    col_start = branch_index * quarter
    row_start = dap_index * res_dev
    mask_rows = lax.dynamic_slice_in_dim(align_mask, row_start, res_dev, 1).astype(jnp.bfloat16)
    mask_cols = lax.dynamic_slice_in_dim(align_mask, col_start, quarter, 1).astype(jnp.bfloat16)
    counts = jnp.einsum("si,sj->ij", mask_rows, mask_cols, preferred_element_type=jnp.float32)
    live_rows = lax.dynamic_slice_in_dim(res_float, row_start, res_dev, 0)
    live_cols = lax.dynamic_slice_in_dim(res_float, col_start, quarter, 0)
    outer_weight = outer_out.astype(jnp.float32)
    right_all = lax.all_gather(right_local, "dap", axis=1, tiled=True)
    right_mine = lax.dynamic_slice_in_dim(right_all, col_start, quarter, 1)
    outer_sums = jnp.einsum(
        "sic,sje->ijce", left_side, right_mine, preferred_element_type=jnp.float32
    )
    outer_sums = outer_sums.reshape(res_dev, quarter, FACTOR_CHANNELS * FACTOR_CHANNELS)
    update = jnp.einsum("ijf,fz->ijz", outer_sums, outer_weight, precision=lax.Precision.HIGHEST)
    live = live_rows[:, None] * live_cols[None, :]
    update = update / (counts[:, :, None] + count_eps) * live[:, :, None]
    pair_out = (pair_rep.astype(jnp.float32) + update).astype(jnp.bfloat16)
    return (updated_alignment, pair_out)


LANES = 128
LOG2E = math.log2(math.e)
LIVE_SCALE = 1.0 / 128.0
BF16 = jnp.bfloat16
F32 = jnp.float32
MIB = 1024 * 1024


def nt_dot(a, b):
    return lax.dot_general(a, b, (((1,), (1,)), ((), ())), preferred_element_type=F32)


def nn_dot(a, b):
    return jnp.dot(a, b, preferred_element_type=F32)


def full_spec(shape):
    zeros = (0,) * len(shape)
    return pl.BlockSpec(shape, lambda *_: zeros)


def params(mib):
    return pltpu.CompilerParams(vmem_limit_bytes=mib * MIB)


def tiled_scratch(rows, cols):
    return pltpu.VMEM((cols // LANES, rows, LANES), F32)


def store_strided(held, first, stride, values):
    rows = values.shape[0]
    for t in range(held.shape[0]):
        held[t, pl.ds(first, rows, stride=stride), :] = values[:, t * LANES : (t + 1) * LANES]


def load_strided(held, first, stride, rows):
    parts = [held[t, pl.ds(first, rows, stride=stride), :] for t in range(held.shape[0])]
    return jnp.concatenate(parts, axis=1)


def joined_tiles(held):
    return jnp.concatenate([held[t] for t in range(held.shape[0])], axis=1)


def in_hbm(*arrays):
    return [pltpu.with_memory_space_constraint(a, pltpu.HBM) for a in arrays]


def in_vmem(*arrays):
    return [pltpu.with_memory_space_constraint(a, pltpu.VMEM) for a in arrays]


def head_lanes(length):
    lane = lax.broadcasted_iota(jnp.int32, (length, LANES), 1) // HEAD_CHANNELS
    return [
        jnp.where(lane == t, 1.0, 0.0).astype(BF16) for t in range(LANES // HEAD_CHANNELS)
    ]


def live_lanes(live_ref, step):
    length, items = live_ref.shape
    at = pl.program_id(0)
    lives = []
    for n in range(step):
        live = live_ref[:, n : n + 1]
        for later in range(1, items // step):
            column = later * step + n
            live = jnp.where(at == later, live_ref[:, column : column + 1], live)
        lives.append(jnp.broadcast_to(live * LIVE_SCALE, (length, LANES)).astype(BF16))
    return lives


def quotient(top, below):
    guess = pl.reciprocal(below, approx=True)
    return top * (guess * (2.0 - below * guess))


def attend_block(query, key, value, live, lanes, bias_of):
    pieces = []
    per_tile = LANES // HEAD_CHANNELS
    rows = query.shape[0]
    for tile in range(query.shape[1] // LANES):
        cut = slice(tile * LANES, (tile + 1) * LANES)
        query_t, key_t = query[:, cut], key[:, cut]
        value_t = value[:, cut] * live
        stacked = jnp.concatenate([query_t * lanes[t][:rows] for t in range(per_tile)], axis=0)
        stacked = nt_dot(stacked, key_t)
        raised, sides = [], []
        for t in range(per_tile):
            scores = stacked[t * rows : (t + 1) * rows]
            if bias_of is not None:
                scores = scores + bias_of(tile * per_tile + t)
            raised.append(jnp.exp2(scores).astype(BF16))
            sides.append(jnp.concatenate([value_t * lanes[t], live * lanes[t]], axis=1))
        total = nn_dot(jnp.concatenate(raised, axis=1), jnp.concatenate(sides, axis=0))
        pieces.append(quotient(total[:, :LANES], total[:, LANES:]))
    return jnp.concatenate(pieces, axis=1)


def project(normed, weight_ref):
    scale = LOG2E / math.sqrt(HEAD_CHANNELS)
    query = (nn_dot(normed, weight_ref[0]) * scale).astype(BF16)
    key = nn_dot(normed, weight_ref[1]).astype(BF16)
    value = nn_dot(normed, weight_ref[2]).astype(BF16)
    gate = 0.5 * jnp.tanh(0.5 * nn_dot(normed, weight_ref[3])) + 0.5
    return query, key, value, gate


def bias_kernel(pair_ref, weight_ref, out_ref, held):
    rows, cols, width = pair_ref.shape
    normed = layer_normalize(pair_ref[...].astype(F32)).astype(BF16).reshape(rows * cols, width)
    bias = nt_dot(weight_ref[...], normed) * LOG2E
    for i in range(rows):
        store_strided(held, i, rows, bias[:, i * cols : (i + 1) * cols])
    out_ref[...] = joined_tiles(held).astype(BF16)


def pair_bias_block(pair_rep, bias_weight):
    rows, cols, width = pair_rep.shape
    out = jax.ShapeDtypeStruct((ATTN_HEAD_COUNT * rows, cols), BF16)
    weight = bias_weight.T
    return pl.pallas_call(
        bias_kernel,
        grid=(1,),
        in_specs=[full_spec(pair_rep.shape), full_spec(weight.shape)],
        out_specs=pl.BlockSpec(memory_space=pltpu.VMEM),
        out_shape=out,
        scratch_shapes=[tiled_scratch(*out.shape)],
        compiler_params=params(16),
        name="pair_bias",
    )(*in_hbm(pair_rep, weight))


def row_project_kernel(x_ref, weight_ref, q_ref, k_ref, v_ref, g_ref):
    for s in range(x_ref.shape[0]):
        normed = layer_normalize(x_ref[s].astype(F32)).astype(BF16)
        q_ref[s], k_ref[s], v_ref[s], g_ref[s] = project(normed, weight_ref)


def row_project(alignment, weight):
    seqs, length, width = alignment.shape
    step = 2
    block = pl.BlockSpec((step, length, width), lambda i: (i, 0, 0))
    return pl.pallas_call(
        row_project_kernel,
        grid=(seqs // step,),
        in_specs=[block, full_spec(weight.shape)],
        out_specs=[block] * 4,
        out_shape=[pltpu.HBM(alignment.shape, BF16)] * 3 + [pltpu.HBM(alignment.shape, F32)],
        compiler_params=params(24),
        name="row_project",
    )(*in_hbm(alignment, weight))


def row_attend_kernel(
    plan, step, me_ref, x_ref, q_ref, k_ref, v_ref, g_ref, live_ref, out_w_ref, *rest
):
    bias_refs, out_ref, bias_all = rest[: len(plan)], rest[-2], rest[-1]
    heads, length, _ = bias_all.shape

    @pl.when(pl.program_id(0) == 0)
    def _():
        for bias_ref, offsets in zip(bias_refs, plan):
            for z, offset in enumerate(offsets):
                block = bias_ref[z].astype(F32).reshape(heads, -1, length)
                rows = block.shape[1]
                owner = me_ref[0] ^ offset
                bias_all[:, pl.ds(pl.multiple_of(owner * rows, rows), rows), :] = block

    lanes = head_lanes(length)
    results = []
    parts, rows = out_ref.shape[0], out_ref.shape[1]
    lives = live_lanes(live_ref, step)
    for s in range(step):
        heads_out = attend_block(
            q_ref[s], k_ref[s], v_ref[s], lives[s], lanes, lambda h: bias_all[h]
        )
        heads_out = (heads_out * g_ref[s]).astype(BF16)
        total = x_ref[s].astype(F32) + nn_dot(heads_out, out_w_ref[...])
        results.append(total.reshape(parts, 1, rows // step, total.shape[1]))
    joined = jnp.concatenate(results, axis=1)
    out_ref[...] = joined.reshape(out_ref.shape).astype(BF16)


def row_attend(me, alignment, projected, live, out_weight, bias_parts, plan, parts):
    seqs, length, width = alignment.shape
    rows = length // parts
    step = 2
    vmem = pl.BlockSpec(memory_space=pltpu.VMEM)
    block = pl.BlockSpec((step, length, width), lambda i: (i, 0, 0))
    return pl.pallas_call(
        functools.partial(row_attend_kernel, plan, step),
        grid=(seqs // step,),
        in_specs=[pl.BlockSpec(memory_space=pltpu.SMEM)]
        + [block] * 5
        + [full_spec(live.shape), full_spec(out_weight.shape)]
        + [vmem] * len(bias_parts),
        out_specs=pl.BlockSpec((parts, step * rows, width), lambda i: (0, i, 0)),
        out_shape=jax.ShapeDtypeStruct((parts, seqs * rows, width), BF16),
        scratch_shapes=[pltpu.VMEM((ATTN_HEAD_COUNT, length, length), F32)],
        compiler_params=params(24),
        name="row_attend",
    )(me, *in_hbm(alignment, *projected, live, out_weight), *in_vmem(*bias_parts))


def column_kernel(
    items, each, x_ref, live_ref, mask_ref, weight_ref, out_w_ref, factor_ref,
    out_ref, left_ref, right_ref, held, right_held,
):
    step = pl.program_id(0)
    total_rows = held.shape[1]
    length = total_rows // items

    @pl.when(step == 0)
    def _():
        for t in range(held.shape[0]):
            part = x_ref[:, :, t * LANES : (t + 1) * LANES].astype(F32)
            held[t] = part.reshape(total_rows, LANES)

    lanes = head_lanes(length)
    lives = live_lanes(live_ref, each)
    rows = [load_strided(held, step * each + n, items, length) for n in range(each)]
    results = []
    for n in range(each):
        normed = layer_normalize(rows[n]).astype(BF16)
        query, key, value, gate = project(normed, weight_ref)
        heads_out = attend_block(query, key, value, lives[n], lanes, None)
        heads_out = (heads_out * gate).astype(BF16)
        updated = (rows[n] + nn_dot(heads_out, out_w_ref[...])).astype(BF16)
        normed = layer_normalize(updated.astype(F32)).astype(BF16)
        factors = nt_dot(factor_ref[...], normed) * mask_ref[pl.ds(step * each + n, 1), :]
        results.append((updated, factors))
    feat = FACTOR_CHANNELS
    for n, (updated, factors) in enumerate(results):
        item = step * each + n
        out_ref[n] = updated
        left_ref[pl.ds(pl.multiple_of(item * feat, feat), feat), :] = factors[:feat].astype(BF16)
        store_strided(right_held, item, items, factors[feat:])

    @pl.when(step == items // each - 1)
    def _():
        right_ref[...] = joined_tiles(right_held).astype(BF16)


def column_attend(moved, live, mask_rows, weight, out_weight, factor_weight, items):
    width = moved.shape[2]
    total_rows = moved.shape[0] * moved.shape[1]
    length = total_rows // items
    each = 4
    side = (items * FACTOR_CHANNELS, length)
    left = right = jax.ShapeDtypeStruct(side, BF16)
    vmem = pl.BlockSpec(memory_space=pltpu.VMEM)
    operands = in_vmem(moved, live, mask_rows, weight, out_weight, factor_weight.T)
    return pl.pallas_call(
        functools.partial(column_kernel, items, each),
        grid=(items // each,),
        in_specs=[vmem] * len(operands),
        out_specs=[pl.BlockSpec((each, length, width), lambda i: (i, 0, 0)), vmem, vmem],
        out_shape=[pltpu.HBM((items, length, width), BF16), left, right],
        scratch_shapes=[tiled_scratch(total_rows, width), tiled_scratch(*side)],
        compiler_params=params(28),
        name="column_attend",
    )(*operands)


def interleave_kernel(rows_ref, out_ref, held):
    items = rows_ref.shape[0]
    for item in range(items):
        store_strided(held, item, items, rows_ref[item].astype(F32))
    out_ref[...] = joined_tiles(held).reshape(out_ref.shape).astype(BF16)


def interleave(rows):
    items, length, width = rows.shape
    step = length // 4
    return pl.pallas_call(
        interleave_kernel,
        grid=(length // step,),
        in_specs=[pl.BlockSpec((items, step, width), lambda i: (0, i, 0))],
        out_specs=pl.BlockSpec((step, items, width), lambda i: (i, 0, 0)),
        out_shape=pltpu.HBM((length, items, width), BF16),
        scratch_shapes=[tiled_scratch(items * step, width)],
        compiler_params=params(16),
        name="interleave",
    )(*in_hbm(rows))


def outer_kernel(group, outer, items, *refs):
    lefts, rights = refs[:group], refs[group : group + outer]
    weight_ref = refs[group + outer]
    outs = refs[group + outer + 1 : -3]
    weight_rows, weight, held = refs[-3:]
    feat = FACTOR_CHANNELS
    quad = LANES // feat
    tiles = items * feat // LANES
    cols = outer * items
    width = weight_ref.shape[1]

    weight_rows[...] = weight_ref[...].astype(F32)
    weight[...] = jnp.zeros_like(weight)
    for e in range(feat):
        block = weight_rows[pl.ds(e, feat, stride=feat), :].astype(BF16)
        for i in range(quad):
            start = e * LANES + i * feat
            weight[start : start + feat, i * width : (i + 1) * width] = block

    right = jnp.concatenate([r[...] for r in rights], axis=0)
    for k in range(group):
        sums = nt_dot(right, lefts[k][...])
        sums = sums.reshape(outer, feat, items, sums.shape[1])
        sums = jnp.transpose(sums, (1, 0, 2, 3)).reshape(feat, cols, sums.shape[3]).astype(BF16)
        for t in range(tiles):
            at = slice((k * tiles + t) * cols, (k * tiles + t + 1) * cols)
            for e in range(feat):
                held[at, e * LANES : (e + 1) * LANES] = sums[e, :, t * LANES : (t + 1) * LANES]
    update = nn_dot(held[...], weight[...])
    for k in range(group):
        for t in range(tiles):
            rows = update[(k * tiles + t) * cols : (k * tiles + t + 1) * cols]
            for i in range(quad):
                outs[k][t * quad + i] = rows[:, i * width : (i + 1) * width].astype(BF16)


def outer_product(lefts, rights, weight, items):
    group, outer = len(lefts), len(rights)
    cols = outer * items
    tiles = items * FACTOR_CHANNELS // LANES
    depth = FACTOR_CHANNELS * LANES
    width = weight.shape[1]
    return pl.pallas_call(
        functools.partial(outer_kernel, group, outer, items),
        out_shape=[jax.ShapeDtypeStruct((items, cols, width), BF16)] * group,
        scratch_shapes=[
            pltpu.VMEM(weight.shape, F32),
            pltpu.VMEM((depth, LANES // FACTOR_CHANNELS * width), BF16),
            pltpu.VMEM((group * tiles * cols, depth), BF16),
        ],
        compiler_params=params(28),
        name="outer_product",
    )(*lefts, *rights, weight)


def finish_kernel(offsets, line, me_ref, pair_ref, scale_ref, *refs):
    parts, out_ref = refs[:-1], refs[-1]
    here = me_ref[0]
    items, cols, width = parts[0].shape
    outer = cols // items
    odd = (here & 1) == 1
    for k, offset in enumerate(offsets):
        for i in range(items):
            both = parts[k][i].astype(F32).reshape(outer // 2, 2, items, width)
            low, high = both[:, 0:1], both[:, 1:2]
            both = jnp.concatenate([jnp.where(odd, high, low), jnp.where(odd, low, high)], axis=1)
            both = both.reshape(outer // 2, 2 * items, width)
            for z in range(outer // 2):
                owner = here ^ (offset | line[z])
                start = pl.multiple_of((owner >> 1) * (2 * items), 2 * items)
                at = pl.ds(start, 2 * items)
                update = both[z] * scale_ref[at, i : i + 1]
                out_ref[i, at, :] = (pair_ref[i, at, :].astype(F32) + update).astype(BF16)


def finish(me, pair_rep, scale, parts, offsets, line):
    vmem = pl.BlockSpec(memory_space=pltpu.VMEM)
    return pl.pallas_call(
        functools.partial(finish_kernel, offsets, line),
        in_specs=[pl.BlockSpec(memory_space=pltpu.SMEM)] + [vmem] * (2 + len(parts)),
        out_specs=vmem,
        out_shape=jax.ShapeDtypeStruct(pair_rep.shape, BF16),
        compiler_params=params(16),
        name="finish",
    )(me, pair_rep, scale, *parts)


def exchange(block, count, offset):
    if offset == 0:
        return block
    return lax.ppermute(block, "dap", [(i, i ^ offset) for i in range(count)])


def per_device_fast(
    alignment,
    pair_rep,
    align_mask,
    residue_mask,
    bias_weight,
    row_proj_weight,
    row_out_weight,
    column_proj_weight,
    column_out_weight,
    outer_factor_weight,
    outer_out,
):
    count = lax.axis_size("dap")
    dap_index = lax.axis_index("dap")
    me = jnp.reshape(dap_index, (1,)).astype(jnp.int32)
    plane, line = offset_groups(count)
    seq_dev = alignment.shape[0]
    items = pair_rep.shape[0]
    total_seqs, total_res = align_mask.shape

    own_seqs = lax.dynamic_slice_in_dim(align_mask, dap_index * seq_dev, seq_dev, 0)
    own_res = lax.dynamic_slice_in_dim(align_mask, dap_index * items, items, 1)
    row_live = own_seqs.astype(F32).T
    col_live = own_res.astype(F32)

    bias = pair_bias_block(pair_rep, bias_weight)
    projected = list(row_project(alignment, row_proj_weight))
    column = [exchange(bias, count, z) for z in line]
    *column, projected[0] = lax.optimization_barrier((*column, projected[0]))
    column = jnp.stack(column)
    bias_parts = [exchange(column, count, k) for k in plane]
    *bias_parts, row_live, col_live = lax.optimization_barrier((*bias_parts, row_live, col_live))
    plan = [[k | z for z in line] for k in plane]
    bias_parts += [exchange(part, count, 1) for part in bias_parts]
    plan += [[offset | 1 for offset in offsets] for offsets in plan]

    counts = jnp.einsum(
        "si,sj->ji", own_res.astype(BF16), align_mask.astype(BF16), preferred_element_type=F32
    )
    res_float = residue_mask.astype(F32)
    live_rows = lax.dynamic_slice_in_dim(res_float, dap_index * items, items, 0)
    scale = live_rows[None, :] * res_float[:, None] / (counts + count_eps)
    mask_rows = own_res.T.astype(F32)

    rows = row_attend(
        me, alignment, projected, row_live, row_out_weight, bias_parts, plan, count
    )
    moved = lax.all_to_all(rows, "dap", split_axis=0, concat_axis=0, tiled=True)
    updated, left, right = column_attend(
        moved,
        col_live,
        mask_rows,
        column_proj_weight,
        column_out_weight,
        outer_factor_weight,
        items,
    )
    rights = [exchange(right, count, z) for z in line]
    updated = interleave(updated)
    *rights, updated = lax.optimization_barrier((*rights, updated))
    rights = [part for own in rights for part in (own, exchange(own, count, 1))]
    lefts = [exchange(left, count, k) for k in plane]
    sent = outer_product(lefts[1:], rights, outer_out, items)
    parts = [exchange(part, count, k) for part, k in zip(sent, plane[1:])]
    own = outer_product([left], rights, outer_out, items)
    parts = list(own) + parts
    pair_out = finish(me, pair_rep, scale, parts, plane, line)
    return updated, pair_out


def offset_groups(count):
    bits = count.bit_length() - 1
    near = (bits - 1) // 2
    plane = [k << 1 for k in range(1 << near)]
    line = [z << (1 + near) for z in range(1 << (bits - 1 - near))]
    return plane, line


def solution(mesh):
    placed = (
        P("dap", None, None),
        P("dap", "branch", None),
        P(),
        P(),
        P(),
        P(None, None, "branch"),
        P(),
        P(None, None, "branch"),
        P(),
        P(),
        P(),
    )
    count = mesh.shape["dap"]
    whole_heads = mesh.shape["branch"] == 1 and count & (count - 1) == 0

    def per_device(*operands):
        alignment, pair_rep = operands[0], operands[1]
        tile = 8
        fits = whole_heads and alignment.shape[0] == tile and pair_rep.shape[0] == tile
        return (per_device_fast if fits else per_device_general)(*operands)

    return jax.shard_map(
        per_device,
        mesh=mesh,
        in_specs=placed,
        out_specs=(P(None, "dap", None), P("dap", "branch", None)),
        check_vma=False,
    )
```

```python
import functools
import math

import jax
import jax.numpy as jnp
from jax import lax
from jax.experimental import pallas as pl
from jax.experimental.pallas import tpu as pltpu
from jax.sharding import PartitionSpec as P

ATTN_HEAD_COUNT = 8
HEAD_CHANNELS = 32
FACTOR_CHANNELS = 32


norm_eps = 1e-05
count_eps = 0.001


def layer_normalize(values):
    centre = jnp.mean(values, axis=-1, keepdims=True)
    centred = values - centre
    spread = jnp.mean(centred * centred, axis=-1, keepdims=True)
    return centred * lax.rsqrt(spread + norm_eps)


def attend_heads(inputs, key_mask, proj_weight, out_weight, score_bias):
    batch = inputs.shape[0]
    length = inputs.shape[1]
    local_width = proj_weight.shape[2]
    local_heads = local_width // HEAD_CHANNELS
    normed = layer_normalize(inputs.astype(jnp.float32)).astype(jnp.bfloat16)
    projected = jnp.einsum("blc,kcd->kbld", normed, proj_weight, preferred_element_type=jnp.float32)
    triple = (
        projected[:3].astype(jnp.bfloat16).reshape(3, batch, length, local_heads, HEAD_CHANNELS)
    )
    gating = jax.nn.sigmoid(projected[3])

    def attend_one(operands):
        queries, key_rows, value_rows, mask_row = operands
        scores = jnp.einsum(
            "ihd,jhd->hij", queries, key_rows, preferred_element_type=jnp.float32
        ) / math.sqrt(HEAD_CHANNELS)
        if score_bias is not None:
            scores = scores + score_bias.astype(jnp.float32)
        raised = jnp.exp(scores) * mask_row[None, None, :]
        weights = (raised / jnp.sum(raised, axis=-1, keepdims=True)).astype(jnp.bfloat16)
        return jnp.einsum("hij,jhd->ihd", weights, value_rows, preferred_element_type=jnp.float32)

    attended_rows = lax.map(attend_one, (triple[0], triple[1], triple[2], key_mask))
    heads_out = (attended_rows.reshape(batch, length, local_width) * gating).astype(jnp.bfloat16)
    gathered = lax.all_gather(heads_out, "branch", axis=2, tiled=True)
    update = jnp.einsum("blf,fc->blc", gathered, out_weight, preferred_element_type=jnp.float32)
    return (inputs.astype(jnp.float32) + update).astype(jnp.bfloat16)


def per_device_general(
    alignment,
    pair_rep,
    align_mask,
    residue_mask,
    bias_weight,
    row_proj_weight,
    row_out_weight,
    column_proj_weight,
    column_out_weight,
    outer_factor_weight,
    outer_out,
):
    branch_count = lax.axis_size("branch")
    dap_count = lax.axis_size("dap")
    branch_index = lax.axis_index("branch")
    dap_index = lax.axis_index("dap")
    seq_dev = alignment.shape[0]
    res_dev = pair_rep.shape[0]
    quarter = pair_rep.shape[1]
    total_seqs = align_mask.shape[0]
    local_heads = ATTN_HEAD_COUNT // branch_count
    float_mask = align_mask.astype(jnp.float32)
    res_float = residue_mask.astype(jnp.float32)
    pair_normed = layer_normalize(pair_rep.astype(jnp.float32)).astype(jnp.bfloat16)
    bias_block = jnp.einsum(
        "ijc,ch->hij", pair_normed, bias_weight, preferred_element_type=jnp.float32
    ).astype(jnp.bfloat16)
    bias_wide = lax.all_gather(bias_block, "branch", axis=2, tiled=True)
    bias_full = lax.all_gather(bias_wide, "dap", axis=1, tiled=True)
    pair_score_bias = lax.dynamic_slice_in_dim(
        bias_full, branch_index * local_heads, local_heads, 0
    )
    sequence_row_mask = lax.dynamic_slice_in_dim(float_mask, dap_index * seq_dev, seq_dev, 0)
    row_alignment = attend_heads(
        alignment, sequence_row_mask, row_proj_weight, row_out_weight, pair_score_bias
    )
    send_mask = sequence_row_mask.astype(jnp.bfloat16)
    blocked_rows = row_alignment.reshape(seq_dev, dap_count, res_dev, row_alignment.shape[2])
    blocked_mask = send_mask.reshape(seq_dev, dap_count, res_dev)
    moved_rows = lax.all_to_all(blocked_rows, "dap", split_axis=1, concat_axis=0, tiled=True)
    moved_mask = lax.all_to_all(blocked_mask, "dap", split_axis=1, concat_axis=0, tiled=True)
    seq_total = moved_rows.shape[0]
    items = moved_rows.shape[2]
    flat_rows = moved_rows.reshape(seq_total, items, moved_rows.shape[3])
    flat_mask = moved_mask.reshape(seq_total, items)
    transposed_rows = jnp.swapaxes(flat_rows, 0, 1)
    key_mask = jnp.swapaxes(flat_mask, 0, 1).astype(jnp.float32)
    attended_rows = attend_heads(
        transposed_rows, key_mask, column_proj_weight, column_out_weight, None
    )
    column_alignment = jnp.swapaxes(attended_rows, 0, 1)
    outer_mean_normed = layer_normalize(column_alignment.astype(jnp.float32)).astype(jnp.bfloat16)
    projected = jnp.einsum(
        "src,ce->sre", outer_mean_normed, outer_factor_weight, preferred_element_type=jnp.float32
    )
    factor_pairs = (projected * flat_mask.astype(jnp.float32)[:, :, None]).astype(jnp.bfloat16)
    column_alignment, factor_pairs = (column_alignment, factor_pairs)
    blocked_out = column_alignment.reshape(seq_total, 1, items, column_alignment.shape[2])
    blocked_factors = factor_pairs.reshape(seq_total, 1, items, factor_pairs.shape[2])
    updated_alignment = blocked_out.reshape(total_seqs, res_dev, blocked_out.shape[3])
    factor_pairs = blocked_factors.reshape(total_seqs, res_dev, blocked_factors.shape[3])
    left_side = factor_pairs[:, :, :FACTOR_CHANNELS]
    right_local = factor_pairs[:, :, FACTOR_CHANNELS:]
    col_start = branch_index * quarter
    row_start = dap_index * res_dev
    mask_rows = lax.dynamic_slice_in_dim(align_mask, row_start, res_dev, 1).astype(jnp.bfloat16)
    mask_cols = lax.dynamic_slice_in_dim(align_mask, col_start, quarter, 1).astype(jnp.bfloat16)
    counts = jnp.einsum("si,sj->ij", mask_rows, mask_cols, preferred_element_type=jnp.float32)
    live_rows = lax.dynamic_slice_in_dim(res_float, row_start, res_dev, 0)
    live_cols = lax.dynamic_slice_in_dim(res_float, col_start, quarter, 0)
    outer_weight = outer_out.astype(jnp.float32)
    right_all = lax.all_gather(right_local, "dap", axis=1, tiled=True)
    right_mine = lax.dynamic_slice_in_dim(right_all, col_start, quarter, 1)
    outer_sums = jnp.einsum(
        "sic,sje->ijce", left_side, right_mine, preferred_element_type=jnp.float32
    )
    outer_sums = outer_sums.reshape(res_dev, quarter, FACTOR_CHANNELS * FACTOR_CHANNELS)
    update = jnp.einsum("ijf,fz->ijz", outer_sums, outer_weight, precision=lax.Precision.HIGHEST)
    live = live_rows[:, None] * live_cols[None, :]
    update = update / (counts[:, :, None] + count_eps) * live[:, :, None]
    pair_out = (pair_rep.astype(jnp.float32) + update).astype(jnp.bfloat16)
    return (updated_alignment, pair_out)


LANES = 128
LOG2E = math.log2(math.e)
LIVE_SCALE = 1.0 / 128.0
BF16 = jnp.bfloat16
F32 = jnp.float32
MIB = 1024 * 1024


def nt_dot(a, b):
    return lax.dot_general(a, b, (((1,), (1,)), ((), ())), preferred_element_type=F32)


def nn_dot(a, b):
    return jnp.dot(a, b, preferred_element_type=F32)


def full_spec(shape):
    zeros = (0,) * len(shape)
    return pl.BlockSpec(shape, lambda *_: zeros)


def params(mib):
    return pltpu.CompilerParams(vmem_limit_bytes=mib * MIB)


def tiled_scratch(rows, cols):
    return pltpu.VMEM((cols // LANES, rows, LANES), F32)


def store_strided(held, first, stride, values):
    rows = values.shape[0]
    for t in range(held.shape[0]):
        held[t, pl.ds(first, rows, stride=stride), :] = values[:, t * LANES : (t + 1) * LANES]


def load_strided(held, first, stride, rows):
    parts = [held[t, pl.ds(first, rows, stride=stride), :] for t in range(held.shape[0])]
    return jnp.concatenate(parts, axis=1)


def joined_tiles(held):
    return jnp.concatenate([held[t] for t in range(held.shape[0])], axis=1)


def in_hbm(*arrays):
    return [pltpu.with_memory_space_constraint(a, pltpu.HBM) for a in arrays]


def in_vmem(*arrays):
    return [pltpu.with_memory_space_constraint(a, pltpu.VMEM) for a in arrays]


def head_lanes(length):
    lane = lax.broadcasted_iota(jnp.int32, (length, LANES), 1) // HEAD_CHANNELS
    return [
        jnp.where(lane == t, 1.0, 0.0).astype(BF16) for t in range(LANES // HEAD_CHANNELS)
    ]


def one_hot(shape, dim, place, value=1.0):
    hit = lax.broadcasted_iota(jnp.int32, shape, dim) == place
    return jnp.where(hit, value, 0.0).astype(BF16)


def quotient(top, below):
    guess = pl.reciprocal(below, approx=True)
    return top * (guess * (2.0 - below * guess))


def attend_all(items, lanes, bias_of):
    per_tile = LANES // HEAD_CHANNELS
    rows, width = items[0][0].shape
    tasks = [(n, tile) for n in range(len(items)) for tile in range(width // LANES)]
    scores, raised, pieces = {}, {}, [[] for _ in items]

    def score(at):
        n, tile = tasks[at]
        cut = slice(tile * LANES, (tile + 1) * LANES)
        query, key = items[n][0][:, cut], items[n][1][:, cut]
        stacked = jnp.concatenate([query * lanes[t] for t in range(per_tile)], axis=0)
        scores[at] = nt_dot(stacked, key)

    def raise_scores(at):
        n, tile = tasks[at]
        stacked = scores.pop(at)
        parts = []
        for t in range(per_tile):
            part = stacked[t * rows : (t + 1) * rows]
            if bias_of is not None:
                part = part + bias_of(tile * per_tile + t)
            parts.append(jnp.exp2(part).astype(BF16))
        raised[at] = jnp.concatenate(parts, axis=1)

    def gather(at):
        n, tile = tasks[at]
        cut = slice(tile * LANES, (tile + 1) * LANES)
        live = items[n][3]
        value = items[n][2][:, cut] * live
        sides = [
            jnp.concatenate([value * lanes[t], live * lanes[t]], axis=1) for t in range(per_tile)
        ]
        total = nn_dot(raised.pop(at), jnp.concatenate(sides, axis=0))
        pieces[n].append(quotient(total[:, :LANES], total[:, LANES:]))

    for at in range(len(tasks) + 2):
        if at < len(tasks):
            score(at)
        if 0 <= at - 2:
            gather(at - 2)
        if 0 <= at - 1 < len(tasks):
            raise_scores(at - 1)
    return [jnp.concatenate(p, axis=1) for p in pieces]


def project(normed, weight_ref):
    scale = LOG2E / math.sqrt(HEAD_CHANNELS)
    query = (nn_dot(normed, weight_ref[0]) * scale).astype(BF16)
    key = nn_dot(normed, weight_ref[1]).astype(BF16)
    value = nn_dot(normed, weight_ref[2]).astype(BF16)
    gate = 0.5 * jnp.tanh(0.5 * nn_dot(normed, weight_ref[3])) + 0.5
    return query, key, value, gate


def bias_kernel(pair_ref, weight_ref, out_ref, held):
    rows, cols, width = pair_ref.shape
    normed = layer_normalize(pair_ref[...].astype(F32)).astype(BF16).reshape(rows * cols, width)
    bias = nt_dot(weight_ref[...], normed) * LOG2E
    for i in range(rows):
        store_strided(held, i, rows, bias[:, i * cols : (i + 1) * cols])
    out_ref[...] = joined_tiles(held).astype(BF16)


def pair_bias_block(pair_rep, bias_weight):
    rows, cols, width = pair_rep.shape
    out = jax.ShapeDtypeStruct((ATTN_HEAD_COUNT * rows, cols), BF16)
    weight = bias_weight.T
    return pl.pallas_call(
        bias_kernel,
        grid=(1,),
        in_specs=[full_spec(pair_rep.shape), full_spec(weight.shape)],
        out_specs=pl.BlockSpec(memory_space=pltpu.VMEM),
        out_shape=out,
        scratch_shapes=[tiled_scratch(*out.shape)],
        compiler_params=params(16),
        name="pair_bias",
    )(*in_hbm(pair_rep, weight))


def row_project_kernel(x_ref, weight_ref, q_ref, k_ref, v_ref, g_ref):
    for s in range(x_ref.shape[0]):
        normed = layer_normalize(x_ref[s].astype(F32)).astype(BF16)
        q_ref[s], k_ref[s], v_ref[s], g_ref[s] = project(normed, weight_ref)


def row_project(alignment, weight):
    seqs, length, width = alignment.shape
    step = 2
    block = pl.BlockSpec((step, length, width), lambda i: (i, 0, 0))
    return pl.pallas_call(
        row_project_kernel,
        grid=(seqs // step,),
        in_specs=[block, full_spec(weight.shape)],
        out_specs=[block] * 4,
        out_shape=[pltpu.HBM(alignment.shape, BF16)] * 3 + [pltpu.HBM(alignment.shape, F32)],
        compiler_params=params(24),
        name="row_project",
    )(*in_hbm(alignment, weight))


def row_attend_kernel(
    plan, step, seqs, me_ref, x_ref, q_ref, k_ref, v_ref, g_ref, mask_ref, out_w_ref, *rest
):
    bias_refs, out_ref, bias_all = rest[: len(plan)], rest[-2], rest[-1]
    heads, length, _ = bias_all.shape

    @pl.when(pl.program_id(0) == 0)
    def _():
        for bias_ref, offsets in zip(bias_refs, plan):
            for z, offset in enumerate(offsets):
                block = bias_ref[z].astype(F32).reshape(heads, -1, length)
                rows = block.shape[1]
                owner = me_ref[0] ^ offset
                bias_all[:, pl.ds(pl.multiple_of(owner * rows, rows), rows), :] = block

    lanes = head_lanes(length)
    parts, rows = out_ref.shape[0], out_ref.shape[1]
    own = mask_ref[pl.ds(pl.multiple_of(me_ref[0] * seqs, seqs), seqs), :]
    own = own.astype(F32).astype(BF16)
    items = []
    for s in range(step):
        place = pl.program_id(0) * step + s
        spot = one_hot((seqs, LANES), 0, place, LIVE_SCALE)
        live = lax.dot_general(
            own, spot, (((0,), (0,)), ((), ())), preferred_element_type=F32
        ).astype(BF16)
        items.append((q_ref[s], k_ref[s], v_ref[s], live))
    results = []
    for s, heads_out in enumerate(attend_all(items, lanes, lambda h: bias_all[h])):
        heads_out = (heads_out * g_ref[s]).astype(BF16)
        total = x_ref[s].astype(F32) + nn_dot(heads_out, out_w_ref[...])
        results.append(total.reshape(parts, 1, rows // step, total.shape[1]))
    joined = jnp.concatenate(results, axis=1)
    out_ref[...] = joined.reshape(out_ref.shape).astype(BF16)


def row_attend(me, alignment, projected, mask, out_weight, bias_parts, plan, parts):
    seqs, length, width = alignment.shape
    rows = length // parts
    step = 2
    vmem = pl.BlockSpec(memory_space=pltpu.VMEM)
    block = pl.BlockSpec((step, length, width), lambda i: (i, 0, 0))
    return pl.pallas_call(
        functools.partial(row_attend_kernel, plan, step, seqs),
        grid=(seqs // step,),
        in_specs=[pl.BlockSpec(memory_space=pltpu.SMEM)]
        + [block] * 5
        + [full_spec(mask.shape), full_spec(out_weight.shape)]
        + [vmem] * len(bias_parts),
        out_specs=pl.BlockSpec((parts, step * rows, width), lambda i: (0, i, 0)),
        out_shape=jax.ShapeDtypeStruct((parts, seqs * rows, width), BF16),
        scratch_shapes=[pltpu.VMEM((ATTN_HEAD_COUNT, length, length), F32)],
        compiler_params=params(24),
        name="row_attend",
    )(me, *in_hbm(alignment, *projected, mask, out_weight), *in_vmem(*bias_parts))


def column_kernel(
    items, each, me_ref, x_ref, mask_ref, weight_ref, out_w_ref, factor_ref,
    out_ref, left_ref, right_ref, held, right_held,
):
    step = pl.program_id(0)
    total_rows = held.shape[1]
    length = total_rows // items

    @pl.when(step == 0)
    def _():
        for t in range(held.shape[0]):
            part = x_ref[:, :, t * LANES : (t + 1) * LANES].astype(F32)
            held[t] = part.reshape(total_rows, LANES)

    lanes = head_lanes(length)
    mask = mask_ref[...].astype(F32).astype(BF16)
    residues = mask.shape[1]
    place = me_ref[0] * items + step * each
    rows = [load_strided(held, step * each + n, items, length) for n in range(each)]
    inputs, gates = [], []
    for n in range(each):
        normed = layer_normalize(rows[n]).astype(BF16)
        query, key, value, gate = project(normed, weight_ref)
        live = nn_dot(mask, one_hot((residues, LANES), 0, place + n, LIVE_SCALE)).astype(BF16)
        inputs.append((query, key, value, live))
        gates.append(gate)
    results = []
    for n, heads_out in enumerate(attend_all(inputs, lanes, None)):
        heads_out = (heads_out * gates[n]).astype(BF16)
        updated = (rows[n] + nn_dot(heads_out, out_w_ref[...])).astype(BF16)
        normed = layer_normalize(updated.astype(F32)).astype(BF16)
        live_row = nt_dot(one_hot((8, residues), 1, place + n), mask)[:1]
        results.append((updated, nt_dot(factor_ref[...], normed) * live_row))
    feat = FACTOR_CHANNELS
    for n, (updated, factors) in enumerate(results):
        item = step * each + n
        out_ref[n] = updated
        left_ref[pl.ds(pl.multiple_of(item * feat, feat), feat), :] = factors[:feat].astype(BF16)
        store_strided(right_held, item, items, factors[feat:])

    @pl.when(step == items // each - 1)
    def _():
        right_ref[...] = joined_tiles(right_held).astype(BF16)


def column_attend(me, moved, mask, weight, out_weight, factor_weight, items):
    width = moved.shape[2]
    total_rows = moved.shape[0] * moved.shape[1]
    length = total_rows // items
    each = 4
    side = (items * FACTOR_CHANNELS, length)
    left = right = jax.ShapeDtypeStruct(side, BF16)
    vmem = pl.BlockSpec(memory_space=pltpu.VMEM)
    operands = in_vmem(moved, mask, weight, out_weight, factor_weight.T)
    return pl.pallas_call(
        functools.partial(column_kernel, items, each),
        grid=(items // each,),
        in_specs=[pl.BlockSpec(memory_space=pltpu.SMEM)] + [vmem] * len(operands),
        out_specs=[pl.BlockSpec((each, length, width), lambda i: (i, 0, 0)), vmem, vmem],
        out_shape=[pltpu.HBM((items, length, width), BF16), left, right],
        scratch_shapes=[tiled_scratch(total_rows, width), tiled_scratch(*side)],
        compiler_params=params(28),
        name="column_attend",
    )(me, *operands)


def interleave_kernel(rows_ref, out_ref, held):
    items = rows_ref.shape[0]
    for item in range(items):
        store_strided(held, item, items, rows_ref[item].astype(F32))
    out_ref[...] = joined_tiles(held).reshape(out_ref.shape).astype(BF16)


def interleave(rows):
    items, length, width = rows.shape
    step = length // 4
    return pl.pallas_call(
        interleave_kernel,
        grid=(length // step,),
        in_specs=[pl.BlockSpec((items, step, width), lambda i: (0, i, 0))],
        out_specs=pl.BlockSpec((step, items, width), lambda i: (i, 0, 0)),
        out_shape=pltpu.HBM((length, items, width), BF16),
        scratch_shapes=[tiled_scratch(items * step, width)],
        compiler_params=params(16),
        name="interleave",
    )(*in_hbm(rows))


def outer_kernel(group, outer, items, *refs):
    lefts, rights = refs[:group], refs[group : group + outer]
    weight_ref = refs[group + outer]
    outs = refs[group + outer + 1 : -3]
    weight_rows, weight, held = refs[-3:]
    feat = FACTOR_CHANNELS
    quad = LANES // feat
    tiles = items * feat // LANES
    cols = outer * items
    width = weight_ref.shape[1]

    weight_rows[...] = weight_ref[...].astype(F32)
    weight[...] = jnp.zeros_like(weight)
    for e in range(feat):
        block = weight_rows[pl.ds(e, feat, stride=feat), :].astype(BF16)
        for i in range(quad):
            start = e * LANES + i * feat
            weight[start : start + feat, i * width : (i + 1) * width] = block

    right = jnp.concatenate([r[...] for r in rights], axis=0)
    for k in range(group):
        sums = nt_dot(right, lefts[k][...])
        sums = sums.reshape(outer, feat, items, sums.shape[1])
        sums = jnp.transpose(sums, (1, 0, 2, 3)).reshape(feat, cols, sums.shape[3]).astype(BF16)
        for t in range(tiles):
            at = slice((k * tiles + t) * cols, (k * tiles + t + 1) * cols)
            for e in range(feat):
                held[at, e * LANES : (e + 1) * LANES] = sums[e, :, t * LANES : (t + 1) * LANES]
    update = nn_dot(held[...], weight[...])
    for k in range(group):
        for t in range(tiles):
            rows = update[(k * tiles + t) * cols : (k * tiles + t + 1) * cols]
            for i in range(quad):
                outs[k][t * quad + i] = rows[:, i * width : (i + 1) * width].astype(BF16)


def outer_product(lefts, rights, weight, items):
    group, outer = len(lefts), len(rights)
    cols = outer * items
    tiles = items * FACTOR_CHANNELS // LANES
    depth = FACTOR_CHANNELS * LANES
    width = weight.shape[1]
    return pl.pallas_call(
        functools.partial(outer_kernel, group, outer, items),
        out_shape=[jax.ShapeDtypeStruct((items, cols, width), BF16)] * group,
        scratch_shapes=[
            pltpu.VMEM(weight.shape, F32),
            pltpu.VMEM((depth, LANES // FACTOR_CHANNELS * width), BF16),
            pltpu.VMEM((group * tiles * cols, depth), BF16),
        ],
        compiler_params=params(28),
        name="outer_product",
    )(*lefts, *rights, weight)


def finish_kernel(offsets, line, me_ref, pair_ref, scale_ref, *refs):
    parts, out_ref = refs[:-1], refs[-1]
    here = me_ref[0]
    items, cols, width = parts[0].shape
    outer = cols // items
    odd = (here & 1) == 1
    for k, offset in enumerate(offsets):
        for i in range(items):
            both = parts[k][i].astype(F32).reshape(outer // 2, 2, items, width)
            low, high = both[:, 0:1], both[:, 1:2]
            both = jnp.concatenate([jnp.where(odd, high, low), jnp.where(odd, low, high)], axis=1)
            both = both.reshape(outer // 2, 2 * items, width)
            for z in range(outer // 2):
                owner = here ^ (offset | line[z])
                start = pl.multiple_of((owner >> 1) * (2 * items), 2 * items)
                at = pl.ds(start, 2 * items)
                update = both[z] * scale_ref[at, i : i + 1]
                out_ref[i, at, :] = (pair_ref[i, at, :].astype(F32) + update).astype(BF16)


def finish(me, pair_rep, scale, parts, offsets, line):
    vmem = pl.BlockSpec(memory_space=pltpu.VMEM)
    return pl.pallas_call(
        functools.partial(finish_kernel, offsets, line),
        in_specs=[pl.BlockSpec(memory_space=pltpu.SMEM)] + [vmem] * (2 + len(parts)),
        out_specs=vmem,
        out_shape=jax.ShapeDtypeStruct(pair_rep.shape, BF16),
        compiler_params=params(16),
        name="finish",
    )(me, pair_rep, scale, *parts)


def exchange(block, count, offset):
    if offset == 0:
        return block
    return lax.ppermute(block, "dap", [(i, i ^ offset) for i in range(count)])


def per_device_fast(
    alignment,
    pair_rep,
    align_mask,
    residue_mask,
    bias_weight,
    row_proj_weight,
    row_out_weight,
    column_proj_weight,
    column_out_weight,
    outer_factor_weight,
    outer_out,
):
    count = lax.axis_size("dap")
    dap_index = lax.axis_index("dap")
    me = jnp.reshape(dap_index, (1,)).astype(jnp.int32)
    plane, line = offset_groups(count)
    items = pair_rep.shape[0]

    bias = pair_bias_block(pair_rep, bias_weight)
    projected = list(row_project(alignment, row_proj_weight))
    column = [exchange(bias, count, z) for z in line]
    *column, projected[0] = lax.optimization_barrier((*column, projected[0]))
    column = jnp.stack(column)
    bias_parts = [exchange(column, count, k) for k in plane]
    plan = [[k | z for z in line] for k in plane]
    bias_parts += [exchange(part, count, 1) for part in bias_parts]
    plan += [[offset | 1 for offset in offsets] for offsets in plan]

    rows = row_attend(
        me, alignment, projected, align_mask, row_out_weight, bias_parts, plan, count
    )
    rows, late_mask = lax.optimization_barrier((rows, align_mask))
    moved = lax.all_to_all(rows, "dap", split_axis=0, concat_axis=0, tiled=True)
    own_res = lax.dynamic_slice_in_dim(late_mask, dap_index * items, items, 1)
    counts = jnp.einsum(
        "si,sj->ji", own_res.astype(BF16), late_mask.astype(BF16), preferred_element_type=F32
    )
    res_float = residue_mask.astype(F32)
    live_rows = lax.dynamic_slice_in_dim(res_float, dap_index * items, items, 0)
    scale = live_rows[None, :] * res_float[:, None] / (counts + count_eps)
    updated, left, right = column_attend(
        me,
        moved,
        align_mask,
        column_proj_weight,
        column_out_weight,
        outer_factor_weight,
        items,
    )
    rights = [exchange(right, count, z) for z in line]
    rights[1], updated = lax.optimization_barrier((rights[1], updated))
    updated = interleave(updated)
    *rights, updated = lax.optimization_barrier((*rights, updated))
    rights = [part for own in rights for part in (own, exchange(own, count, 1))]
    lefts = [exchange(left, count, k) for k in plane]
    sent = outer_product(lefts[1:], rights, outer_out, items)
    parts = [exchange(part, count, k) for part, k in zip(sent, plane[1:])]
    own = outer_product([left], rights, outer_out, items)
    parts = list(own) + parts
    pair_out = finish(me, pair_rep, scale, parts, plane, line)
    return updated, pair_out


def offset_groups(count):
    bits = count.bit_length() - 1
    near = (bits - 1) // 2
    plane = [k << 1 for k in range(1 << near)]
    line = [z << (1 + near) for z in range(1 << (bits - 1 - near))]
    return plane, line


def solution(mesh):
    placed = (
        P("dap", None, None),
        P("dap", "branch", None),
        P(),
        P(),
        P(),
        P(None, None, "branch"),
        P(),
        P(None, None, "branch"),
        P(),
        P(),
        P(),
    )
    count = mesh.shape["dap"]
    whole_heads = mesh.shape["branch"] == 1 and count & (count - 1) == 0

    def per_device(*operands):
        alignment, pair_rep = operands[0], operands[1]
        tile = 8
        fits = whole_heads and alignment.shape[0] == tile and pair_rep.shape[0] == tile
        return (per_device_fast if fits else per_device_general)(*operands)

    return jax.shard_map(
        per_device,
        mesh=mesh,
        in_specs=placed,
        out_specs=(P(None, "dap", None), P("dap", "branch", None)),
        check_vma=False,
    )
```

```python
import functools
import math

import jax
import jax.numpy as jnp
from jax import lax
from jax.experimental import pallas as pl
from jax.experimental.pallas import tpu as pltpu
from jax.sharding import PartitionSpec as P

ATTN_HEAD_COUNT = 8
HEAD_CHANNELS = 32
FACTOR_CHANNELS = 32


norm_eps = 1e-05
count_eps = 0.001


def layer_normalize(values):
    centre = jnp.mean(values, axis=-1, keepdims=True)
    centred = values - centre
    spread = jnp.mean(centred * centred, axis=-1, keepdims=True)
    return centred * lax.rsqrt(spread + norm_eps)


def attend_heads(inputs, key_mask, proj_weight, out_weight, score_bias):
    batch = inputs.shape[0]
    length = inputs.shape[1]
    local_width = proj_weight.shape[2]
    local_heads = local_width // HEAD_CHANNELS
    normed = layer_normalize(inputs.astype(jnp.float32)).astype(jnp.bfloat16)
    projected = jnp.einsum("blc,kcd->kbld", normed, proj_weight, preferred_element_type=jnp.float32)
    triple = (
        projected[:3].astype(jnp.bfloat16).reshape(3, batch, length, local_heads, HEAD_CHANNELS)
    )
    gating = jax.nn.sigmoid(projected[3])

    def attend_one(operands):
        queries, key_rows, value_rows, mask_row = operands
        scores = jnp.einsum(
            "ihd,jhd->hij", queries, key_rows, preferred_element_type=jnp.float32
        ) / math.sqrt(HEAD_CHANNELS)
        if score_bias is not None:
            scores = scores + score_bias.astype(jnp.float32)
        raised = jnp.exp(scores) * mask_row[None, None, :]
        weights = (raised / jnp.sum(raised, axis=-1, keepdims=True)).astype(jnp.bfloat16)
        return jnp.einsum("hij,jhd->ihd", weights, value_rows, preferred_element_type=jnp.float32)

    attended_rows = lax.map(attend_one, (triple[0], triple[1], triple[2], key_mask))
    heads_out = (attended_rows.reshape(batch, length, local_width) * gating).astype(jnp.bfloat16)
    gathered = lax.all_gather(heads_out, "branch", axis=2, tiled=True)
    update = jnp.einsum("blf,fc->blc", gathered, out_weight, preferred_element_type=jnp.float32)
    return (inputs.astype(jnp.float32) + update).astype(jnp.bfloat16)


def per_device_general(
    alignment,
    pair_rep,
    align_mask,
    residue_mask,
    bias_weight,
    row_proj_weight,
    row_out_weight,
    column_proj_weight,
    column_out_weight,
    outer_factor_weight,
    outer_out,
):
    branch_count = lax.axis_size("branch")
    dap_count = lax.axis_size("dap")
    branch_index = lax.axis_index("branch")
    dap_index = lax.axis_index("dap")
    seq_dev = alignment.shape[0]
    res_dev = pair_rep.shape[0]
    quarter = pair_rep.shape[1]
    total_seqs = align_mask.shape[0]
    local_heads = ATTN_HEAD_COUNT // branch_count
    float_mask = align_mask.astype(jnp.float32)
    res_float = residue_mask.astype(jnp.float32)
    pair_normed = layer_normalize(pair_rep.astype(jnp.float32)).astype(jnp.bfloat16)
    bias_block = jnp.einsum(
        "ijc,ch->hij", pair_normed, bias_weight, preferred_element_type=jnp.float32
    ).astype(jnp.bfloat16)
    bias_wide = lax.all_gather(bias_block, "branch", axis=2, tiled=True)
    bias_full = lax.all_gather(bias_wide, "dap", axis=1, tiled=True)
    pair_score_bias = lax.dynamic_slice_in_dim(
        bias_full, branch_index * local_heads, local_heads, 0
    )
    sequence_row_mask = lax.dynamic_slice_in_dim(float_mask, dap_index * seq_dev, seq_dev, 0)
    row_alignment = attend_heads(
        alignment, sequence_row_mask, row_proj_weight, row_out_weight, pair_score_bias
    )
    send_mask = sequence_row_mask.astype(jnp.bfloat16)
    blocked_rows = row_alignment.reshape(seq_dev, dap_count, res_dev, row_alignment.shape[2])
    blocked_mask = send_mask.reshape(seq_dev, dap_count, res_dev)
    moved_rows = lax.all_to_all(blocked_rows, "dap", split_axis=1, concat_axis=0, tiled=True)
    moved_mask = lax.all_to_all(blocked_mask, "dap", split_axis=1, concat_axis=0, tiled=True)
    seq_total = moved_rows.shape[0]
    items = moved_rows.shape[2]
    flat_rows = moved_rows.reshape(seq_total, items, moved_rows.shape[3])
    flat_mask = moved_mask.reshape(seq_total, items)
    transposed_rows = jnp.swapaxes(flat_rows, 0, 1)
    key_mask = jnp.swapaxes(flat_mask, 0, 1).astype(jnp.float32)
    attended_rows = attend_heads(
        transposed_rows, key_mask, column_proj_weight, column_out_weight, None
    )
    column_alignment = jnp.swapaxes(attended_rows, 0, 1)
    outer_mean_normed = layer_normalize(column_alignment.astype(jnp.float32)).astype(jnp.bfloat16)
    projected = jnp.einsum(
        "src,ce->sre", outer_mean_normed, outer_factor_weight, preferred_element_type=jnp.float32
    )
    factor_pairs = (projected * flat_mask.astype(jnp.float32)[:, :, None]).astype(jnp.bfloat16)
    column_alignment, factor_pairs = (column_alignment, factor_pairs)
    blocked_out = column_alignment.reshape(seq_total, 1, items, column_alignment.shape[2])
    blocked_factors = factor_pairs.reshape(seq_total, 1, items, factor_pairs.shape[2])
    updated_alignment = blocked_out.reshape(total_seqs, res_dev, blocked_out.shape[3])
    factor_pairs = blocked_factors.reshape(total_seqs, res_dev, blocked_factors.shape[3])
    left_side = factor_pairs[:, :, :FACTOR_CHANNELS]
    right_local = factor_pairs[:, :, FACTOR_CHANNELS:]
    col_start = branch_index * quarter
    row_start = dap_index * res_dev
    mask_rows = lax.dynamic_slice_in_dim(align_mask, row_start, res_dev, 1).astype(jnp.bfloat16)
    mask_cols = lax.dynamic_slice_in_dim(align_mask, col_start, quarter, 1).astype(jnp.bfloat16)
    counts = jnp.einsum("si,sj->ij", mask_rows, mask_cols, preferred_element_type=jnp.float32)
    live_rows = lax.dynamic_slice_in_dim(res_float, row_start, res_dev, 0)
    live_cols = lax.dynamic_slice_in_dim(res_float, col_start, quarter, 0)
    outer_weight = outer_out.astype(jnp.float32)
    right_all = lax.all_gather(right_local, "dap", axis=1, tiled=True)
    right_mine = lax.dynamic_slice_in_dim(right_all, col_start, quarter, 1)
    outer_sums = jnp.einsum(
        "sic,sje->ijce", left_side, right_mine, preferred_element_type=jnp.float32
    )
    outer_sums = outer_sums.reshape(res_dev, quarter, FACTOR_CHANNELS * FACTOR_CHANNELS)
    update = jnp.einsum("ijf,fz->ijz", outer_sums, outer_weight, precision=lax.Precision.HIGHEST)
    live = live_rows[:, None] * live_cols[None, :]
    update = update / (counts[:, :, None] + count_eps) * live[:, :, None]
    pair_out = (pair_rep.astype(jnp.float32) + update).astype(jnp.bfloat16)
    return (updated_alignment, pair_out)


LANES = 128
LOG2E = math.log2(math.e)
LIVE_SCALE = 1.0 / 128.0
BF16 = jnp.bfloat16
F32 = jnp.float32
MIB = 1024 * 1024


def nt_dot(a, b):
    return lax.dot_general(a, b, (((1,), (1,)), ((), ())), preferred_element_type=F32)


def nn_dot(a, b):
    return jnp.dot(a, b, preferred_element_type=F32)


def full_spec(shape):
    zeros = (0,) * len(shape)
    return pl.BlockSpec(shape, lambda *_: zeros)


def params(mib):
    return pltpu.CompilerParams(vmem_limit_bytes=mib * MIB)


def tiled_scratch(rows, cols):
    return pltpu.VMEM((cols // LANES, rows, LANES), F32)


def store_strided(held, first, stride, values):
    rows = values.shape[0]
    for t in range(held.shape[0]):
        held[t, pl.ds(first, rows, stride=stride), :] = values[:, t * LANES : (t + 1) * LANES]


def load_strided(held, first, stride, rows):
    parts = [held[t, pl.ds(first, rows, stride=stride), :] for t in range(held.shape[0])]
    return jnp.concatenate(parts, axis=1)


def joined_tiles(held):
    return jnp.concatenate([held[t] for t in range(held.shape[0])], axis=1)


def in_hbm(*arrays):
    return [pltpu.with_memory_space_constraint(a, pltpu.HBM) for a in arrays]


def in_vmem(*arrays):
    return [pltpu.with_memory_space_constraint(a, pltpu.VMEM) for a in arrays]


def head_lanes(length):
    lane = lax.broadcasted_iota(jnp.int32, (length, LANES), 1) // HEAD_CHANNELS
    return [
        jnp.where(lane == t, 1.0, 0.0).astype(BF16) for t in range(LANES // HEAD_CHANNELS)
    ]


def one_hot(shape, dim, place, value=1.0):
    hit = lax.broadcasted_iota(jnp.int32, shape, dim) == place
    return jnp.where(hit, value, 0.0).astype(BF16)


def quotient(top, below):
    guess = pl.reciprocal(below, approx=True)
    return top * (guess * (2.0 - below * guess))


def attend_all(count, prepare, close, lanes, bias_of):
    per_tile = LANES // HEAD_CHANNELS
    items = {0: prepare(0)}
    rows, width = items[0][0].shape
    tiles = width // LANES
    tasks = [(n, tile) for n in range(count) for tile in range(tiles)]
    scores, raised, pieces = {}, {}, [[] for _ in range(count)]

    def score(at):
        n, tile = tasks[at]
        cut = slice(tile * LANES, (tile + 1) * LANES)
        query, key = items[n][0][:, cut], items[n][1][:, cut]
        stacked = jnp.concatenate([query * lanes[t] for t in range(per_tile)], axis=0)
        scores[at] = nt_dot(stacked, key)

    def raise_scores(at):
        n, tile = tasks[at]
        stacked = scores.pop(at)
        parts = []
        for t in range(per_tile):
            part = stacked[t * rows : (t + 1) * rows]
            if bias_of is not None:
                part = part + bias_of(tile * per_tile + t)
            parts.append(jnp.exp2(part).astype(BF16))
        raised[at] = jnp.concatenate(parts, axis=1)

    def gather(at):
        n, tile = tasks[at]
        cut = slice(tile * LANES, (tile + 1) * LANES)
        live = items[n][3]
        value = items[n][2][:, cut] * live
        sides = [
            jnp.concatenate([value * lanes[t], live * lanes[t]], axis=1) for t in range(per_tile)
        ]
        total = nn_dot(raised.pop(at), jnp.concatenate(sides, axis=0))
        pieces[n].append(quotient(total[:, :LANES], total[:, LANES:]))

    for at in range(len(tasks) + 2):
        if at < len(tasks):
            score(at)
            n, tile = tasks[at]
            if tile == 0 and n + 1 < count:
                items[n + 1] = prepare(n + 1)
        if 0 <= at - 2:
            gather(at - 2)
        if 0 <= at - 1 < len(tasks):
            raise_scores(at - 1)
        if 0 <= at - 2 and tasks[at - 2][1] == tiles - 1:
            n = tasks[at - 2][0]
            close(n, jnp.concatenate(pieces[n], axis=1))


def project(normed, weight_ref):
    scale = LOG2E / math.sqrt(HEAD_CHANNELS)
    query = (nn_dot(normed, weight_ref[0]) * scale).astype(BF16)
    key = nn_dot(normed, weight_ref[1]).astype(BF16)
    value = nn_dot(normed, weight_ref[2]).astype(BF16)
    gate = 0.5 * jnp.tanh(0.5 * nn_dot(normed, weight_ref[3])) + 0.5
    return query, key, value, gate


def bias_kernel(pair_ref, weight_ref, out_ref, held):
    rows, cols, width = pair_ref.shape
    normed = layer_normalize(pair_ref[...].astype(F32)).astype(BF16).reshape(rows * cols, width)
    bias = nt_dot(weight_ref[...], normed) * LOG2E
    for i in range(rows):
        store_strided(held, i, rows, bias[:, i * cols : (i + 1) * cols])
    out_ref[...] = joined_tiles(held).astype(BF16)


def pair_bias_block(pair_rep, bias_weight):
    rows, cols, width = pair_rep.shape
    out = jax.ShapeDtypeStruct((ATTN_HEAD_COUNT * rows, cols), BF16)
    weight = bias_weight.T
    return pl.pallas_call(
        bias_kernel,
        grid=(1,),
        in_specs=[full_spec(pair_rep.shape), full_spec(weight.shape)],
        out_specs=pl.BlockSpec(memory_space=pltpu.VMEM),
        out_shape=out,
        scratch_shapes=[tiled_scratch(*out.shape)],
        compiler_params=params(16),
        name="pair_bias",
    )(*in_hbm(pair_rep, weight))


def row_project_kernel(x_ref, weight_ref, q_ref, k_ref, v_ref, g_ref):
    for s in range(x_ref.shape[0]):
        normed = layer_normalize(x_ref[s].astype(F32)).astype(BF16)
        q_ref[s], k_ref[s], v_ref[s], g_ref[s] = project(normed, weight_ref)


def row_project(alignment, weight):
    seqs, length, width = alignment.shape
    step = 2
    block = pl.BlockSpec((step, length, width), lambda i: (i, 0, 0))
    return pl.pallas_call(
        row_project_kernel,
        grid=(seqs // step,),
        in_specs=[block, full_spec(weight.shape)],
        out_specs=[block] * 4,
        out_shape=[pltpu.HBM(alignment.shape, BF16)] * 3 + [pltpu.HBM(alignment.shape, F32)],
        compiler_params=params(24),
        name="row_project",
    )(*in_hbm(alignment, weight))


def row_attend_kernel(
    plan, step, seqs, me_ref, x_ref, q_ref, k_ref, v_ref, g_ref, mask_ref, out_w_ref, *rest
):
    bias_refs, out_ref, bias_all = rest[: len(plan)], rest[-2], rest[-1]
    heads, length, _ = bias_all.shape

    @pl.when(pl.program_id(0) == 0)
    def _():
        for bias_ref, offsets in zip(bias_refs, plan):
            for z, offset in enumerate(offsets):
                block = bias_ref[z].astype(F32).reshape(heads, -1, length)
                rows = block.shape[1]
                owner = me_ref[0] ^ offset
                bias_all[:, pl.ds(pl.multiple_of(owner * rows, rows), rows), :] = block

    lanes = head_lanes(length)
    parts, rows = out_ref.shape[0], out_ref.shape[1]
    own = mask_ref[pl.ds(pl.multiple_of(me_ref[0] * seqs, seqs), seqs), :]
    own = own.astype(F32).astype(BF16)
    results = []

    def prepare(s):
        place = pl.program_id(0) * step + s
        spot = one_hot((seqs, LANES), 0, place, LIVE_SCALE)
        live = lax.dot_general(
            own, spot, (((0,), (0,)), ((), ())), preferred_element_type=F32
        ).astype(BF16)
        return q_ref[s], k_ref[s], v_ref[s], live

    def close(s, heads_out):
        heads_out = (heads_out * g_ref[s]).astype(BF16)
        total = x_ref[s].astype(F32) + nn_dot(heads_out, out_w_ref[...])
        results.append(total.reshape(parts, 1, rows // step, total.shape[1]))
        if len(results) == 2:
            joined = jnp.concatenate(results, axis=1)
            height = 2 * rows // step
            joined = joined.reshape(parts, height, total.shape[1]).astype(BF16)
            out_ref[:, (s // 2) * height : (s // 2 + 1) * height, :] = joined
            results.clear()

    attend_all(step, prepare, close, lanes, lambda h: bias_all[h])


def row_attend(me, alignment, projected, mask, out_weight, bias_parts, plan, parts):
    seqs, length, width = alignment.shape
    rows = length // parts
    step = 4
    vmem = pl.BlockSpec(memory_space=pltpu.VMEM)
    block = pl.BlockSpec((step, length, width), lambda i: (i, 0, 0))
    return pl.pallas_call(
        functools.partial(row_attend_kernel, plan, step, seqs),
        grid=(seqs // step,),
        in_specs=[pl.BlockSpec(memory_space=pltpu.SMEM)]
        + [block] * 5
        + [full_spec(mask.shape), full_spec(out_weight.shape)]
        + [vmem] * len(bias_parts),
        out_specs=pl.BlockSpec((parts, step * rows, width), lambda i: (0, i, 0)),
        out_shape=jax.ShapeDtypeStruct((parts, seqs * rows, width), BF16),
        scratch_shapes=[pltpu.VMEM((ATTN_HEAD_COUNT, length, length), F32)],
        compiler_params=params(40),
        name="row_attend",
    )(me, *in_hbm(alignment, *projected, mask, out_weight), *in_vmem(*bias_parts))


def column_kernel(
    items, each, me_ref, x_ref, mask_ref, weight_ref, out_w_ref, factor_ref,
    out_ref, left_ref, right_ref, held, right_held,
):
    step = pl.program_id(0)
    total_rows = held.shape[1]
    length = total_rows // items

    @pl.when(step == 0)
    def _():
        for t in range(held.shape[0]):
            part = x_ref[:, :, t * LANES : (t + 1) * LANES].astype(F32)
            held[t] = part.reshape(total_rows, LANES)

    lanes = head_lanes(length)
    mask = mask_ref[...].astype(F32).astype(BF16)
    residues = mask.shape[1]
    place = me_ref[0] * items + step * each
    feat = FACTOR_CHANNELS
    rows, gates = {}, {}

    def prepare(n):
        rows[n] = load_strided(held, step * each + n, items, length)
        normed = layer_normalize(rows[n]).astype(BF16)
        query, key, value, gates[n] = project(normed, weight_ref)
        live = nn_dot(mask, one_hot((residues, LANES), 0, place + n, LIVE_SCALE)).astype(BF16)
        return query, key, value, live

    def close(n, heads_out):
        heads_out = (heads_out * gates[n]).astype(BF16)
        updated = (rows[n] + nn_dot(heads_out, out_w_ref[...])).astype(BF16)
        out_ref[n] = updated
        normed = layer_normalize(updated.astype(F32)).astype(BF16)
        live_row = nt_dot(one_hot((8, residues), 1, place + n), mask)[:1]
        factors = nt_dot(factor_ref[...], normed) * live_row
        item = step * each + n
        left_ref[pl.ds(pl.multiple_of(item * feat, feat), feat), :] = factors[:feat].astype(BF16)
        store_strided(right_held, item, items, factors[feat:])

    attend_all(each, prepare, close, lanes, None)

    @pl.when(step == items // each - 1)
    def _():
        right_ref[...] = joined_tiles(right_held).astype(BF16)


def column_attend(me, moved, mask, weight, out_weight, factor_weight, items):
    width = moved.shape[2]
    total_rows = moved.shape[0] * moved.shape[1]
    length = total_rows // items
    each = 4
    side = (items * FACTOR_CHANNELS, length)
    left = right = jax.ShapeDtypeStruct(side, BF16)
    vmem = pl.BlockSpec(memory_space=pltpu.VMEM)
    operands = in_vmem(moved, mask, weight, out_weight, factor_weight.T)
    return pl.pallas_call(
        functools.partial(column_kernel, items, each),
        grid=(items // each,),
        in_specs=[pl.BlockSpec(memory_space=pltpu.SMEM)] + [vmem] * len(operands),
        out_specs=[pl.BlockSpec((each, length, width), lambda i: (i, 0, 0)), vmem, vmem],
        out_shape=[pltpu.HBM((items, length, width), BF16), left, right],
        scratch_shapes=[tiled_scratch(total_rows, width), tiled_scratch(*side)],
        compiler_params=params(40),
        name="column_attend",
    )(me, *operands)


def interleave_kernel(rows_ref, out_ref, held):
    items = rows_ref.shape[0]
    for item in range(items):
        store_strided(held, item, items, rows_ref[item].astype(F32))
    out_ref[...] = joined_tiles(held).reshape(out_ref.shape).astype(BF16)


def interleave(rows):
    items, length, width = rows.shape
    step = length // 4
    return pl.pallas_call(
        interleave_kernel,
        grid=(length // step,),
        in_specs=[pl.BlockSpec((items, step, width), lambda i: (0, i, 0))],
        out_specs=pl.BlockSpec((step, items, width), lambda i: (i, 0, 0)),
        out_shape=pltpu.HBM((length, items, width), BF16),
        scratch_shapes=[tiled_scratch(items * step, width)],
        compiler_params=params(16),
        name="interleave",
    )(*in_hbm(rows))


def outer_kernel(group, outer, items, *refs):
    lefts, rights = refs[:group], refs[group : group + outer]
    weight_ref = refs[group + outer]
    outs = refs[group + outer + 1 : -3]
    weight_rows, weight, held = refs[-3:]
    feat = FACTOR_CHANNELS
    quad = LANES // feat
    tiles = items * feat // LANES
    cols = outer * items
    width = weight_ref.shape[1]

    weight_rows[...] = weight_ref[...].astype(F32)
    weight[...] = jnp.zeros_like(weight)
    for e in range(feat):
        block = weight_rows[pl.ds(e, feat, stride=feat), :].astype(BF16)
        for i in range(quad):
            start = e * LANES + i * feat
            weight[start : start + feat, i * width : (i + 1) * width] = block

    right = jnp.concatenate([r[...] for r in rights], axis=0)
    for k in range(group):
        sums = nt_dot(right, lefts[k][...])
        sums = sums.reshape(outer, feat, items, sums.shape[1])
        sums = jnp.transpose(sums, (1, 0, 2, 3)).reshape(feat, cols, sums.shape[3]).astype(BF16)
        for t in range(tiles):
            at = slice((k * tiles + t) * cols, (k * tiles + t + 1) * cols)
            for e in range(feat):
                held[at, e * LANES : (e + 1) * LANES] = sums[e, :, t * LANES : (t + 1) * LANES]
    update = nn_dot(held[...], weight[...])
    for k in range(group):
        for t in range(tiles):
            rows = update[(k * tiles + t) * cols : (k * tiles + t + 1) * cols]
            for i in range(quad):
                outs[k][t * quad + i] = rows[:, i * width : (i + 1) * width].astype(BF16)


def outer_product(lefts, rights, weight, items):
    group, outer = len(lefts), len(rights)
    cols = outer * items
    tiles = items * FACTOR_CHANNELS // LANES
    depth = FACTOR_CHANNELS * LANES
    width = weight.shape[1]
    return pl.pallas_call(
        functools.partial(outer_kernel, group, outer, items),
        out_shape=[jax.ShapeDtypeStruct((items, cols, width), BF16)] * group,
        scratch_shapes=[
            pltpu.VMEM(weight.shape, F32),
            pltpu.VMEM((depth, LANES // FACTOR_CHANNELS * width), BF16),
            pltpu.VMEM((group * tiles * cols, depth), BF16),
        ],
        compiler_params=params(28),
        name="outer_product",
    )(*lefts, *rights, weight)


def finish_kernel(offsets, line, me_ref, pair_ref, scale_ref, *refs):
    parts, out_ref = refs[:-1], refs[-1]
    here = me_ref[0]
    items, cols, width = parts[0].shape
    outer = cols // items
    odd = (here & 1) == 1
    for k, offset in enumerate(offsets):
        for i in range(items):
            both = parts[k][i].astype(F32).reshape(outer // 2, 2, items, width)
            low, high = both[:, 0:1], both[:, 1:2]
            both = jnp.concatenate([jnp.where(odd, high, low), jnp.where(odd, low, high)], axis=1)
            both = both.reshape(outer // 2, 2 * items, width)
            for z in range(outer // 2):
                owner = here ^ (offset | line[z])
                start = pl.multiple_of((owner >> 1) * (2 * items), 2 * items)
                at = pl.ds(start, 2 * items)
                update = both[z] * scale_ref[at, i : i + 1]
                out_ref[i, at, :] = (pair_ref[i, at, :].astype(F32) + update).astype(BF16)


def finish(me, pair_rep, scale, parts, offsets, line):
    vmem = pl.BlockSpec(memory_space=pltpu.VMEM)
    return pl.pallas_call(
        functools.partial(finish_kernel, offsets, line),
        in_specs=[pl.BlockSpec(memory_space=pltpu.SMEM)] + [vmem] * (2 + len(parts)),
        out_specs=vmem,
        out_shape=jax.ShapeDtypeStruct(pair_rep.shape, BF16),
        compiler_params=params(16),
        name="finish",
    )(me, pair_rep, scale, *parts)


def exchange(block, count, offset):
    if offset == 0:
        return block
    return lax.ppermute(block, "dap", [(i, i ^ offset) for i in range(count)])


def per_device_fast(
    alignment,
    pair_rep,
    align_mask,
    residue_mask,
    bias_weight,
    row_proj_weight,
    row_out_weight,
    column_proj_weight,
    column_out_weight,
    outer_factor_weight,
    outer_out,
):
    count = lax.axis_size("dap")
    dap_index = lax.axis_index("dap")
    me = jnp.reshape(dap_index, (1,)).astype(jnp.int32)
    plane, line = offset_groups(count)
    items = pair_rep.shape[0]

    bias = pair_bias_block(pair_rep, bias_weight)
    projected = list(row_project(alignment, row_proj_weight))
    column = [exchange(bias, count, z) for z in line]
    *column, projected[0] = lax.optimization_barrier((*column, projected[0]))
    column = jnp.stack(column)
    bias_parts = [exchange(column, count, k) for k in plane]
    plan = [[k | z for z in line] for k in plane]
    bias_parts += [exchange(part, count, 1) for part in bias_parts]
    plan += [[offset | 1 for offset in offsets] for offsets in plan]

    rows = row_attend(
        me, alignment, projected, align_mask, row_out_weight, bias_parts, plan, count
    )
    rows, late_mask = lax.optimization_barrier((rows, align_mask))
    moved = lax.all_to_all(rows, "dap", split_axis=0, concat_axis=0, tiled=True)
    own_res = lax.dynamic_slice_in_dim(late_mask, dap_index * items, items, 1)
    counts = jnp.einsum(
        "si,sj->ji", own_res.astype(BF16), late_mask.astype(BF16), preferred_element_type=F32
    )
    res_float = residue_mask.astype(F32)
    live_rows = lax.dynamic_slice_in_dim(res_float, dap_index * items, items, 0)
    scale = live_rows[None, :] * res_float[:, None] / (counts + count_eps)
    updated, left, right = column_attend(
        me,
        moved,
        align_mask,
        column_proj_weight,
        column_out_weight,
        outer_factor_weight,
        items,
    )
    rights = [exchange(right, count, z) for z in line]
    rights[1], updated = lax.optimization_barrier((rights[1], updated))
    updated = interleave(updated)
    *rights, updated = lax.optimization_barrier((*rights, updated))
    rights = [part for own in rights for part in (own, exchange(own, count, 1))]
    lefts = [exchange(left, count, k) for k in plane]
    sent = outer_product(lefts[1:], rights, outer_out, items)
    parts = [exchange(part, count, k) for part, k in zip(sent, plane[1:])]
    own = outer_product([left], rights, outer_out, items)
    parts = list(own) + parts
    pair_out = finish(me, pair_rep, scale, parts, plane, line)
    return updated, pair_out


def offset_groups(count):
    bits = count.bit_length() - 1
    near = (bits - 1) // 2
    plane = [k << 1 for k in range(1 << near)]
    line = [z << (1 + near) for z in range(1 << (bits - 1 - near))]
    return plane, line


def solution(mesh):
    placed = (
        P("dap", None, None),
        P("dap", "branch", None),
        P(),
        P(),
        P(),
        P(None, None, "branch"),
        P(),
        P(None, None, "branch"),
        P(),
        P(),
        P(),
    )
    count = mesh.shape["dap"]
    whole_heads = mesh.shape["branch"] == 1 and count & (count - 1) == 0

    def per_device(*operands):
        alignment, pair_rep = operands[0], operands[1]
        tile = 8
        fits = whole_heads and alignment.shape[0] == tile and pair_rep.shape[0] == tile
        return (per_device_fast if fits else per_device_general)(*operands)

    return jax.shard_map(
        per_device,
        mesh=mesh,
        in_specs=placed,
        out_specs=(P(None, "dap", None), P("dap", "branch", None)),
        check_vma=False,
    )
```

```python
import functools
import math

import jax
import jax.numpy as jnp
from jax import lax
from jax.experimental import pallas as pl
from jax.experimental.pallas import tpu as pltpu
from jax.sharding import PartitionSpec as P

ATTN_HEAD_COUNT = 8
HEAD_CHANNELS = 32
FACTOR_CHANNELS = 32


norm_eps = 1e-05
count_eps = 0.001


def layer_normalize(values):
    centre = jnp.mean(values, axis=-1, keepdims=True)
    centred = values - centre
    spread = jnp.mean(centred * centred, axis=-1, keepdims=True)
    return centred * lax.rsqrt(spread + norm_eps)


def attend_heads(inputs, key_mask, proj_weight, out_weight, score_bias):
    batch = inputs.shape[0]
    length = inputs.shape[1]
    local_width = proj_weight.shape[2]
    local_heads = local_width // HEAD_CHANNELS
    normed = layer_normalize(inputs.astype(jnp.float32)).astype(jnp.bfloat16)
    projected = jnp.einsum("blc,kcd->kbld", normed, proj_weight, preferred_element_type=jnp.float32)
    triple = (
        projected[:3].astype(jnp.bfloat16).reshape(3, batch, length, local_heads, HEAD_CHANNELS)
    )
    gating = jax.nn.sigmoid(projected[3])

    def attend_one(operands):
        queries, key_rows, value_rows, mask_row = operands
        scores = jnp.einsum(
            "ihd,jhd->hij", queries, key_rows, preferred_element_type=jnp.float32
        ) / math.sqrt(HEAD_CHANNELS)
        if score_bias is not None:
            scores = scores + score_bias.astype(jnp.float32)
        raised = jnp.exp(scores) * mask_row[None, None, :]
        weights = (raised / jnp.sum(raised, axis=-1, keepdims=True)).astype(jnp.bfloat16)
        return jnp.einsum("hij,jhd->ihd", weights, value_rows, preferred_element_type=jnp.float32)

    attended_rows = lax.map(attend_one, (triple[0], triple[1], triple[2], key_mask))
    heads_out = (attended_rows.reshape(batch, length, local_width) * gating).astype(jnp.bfloat16)
    gathered = lax.all_gather(heads_out, "branch", axis=2, tiled=True)
    update = jnp.einsum("blf,fc->blc", gathered, out_weight, preferred_element_type=jnp.float32)
    return (inputs.astype(jnp.float32) + update).astype(jnp.bfloat16)


def per_device_general(
    alignment,
    pair_rep,
    align_mask,
    residue_mask,
    bias_weight,
    row_proj_weight,
    row_out_weight,
    column_proj_weight,
    column_out_weight,
    outer_factor_weight,
    outer_out,
):
    branch_count = lax.axis_size("branch")
    dap_count = lax.axis_size("dap")
    branch_index = lax.axis_index("branch")
    dap_index = lax.axis_index("dap")
    seq_dev = alignment.shape[0]
    res_dev = pair_rep.shape[0]
    quarter = pair_rep.shape[1]
    total_seqs = align_mask.shape[0]
    local_heads = ATTN_HEAD_COUNT // branch_count
    float_mask = align_mask.astype(jnp.float32)
    res_float = residue_mask.astype(jnp.float32)
    pair_normed = layer_normalize(pair_rep.astype(jnp.float32)).astype(jnp.bfloat16)
    bias_block = jnp.einsum(
        "ijc,ch->hij", pair_normed, bias_weight, preferred_element_type=jnp.float32
    ).astype(jnp.bfloat16)
    bias_wide = lax.all_gather(bias_block, "branch", axis=2, tiled=True)
    bias_full = lax.all_gather(bias_wide, "dap", axis=1, tiled=True)
    pair_score_bias = lax.dynamic_slice_in_dim(
        bias_full, branch_index * local_heads, local_heads, 0
    )
    sequence_row_mask = lax.dynamic_slice_in_dim(float_mask, dap_index * seq_dev, seq_dev, 0)
    row_alignment = attend_heads(
        alignment, sequence_row_mask, row_proj_weight, row_out_weight, pair_score_bias
    )
    send_mask = sequence_row_mask.astype(jnp.bfloat16)
    blocked_rows = row_alignment.reshape(seq_dev, dap_count, res_dev, row_alignment.shape[2])
    blocked_mask = send_mask.reshape(seq_dev, dap_count, res_dev)
    moved_rows = lax.all_to_all(blocked_rows, "dap", split_axis=1, concat_axis=0, tiled=True)
    moved_mask = lax.all_to_all(blocked_mask, "dap", split_axis=1, concat_axis=0, tiled=True)
    seq_total = moved_rows.shape[0]
    items = moved_rows.shape[2]
    flat_rows = moved_rows.reshape(seq_total, items, moved_rows.shape[3])
    flat_mask = moved_mask.reshape(seq_total, items)
    transposed_rows = jnp.swapaxes(flat_rows, 0, 1)
    key_mask = jnp.swapaxes(flat_mask, 0, 1).astype(jnp.float32)
    attended_rows = attend_heads(
        transposed_rows, key_mask, column_proj_weight, column_out_weight, None
    )
    column_alignment = jnp.swapaxes(attended_rows, 0, 1)
    outer_mean_normed = layer_normalize(column_alignment.astype(jnp.float32)).astype(jnp.bfloat16)
    projected = jnp.einsum(
        "src,ce->sre", outer_mean_normed, outer_factor_weight, preferred_element_type=jnp.float32
    )
    factor_pairs = (projected * flat_mask.astype(jnp.float32)[:, :, None]).astype(jnp.bfloat16)
    column_alignment, factor_pairs = (column_alignment, factor_pairs)
    blocked_out = column_alignment.reshape(seq_total, 1, items, column_alignment.shape[2])
    blocked_factors = factor_pairs.reshape(seq_total, 1, items, factor_pairs.shape[2])
    updated_alignment = blocked_out.reshape(total_seqs, res_dev, blocked_out.shape[3])
    factor_pairs = blocked_factors.reshape(total_seqs, res_dev, blocked_factors.shape[3])
    left_side = factor_pairs[:, :, :FACTOR_CHANNELS]
    right_local = factor_pairs[:, :, FACTOR_CHANNELS:]
    col_start = branch_index * quarter
    row_start = dap_index * res_dev
    mask_rows = lax.dynamic_slice_in_dim(align_mask, row_start, res_dev, 1).astype(jnp.bfloat16)
    mask_cols = lax.dynamic_slice_in_dim(align_mask, col_start, quarter, 1).astype(jnp.bfloat16)
    counts = jnp.einsum("si,sj->ij", mask_rows, mask_cols, preferred_element_type=jnp.float32)
    live_rows = lax.dynamic_slice_in_dim(res_float, row_start, res_dev, 0)
    live_cols = lax.dynamic_slice_in_dim(res_float, col_start, quarter, 0)
    outer_weight = outer_out.astype(jnp.float32)
    right_all = lax.all_gather(right_local, "dap", axis=1, tiled=True)
    right_mine = lax.dynamic_slice_in_dim(right_all, col_start, quarter, 1)
    outer_sums = jnp.einsum(
        "sic,sje->ijce", left_side, right_mine, preferred_element_type=jnp.float32
    )
    outer_sums = outer_sums.reshape(res_dev, quarter, FACTOR_CHANNELS * FACTOR_CHANNELS)
    update = jnp.einsum("ijf,fz->ijz", outer_sums, outer_weight, precision=lax.Precision.HIGHEST)
    live = live_rows[:, None] * live_cols[None, :]
    update = update / (counts[:, :, None] + count_eps) * live[:, :, None]
    pair_out = (pair_rep.astype(jnp.float32) + update).astype(jnp.bfloat16)
    return (updated_alignment, pair_out)


LANES = 128
LOG2E = math.log2(math.e)
LIVE_SCALE = 1.0 / 128.0
BF16 = jnp.bfloat16
F32 = jnp.float32
MIB = 1024 * 1024


def nt_dot(a, b):
    return lax.dot_general(a, b, (((1,), (1,)), ((), ())), preferred_element_type=F32)


def nn_dot(a, b):
    return jnp.dot(a, b, preferred_element_type=F32)


def full_spec(shape):
    zeros = (0,) * len(shape)
    return pl.BlockSpec(shape, lambda *_: zeros)


def params(mib):
    return pltpu.CompilerParams(vmem_limit_bytes=mib * MIB)


def tiled_scratch(rows, cols):
    return pltpu.VMEM((cols // LANES, rows, LANES), F32)


def store_strided(held, first, stride, values):
    rows = values.shape[0]
    for t in range(held.shape[0]):
        held[t, pl.ds(first, rows, stride=stride), :] = values[:, t * LANES : (t + 1) * LANES]


def load_strided(held, first, stride, rows):
    parts = [held[t, pl.ds(first, rows, stride=stride), :] for t in range(held.shape[0])]
    return jnp.concatenate(parts, axis=1)


def joined_tiles(held):
    return jnp.concatenate([held[t] for t in range(held.shape[0])], axis=1)


def in_hbm(*arrays):
    return [pltpu.with_memory_space_constraint(a, pltpu.HBM) for a in arrays]


def in_vmem(*arrays):
    return [pltpu.with_memory_space_constraint(a, pltpu.VMEM) for a in arrays]


def head_lanes(length):
    lane = lax.broadcasted_iota(jnp.int32, (length, LANES), 1) // HEAD_CHANNELS
    return [
        jnp.where(lane == t, 1.0, 0.0).astype(BF16) for t in range(LANES // HEAD_CHANNELS)
    ]


def one_hot(shape, dim, place, value=1.0):
    hit = lax.broadcasted_iota(jnp.int32, shape, dim) == place
    return jnp.where(hit, value, 0.0).astype(BF16)


def quotient(top, below):
    guess = pl.reciprocal(below, approx=True)
    return top * (guess * (2.0 - below * guess))


def attend_all(items, lanes, bias_of):
    per_tile = LANES // HEAD_CHANNELS
    rows, width = items[0][0].shape
    tasks = [(n, tile) for n in range(len(items)) for tile in range(width // LANES)]
    scores, raised, pieces = {}, {}, [[] for _ in items]

    def score(at):
        n, tile = tasks[at]
        cut = slice(tile * LANES, (tile + 1) * LANES)
        query, key = items[n][0][:, cut], items[n][1][:, cut]
        stacked = jnp.concatenate([query * lanes[t] for t in range(per_tile)], axis=0)
        scores[at] = nt_dot(stacked, key)

    def raise_scores(at):
        n, tile = tasks[at]
        stacked = scores.pop(at)
        parts = []
        for t in range(per_tile):
            part = stacked[t * rows : (t + 1) * rows]
            if bias_of is not None:
                part = part + bias_of(tile * per_tile + t)
            parts.append(jnp.exp2(part).astype(BF16))
        raised[at] = jnp.concatenate(parts, axis=1)

    def gather(at):
        n, tile = tasks[at]
        cut = slice(tile * LANES, (tile + 1) * LANES)
        live = items[n][3]
        value = items[n][2][:, cut] * live
        sides = [
            jnp.concatenate([value * lanes[t], live * lanes[t]], axis=1) for t in range(per_tile)
        ]
        total = nn_dot(raised.pop(at), jnp.concatenate(sides, axis=0))
        pieces[n].append(quotient(total[:, :LANES], total[:, LANES:]))

    for at in range(len(tasks) + 2):
        if at < len(tasks):
            score(at)
        if 0 <= at - 2:
            gather(at - 2)
        if 0 <= at - 1 < len(tasks):
            raise_scores(at - 1)
    return [jnp.concatenate(p, axis=1) for p in pieces]


def attend_heads_all(items, lanes, bias_of):
    per_tile = LANES // HEAD_CHANNELS
    width = items[0][0].shape[1]
    tiles = width // LANES
    tasks = [(n, h) for n in range(len(items)) for h in range(tiles * per_tile)]
    scores, raised, totals, pieces = {}, {}, {}, [[] for _ in items]

    def split(h):
        tile = h // per_tile
        return slice(tile * LANES, (tile + 1) * LANES), lanes[h % per_tile]

    def score(at):
        n, h = tasks[at]
        cut, own = split(h)
        scores[at] = nt_dot(items[n][0][:, cut] * own, items[n][1][:, cut])

    def raise_scores(at):
        part = scores.pop(at)
        if bias_of is not None:
            part = part + bias_of(tasks[at][1])
        raised[at] = jnp.exp2(part).astype(BF16)

    def gather(at):
        n, h = tasks[at]
        cut, own = split(h)
        live = items[n][3]
        side = jnp.concatenate([items[n][2][:, cut] * live * own, live * own], axis=1)
        part = nn_dot(raised.pop(at), side)
        totals[n] = part if h % per_tile == 0 else totals[n] + part
        if h % per_tile == per_tile - 1:
            total = totals.pop(n)
            pieces[n].append(quotient(total[:, :LANES], total[:, LANES:]))

    for at in range(len(tasks) + 2):
        if at < len(tasks):
            score(at)
        if 0 <= at - 2:
            gather(at - 2)
        if 0 <= at - 1 < len(tasks):
            raise_scores(at - 1)
    return [jnp.concatenate(p, axis=1) for p in pieces]


def project(normed, weight_ref):
    scale = LOG2E / math.sqrt(HEAD_CHANNELS)
    query = (nn_dot(normed, weight_ref[0]) * scale).astype(BF16)
    key = nn_dot(normed, weight_ref[1]).astype(BF16)
    value = nn_dot(normed, weight_ref[2]).astype(BF16)
    gate = 0.5 * jnp.tanh(0.5 * nn_dot(normed, weight_ref[3])) + 0.5
    return query, key, value, gate


def bias_kernel(pair_ref, weight_ref, out_ref, held):
    rows, cols, width = pair_ref.shape
    normed = layer_normalize(pair_ref[...].astype(F32)).astype(BF16).reshape(rows * cols, width)
    bias = nt_dot(weight_ref[...], normed) * LOG2E
    for i in range(rows):
        store_strided(held, i, rows, bias[:, i * cols : (i + 1) * cols])
    out_ref[...] = joined_tiles(held).astype(BF16)


def pair_bias_block(pair_rep, bias_weight):
    rows, cols, width = pair_rep.shape
    out = jax.ShapeDtypeStruct((ATTN_HEAD_COUNT * rows, cols), BF16)
    weight = bias_weight.T
    return pl.pallas_call(
        bias_kernel,
        grid=(1,),
        in_specs=[full_spec(pair_rep.shape), full_spec(weight.shape)],
        out_specs=pl.BlockSpec(memory_space=pltpu.VMEM),
        out_shape=out,
        scratch_shapes=[tiled_scratch(*out.shape)],
        compiler_params=params(16),
        name="pair_bias",
    )(*in_hbm(pair_rep, weight))


def row_project_kernel(x_ref, weight_ref, q_ref, k_ref, v_ref, g_ref):
    for s in range(x_ref.shape[0]):
        normed = layer_normalize(x_ref[s].astype(F32)).astype(BF16)
        q_ref[s], k_ref[s], v_ref[s], g_ref[s] = project(normed, weight_ref)


def row_project(alignment, weight):
    seqs, length, width = alignment.shape
    step = 2
    block = pl.BlockSpec((step, length, width), lambda i: (i, 0, 0))
    return pl.pallas_call(
        row_project_kernel,
        grid=(seqs // step,),
        in_specs=[block, full_spec(weight.shape)],
        out_specs=[block] * 4,
        out_shape=[pltpu.HBM(alignment.shape, BF16)] * 3 + [pltpu.HBM(alignment.shape, F32)],
        compiler_params=params(24),
        name="row_project",
    )(*in_hbm(alignment, weight))


def row_attend_kernel(
    plan, step, seqs, me_ref, x_ref, q_ref, k_ref, v_ref, g_ref, mask_ref, out_w_ref, *rest
):
    bias_refs, out_ref, bias_all = rest[: len(plan)], rest[-2], rest[-1]
    heads, length, _ = bias_all.shape

    @pl.when(pl.program_id(0) == 0)
    def _():
        for bias_ref, offsets in zip(bias_refs, plan):
            for z, offset in enumerate(offsets):
                block = bias_ref[z].astype(F32).reshape(heads, -1, length)
                rows = block.shape[1]
                owner = me_ref[0] ^ offset
                bias_all[:, pl.ds(pl.multiple_of(owner * rows, rows), rows), :] = block

    lanes = head_lanes(length)
    parts, rows = out_ref.shape[0], out_ref.shape[1]
    own = mask_ref[pl.ds(pl.multiple_of(me_ref[0] * seqs, seqs), seqs), :]
    own = own.astype(F32).astype(BF16)
    items = []
    for s in range(step):
        place = pl.program_id(0) * step + s
        spot = one_hot((seqs, LANES), 0, place, LIVE_SCALE)
        live = lax.dot_general(
            own, spot, (((0,), (0,)), ((), ())), preferred_element_type=F32
        ).astype(BF16)
        items.append((q_ref[s], k_ref[s], v_ref[s], live))
    results = []
    for s, heads_out in enumerate(attend_heads_all(items, lanes, lambda h: bias_all[h])):
        heads_out = (heads_out * g_ref[s]).astype(BF16)
        total = x_ref[s].astype(F32) + nn_dot(heads_out, out_w_ref[...])
        results.append(total.reshape(parts, 1, rows // step, total.shape[1]))
    joined = jnp.concatenate(results, axis=1)
    out_ref[...] = joined.reshape(out_ref.shape).astype(BF16)


def row_attend(me, alignment, projected, mask, out_weight, bias_parts, plan, parts):
    seqs, length, width = alignment.shape
    rows = length // parts
    step = 2
    vmem = pl.BlockSpec(memory_space=pltpu.VMEM)
    block = pl.BlockSpec((step, length, width), lambda i: (i, 0, 0))
    return pl.pallas_call(
        functools.partial(row_attend_kernel, plan, step, seqs),
        grid=(seqs // step,),
        in_specs=[pl.BlockSpec(memory_space=pltpu.SMEM)]
        + [block] * 5
        + [full_spec(mask.shape), full_spec(out_weight.shape)]
        + [vmem] * len(bias_parts),
        out_specs=pl.BlockSpec((parts, step * rows, width), lambda i: (0, i, 0)),
        out_shape=jax.ShapeDtypeStruct((parts, seqs * rows, width), BF16),
        scratch_shapes=[pltpu.VMEM((ATTN_HEAD_COUNT, length, length), F32)],
        compiler_params=params(24),
        name="row_attend",
    )(me, *in_hbm(alignment, *projected, mask, out_weight), *in_vmem(*bias_parts))


def column_kernel(
    items, each, me_ref, x_ref, mask_ref, weight_ref, out_w_ref, factor_ref,
    out_ref, left_ref, right_ref, held, right_held,
):
    step = pl.program_id(0)
    total_rows = held.shape[1]
    length = total_rows // items

    @pl.when(step == 0)
    def _():
        for t in range(held.shape[0]):
            part = x_ref[:, :, t * LANES : (t + 1) * LANES].astype(F32)
            held[t] = part.reshape(total_rows, LANES)

    lanes = head_lanes(length)
    mask = mask_ref[...].astype(F32).astype(BF16)
    residues = mask.shape[1]
    place = me_ref[0] * items + step * each
    rows = [load_strided(held, step * each + n, items, length) for n in range(each)]
    inputs, gates, normed = [], [], {0: layer_normalize(rows[0]).astype(BF16)}
    for n in range(each):
        if n + 1 < each:
            normed[n + 1] = layer_normalize(rows[n + 1]).astype(BF16)
        query, key, value, gate = project(normed[n], weight_ref)
        live = nn_dot(mask, one_hot((residues, LANES), 0, place + n, LIVE_SCALE)).astype(BF16)
        inputs.append((query, key, value, live))
        gates.append(gate)
    heads = attend_all(inputs, lanes, None)
    feat = FACTOR_CHANNELS
    updated = {}
    for at in range(each + 2):
        if at < each:
            heads_out = (heads[at] * gates[at]).astype(BF16)
            updated[at] = (rows[at] + nn_dot(heads_out, out_w_ref[...])).astype(BF16)
            out_ref[at] = updated[at]
        if 0 <= at - 2:
            n = at - 2
            item = step * each + n
            live_row = nt_dot(one_hot((8, residues), 1, place + n), mask)[:1]
            factors = nt_dot(factor_ref[...], normed[n]) * live_row
            left_at = pl.ds(pl.multiple_of(item * feat, feat), feat)
            left_ref[left_at, :] = factors[:feat].astype(BF16)
            store_strided(right_held, item, items, factors[feat:])
        if 0 <= at - 1 < each:
            normed[at - 1] = layer_normalize(updated[at - 1].astype(F32)).astype(BF16)

    @pl.when(step == items // each - 1)
    def _():
        right_ref[...] = joined_tiles(right_held).astype(BF16)


def column_attend(me, moved, mask, weight, out_weight, factor_weight, items):
    width = moved.shape[2]
    total_rows = moved.shape[0] * moved.shape[1]
    length = total_rows // items
    each = 4
    side = (items * FACTOR_CHANNELS, length)
    left = right = jax.ShapeDtypeStruct(side, BF16)
    vmem = pl.BlockSpec(memory_space=pltpu.VMEM)
    operands = in_vmem(moved, mask, weight, out_weight, factor_weight.T)
    return pl.pallas_call(
        functools.partial(column_kernel, items, each),
        grid=(items // each,),
        in_specs=[pl.BlockSpec(memory_space=pltpu.SMEM)] + [vmem] * len(operands),
        out_specs=[pl.BlockSpec((each, length, width), lambda i: (i, 0, 0)), vmem, vmem],
        out_shape=[pltpu.HBM((items, length, width), BF16), left, right],
        scratch_shapes=[tiled_scratch(total_rows, width), tiled_scratch(*side)],
        compiler_params=params(28),
        name="column_attend",
    )(me, *operands)


def interleave_kernel(rows_ref, out_ref, held):
    items = rows_ref.shape[0]
    for item in range(items):
        store_strided(held, item, items, rows_ref[item].astype(F32))
    out_ref[...] = joined_tiles(held).reshape(out_ref.shape).astype(BF16)


def interleave(rows):
    items, length, width = rows.shape
    step = length // 4
    return pl.pallas_call(
        interleave_kernel,
        grid=(length // step,),
        in_specs=[pl.BlockSpec((items, step, width), lambda i: (0, i, 0))],
        out_specs=pl.BlockSpec((step, items, width), lambda i: (i, 0, 0)),
        out_shape=pltpu.HBM((length, items, width), BF16),
        scratch_shapes=[tiled_scratch(items * step, width)],
        compiler_params=params(16),
        name="interleave",
    )(*in_hbm(rows))


def outer_kernel(group, outer, items, *refs):
    lefts, rights = refs[:group], refs[group : group + outer]
    weight_ref = refs[group + outer]
    outs = refs[group + outer + 1 : -3]
    weight_rows, weight, held = refs[-3:]
    feat = FACTOR_CHANNELS
    quad = LANES // feat
    tiles = items * feat // LANES
    cols = outer * items
    width = weight_ref.shape[1]

    weight_rows[...] = weight_ref[...].astype(F32)
    weight[...] = jnp.zeros_like(weight)
    for e in range(feat):
        block = weight_rows[pl.ds(e, feat, stride=feat), :].astype(BF16)
        for i in range(quad):
            start = e * LANES + i * feat
            weight[start : start + feat, i * width : (i + 1) * width] = block

    right = jnp.concatenate([r[...] for r in rights], axis=0)
    for k in range(group):
        sums = nt_dot(right, lefts[k][...])
        sums = sums.reshape(outer, feat, items, sums.shape[1])
        sums = jnp.transpose(sums, (1, 0, 2, 3)).reshape(feat, cols, sums.shape[3]).astype(BF16)
        for t in range(tiles):
            at = slice((k * tiles + t) * cols, (k * tiles + t + 1) * cols)
            for e in range(feat):
                held[at, e * LANES : (e + 1) * LANES] = sums[e, :, t * LANES : (t + 1) * LANES]
    update = nn_dot(held[...], weight[...])
    for k in range(group):
        for t in range(tiles):
            rows = update[(k * tiles + t) * cols : (k * tiles + t + 1) * cols]
            for i in range(quad):
                outs[k][t * quad + i] = rows[:, i * width : (i + 1) * width].astype(BF16)


def outer_product(lefts, rights, weight, items):
    group, outer = len(lefts), len(rights)
    cols = outer * items
    tiles = items * FACTOR_CHANNELS // LANES
    depth = FACTOR_CHANNELS * LANES
    width = weight.shape[1]
    return pl.pallas_call(
        functools.partial(outer_kernel, group, outer, items),
        out_shape=[jax.ShapeDtypeStruct((items, cols, width), BF16)] * group,
        scratch_shapes=[
            pltpu.VMEM(weight.shape, F32),
            pltpu.VMEM((depth, LANES // FACTOR_CHANNELS * width), BF16),
            pltpu.VMEM((group * tiles * cols, depth), BF16),
        ],
        compiler_params=params(28),
        name="outer_product",
    )(*lefts, *rights, weight)


def finish_kernel(offsets, line, me_ref, pair_ref, scale_ref, *refs):
    parts, out_ref = refs[:-1], refs[-1]
    here = me_ref[0]
    items, cols, width = parts[0].shape
    outer = cols // items
    odd = (here & 1) == 1
    for k, offset in enumerate(offsets):
        for i in range(items):
            both = parts[k][i].astype(F32).reshape(outer // 2, 2, items, width)
            low, high = both[:, 0:1], both[:, 1:2]
            both = jnp.concatenate([jnp.where(odd, high, low), jnp.where(odd, low, high)], axis=1)
            both = both.reshape(outer // 2, 2 * items, width)
            for z in range(outer // 2):
                owner = here ^ (offset | line[z])
                start = pl.multiple_of((owner >> 1) * (2 * items), 2 * items)
                at = pl.ds(start, 2 * items)
                update = both[z] * scale_ref[at, i : i + 1]
                out_ref[i, at, :] = (pair_ref[i, at, :].astype(F32) + update).astype(BF16)


def finish(me, pair_rep, scale, parts, offsets, line):
    vmem = pl.BlockSpec(memory_space=pltpu.VMEM)
    return pl.pallas_call(
        functools.partial(finish_kernel, offsets, line),
        in_specs=[pl.BlockSpec(memory_space=pltpu.SMEM)] + [vmem] * (2 + len(parts)),
        out_specs=vmem,
        out_shape=jax.ShapeDtypeStruct(pair_rep.shape, BF16),
        compiler_params=params(16),
        name="finish",
    )(me, pair_rep, scale, *parts)


def exchange(block, count, offset):
    if offset == 0:
        return block
    return lax.ppermute(block, "dap", [(i, i ^ offset) for i in range(count)])


def per_device_fast(
    alignment,
    pair_rep,
    align_mask,
    residue_mask,
    bias_weight,
    row_proj_weight,
    row_out_weight,
    column_proj_weight,
    column_out_weight,
    outer_factor_weight,
    outer_out,
):
    count = lax.axis_size("dap")
    dap_index = lax.axis_index("dap")
    me = jnp.reshape(dap_index, (1,)).astype(jnp.int32)
    plane, line = offset_groups(count)
    items = pair_rep.shape[0]

    bias = pair_bias_block(pair_rep, bias_weight)
    projected = list(row_project(alignment, row_proj_weight))
    column = [exchange(bias, count, z) for z in line]
    *column, projected[0] = lax.optimization_barrier((*column, projected[0]))
    column = jnp.stack(column)
    bias_parts = [exchange(column, count, k) for k in plane]
    plan = [[k | z for z in line] for k in plane]
    bias_parts += [exchange(part, count, 1) for part in bias_parts]
    plan += [[offset | 1 for offset in offsets] for offsets in plan]

    rows = row_attend(
        me, alignment, projected, align_mask, row_out_weight, bias_parts, plan, count
    )
    rows, late_mask = lax.optimization_barrier((rows, align_mask))
    moved = lax.all_to_all(rows, "dap", split_axis=0, concat_axis=0, tiled=True)
    own_res = lax.dynamic_slice_in_dim(late_mask, dap_index * items, items, 1)
    counts = jnp.einsum(
        "si,sj->ji", own_res.astype(BF16), late_mask.astype(BF16), preferred_element_type=F32
    )
    res_float = residue_mask.astype(F32)
    live_rows = lax.dynamic_slice_in_dim(res_float, dap_index * items, items, 0)
    scale = live_rows[None, :] * res_float[:, None] / (counts + count_eps)
    updated, left, right = column_attend(
        me,
        moved,
        align_mask,
        column_proj_weight,
        column_out_weight,
        outer_factor_weight,
        items,
    )
    rights = [exchange(right, count, z) for z in line]
    rights[1], updated = lax.optimization_barrier((rights[1], updated))
    updated = interleave(updated)
    *rights, updated = lax.optimization_barrier((*rights, updated))
    rights = [part for own in rights for part in (own, exchange(own, count, 1))]
    lefts = [exchange(left, count, k) for k in plane]
    sent = outer_product(lefts[1:], rights, outer_out, items)
    parts = [exchange(part, count, k) for part, k in zip(sent, plane[1:])]
    own = outer_product([left], rights, outer_out, items)
    parts = list(own) + parts
    pair_out = finish(me, pair_rep, scale, parts, plane, line)
    return updated, pair_out


def offset_groups(count):
    bits = count.bit_length() - 1
    near = (bits - 1) // 2
    plane = [k << 1 for k in range(1 << near)]
    line = [z << (1 + near) for z in range(1 << (bits - 1 - near))]
    return plane, line


def solution(mesh):
    placed = (
        P("dap", None, None),
        P("dap", "branch", None),
        P(),
        P(),
        P(),
        P(None, None, "branch"),
        P(),
        P(None, None, "branch"),
        P(),
        P(),
        P(),
    )
    count = mesh.shape["dap"]
    whole_heads = mesh.shape["branch"] == 1 and count & (count - 1) == 0

    def per_device(*operands):
        alignment, pair_rep = operands[0], operands[1]
        tile = 8
        fits = whole_heads and alignment.shape[0] == tile and pair_rep.shape[0] == tile
        return (per_device_fast if fits else per_device_general)(*operands)

    return jax.shard_map(
        per_device,
        mesh=mesh,
        in_specs=placed,
        out_specs=(P(None, "dap", None), P("dap", "branch", None)),
        check_vma=False,
    )
```

```python
import functools
import math

import jax
import jax.numpy as jnp
from jax import lax
from jax.experimental import pallas as pl
from jax.experimental.pallas import tpu as pltpu
from jax.sharding import PartitionSpec as P

ATTN_HEAD_COUNT = 8
HEAD_CHANNELS = 32
FACTOR_CHANNELS = 32


norm_eps = 1e-05
count_eps = 0.001


def layer_normalize(values):
    centre = jnp.mean(values, axis=-1, keepdims=True)
    centred = values - centre
    spread = jnp.mean(centred * centred, axis=-1, keepdims=True)
    return centred * lax.rsqrt(spread + norm_eps)


def attend_heads(inputs, key_mask, proj_weight, out_weight, score_bias):
    batch = inputs.shape[0]
    length = inputs.shape[1]
    local_width = proj_weight.shape[2]
    local_heads = local_width // HEAD_CHANNELS
    normed = layer_normalize(inputs.astype(jnp.float32)).astype(jnp.bfloat16)
    projected = jnp.einsum("blc,kcd->kbld", normed, proj_weight, preferred_element_type=jnp.float32)
    triple = (
        projected[:3].astype(jnp.bfloat16).reshape(3, batch, length, local_heads, HEAD_CHANNELS)
    )
    gating = jax.nn.sigmoid(projected[3])

    def attend_one(operands):
        queries, key_rows, value_rows, mask_row = operands
        scores = jnp.einsum(
            "ihd,jhd->hij", queries, key_rows, preferred_element_type=jnp.float32
        ) / math.sqrt(HEAD_CHANNELS)
        if score_bias is not None:
            scores = scores + score_bias.astype(jnp.float32)
        raised = jnp.exp(scores) * mask_row[None, None, :]
        weights = (raised / jnp.sum(raised, axis=-1, keepdims=True)).astype(jnp.bfloat16)
        return jnp.einsum("hij,jhd->ihd", weights, value_rows, preferred_element_type=jnp.float32)

    attended_rows = lax.map(attend_one, (triple[0], triple[1], triple[2], key_mask))
    heads_out = (attended_rows.reshape(batch, length, local_width) * gating).astype(jnp.bfloat16)
    gathered = lax.all_gather(heads_out, "branch", axis=2, tiled=True)
    update = jnp.einsum("blf,fc->blc", gathered, out_weight, preferred_element_type=jnp.float32)
    return (inputs.astype(jnp.float32) + update).astype(jnp.bfloat16)


def per_device_general(
    alignment,
    pair_rep,
    align_mask,
    residue_mask,
    bias_weight,
    row_proj_weight,
    row_out_weight,
    column_proj_weight,
    column_out_weight,
    outer_factor_weight,
    outer_out,
):
    branch_count = lax.axis_size("branch")
    dap_count = lax.axis_size("dap")
    branch_index = lax.axis_index("branch")
    dap_index = lax.axis_index("dap")
    seq_dev = alignment.shape[0]
    res_dev = pair_rep.shape[0]
    quarter = pair_rep.shape[1]
    total_seqs = align_mask.shape[0]
    local_heads = ATTN_HEAD_COUNT // branch_count
    float_mask = align_mask.astype(jnp.float32)
    res_float = residue_mask.astype(jnp.float32)
    pair_normed = layer_normalize(pair_rep.astype(jnp.float32)).astype(jnp.bfloat16)
    bias_block = jnp.einsum(
        "ijc,ch->hij", pair_normed, bias_weight, preferred_element_type=jnp.float32
    ).astype(jnp.bfloat16)
    bias_wide = lax.all_gather(bias_block, "branch", axis=2, tiled=True)
    bias_full = lax.all_gather(bias_wide, "dap", axis=1, tiled=True)
    pair_score_bias = lax.dynamic_slice_in_dim(
        bias_full, branch_index * local_heads, local_heads, 0
    )
    sequence_row_mask = lax.dynamic_slice_in_dim(float_mask, dap_index * seq_dev, seq_dev, 0)
    row_alignment = attend_heads(
        alignment, sequence_row_mask, row_proj_weight, row_out_weight, pair_score_bias
    )
    send_mask = sequence_row_mask.astype(jnp.bfloat16)
    blocked_rows = row_alignment.reshape(seq_dev, dap_count, res_dev, row_alignment.shape[2])
    blocked_mask = send_mask.reshape(seq_dev, dap_count, res_dev)
    moved_rows = lax.all_to_all(blocked_rows, "dap", split_axis=1, concat_axis=0, tiled=True)
    moved_mask = lax.all_to_all(blocked_mask, "dap", split_axis=1, concat_axis=0, tiled=True)
    seq_total = moved_rows.shape[0]
    items = moved_rows.shape[2]
    flat_rows = moved_rows.reshape(seq_total, items, moved_rows.shape[3])
    flat_mask = moved_mask.reshape(seq_total, items)
    transposed_rows = jnp.swapaxes(flat_rows, 0, 1)
    key_mask = jnp.swapaxes(flat_mask, 0, 1).astype(jnp.float32)
    attended_rows = attend_heads(
        transposed_rows, key_mask, column_proj_weight, column_out_weight, None
    )
    column_alignment = jnp.swapaxes(attended_rows, 0, 1)
    outer_mean_normed = layer_normalize(column_alignment.astype(jnp.float32)).astype(jnp.bfloat16)
    projected = jnp.einsum(
        "src,ce->sre", outer_mean_normed, outer_factor_weight, preferred_element_type=jnp.float32
    )
    factor_pairs = (projected * flat_mask.astype(jnp.float32)[:, :, None]).astype(jnp.bfloat16)
    column_alignment, factor_pairs = (column_alignment, factor_pairs)
    blocked_out = column_alignment.reshape(seq_total, 1, items, column_alignment.shape[2])
    blocked_factors = factor_pairs.reshape(seq_total, 1, items, factor_pairs.shape[2])
    updated_alignment = blocked_out.reshape(total_seqs, res_dev, blocked_out.shape[3])
    factor_pairs = blocked_factors.reshape(total_seqs, res_dev, blocked_factors.shape[3])
    left_side = factor_pairs[:, :, :FACTOR_CHANNELS]
    right_local = factor_pairs[:, :, FACTOR_CHANNELS:]
    col_start = branch_index * quarter
    row_start = dap_index * res_dev
    mask_rows = lax.dynamic_slice_in_dim(align_mask, row_start, res_dev, 1).astype(jnp.bfloat16)
    mask_cols = lax.dynamic_slice_in_dim(align_mask, col_start, quarter, 1).astype(jnp.bfloat16)
    counts = jnp.einsum("si,sj->ij", mask_rows, mask_cols, preferred_element_type=jnp.float32)
    live_rows = lax.dynamic_slice_in_dim(res_float, row_start, res_dev, 0)
    live_cols = lax.dynamic_slice_in_dim(res_float, col_start, quarter, 0)
    outer_weight = outer_out.astype(jnp.float32)
    right_all = lax.all_gather(right_local, "dap", axis=1, tiled=True)
    right_mine = lax.dynamic_slice_in_dim(right_all, col_start, quarter, 1)
    outer_sums = jnp.einsum(
        "sic,sje->ijce", left_side, right_mine, preferred_element_type=jnp.float32
    )
    outer_sums = outer_sums.reshape(res_dev, quarter, FACTOR_CHANNELS * FACTOR_CHANNELS)
    update = jnp.einsum("ijf,fz->ijz", outer_sums, outer_weight, precision=lax.Precision.HIGHEST)
    live = live_rows[:, None] * live_cols[None, :]
    update = update / (counts[:, :, None] + count_eps) * live[:, :, None]
    pair_out = (pair_rep.astype(jnp.float32) + update).astype(jnp.bfloat16)
    return (updated_alignment, pair_out)


LANES = 128
LOG2E = math.log2(math.e)
LIVE_SCALE = 1.0 / 128.0
BF16 = jnp.bfloat16
F32 = jnp.float32
MIB = 1024 * 1024


def nt_dot(a, b):
    return lax.dot_general(a, b, (((1,), (1,)), ((), ())), preferred_element_type=F32)


def nn_dot(a, b):
    return jnp.dot(a, b, preferred_element_type=F32)


def full_spec(shape):
    zeros = (0,) * len(shape)
    return pl.BlockSpec(shape, lambda *_: zeros)


def params(mib):
    return pltpu.CompilerParams(vmem_limit_bytes=mib * MIB)


def tiled_scratch(rows, cols):
    return pltpu.VMEM((cols // LANES, rows, LANES), F32)


def store_strided(held, first, stride, values):
    rows = values.shape[0]
    for t in range(held.shape[0]):
        held[t, pl.ds(first, rows, stride=stride), :] = values[:, t * LANES : (t + 1) * LANES]


def load_strided(held, first, stride, rows):
    parts = [held[t, pl.ds(first, rows, stride=stride), :] for t in range(held.shape[0])]
    return jnp.concatenate(parts, axis=1)


def joined_tiles(held):
    return jnp.concatenate([held[t] for t in range(held.shape[0])], axis=1)


def in_hbm(*arrays):
    return [pltpu.with_memory_space_constraint(a, pltpu.HBM) for a in arrays]


def in_vmem(*arrays):
    return [pltpu.with_memory_space_constraint(a, pltpu.VMEM) for a in arrays]


def head_lanes(length):
    lane = lax.broadcasted_iota(jnp.int32, (length, LANES), 1) // HEAD_CHANNELS
    return [
        jnp.where(lane == t, 1.0, 0.0).astype(BF16) for t in range(LANES // HEAD_CHANNELS)
    ]


def one_hot(shape, dim, place, value=1.0):
    hit = lax.broadcasted_iota(jnp.int32, shape, dim) == place
    return jnp.where(hit, value, 0.0).astype(BF16)


def quotient(top, below):
    guess = pl.reciprocal(below, approx=True)
    return top * (guess * (2.0 - below * guess))


def attend_all(items, lanes, bias_of):
    per_tile = LANES // HEAD_CHANNELS
    rows, width = items[0][0].shape
    tasks = [(n, tile) for n in range(len(items)) for tile in range(width // LANES)]
    scores, raised, pieces = {}, {}, [[] for _ in items]

    def score(at):
        n, tile = tasks[at]
        cut = slice(tile * LANES, (tile + 1) * LANES)
        query, key = items[n][0][:, cut], items[n][1][:, cut]
        stacked = jnp.concatenate([query * lanes[t] for t in range(per_tile)], axis=0)
        scores[at] = nt_dot(stacked, key)

    def raise_scores(at):
        n, tile = tasks[at]
        stacked = scores.pop(at)
        parts = []
        for t in range(per_tile):
            part = stacked[t * rows : (t + 1) * rows]
            if bias_of is not None:
                part = part + bias_of(tile * per_tile + t)
            parts.append(jnp.exp2(part).astype(BF16))
        raised[at] = jnp.concatenate(parts, axis=1)

    def gather(at):
        n, tile = tasks[at]
        cut = slice(tile * LANES, (tile + 1) * LANES)
        live = items[n][3]
        value = items[n][2][:, cut] * live
        sides = [
            jnp.concatenate([value * lanes[t], live * lanes[t]], axis=1) for t in range(per_tile)
        ]
        total = nn_dot(raised.pop(at), jnp.concatenate(sides, axis=0))
        pieces[n].append(quotient(total[:, :LANES], total[:, LANES:]))

    for at in range(len(tasks) + 2):
        if at < len(tasks):
            score(at)
        if 0 <= at - 2:
            gather(at - 2)
        if 0 <= at - 1 < len(tasks):
            raise_scores(at - 1)
    return [jnp.concatenate(p, axis=1) for p in pieces]


def project(normed, weight_ref):
    scale = LOG2E / math.sqrt(HEAD_CHANNELS)
    query = (nn_dot(normed, weight_ref[0]) * scale).astype(BF16)
    key = nn_dot(normed, weight_ref[1]).astype(BF16)
    value = nn_dot(normed, weight_ref[2]).astype(BF16)
    gate = 0.5 * jnp.tanh(0.5 * nn_dot(normed, weight_ref[3])) + 0.5
    return query, key, value, gate


def bias_kernel(pair_ref, weight_ref, out_ref, held):
    rows, cols, width = pair_ref.shape
    normed = layer_normalize(pair_ref[...].astype(F32)).astype(BF16).reshape(rows * cols, width)
    bias = nt_dot(weight_ref[...], normed) * LOG2E
    for i in range(rows):
        store_strided(held, i, rows, bias[:, i * cols : (i + 1) * cols])
    out_ref[...] = joined_tiles(held).astype(BF16)


def pair_bias_block(pair_rep, bias_weight):
    rows, cols, width = pair_rep.shape
    out = jax.ShapeDtypeStruct((ATTN_HEAD_COUNT * rows, cols), BF16)
    weight = bias_weight.T
    return pl.pallas_call(
        bias_kernel,
        grid=(1,),
        in_specs=[full_spec(pair_rep.shape), full_spec(weight.shape)],
        out_specs=pl.BlockSpec(memory_space=pltpu.VMEM),
        out_shape=out,
        scratch_shapes=[tiled_scratch(*out.shape)],
        compiler_params=params(16),
        name="pair_bias",
    )(*in_hbm(pair_rep, weight))


def row_project_kernel(x_ref, weight_ref, q_ref, k_ref, v_ref, g_ref):
    for s in range(x_ref.shape[0]):
        normed = layer_normalize(x_ref[s].astype(F32)).astype(BF16)
        q_ref[s], k_ref[s], v_ref[s], g_ref[s] = project(normed, weight_ref)


def row_project(alignment, weight):
    seqs, length, width = alignment.shape
    step = 2
    block = pl.BlockSpec((step, length, width), lambda i: (i, 0, 0))
    return pl.pallas_call(
        row_project_kernel,
        grid=(seqs // step,),
        in_specs=[block, full_spec(weight.shape)],
        out_specs=[block] * 4,
        out_shape=[pltpu.HBM(alignment.shape, BF16)] * 3 + [pltpu.HBM(alignment.shape, F32)],
        compiler_params=params(24),
        name="row_project",
    )(*in_hbm(alignment, weight))


def row_attend_kernel(
    plan, step, seqs, me_ref, x_ref, q_ref, k_ref, v_ref, g_ref, mask_ref, out_w_ref, *rest
):
    bias_refs, out_ref, bias_all = rest[: len(plan)], rest[-2], rest[-1]
    heads, length, _ = bias_all.shape

    @pl.when(pl.program_id(0) == 0)
    def _():
        for bias_ref, offsets in zip(bias_refs, plan):
            for z, offset in enumerate(offsets):
                block = bias_ref[z].astype(F32).reshape(heads, -1, length)
                rows = block.shape[1]
                owner = me_ref[0] ^ offset
                bias_all[:, pl.ds(pl.multiple_of(owner * rows, rows), rows), :] = block

    lanes = head_lanes(length)
    parts, rows = out_ref.shape[0], out_ref.shape[1]
    own = mask_ref[pl.ds(pl.multiple_of(me_ref[0] * seqs, seqs), seqs), :]
    own = own.astype(F32).astype(BF16)
    items = []
    for s in range(step):
        place = pl.program_id(0) * step + s
        spot = one_hot((seqs, LANES), 0, place, LIVE_SCALE)
        live = lax.dot_general(
            own, spot, (((0,), (0,)), ((), ())), preferred_element_type=F32
        ).astype(BF16)
        items.append((q_ref[s], k_ref[s], v_ref[s], live))
    results = []
    for s, heads_out in enumerate(attend_all(items, lanes, lambda h: bias_all[h])):
        heads_out = (heads_out * g_ref[s]).astype(BF16)
        total = x_ref[s].astype(F32) + nn_dot(heads_out, out_w_ref[...])
        results.append(total.reshape(parts, 1, rows // step, total.shape[1]))
    joined = jnp.concatenate(results, axis=1)
    out_ref[...] = joined.reshape(out_ref.shape).astype(BF16)


def row_attend(me, alignment, projected, mask, out_weight, bias_parts, plan, parts):
    seqs, length, width = alignment.shape
    rows = length // parts
    step = 2
    vmem = pl.BlockSpec(memory_space=pltpu.VMEM)
    block = pl.BlockSpec((step, length, width), lambda i: (i, 0, 0))
    return pl.pallas_call(
        functools.partial(row_attend_kernel, plan, step, seqs),
        grid=(seqs // step,),
        in_specs=[pl.BlockSpec(memory_space=pltpu.SMEM)]
        + [block] * 5
        + [full_spec(mask.shape), full_spec(out_weight.shape)]
        + [vmem] * len(bias_parts),
        out_specs=pl.BlockSpec((parts, step * rows, width), lambda i: (0, i, 0)),
        out_shape=jax.ShapeDtypeStruct((parts, seqs * rows, width), BF16),
        scratch_shapes=[pltpu.VMEM((ATTN_HEAD_COUNT, length, length), F32)],
        compiler_params=params(24),
        name="row_attend",
    )(me, *in_hbm(alignment, *projected, mask, out_weight), *in_vmem(*bias_parts))


def column_kernel(
    items, me_ref, x_ref, mask_ref, weight_ref, out_w_ref, factor_ref,
    out_ref, left_ref, right_ref, held, right_held,
):
    total_rows = held.shape[1]
    length = total_rows // items
    for t in range(held.shape[0]):
        part = x_ref[:, :, t * LANES : (t + 1) * LANES].astype(F32)
        held[t] = part.reshape(total_rows, LANES)

    lanes = head_lanes(length)
    mask = mask_ref[...].astype(F32).astype(BF16)
    residues = mask.shape[1]
    place = me_ref[0] * items
    rows = [load_strided(held, n, items, length) for n in range(items)]
    inputs, gates, normed = [], [], {0: layer_normalize(rows[0]).astype(BF16)}
    for n in range(items):
        if n + 1 < items:
            normed[n + 1] = layer_normalize(rows[n + 1]).astype(BF16)
        query, key, value, gate = project(normed[n], weight_ref)
        live = nn_dot(mask, one_hot((residues, LANES), 0, place + n, LIVE_SCALE)).astype(BF16)
        inputs.append((query, key, value, live))
        gates.append(gate)
    heads = attend_all(inputs, lanes, None)
    feat = FACTOR_CHANNELS
    live_rows = nt_dot(
        one_hot((items, residues), 1, place + lax.broadcasted_iota(jnp.int32, (items, residues), 0)),
        mask,
    )
    updated = {}
    for at in range(items + 2):
        if at < items:
            heads_out = (heads[at] * gates[at]).astype(BF16)
            updated[at] = (rows[at] + nn_dot(heads_out, out_w_ref[...])).astype(BF16)
            out_ref[at] = updated[at]
        if 0 <= at - 2:
            n = at - 2
            factors = nt_dot(factor_ref[...], normed[n]) * live_rows[n : n + 1]
            left_ref[n * feat : (n + 1) * feat, :] = factors[:feat].astype(BF16)
            store_strided(right_held, n, items, factors[feat:])
        if 0 <= at - 1 < items:
            normed[at - 1] = layer_normalize(updated[at - 1].astype(F32)).astype(BF16)
    right_ref[...] = joined_tiles(right_held).astype(BF16)


def column_attend(me, moved, mask, weight, out_weight, factor_weight, items):
    width = moved.shape[2]
    total_rows = moved.shape[0] * moved.shape[1]
    length = total_rows // items
    side = (items * FACTOR_CHANNELS, length)
    left = right = jax.ShapeDtypeStruct(side, BF16)
    vmem = pl.BlockSpec(memory_space=pltpu.VMEM)
    operands = in_vmem(moved, mask, weight, out_weight, factor_weight.T)
    return pl.pallas_call(
        functools.partial(column_kernel, items),
        in_specs=[pl.BlockSpec(memory_space=pltpu.SMEM)] + [vmem] * len(operands),
        out_specs=[vmem] * 3,
        out_shape=[pltpu.VMEM((items, length, width), BF16), left, right],
        scratch_shapes=[tiled_scratch(total_rows, width), tiled_scratch(*side)],
        compiler_params=params(48),
        name="column_attend",
    )(me, *operands)


def interleave_kernel(rows_ref, out_ref, held):
    items, step = rows_ref.shape[0], out_ref.shape[0]
    at = pl.ds(pl.multiple_of(pl.program_id(0) * step, step), step)
    for item in range(items):
        store_strided(held, item, items, rows_ref[item, at, :].astype(F32))
    out_ref[...] = joined_tiles(held).reshape(out_ref.shape).astype(BF16)


def interleave(rows):
    items, length, width = rows.shape
    step = length // 4
    return pl.pallas_call(
        interleave_kernel,
        grid=(length // step,),
        in_specs=[pl.BlockSpec(memory_space=pltpu.VMEM)],
        out_specs=pl.BlockSpec((step, items, width), lambda i: (i, 0, 0)),
        out_shape=pltpu.HBM((length, items, width), BF16),
        scratch_shapes=[tiled_scratch(items * step, width)],
        compiler_params=params(16),
        name="interleave",
    )(*in_vmem(rows))


def outer_kernel(group, outer, items, *refs):
    lefts, rights = refs[:group], refs[group : group + outer]
    weight_ref = refs[group + outer]
    outs = refs[group + outer + 1 : -3]
    weight_rows, weight, held = refs[-3:]
    feat = FACTOR_CHANNELS
    half = LANES // 2
    duo = half // feat
    tiles = items * feat // half
    cols = outer * items
    width = weight_ref.shape[1]

    weight_rows[...] = weight_ref[...].astype(F32)
    weight[...] = jnp.zeros_like(weight)
    for e in range(feat):
        block = weight_rows[pl.ds(e, feat, stride=feat), :].astype(BF16)
        for i in range(duo):
            start = (e * duo + i) * feat
            weight[start : start + feat, i * width : (i + 1) * width] = block

    right = jnp.concatenate([r[...] for r in rights], axis=0)
    for k in range(group):
        sums = nt_dot(right, lefts[k][...])
        sums = sums.reshape(outer, feat, items, sums.shape[1])
        sums = jnp.transpose(sums, (1, 0, 2, 3)).reshape(feat, cols, sums.shape[3]).astype(BF16)
        for e in range(0, feat, 2):
            for t in range(tiles):
                at = slice((k * tiles + t) * cols, (k * tiles + t + 1) * cols)
                cut = slice(t * half, (t + 1) * half)
                both = jnp.concatenate([sums[e, :, cut], sums[e + 1, :, cut]], axis=1)
                held[at, e * half : (e + 2) * half] = both
    update = nn_dot(held[...], weight[...])
    for k in range(group):
        for t in range(tiles):
            rows = update[(k * tiles + t) * cols : (k * tiles + t + 1) * cols]
            for i in range(duo):
                outs[k][t * duo + i] = rows[:, i * width : (i + 1) * width].astype(BF16)


def outer_product(lefts, rights, weight, items):
    group, outer = len(lefts), len(rights)
    cols = outer * items
    half = LANES // 2
    tiles = items * FACTOR_CHANNELS // half
    depth = FACTOR_CHANNELS * half
    width = weight.shape[1]
    return pl.pallas_call(
        functools.partial(outer_kernel, group, outer, items),
        out_shape=[jax.ShapeDtypeStruct((items, cols, width), BF16)] * group,
        scratch_shapes=[
            pltpu.VMEM(weight.shape, F32),
            pltpu.VMEM((depth, half // FACTOR_CHANNELS * width), BF16),
            pltpu.VMEM((group * tiles * cols, depth), BF16),
        ],
        compiler_params=params(28),
        name="outer_product",
    )(*lefts, *rights, weight)


def finish_kernel(offsets, line, me_ref, pair_ref, scale_ref, *refs):
    parts, out_ref = refs[:-1], refs[-1]
    here = me_ref[0]
    items, cols, width = parts[0].shape
    outer = cols // items
    odd = (here & 1) == 1
    for k, offset in enumerate(offsets):
        for i in range(items):
            both = parts[k][i].astype(F32).reshape(outer // 2, 2, items, width)
            low, high = both[:, 0:1], both[:, 1:2]
            both = jnp.concatenate([jnp.where(odd, high, low), jnp.where(odd, low, high)], axis=1)
            both = both.reshape(outer // 2, 2 * items, width)
            for z in range(outer // 2):
                owner = here ^ (offset | line[z])
                start = pl.multiple_of((owner >> 1) * (2 * items), 2 * items)
                at = pl.ds(start, 2 * items)
                update = both[z] * scale_ref[at, i : i + 1]
                out_ref[i, at, :] = (pair_ref[i, at, :].astype(F32) + update).astype(BF16)


def finish(me, pair_rep, scale, parts, offsets, line):
    vmem = pl.BlockSpec(memory_space=pltpu.VMEM)
    return pl.pallas_call(
        functools.partial(finish_kernel, offsets, line),
        in_specs=[pl.BlockSpec(memory_space=pltpu.SMEM)] + [vmem] * (2 + len(parts)),
        out_specs=vmem,
        out_shape=jax.ShapeDtypeStruct(pair_rep.shape, BF16),
        compiler_params=params(16),
        name="finish",
    )(me, pair_rep, scale, *parts)


def exchange(block, count, offset):
    if offset == 0:
        return block
    return lax.ppermute(block, "dap", [(i, i ^ offset) for i in range(count)])


def per_device_fast(
    alignment,
    pair_rep,
    align_mask,
    residue_mask,
    bias_weight,
    row_proj_weight,
    row_out_weight,
    column_proj_weight,
    column_out_weight,
    outer_factor_weight,
    outer_out,
):
    count = lax.axis_size("dap")
    dap_index = lax.axis_index("dap")
    me = jnp.reshape(dap_index, (1,)).astype(jnp.int32)
    plane, line = offset_groups(count)
    items = pair_rep.shape[0]

    bias = pair_bias_block(pair_rep, bias_weight)
    projected = list(row_project(alignment, row_proj_weight))
    column = [exchange(bias, count, z) for z in line]
    *column, projected[0] = lax.optimization_barrier((*column, projected[0]))
    column = jnp.stack(column)
    bias_parts = [exchange(column, count, k) for k in plane]
    plan = [[k | z for z in line] for k in plane]
    bias_parts += [exchange(part, count, 1) for part in bias_parts]
    plan += [[offset | 1 for offset in offsets] for offsets in plan]

    rows = row_attend(
        me, alignment, projected, align_mask, row_out_weight, bias_parts, plan, count
    )
    rows, late_mask = lax.optimization_barrier((rows, align_mask))
    moved = lax.all_to_all(rows, "dap", split_axis=0, concat_axis=0, tiled=True)
    own_res = lax.dynamic_slice_in_dim(late_mask, dap_index * items, items, 1)
    counts = jnp.einsum(
        "si,sj->ji", own_res.astype(BF16), late_mask.astype(BF16), preferred_element_type=F32
    )
    res_float = residue_mask.astype(F32)
    live_rows = lax.dynamic_slice_in_dim(res_float, dap_index * items, items, 0)
    scale = live_rows[None, :] * res_float[:, None] / (counts + count_eps)
    updated, left, right = column_attend(
        me,
        moved,
        align_mask,
        column_proj_weight,
        column_out_weight,
        outer_factor_weight,
        items,
    )
    rights = [exchange(right, count, z) for z in line]
    rights[1], updated = lax.optimization_barrier((rights[1], updated))
    updated = interleave(updated)
    *rights, updated = lax.optimization_barrier((*rights, updated))
    rights = [part for own in rights for part in (own, exchange(own, count, 1))]
    lefts = [exchange(left, count, k) for k in plane]
    sent = outer_product(lefts[1:], rights, outer_out, items)
    parts = [exchange(part, count, k) for part, k in zip(sent, plane[1:])]
    own = outer_product([left], rights, outer_out, items)
    parts = list(own) + parts
    pair_out = finish(me, pair_rep, scale, parts, plane, line)
    return updated, pair_out


def offset_groups(count):
    bits = count.bit_length() - 1
    near = (bits - 1) // 2
    plane = [k << 1 for k in range(1 << near)]
    line = [z << (1 + near) for z in range(1 << (bits - 1 - near))]
    return plane, line


def solution(mesh):
    placed = (
        P("dap", None, None),
        P("dap", "branch", None),
        P(),
        P(),
        P(),
        P(None, None, "branch"),
        P(),
        P(None, None, "branch"),
        P(),
        P(),
        P(),
    )
    count = mesh.shape["dap"]
    whole_heads = mesh.shape["branch"] == 1 and count & (count - 1) == 0

    def per_device(*operands):
        alignment, pair_rep = operands[0], operands[1]
        tile = 8
        fits = whole_heads and alignment.shape[0] == tile and pair_rep.shape[0] == tile
        return (per_device_fast if fits else per_device_general)(*operands)

    return jax.shard_map(
        per_device,
        mesh=mesh,
        in_specs=placed,
        out_specs=(P(None, "dap", None), P("dap", "branch", None)),
        check_vma=False,
    )
```

```python
import functools
import math

import jax
import jax.numpy as jnp
from jax import lax
from jax.experimental import pallas as pl
from jax.experimental.pallas import tpu as pltpu
from jax.sharding import PartitionSpec as P

ATTN_HEAD_COUNT = 8
HEAD_CHANNELS = 32
FACTOR_CHANNELS = 32


norm_eps = 1e-05
count_eps = 0.001


def layer_normalize(values):
    centre = jnp.mean(values, axis=-1, keepdims=True)
    centred = values - centre
    spread = jnp.mean(centred * centred, axis=-1, keepdims=True)
    return centred * lax.rsqrt(spread + norm_eps)


def attend_heads(inputs, key_mask, proj_weight, out_weight, score_bias):
    batch = inputs.shape[0]
    length = inputs.shape[1]
    local_width = proj_weight.shape[2]
    local_heads = local_width // HEAD_CHANNELS
    normed = layer_normalize(inputs.astype(jnp.float32)).astype(jnp.bfloat16)
    projected = jnp.einsum("blc,kcd->kbld", normed, proj_weight, preferred_element_type=jnp.float32)
    triple = (
        projected[:3].astype(jnp.bfloat16).reshape(3, batch, length, local_heads, HEAD_CHANNELS)
    )
    gating = jax.nn.sigmoid(projected[3])

    def attend_one(operands):
        queries, key_rows, value_rows, mask_row = operands
        scores = jnp.einsum(
            "ihd,jhd->hij", queries, key_rows, preferred_element_type=jnp.float32
        ) / math.sqrt(HEAD_CHANNELS)
        if score_bias is not None:
            scores = scores + score_bias.astype(jnp.float32)
        raised = jnp.exp(scores) * mask_row[None, None, :]
        weights = (raised / jnp.sum(raised, axis=-1, keepdims=True)).astype(jnp.bfloat16)
        return jnp.einsum("hij,jhd->ihd", weights, value_rows, preferred_element_type=jnp.float32)

    attended_rows = lax.map(attend_one, (triple[0], triple[1], triple[2], key_mask))
    heads_out = (attended_rows.reshape(batch, length, local_width) * gating).astype(jnp.bfloat16)
    gathered = lax.all_gather(heads_out, "branch", axis=2, tiled=True)
    update = jnp.einsum("blf,fc->blc", gathered, out_weight, preferred_element_type=jnp.float32)
    return (inputs.astype(jnp.float32) + update).astype(jnp.bfloat16)


def per_device_general(
    alignment,
    pair_rep,
    align_mask,
    residue_mask,
    bias_weight,
    row_proj_weight,
    row_out_weight,
    column_proj_weight,
    column_out_weight,
    outer_factor_weight,
    outer_out,
):
    branch_count = lax.axis_size("branch")
    dap_count = lax.axis_size("dap")
    branch_index = lax.axis_index("branch")
    dap_index = lax.axis_index("dap")
    seq_dev = alignment.shape[0]
    res_dev = pair_rep.shape[0]
    quarter = pair_rep.shape[1]
    total_seqs = align_mask.shape[0]
    local_heads = ATTN_HEAD_COUNT // branch_count
    float_mask = align_mask.astype(jnp.float32)
    res_float = residue_mask.astype(jnp.float32)
    pair_normed = layer_normalize(pair_rep.astype(jnp.float32)).astype(jnp.bfloat16)
    bias_block = jnp.einsum(
        "ijc,ch->hij", pair_normed, bias_weight, preferred_element_type=jnp.float32
    ).astype(jnp.bfloat16)
    bias_wide = lax.all_gather(bias_block, "branch", axis=2, tiled=True)
    bias_full = lax.all_gather(bias_wide, "dap", axis=1, tiled=True)
    pair_score_bias = lax.dynamic_slice_in_dim(
        bias_full, branch_index * local_heads, local_heads, 0
    )
    sequence_row_mask = lax.dynamic_slice_in_dim(float_mask, dap_index * seq_dev, seq_dev, 0)
    row_alignment = attend_heads(
        alignment, sequence_row_mask, row_proj_weight, row_out_weight, pair_score_bias
    )
    send_mask = sequence_row_mask.astype(jnp.bfloat16)
    blocked_rows = row_alignment.reshape(seq_dev, dap_count, res_dev, row_alignment.shape[2])
    blocked_mask = send_mask.reshape(seq_dev, dap_count, res_dev)
    moved_rows = lax.all_to_all(blocked_rows, "dap", split_axis=1, concat_axis=0, tiled=True)
    moved_mask = lax.all_to_all(blocked_mask, "dap", split_axis=1, concat_axis=0, tiled=True)
    seq_total = moved_rows.shape[0]
    items = moved_rows.shape[2]
    flat_rows = moved_rows.reshape(seq_total, items, moved_rows.shape[3])
    flat_mask = moved_mask.reshape(seq_total, items)
    transposed_rows = jnp.swapaxes(flat_rows, 0, 1)
    key_mask = jnp.swapaxes(flat_mask, 0, 1).astype(jnp.float32)
    attended_rows = attend_heads(
        transposed_rows, key_mask, column_proj_weight, column_out_weight, None
    )
    column_alignment = jnp.swapaxes(attended_rows, 0, 1)
    outer_mean_normed = layer_normalize(column_alignment.astype(jnp.float32)).astype(jnp.bfloat16)
    projected = jnp.einsum(
        "src,ce->sre", outer_mean_normed, outer_factor_weight, preferred_element_type=jnp.float32
    )
    factor_pairs = (projected * flat_mask.astype(jnp.float32)[:, :, None]).astype(jnp.bfloat16)
    column_alignment, factor_pairs = (column_alignment, factor_pairs)
    blocked_out = column_alignment.reshape(seq_total, 1, items, column_alignment.shape[2])
    blocked_factors = factor_pairs.reshape(seq_total, 1, items, factor_pairs.shape[2])
    updated_alignment = blocked_out.reshape(total_seqs, res_dev, blocked_out.shape[3])
    factor_pairs = blocked_factors.reshape(total_seqs, res_dev, blocked_factors.shape[3])
    left_side = factor_pairs[:, :, :FACTOR_CHANNELS]
    right_local = factor_pairs[:, :, FACTOR_CHANNELS:]
    col_start = branch_index * quarter
    row_start = dap_index * res_dev
    mask_rows = lax.dynamic_slice_in_dim(align_mask, row_start, res_dev, 1).astype(jnp.bfloat16)
    mask_cols = lax.dynamic_slice_in_dim(align_mask, col_start, quarter, 1).astype(jnp.bfloat16)
    counts = jnp.einsum("si,sj->ij", mask_rows, mask_cols, preferred_element_type=jnp.float32)
    live_rows = lax.dynamic_slice_in_dim(res_float, row_start, res_dev, 0)
    live_cols = lax.dynamic_slice_in_dim(res_float, col_start, quarter, 0)
    outer_weight = outer_out.astype(jnp.float32)
    right_all = lax.all_gather(right_local, "dap", axis=1, tiled=True)
    right_mine = lax.dynamic_slice_in_dim(right_all, col_start, quarter, 1)
    outer_sums = jnp.einsum(
        "sic,sje->ijce", left_side, right_mine, preferred_element_type=jnp.float32
    )
    outer_sums = outer_sums.reshape(res_dev, quarter, FACTOR_CHANNELS * FACTOR_CHANNELS)
    update = jnp.einsum("ijf,fz->ijz", outer_sums, outer_weight, precision=lax.Precision.HIGHEST)
    live = live_rows[:, None] * live_cols[None, :]
    update = update / (counts[:, :, None] + count_eps) * live[:, :, None]
    pair_out = (pair_rep.astype(jnp.float32) + update).astype(jnp.bfloat16)
    return (updated_alignment, pair_out)


LANES = 128
LOG2E = math.log2(math.e)
LIVE_SCALE = 1.0 / 128.0
BF16 = jnp.bfloat16
F32 = jnp.float32
MIB = 1024 * 1024


def nt_dot(a, b):
    return lax.dot_general(a, b, (((1,), (1,)), ((), ())), preferred_element_type=F32)


def nn_dot(a, b):
    return jnp.dot(a, b, preferred_element_type=F32)


def full_spec(shape):
    zeros = (0,) * len(shape)
    return pl.BlockSpec(shape, lambda *_: zeros)


def params(mib):
    return pltpu.CompilerParams(vmem_limit_bytes=mib * MIB)


def tiled_scratch(rows, cols):
    return pltpu.VMEM((cols // LANES, rows, LANES), F32)


def store_strided(held, first, stride, values):
    rows = values.shape[0]
    for t in range(held.shape[0]):
        held[t, pl.ds(first, rows, stride=stride), :] = values[:, t * LANES : (t + 1) * LANES]


def load_strided(held, first, stride, rows):
    parts = [held[t, pl.ds(first, rows, stride=stride), :] for t in range(held.shape[0])]
    return jnp.concatenate(parts, axis=1)


def joined_tiles(held):
    return jnp.concatenate([held[t] for t in range(held.shape[0])], axis=1)


def in_hbm(*arrays):
    return [pltpu.with_memory_space_constraint(a, pltpu.HBM) for a in arrays]


def in_vmem(*arrays):
    return [pltpu.with_memory_space_constraint(a, pltpu.VMEM) for a in arrays]


def head_lanes(length):
    lane = lax.broadcasted_iota(jnp.int32, (length, LANES), 1) // HEAD_CHANNELS
    return [
        jnp.where(lane == t, 1.0, 0.0).astype(BF16) for t in range(LANES // HEAD_CHANNELS)
    ]


def one_hot(shape, dim, place, value=1.0):
    hit = lax.broadcasted_iota(jnp.int32, shape, dim) == place
    return jnp.where(hit, value, 0.0).astype(BF16)


def quotient(top, below):
    guess = pl.reciprocal(below, approx=True)
    return top * (guess * (2.0 - below * guess))


def attend_all(items, lanes, bias_of):
    per_tile = LANES // HEAD_CHANNELS
    rows, width = items[0][0].shape
    tasks = [(n, tile) for n in range(len(items)) for tile in range(width // LANES)]
    scores, raised, pieces = {}, {}, [[] for _ in items]

    def score(at):
        n, tile = tasks[at]
        cut = slice(tile * LANES, (tile + 1) * LANES)
        query, key = items[n][0][:, cut], items[n][1][:, cut]
        stacked = jnp.concatenate([query * lanes[t] for t in range(per_tile)], axis=0)
        scores[at] = nt_dot(stacked, key)

    def raise_scores(at):
        n, tile = tasks[at]
        stacked = scores.pop(at)
        parts = []
        for t in range(per_tile):
            part = stacked[t * rows : (t + 1) * rows]
            if bias_of is not None:
                part = part + bias_of(tile * per_tile + t)
            parts.append(jnp.exp2(part).astype(BF16))
        raised[at] = jnp.concatenate(parts, axis=1)

    def gather(at):
        n, tile = tasks[at]
        cut = slice(tile * LANES, (tile + 1) * LANES)
        live = items[n][3]
        value = items[n][2][:, cut] * live
        sides = [
            jnp.concatenate([value * lanes[t], live * lanes[t]], axis=1) for t in range(per_tile)
        ]
        total = nn_dot(raised.pop(at), jnp.concatenate(sides, axis=0))
        pieces[n].append(quotient(total[:, :LANES], total[:, LANES:]))

    for at in range(len(tasks) + 2):
        if at < len(tasks):
            score(at)
        if 0 <= at - 2:
            gather(at - 2)
        if 0 <= at - 1 < len(tasks):
            raise_scores(at - 1)
    return [jnp.concatenate(p, axis=1) for p in pieces]


def project(normed, weight_ref):
    scale = LOG2E / math.sqrt(HEAD_CHANNELS)
    query = (nn_dot(normed, weight_ref[0]) * scale).astype(BF16)
    key = nn_dot(normed, weight_ref[1]).astype(BF16)
    value = nn_dot(normed, weight_ref[2]).astype(BF16)
    gate = 0.5 * jnp.tanh(0.5 * nn_dot(normed, weight_ref[3])) + 0.5
    return query, key, value, gate


def bias_kernel(pair_ref, weight_ref, out_ref, held):
    rows, cols, width = pair_ref.shape
    normed = layer_normalize(pair_ref[...].astype(F32)).astype(BF16).reshape(rows * cols, width)
    bias = nt_dot(weight_ref[...], normed) * LOG2E
    for i in range(rows):
        store_strided(held, i, rows, bias[:, i * cols : (i + 1) * cols])
    out_ref[...] = joined_tiles(held).astype(BF16)


def pair_bias_block(pair_rep, bias_weight):
    rows, cols, width = pair_rep.shape
    out = jax.ShapeDtypeStruct((ATTN_HEAD_COUNT * rows, cols), BF16)
    weight = bias_weight.T
    return pl.pallas_call(
        bias_kernel,
        grid=(1,),
        in_specs=[full_spec(pair_rep.shape), full_spec(weight.shape)],
        out_specs=pl.BlockSpec(memory_space=pltpu.VMEM),
        out_shape=out,
        scratch_shapes=[tiled_scratch(*out.shape)],
        compiler_params=params(16),
        name="pair_bias",
    )(*in_hbm(pair_rep, weight))


def row_project_kernel(x_ref, weight_ref, q_ref, k_ref, v_ref, g_ref):
    for s in range(x_ref.shape[0]):
        normed = layer_normalize(x_ref[s].astype(F32)).astype(BF16)
        q_ref[s], k_ref[s], v_ref[s], g_ref[s] = project(normed, weight_ref)


def row_project(alignment, weight):
    seqs, length, width = alignment.shape
    step = 2
    block = pl.BlockSpec((step, length, width), lambda i: (i, 0, 0))
    return pl.pallas_call(
        row_project_kernel,
        grid=(seqs // step,),
        in_specs=[block, full_spec(weight.shape)],
        out_specs=[block] * 4,
        out_shape=[pltpu.HBM(alignment.shape, BF16)] * 3 + [pltpu.HBM(alignment.shape, F32)],
        compiler_params=params(24),
        name="row_project",
    )(*in_hbm(alignment, weight))


def row_attend_kernel(
    plan, step, seqs, me_ref, x_ref, q_ref, k_ref, v_ref, g_ref, mask_ref, out_w_ref, *rest
):
    bias_refs, out_ref, bias_all = rest[: len(plan)], rest[-2], rest[-1]
    heads, length, _ = bias_all.shape

    @pl.when(pl.program_id(0) == 0)
    def _():
        for bias_ref, offsets in zip(bias_refs, plan):
            for z, offset in enumerate(offsets):
                block = bias_ref[z].astype(F32).reshape(heads, -1, length)
                rows = block.shape[1]
                owner = me_ref[0] ^ offset
                bias_all[:, pl.ds(pl.multiple_of(owner * rows, rows), rows), :] = block

    lanes = head_lanes(length)
    parts, rows = out_ref.shape[0], out_ref.shape[1]
    own = mask_ref[pl.ds(pl.multiple_of(me_ref[0] * seqs, seqs), seqs), :]
    own = own.astype(F32).astype(BF16)
    items = []
    for s in range(step):
        place = pl.program_id(0) * step + s
        spot = one_hot((seqs, LANES), 0, place, LIVE_SCALE)
        live = lax.dot_general(
            own, spot, (((0,), (0,)), ((), ())), preferred_element_type=F32
        ).astype(BF16)
        items.append((q_ref[s], k_ref[s], v_ref[s], live))
    heads = attend_all(items, lanes, lambda h: bias_all[h])
    gated = [(heads[s] * g_ref[s]).astype(BF16) for s in range(step)]
    results = []
    for s in range(step):
        total = x_ref[s].astype(F32) + nn_dot(gated[s], out_w_ref[...])
        results.append(total.reshape(parts, 1, rows // step, total.shape[1]))
    joined = jnp.concatenate(results, axis=1)
    out_ref[...] = joined.reshape(out_ref.shape).astype(BF16)


def row_attend(me, alignment, projected, mask, out_weight, bias_parts, plan, parts):
    seqs, length, width = alignment.shape
    rows = length // parts
    step = 4
    vmem = pl.BlockSpec(memory_space=pltpu.VMEM)
    block = pl.BlockSpec((step, length, width), lambda i: (i, 0, 0))
    return pl.pallas_call(
        functools.partial(row_attend_kernel, plan, step, seqs),
        grid=(seqs // step,),
        in_specs=[pl.BlockSpec(memory_space=pltpu.SMEM)]
        + [block] * 5
        + [full_spec(mask.shape), full_spec(out_weight.shape)]
        + [vmem] * len(bias_parts),
        out_specs=pl.BlockSpec((parts, step * rows, width), lambda i: (0, i, 0)),
        out_shape=jax.ShapeDtypeStruct((parts, seqs * rows, width), BF16),
        scratch_shapes=[pltpu.VMEM((ATTN_HEAD_COUNT, length, length), F32)],
        compiler_params=params(40),
        name="row_attend",
    )(me, *in_hbm(alignment, *projected, mask, out_weight), *in_vmem(*bias_parts))


def column_kernel(
    items, me_ref, x_ref, mask_ref, weight_ref, out_w_ref, factor_ref,
    out_ref, left_ref, right_ref, held, right_held,
):
    total_rows = held.shape[1]
    length = total_rows // items
    for t in range(held.shape[0]):
        part = x_ref[:, :, t * LANES : (t + 1) * LANES].astype(F32)
        held[t] = part.reshape(total_rows, LANES)

    lanes = head_lanes(length)
    mask = mask_ref[...].astype(F32).astype(BF16)
    residues = mask.shape[1]
    place = me_ref[0] * items
    rows = [load_strided(held, n, items, length) for n in range(items)]
    inputs, gates, normed = [], [], {0: layer_normalize(rows[0]).astype(BF16)}
    for n in range(items):
        if n + 1 < items:
            normed[n + 1] = layer_normalize(rows[n + 1]).astype(BF16)
        query, key, value, gate = project(normed[n], weight_ref)
        live = nn_dot(mask, one_hot((residues, LANES), 0, place + n, LIVE_SCALE)).astype(BF16)
        inputs.append((query, key, value, live))
        gates.append(gate)
    heads = attend_all(inputs, lanes, None)
    feat = FACTOR_CHANNELS
    live_rows = nt_dot(
        one_hot((items, residues), 1, place + lax.broadcasted_iota(jnp.int32, (items, residues), 0)),
        mask,
    )
    updated = {}
    for at in range(items + 2):
        if at < items:
            heads_out = (heads[at] * gates[at]).astype(BF16)
            updated[at] = (rows[at] + nn_dot(heads_out, out_w_ref[...])).astype(BF16)
            out_ref[at] = updated[at]
        if 0 <= at - 2:
            n = at - 2
            factors = nt_dot(factor_ref[...], normed[n]) * live_rows[n : n + 1]
            left_ref[n * feat : (n + 1) * feat, :] = factors[:feat].astype(BF16)
            store_strided(right_held, n, items, factors[feat:])
        if 0 <= at - 1 < items:
            normed[at - 1] = layer_normalize(updated[at - 1].astype(F32)).astype(BF16)
    right_ref[...] = joined_tiles(right_held).astype(BF16)


def column_attend(me, moved, mask, weight, out_weight, factor_weight, items):
    width = moved.shape[2]
    total_rows = moved.shape[0] * moved.shape[1]
    length = total_rows // items
    side = (items * FACTOR_CHANNELS, length)
    left = right = jax.ShapeDtypeStruct(side, BF16)
    vmem = pl.BlockSpec(memory_space=pltpu.VMEM)
    operands = in_vmem(moved, mask, weight, out_weight, factor_weight.T)
    return pl.pallas_call(
        functools.partial(column_kernel, items),
        in_specs=[pl.BlockSpec(memory_space=pltpu.SMEM)] + [vmem] * len(operands),
        out_specs=[vmem] * 3,
        out_shape=[pltpu.VMEM((items, length, width), BF16), left, right],
        scratch_shapes=[tiled_scratch(total_rows, width), tiled_scratch(*side)],
        compiler_params=params(48),
        name="column_attend",
    )(me, *operands)


def interleave_kernel(rows_ref, out_ref, held):
    items, step = rows_ref.shape[0], out_ref.shape[0]
    at = pl.ds(pl.multiple_of(pl.program_id(0) * step, step), step)
    for item in range(items):
        store_strided(held, item, items, rows_ref[item, at, :].astype(F32))
    out_ref[...] = joined_tiles(held).reshape(out_ref.shape).astype(BF16)


def interleave(rows):
    items, length, width = rows.shape
    step = length // 4
    return pl.pallas_call(
        interleave_kernel,
        grid=(length // step,),
        in_specs=[pl.BlockSpec(memory_space=pltpu.VMEM)],
        out_specs=pl.BlockSpec((step, items, width), lambda i: (i, 0, 0)),
        out_shape=pltpu.HBM((length, items, width), BF16),
        scratch_shapes=[tiled_scratch(items * step, width)],
        compiler_params=params(16),
        name="interleave",
    )(*in_vmem(rows))


def outer_kernel(group, outer, items, *refs):
    lefts, rights = refs[:group], refs[group : group + outer]
    weight_ref = refs[group + outer]
    outs = refs[group + outer + 1 : -3]
    weight_rows, weight, held = refs[-3:]
    feat = FACTOR_CHANNELS
    quad = LANES // feat
    tiles = items * feat // LANES
    cols = outer * items
    width = weight_ref.shape[1]

    weight_rows[...] = weight_ref[...].astype(F32)
    weight[...] = jnp.zeros_like(weight)
    for e in range(feat):
        block = weight_rows[pl.ds(e, feat, stride=feat), :].astype(BF16)
        for i in range(quad):
            start = e * LANES + i * feat
            weight[start : start + feat, i * width : (i + 1) * width] = block

    right = jnp.concatenate([r[...] for r in rights], axis=0)
    def product(k):
        return nt_dot(right, lefts[k][...])

    later = product(0)
    for k in range(group):
        sums, later = later, product(k + 1) if k + 1 < group else None
        sums = sums.reshape(outer, feat, items, sums.shape[1])
        sums = jnp.transpose(sums, (1, 0, 2, 3)).reshape(feat, cols, sums.shape[3]).astype(BF16)
        for t in range(tiles):
            at = slice((k * tiles + t) * cols, (k * tiles + t + 1) * cols)
            for e in range(feat):
                held[at, e * LANES : (e + 1) * LANES] = sums[e, :, t * LANES : (t + 1) * LANES]
    update = nn_dot(held[...], weight[...])
    for k in range(group):
        for t in range(tiles):
            rows = update[(k * tiles + t) * cols : (k * tiles + t + 1) * cols]
            for i in range(quad):
                outs[k][t * quad + i] = rows[:, i * width : (i + 1) * width].astype(BF16)


def outer_product(lefts, rights, weight, items):
    group, outer = len(lefts), len(rights)
    cols = outer * items
    tiles = items * FACTOR_CHANNELS // LANES
    depth = FACTOR_CHANNELS * LANES
    width = weight.shape[1]
    return pl.pallas_call(
        functools.partial(outer_kernel, group, outer, items),
        out_shape=[jax.ShapeDtypeStruct((items, cols, width), BF16)] * group,
        scratch_shapes=[
            pltpu.VMEM(weight.shape, F32),
            pltpu.VMEM((depth, LANES // FACTOR_CHANNELS * width), BF16),
            pltpu.VMEM((group * tiles * cols, depth), BF16),
        ],
        compiler_params=params(28),
        name="outer_product",
    )(*lefts, *rights, weight)


def finish_kernel(offsets, line, me_ref, pair_ref, scale_ref, *refs):
    parts, (out_ref, done, sems) = refs[:-3], refs[-3:]
    here = me_ref[0]
    items, cols, width = parts[0].shape
    outer = cols // items
    odd = (here & 1) == 1
    copies = []
    for i in range(items):
        for k, offset in enumerate(offsets):
            both = parts[k][i].astype(F32).reshape(outer // 2, 2, items, width)
            low, high = both[:, 0:1], both[:, 1:2]
            both = jnp.concatenate([jnp.where(odd, high, low), jnp.where(odd, low, high)], axis=1)
            both = both.reshape(outer // 2, 2 * items, width)
            for z in range(outer // 2):
                owner = here ^ (offset | line[z])
                start = pl.multiple_of((owner >> 1) * (2 * items), 2 * items)
                at = pl.ds(start, 2 * items)
                update = both[z] * scale_ref[at, i : i + 1]
                done[i, at, :] = (pair_ref[i, at, :].astype(F32) + update).astype(BF16)
        copies.append(pltpu.make_async_copy(done.at[i], out_ref.at[i], sems.at[i]))
        copies[i].start()
    for copy in copies:
        copy.wait()


def finish(me, pair_rep, scale, parts, offsets, line):
    vmem = pl.BlockSpec(memory_space=pltpu.VMEM)
    return pl.pallas_call(
        functools.partial(finish_kernel, offsets, line),
        in_specs=[pl.BlockSpec(memory_space=pltpu.SMEM)] + [vmem] * (2 + len(parts)),
        out_specs=pl.BlockSpec(memory_space=pltpu.HBM),
        out_shape=pltpu.HBM(pair_rep.shape, BF16),
        scratch_shapes=[
            pltpu.VMEM(pair_rep.shape, BF16),
            pltpu.SemaphoreType.DMA((pair_rep.shape[0],)),
        ],
        compiler_params=params(16),
        name="finish",
    )(me, pair_rep, scale, *parts)


def exchange(block, count, offset):
    if offset == 0:
        return block
    return lax.ppermute(block, "dap", [(i, i ^ offset) for i in range(count)])


def per_device_fast(
    alignment,
    pair_rep,
    align_mask,
    residue_mask,
    bias_weight,
    row_proj_weight,
    row_out_weight,
    column_proj_weight,
    column_out_weight,
    outer_factor_weight,
    outer_out,
):
    count = lax.axis_size("dap")
    dap_index = lax.axis_index("dap")
    me = jnp.reshape(dap_index, (1,)).astype(jnp.int32)
    plane, line = offset_groups(count)
    items = pair_rep.shape[0]

    bias = pair_bias_block(pair_rep, bias_weight)
    projected = list(row_project(alignment, row_proj_weight))
    column = [exchange(bias, count, z) for z in line]
    *column, projected[0] = lax.optimization_barrier((*column, projected[0]))
    column = jnp.stack(column)
    bias_parts = [exchange(column, count, k) for k in plane]
    plan = [[k | z for z in line] for k in plane]
    bias_parts += [exchange(part, count, 1) for part in bias_parts]
    plan += [[offset | 1 for offset in offsets] for offsets in plan]

    rows = row_attend(
        me, alignment, projected, align_mask, row_out_weight, bias_parts, plan, count
    )
    rows, late_mask = lax.optimization_barrier((rows, align_mask))
    moved = lax.all_to_all(rows, "dap", split_axis=0, concat_axis=0, tiled=True)
    own_res = lax.dynamic_slice_in_dim(late_mask, dap_index * items, items, 1)
    counts = jnp.einsum(
        "si,sj->ji", own_res.astype(BF16), late_mask.astype(BF16), preferred_element_type=F32
    )
    res_float = residue_mask.astype(F32)
    live_rows = lax.dynamic_slice_in_dim(res_float, dap_index * items, items, 0)
    scale = live_rows[None, :] * res_float[:, None] / (counts + count_eps)
    updated, left, right = column_attend(
        me,
        moved,
        align_mask,
        column_proj_weight,
        column_out_weight,
        outer_factor_weight,
        items,
    )
    rights = [exchange(right, count, z) for z in line]
    rights[1], updated = lax.optimization_barrier((rights[1], updated))
    updated = interleave(updated)
    *rights, updated = lax.optimization_barrier((*rights, updated))
    rights = [part for own in rights for part in (own, exchange(own, count, 1))]
    lefts = [exchange(left, count, k) for k in plane]
    sent = outer_product(lefts[1:], rights, outer_out, items)
    parts = [exchange(part, count, k) for part, k in zip(sent, plane[1:])]
    own = outer_product([left], rights, outer_out, items)
    parts = list(own) + parts
    pair_out = finish(me, pair_rep, scale, parts, plane, line)
    return updated, pair_out


def offset_groups(count):
    bits = count.bit_length() - 1
    near = (bits - 1) // 2
    plane = [k << 1 for k in range(1 << near)]
    line = [z << (1 + near) for z in range(1 << (bits - 1 - near))]
    return plane, line


def solution(mesh):
    placed = (
        P("dap", None, None),
        P("dap", "branch", None),
        P(),
        P(),
        P(),
        P(None, None, "branch"),
        P(),
        P(None, None, "branch"),
        P(),
        P(),
        P(),
    )
    count = mesh.shape["dap"]
    whole_heads = mesh.shape["branch"] == 1 and count & (count - 1) == 0

    def per_device(*operands):
        alignment, pair_rep = operands[0], operands[1]
        tile = 8
        fits = whole_heads and alignment.shape[0] == tile and pair_rep.shape[0] == tile
        return (per_device_fast if fits else per_device_general)(*operands)

    return jax.shard_map(
        per_device,
        mesh=mesh,
        in_specs=placed,
        out_specs=(P(None, "dap", None), P("dap", "branch", None)),
        check_vma=False,
    )
```

```python
import functools
import math

import jax
import jax.numpy as jnp
from jax import lax
from jax.experimental import pallas as pl
from jax.experimental.pallas import tpu as pltpu
from jax.sharding import PartitionSpec as P

ATTN_HEAD_COUNT = 8
HEAD_CHANNELS = 32
FACTOR_CHANNELS = 32


norm_eps = 1e-05
count_eps = 0.001


def layer_normalize(values):
    centre = jnp.mean(values, axis=-1, keepdims=True)
    centred = values - centre
    spread = jnp.mean(centred * centred, axis=-1, keepdims=True)
    return centred * lax.rsqrt(spread + norm_eps)


def attend_heads(inputs, key_mask, proj_weight, out_weight, score_bias):
    batch = inputs.shape[0]
    length = inputs.shape[1]
    local_width = proj_weight.shape[2]
    local_heads = local_width // HEAD_CHANNELS
    normed = layer_normalize(inputs.astype(jnp.float32)).astype(jnp.bfloat16)
    projected = jnp.einsum("blc,kcd->kbld", normed, proj_weight, preferred_element_type=jnp.float32)
    triple = (
        projected[:3].astype(jnp.bfloat16).reshape(3, batch, length, local_heads, HEAD_CHANNELS)
    )
    gating = jax.nn.sigmoid(projected[3])

    def attend_one(operands):
        queries, key_rows, value_rows, mask_row = operands
        scores = jnp.einsum(
            "ihd,jhd->hij", queries, key_rows, preferred_element_type=jnp.float32
        ) / math.sqrt(HEAD_CHANNELS)
        if score_bias is not None:
            scores = scores + score_bias.astype(jnp.float32)
        raised = jnp.exp(scores) * mask_row[None, None, :]
        weights = (raised / jnp.sum(raised, axis=-1, keepdims=True)).astype(jnp.bfloat16)
        return jnp.einsum("hij,jhd->ihd", weights, value_rows, preferred_element_type=jnp.float32)

    attended_rows = lax.map(attend_one, (triple[0], triple[1], triple[2], key_mask))
    heads_out = (attended_rows.reshape(batch, length, local_width) * gating).astype(jnp.bfloat16)
    gathered = lax.all_gather(heads_out, "branch", axis=2, tiled=True)
    update = jnp.einsum("blf,fc->blc", gathered, out_weight, preferred_element_type=jnp.float32)
    return (inputs.astype(jnp.float32) + update).astype(jnp.bfloat16)


def per_device_general(
    alignment,
    pair_rep,
    align_mask,
    residue_mask,
    bias_weight,
    row_proj_weight,
    row_out_weight,
    column_proj_weight,
    column_out_weight,
    outer_factor_weight,
    outer_out,
):
    branch_count = lax.axis_size("branch")
    dap_count = lax.axis_size("dap")
    branch_index = lax.axis_index("branch")
    dap_index = lax.axis_index("dap")
    seq_dev = alignment.shape[0]
    res_dev = pair_rep.shape[0]
    quarter = pair_rep.shape[1]
    total_seqs = align_mask.shape[0]
    local_heads = ATTN_HEAD_COUNT // branch_count
    float_mask = align_mask.astype(jnp.float32)
    res_float = residue_mask.astype(jnp.float32)
    pair_normed = layer_normalize(pair_rep.astype(jnp.float32)).astype(jnp.bfloat16)
    bias_block = jnp.einsum(
        "ijc,ch->hij", pair_normed, bias_weight, preferred_element_type=jnp.float32
    ).astype(jnp.bfloat16)
    bias_wide = lax.all_gather(bias_block, "branch", axis=2, tiled=True)
    bias_full = lax.all_gather(bias_wide, "dap", axis=1, tiled=True)
    pair_score_bias = lax.dynamic_slice_in_dim(
        bias_full, branch_index * local_heads, local_heads, 0
    )
    sequence_row_mask = lax.dynamic_slice_in_dim(float_mask, dap_index * seq_dev, seq_dev, 0)
    row_alignment = attend_heads(
        alignment, sequence_row_mask, row_proj_weight, row_out_weight, pair_score_bias
    )
    send_mask = sequence_row_mask.astype(jnp.bfloat16)
    blocked_rows = row_alignment.reshape(seq_dev, dap_count, res_dev, row_alignment.shape[2])
    blocked_mask = send_mask.reshape(seq_dev, dap_count, res_dev)
    moved_rows = lax.all_to_all(blocked_rows, "dap", split_axis=1, concat_axis=0, tiled=True)
    moved_mask = lax.all_to_all(blocked_mask, "dap", split_axis=1, concat_axis=0, tiled=True)
    seq_total = moved_rows.shape[0]
    items = moved_rows.shape[2]
    flat_rows = moved_rows.reshape(seq_total, items, moved_rows.shape[3])
    flat_mask = moved_mask.reshape(seq_total, items)
    transposed_rows = jnp.swapaxes(flat_rows, 0, 1)
    key_mask = jnp.swapaxes(flat_mask, 0, 1).astype(jnp.float32)
    attended_rows = attend_heads(
        transposed_rows, key_mask, column_proj_weight, column_out_weight, None
    )
    column_alignment = jnp.swapaxes(attended_rows, 0, 1)
    outer_mean_normed = layer_normalize(column_alignment.astype(jnp.float32)).astype(jnp.bfloat16)
    projected = jnp.einsum(
        "src,ce->sre", outer_mean_normed, outer_factor_weight, preferred_element_type=jnp.float32
    )
    factor_pairs = (projected * flat_mask.astype(jnp.float32)[:, :, None]).astype(jnp.bfloat16)
    column_alignment, factor_pairs = (column_alignment, factor_pairs)
    blocked_out = column_alignment.reshape(seq_total, 1, items, column_alignment.shape[2])
    blocked_factors = factor_pairs.reshape(seq_total, 1, items, factor_pairs.shape[2])
    updated_alignment = blocked_out.reshape(total_seqs, res_dev, blocked_out.shape[3])
    factor_pairs = blocked_factors.reshape(total_seqs, res_dev, blocked_factors.shape[3])
    left_side = factor_pairs[:, :, :FACTOR_CHANNELS]
    right_local = factor_pairs[:, :, FACTOR_CHANNELS:]
    col_start = branch_index * quarter
    row_start = dap_index * res_dev
    mask_rows = lax.dynamic_slice_in_dim(align_mask, row_start, res_dev, 1).astype(jnp.bfloat16)
    mask_cols = lax.dynamic_slice_in_dim(align_mask, col_start, quarter, 1).astype(jnp.bfloat16)
    counts = jnp.einsum("si,sj->ij", mask_rows, mask_cols, preferred_element_type=jnp.float32)
    live_rows = lax.dynamic_slice_in_dim(res_float, row_start, res_dev, 0)
    live_cols = lax.dynamic_slice_in_dim(res_float, col_start, quarter, 0)
    outer_weight = outer_out.astype(jnp.float32)
    right_all = lax.all_gather(right_local, "dap", axis=1, tiled=True)
    right_mine = lax.dynamic_slice_in_dim(right_all, col_start, quarter, 1)
    outer_sums = jnp.einsum(
        "sic,sje->ijce", left_side, right_mine, preferred_element_type=jnp.float32
    )
    outer_sums = outer_sums.reshape(res_dev, quarter, FACTOR_CHANNELS * FACTOR_CHANNELS)
    update = jnp.einsum("ijf,fz->ijz", outer_sums, outer_weight, precision=lax.Precision.HIGHEST)
    live = live_rows[:, None] * live_cols[None, :]
    update = update / (counts[:, :, None] + count_eps) * live[:, :, None]
    pair_out = (pair_rep.astype(jnp.float32) + update).astype(jnp.bfloat16)
    return (updated_alignment, pair_out)


LANES = 128
LOG2E = math.log2(math.e)
LIVE_SCALE = 1.0 / 128.0
BF16 = jnp.bfloat16
F32 = jnp.float32
MIB = 1024 * 1024


def nt_dot(a, b):
    return lax.dot_general(a, b, (((1,), (1,)), ((), ())), preferred_element_type=F32)


def nn_dot(a, b):
    return jnp.dot(a, b, preferred_element_type=F32)


def full_spec(shape):
    zeros = (0,) * len(shape)
    return pl.BlockSpec(shape, lambda *_: zeros)


def params(mib):
    return pltpu.CompilerParams(vmem_limit_bytes=mib * MIB)


def tiled_scratch(rows, cols):
    return pltpu.VMEM((cols // LANES, rows, LANES), F32)


def store_strided(held, first, stride, values):
    rows = values.shape[0]
    for t in range(held.shape[0]):
        held[t, pl.ds(first, rows, stride=stride), :] = values[:, t * LANES : (t + 1) * LANES]


def load_strided(held, first, stride, rows):
    parts = [held[t, pl.ds(first, rows, stride=stride), :] for t in range(held.shape[0])]
    return jnp.concatenate(parts, axis=1)


def joined_tiles(held):
    return jnp.concatenate([held[t] for t in range(held.shape[0])], axis=1)


def in_hbm(*arrays):
    return [pltpu.with_memory_space_constraint(a, pltpu.HBM) for a in arrays]


def in_vmem(*arrays):
    return [pltpu.with_memory_space_constraint(a, pltpu.VMEM) for a in arrays]


def head_lanes(length):
    lane = lax.broadcasted_iota(jnp.int32, (length, LANES), 1) // HEAD_CHANNELS
    return [
        jnp.where(lane == t, 1.0, 0.0).astype(BF16) for t in range(LANES // HEAD_CHANNELS)
    ]


def one_hot(shape, dim, place, value=1.0):
    hit = lax.broadcasted_iota(jnp.int32, shape, dim) == place
    return jnp.where(hit, value, 0.0).astype(BF16)


def quotient(top, below):
    guess = pl.reciprocal(below, approx=True)
    return top * (guess * (2.0 - below * guess))


def attend_all(items, lanes, bias_of):
    per_tile = LANES // HEAD_CHANNELS
    rows, width = items[0][0].shape
    tasks = [(n, tile) for n in range(len(items)) for tile in range(width // LANES)]
    scores, raised, pieces = {}, {}, [[] for _ in items]

    def score(at):
        n, tile = tasks[at]
        cut = slice(tile * LANES, (tile + 1) * LANES)
        query, key = items[n][0][:, cut], items[n][1][:, cut]
        stacked = jnp.concatenate([query * lanes[t] for t in range(per_tile)], axis=0)
        scores[at] = nt_dot(stacked, key)

    def raise_scores(at):
        n, tile = tasks[at]
        stacked = scores.pop(at)
        parts = []
        for t in range(per_tile):
            part = stacked[t * rows : (t + 1) * rows]
            if bias_of is not None:
                part = part + bias_of(tile * per_tile + t)
            parts.append(jnp.exp2(part).astype(BF16))
        raised[at] = jnp.concatenate(parts, axis=1)

    def gather(at):
        n, tile = tasks[at]
        cut = slice(tile * LANES, (tile + 1) * LANES)
        live = items[n][3]
        value = items[n][2][:, cut] * live
        sides = [
            jnp.concatenate([value * lanes[t], live * lanes[t]], axis=1) for t in range(per_tile)
        ]
        total = nn_dot(raised.pop(at), jnp.concatenate(sides, axis=0))
        pieces[n].append(quotient(total[:, :LANES], total[:, LANES:]))

    for at in range(len(tasks) + 2):
        if at < len(tasks):
            score(at)
        if 0 <= at - 2:
            gather(at - 2)
        if 0 <= at - 1 < len(tasks):
            raise_scores(at - 1)
    return [jnp.concatenate(p, axis=1) for p in pieces]


def project(normed, weight_ref):
    scale = LOG2E / math.sqrt(HEAD_CHANNELS)
    query = (nn_dot(normed, weight_ref[0]) * scale).astype(BF16)
    key = nn_dot(normed, weight_ref[1]).astype(BF16)
    value = nn_dot(normed, weight_ref[2]).astype(BF16)
    gate = 0.5 * jnp.tanh(0.5 * nn_dot(normed, weight_ref[3])) + 0.5
    return query, key, value, gate


def bias_kernel(pair_ref, weight_ref, out_ref, held):
    rows, cols, width = pair_ref.shape
    normed = layer_normalize(pair_ref[...].astype(F32)).astype(BF16).reshape(rows * cols, width)
    bias = nt_dot(weight_ref[...], normed) * LOG2E
    for i in range(rows):
        store_strided(held, i, rows, bias[:, i * cols : (i + 1) * cols])
    out_ref[...] = joined_tiles(held).astype(BF16)


def pair_bias_block(pair_rep, bias_weight):
    rows, cols, width = pair_rep.shape
    out = jax.ShapeDtypeStruct((ATTN_HEAD_COUNT * rows, cols), BF16)
    weight = bias_weight.T
    return pl.pallas_call(
        bias_kernel,
        grid=(1,),
        in_specs=[full_spec(pair_rep.shape), full_spec(weight.shape)],
        out_specs=pl.BlockSpec(memory_space=pltpu.VMEM),
        out_shape=out,
        scratch_shapes=[tiled_scratch(*out.shape)],
        compiler_params=params(16),
        name="pair_bias",
    )(*in_hbm(pair_rep, weight))


def row_project_kernel(
    me_ref, x_ref, weight_ref, mask_ref, out_w_ref, q_ref, k_ref, v_ref, g_ref, own_ref, out_w_out
):
    step = x_ref.shape[0]
    seqs = own_ref.shape[0]

    @pl.when(pl.program_id(0) == 0)
    def _():
        rows = pl.ds(pl.multiple_of(me_ref[0] * seqs, seqs), seqs)
        own_ref[...] = mask_ref[rows, :].astype(F32)
        out_w_out[...] = out_w_ref[...]

    for s in range(step):
        at = pl.program_id(0) * step + s
        normed = layer_normalize(x_ref[s].astype(F32)).astype(BF16)
        q_ref[at], k_ref[at], v_ref[at], g_ref[s] = project(normed, weight_ref)


def row_project(me, alignment, weight, mask, out_weight):
    seqs, length, width = alignment.shape
    step = 2
    vmem = pl.BlockSpec(memory_space=pltpu.VMEM)
    block = pl.BlockSpec((step, length, width), lambda i: (i, 0, 0))
    return pl.pallas_call(
        row_project_kernel,
        grid=(seqs // step,),
        in_specs=[pl.BlockSpec(memory_space=pltpu.SMEM), block]
        + [full_spec(a.shape) for a in (weight, mask, out_weight)],
        out_specs=[vmem] * 3 + [block] + [vmem] * 2,
        out_shape=[pltpu.VMEM(alignment.shape, BF16)] * 3
        + [
            pltpu.HBM(alignment.shape, F32),
            pltpu.VMEM((seqs, mask.shape[1]), F32),
            pltpu.VMEM(out_weight.shape, BF16),
        ],
        compiler_params=params(24),
        name="row_project",
    )(me, *in_hbm(alignment, weight, mask, out_weight))


def row_attend_kernel(plan, me_ref, x_hbm, g_hbm, q_ref, k_ref, v_ref, own_ref, out_w_ref, *rest):
    bias_refs = rest[: len(plan)]
    out_ref, bias_all, x_ref, g_ref, sems = rest[len(plan) :]
    heads, length, _ = bias_all.shape
    seqs = q_ref.shape[0]
    parts = out_ref.shape[0]

    copies = [
        pltpu.make_async_copy(x_hbm, x_ref, sems.at[0]),
        pltpu.make_async_copy(g_hbm, g_ref, sems.at[1]),
    ]
    for copy in copies:
        copy.start()
    for bias_ref, offsets in zip(bias_refs, plan):
        for z, offset in enumerate(offsets):
            block = bias_ref[z].astype(F32).reshape(heads, -1, length)
            rows = block.shape[1]
            owner = me_ref[0] ^ offset
            bias_all[:, pl.ds(pl.multiple_of(owner * rows, rows), rows), :] = block

    lanes = head_lanes(length)
    own = own_ref[...].astype(BF16)
    items = []
    for s in range(seqs):
        spot = one_hot((seqs, LANES), 0, s, LIVE_SCALE)
        live = lax.dot_general(
            own, spot, (((0,), (0,)), ((), ())), preferred_element_type=F32
        ).astype(BF16)
        items.append((q_ref[s], k_ref[s], v_ref[s], live))
    attended = attend_all(items, lanes, lambda h: bias_all[h])
    for copy in copies:
        copy.wait()
    for pair in range(0, seqs, 2):
        results = []
        for s in (pair, pair + 1):
            gated = (attended[s] * g_ref[s]).astype(BF16)
            total = x_ref[s].astype(F32) + nn_dot(gated, out_w_ref[...])
            results.append(total.reshape(parts, 1, length // parts, total.shape[1]))
        joined = jnp.concatenate(results, axis=1)
        height = 2 * length // parts
        rows = slice(pair // 2 * height, (pair // 2 + 1) * height)
        out_ref[:, rows, :] = joined.reshape(parts, height, joined.shape[3]).astype(BF16)


def row_attend(me, alignment, gate, pinned, bias_parts, plan, parts):
    seqs, length, width = alignment.shape
    vmem = pl.BlockSpec(memory_space=pltpu.VMEM)
    hbm = pl.BlockSpec(memory_space=pltpu.HBM)
    held = in_vmem(*pinned, *bias_parts)
    return pl.pallas_call(
        functools.partial(row_attend_kernel, plan),
        in_specs=[pl.BlockSpec(memory_space=pltpu.SMEM), hbm, hbm] + [vmem] * len(held),
        out_specs=vmem,
        out_shape=jax.ShapeDtypeStruct((parts, seqs * length // parts, width), BF16),
        scratch_shapes=[
            pltpu.VMEM((ATTN_HEAD_COUNT, length, length), F32),
            pltpu.VMEM(alignment.shape, BF16),
            pltpu.VMEM(alignment.shape, F32),
            pltpu.SemaphoreType.DMA((2,)),
        ],
        compiler_params=params(44),
        name="row_attend",
    )(me, *in_hbm(alignment, gate), *held)


def column_kernel(
    items, me_ref, x_ref, mask_ref, weight_ref, out_w_ref, factor_ref,
    out_ref, left_ref, right_ref, held, right_held,
):
    total_rows = held.shape[1]
    length = total_rows // items
    for t in range(held.shape[0]):
        part = x_ref[:, :, t * LANES : (t + 1) * LANES].astype(F32)
        held[t] = part.reshape(total_rows, LANES)

    lanes = head_lanes(length)
    mask = mask_ref[...].astype(F32).astype(BF16)
    residues = mask.shape[1]
    place = me_ref[0] * items
    rows = [load_strided(held, n, items, length) for n in range(items)]
    inputs, gates, normed = [], [], {0: layer_normalize(rows[0]).astype(BF16)}
    for n in range(items):
        if n + 1 < items:
            normed[n + 1] = layer_normalize(rows[n + 1]).astype(BF16)
        query, key, value, gate = project(normed[n], weight_ref)
        live = nn_dot(mask, one_hot((residues, LANES), 0, place + n, LIVE_SCALE)).astype(BF16)
        inputs.append((query, key, value, live))
        gates.append(gate)
    heads = attend_all(inputs, lanes, None)
    feat = FACTOR_CHANNELS
    live_rows = nt_dot(
        one_hot((items, residues), 1, place + lax.broadcasted_iota(jnp.int32, (items, residues), 0)),
        mask,
    )
    updated = {}
    for at in range(items + 2):
        if at < items:
            heads_out = (heads[at] * gates[at]).astype(BF16)
            updated[at] = (rows[at] + nn_dot(heads_out, out_w_ref[...])).astype(BF16)
            out_ref[at] = updated[at]
        if 0 <= at - 2:
            n = at - 2
            factors = nt_dot(factor_ref[...], normed[n]) * live_rows[n : n + 1]
            left_ref[n * feat : (n + 1) * feat, :] = factors[:feat].astype(BF16)
            store_strided(right_held, n, items, factors[feat:])
        if 0 <= at - 1 < items:
            normed[at - 1] = layer_normalize(updated[at - 1].astype(F32)).astype(BF16)
    right_ref[...] = joined_tiles(right_held).astype(BF16)


def column_attend(me, moved, mask, weight, out_weight, factor_weight, items):
    width = moved.shape[2]
    total_rows = moved.shape[0] * moved.shape[1]
    length = total_rows // items
    side = (items * FACTOR_CHANNELS, length)
    left = right = jax.ShapeDtypeStruct(side, BF16)
    vmem = pl.BlockSpec(memory_space=pltpu.VMEM)
    operands = in_vmem(moved, mask, weight, out_weight, factor_weight.T)
    return pl.pallas_call(
        functools.partial(column_kernel, items),
        in_specs=[pl.BlockSpec(memory_space=pltpu.SMEM)] + [vmem] * len(operands),
        out_specs=[vmem] * 3,
        out_shape=[pltpu.VMEM((items, length, width), BF16), left, right],
        scratch_shapes=[tiled_scratch(total_rows, width), tiled_scratch(*side)],
        compiler_params=params(48),
        name="column_attend",
    )(me, *operands)


def interleave_kernel(rows_ref, out_ref, held):
    items, step = rows_ref.shape[0], out_ref.shape[0]
    at = pl.ds(pl.multiple_of(pl.program_id(0) * step, step), step)
    for item in range(items):
        store_strided(held, item, items, rows_ref[item, at, :].astype(F32))
    out_ref[...] = joined_tiles(held).reshape(out_ref.shape).astype(BF16)


def interleave(rows):
    items, length, width = rows.shape
    step = length // 4
    return pl.pallas_call(
        interleave_kernel,
        grid=(length // step,),
        in_specs=[pl.BlockSpec(memory_space=pltpu.VMEM)],
        out_specs=pl.BlockSpec((step, items, width), lambda i: (i, 0, 0)),
        out_shape=pltpu.HBM((length, items, width), BF16),
        scratch_shapes=[tiled_scratch(items * step, width)],
        compiler_params=params(16),
        name="interleave",
    )(*in_vmem(rows))


def outer_kernel(group, outer, items, *refs):
    lefts, rights = refs[:group], refs[group : group + outer]
    weight_ref = refs[group + outer]
    outs = refs[group + outer + 1 : -3]
    weight_rows, weight, held = refs[-3:]
    feat = FACTOR_CHANNELS
    quad = LANES // feat
    tiles = items * feat // LANES
    cols = outer * items
    width = weight_ref.shape[1]

    weight_rows[...] = weight_ref[...].astype(F32)
    weight[...] = jnp.zeros_like(weight)
    for e in range(feat):
        block = weight_rows[pl.ds(e, feat, stride=feat), :].astype(BF16)
        for i in range(quad):
            start = e * LANES + i * feat
            weight[start : start + feat, i * width : (i + 1) * width] = block

    right = jnp.concatenate([r[...] for r in rights], axis=0)
    def product(k):
        return nt_dot(right, lefts[k][...])

    later = product(0)
    for k in range(group):
        sums, later = later, product(k + 1) if k + 1 < group else None
        sums = sums.reshape(outer, feat, items, sums.shape[1])
        sums = jnp.transpose(sums, (1, 0, 2, 3)).reshape(feat, cols, sums.shape[3]).astype(BF16)
        for t in range(tiles):
            at = slice((k * tiles + t) * cols, (k * tiles + t + 1) * cols)
            for e in range(feat):
                held[at, e * LANES : (e + 1) * LANES] = sums[e, :, t * LANES : (t + 1) * LANES]
    update = nn_dot(held[...], weight[...])
    for k in range(group):
        for t in range(tiles):
            rows = update[(k * tiles + t) * cols : (k * tiles + t + 1) * cols]
            for i in range(quad):
                outs[k][t * quad + i] = rows[:, i * width : (i + 1) * width].astype(BF16)


def outer_product(lefts, rights, weight, items):
    group, outer = len(lefts), len(rights)
    cols = outer * items
    tiles = items * FACTOR_CHANNELS // LANES
    depth = FACTOR_CHANNELS * LANES
    width = weight.shape[1]
    return pl.pallas_call(
        functools.partial(outer_kernel, group, outer, items),
        out_shape=[jax.ShapeDtypeStruct((items, cols, width), BF16)] * group,
        scratch_shapes=[
            pltpu.VMEM(weight.shape, F32),
            pltpu.VMEM((depth, LANES // FACTOR_CHANNELS * width), BF16),
            pltpu.VMEM((group * tiles * cols, depth), BF16),
        ],
        compiler_params=params(28),
        name="outer_product",
    )(*lefts, *rights, weight)


def finish_kernel(offsets, line, me_ref, pair_ref, scale_ref, *refs):
    parts, (out_ref, done, sems) = refs[:-3], refs[-3:]
    here = me_ref[0]
    items, cols, width = parts[0].shape
    outer = cols // items
    odd = (here & 1) == 1
    copies = []
    for i in range(items):
        for k, offset in enumerate(offsets):
            both = parts[k][i].astype(F32).reshape(outer // 2, 2, items, width)
            low, high = both[:, 0:1], both[:, 1:2]
            both = jnp.concatenate([jnp.where(odd, high, low), jnp.where(odd, low, high)], axis=1)
            both = both.reshape(outer // 2, 2 * items, width)
            for z in range(outer // 2):
                owner = here ^ (offset | line[z])
                start = pl.multiple_of((owner >> 1) * (2 * items), 2 * items)
                at = pl.ds(start, 2 * items)
                update = both[z] * scale_ref[at, i : i + 1]
                done[i, at, :] = (pair_ref[i, at, :].astype(F32) + update).astype(BF16)
        copies.append(pltpu.make_async_copy(done.at[i], out_ref.at[i], sems.at[i]))
        copies[i].start()
    for copy in copies:
        copy.wait()


def finish(me, pair_rep, scale, parts, offsets, line):
    vmem = pl.BlockSpec(memory_space=pltpu.VMEM)
    return pl.pallas_call(
        functools.partial(finish_kernel, offsets, line),
        in_specs=[pl.BlockSpec(memory_space=pltpu.SMEM)] + [vmem] * (2 + len(parts)),
        out_specs=pl.BlockSpec(memory_space=pltpu.HBM),
        out_shape=pltpu.HBM(pair_rep.shape, BF16),
        scratch_shapes=[
            pltpu.VMEM(pair_rep.shape, BF16),
            pltpu.SemaphoreType.DMA((pair_rep.shape[0],)),
        ],
        compiler_params=params(16),
        name="finish",
    )(me, pair_rep, scale, *parts)


def exchange(block, count, offset):
    if offset == 0:
        return block
    return lax.ppermute(block, "dap", [(i, i ^ offset) for i in range(count)])


def per_device_fast(
    alignment,
    pair_rep,
    align_mask,
    residue_mask,
    bias_weight,
    row_proj_weight,
    row_out_weight,
    column_proj_weight,
    column_out_weight,
    outer_factor_weight,
    outer_out,
):
    count = lax.axis_size("dap")
    dap_index = lax.axis_index("dap")
    me = jnp.reshape(dap_index, (1,)).astype(jnp.int32)
    plane, line = offset_groups(count)
    items = pair_rep.shape[0]

    bias = pair_bias_block(pair_rep, bias_weight)
    query, key, value, gate, own_mask, out_weight = row_project(
        me, alignment, row_proj_weight, align_mask, row_out_weight
    )
    column = [exchange(bias, count, z) for z in line]
    *column, gate = lax.optimization_barrier((*column, gate))
    column = jnp.stack(column)
    bias_parts = [exchange(column, count, k) for k in plane]
    plan = [[k | z for z in line] for k in plane]
    bias_parts += [exchange(part, count, 1) for part in bias_parts]
    plan += [[offset | 1 for offset in offsets] for offsets in plan]

    pinned = (query, key, value, own_mask, out_weight)
    rows = row_attend(me, alignment, gate, pinned, bias_parts, plan, count)
    rows, late_mask = lax.optimization_barrier((rows, align_mask))
    moved = lax.all_to_all(rows, "dap", split_axis=0, concat_axis=0, tiled=True)
    own_res = lax.dynamic_slice_in_dim(late_mask, dap_index * items, items, 1)
    counts = jnp.einsum(
        "si,sj->ji", own_res.astype(BF16), late_mask.astype(BF16), preferred_element_type=F32
    )
    res_float = residue_mask.astype(F32)
    live_rows = lax.dynamic_slice_in_dim(res_float, dap_index * items, items, 0)
    scale = live_rows[None, :] * res_float[:, None] / (counts + count_eps)
    updated, left, right = column_attend(
        me,
        moved,
        align_mask,
        column_proj_weight,
        column_out_weight,
        outer_factor_weight,
        items,
    )
    rights = [exchange(right, count, z) for z in line]
    rights[1], updated = lax.optimization_barrier((rights[1], updated))
    updated = interleave(updated)
    *rights, updated = lax.optimization_barrier((*rights, updated))
    rights = [part for own in rights for part in (own, exchange(own, count, 1))]
    lefts = [exchange(left, count, k) for k in plane]
    sent = outer_product(lefts[1:], rights, outer_out, items)
    parts = [exchange(part, count, k) for part, k in zip(sent, plane[1:])]
    own = outer_product([left], rights, outer_out, items)
    parts = list(own) + parts
    pair_out = finish(me, pair_rep, scale, parts, plane, line)
    return updated, pair_out


def offset_groups(count):
    bits = count.bit_length() - 1
    near = (bits - 1) // 2
    plane = [k << 1 for k in range(1 << near)]
    line = [z << (1 + near) for z in range(1 << (bits - 1 - near))]
    return plane, line


def solution(mesh):
    placed = (
        P("dap", None, None),
        P("dap", "branch", None),
        P(),
        P(),
        P(),
        P(None, None, "branch"),
        P(),
        P(None, None, "branch"),
        P(),
        P(),
        P(),
    )
    count = mesh.shape["dap"]
    whole_heads = mesh.shape["branch"] == 1 and count & (count - 1) == 0

    def per_device(*operands):
        alignment, pair_rep = operands[0], operands[1]
        tile = 8
        fits = whole_heads and alignment.shape[0] == tile and pair_rep.shape[0] == tile
        return (per_device_fast if fits else per_device_general)(*operands)

    return jax.shard_map(
        per_device,
        mesh=mesh,
        in_specs=placed,
        out_specs=(P(None, "dap", None), P("dap", "branch", None)),
        check_vma=False,
    )
```

```python
import functools
import math

import jax
import jax.numpy as jnp
from jax import lax
from jax.experimental import pallas as pl
from jax.experimental.pallas import tpu as pltpu
from jax.sharding import PartitionSpec as P

ATTN_HEAD_COUNT = 8
HEAD_CHANNELS = 32
FACTOR_CHANNELS = 32


norm_eps = 1e-05
count_eps = 0.001


def layer_normalize(values):
    centre = jnp.mean(values, axis=-1, keepdims=True)
    centred = values - centre
    spread = jnp.mean(centred * centred, axis=-1, keepdims=True)
    return centred * lax.rsqrt(spread + norm_eps)


def attend_heads(inputs, key_mask, proj_weight, out_weight, score_bias):
    batch = inputs.shape[0]
    length = inputs.shape[1]
    local_width = proj_weight.shape[2]
    local_heads = local_width // HEAD_CHANNELS
    normed = layer_normalize(inputs.astype(jnp.float32)).astype(jnp.bfloat16)
    projected = jnp.einsum("blc,kcd->kbld", normed, proj_weight, preferred_element_type=jnp.float32)
    triple = (
        projected[:3].astype(jnp.bfloat16).reshape(3, batch, length, local_heads, HEAD_CHANNELS)
    )
    gating = jax.nn.sigmoid(projected[3])

    def attend_one(operands):
        queries, key_rows, value_rows, mask_row = operands
        scores = jnp.einsum(
            "ihd,jhd->hij", queries, key_rows, preferred_element_type=jnp.float32
        ) / math.sqrt(HEAD_CHANNELS)
        if score_bias is not None:
            scores = scores + score_bias.astype(jnp.float32)
        raised = jnp.exp(scores) * mask_row[None, None, :]
        weights = (raised / jnp.sum(raised, axis=-1, keepdims=True)).astype(jnp.bfloat16)
        return jnp.einsum("hij,jhd->ihd", weights, value_rows, preferred_element_type=jnp.float32)

    attended_rows = lax.map(attend_one, (triple[0], triple[1], triple[2], key_mask))
    heads_out = (attended_rows.reshape(batch, length, local_width) * gating).astype(jnp.bfloat16)
    gathered = lax.all_gather(heads_out, "branch", axis=2, tiled=True)
    update = jnp.einsum("blf,fc->blc", gathered, out_weight, preferred_element_type=jnp.float32)
    return (inputs.astype(jnp.float32) + update).astype(jnp.bfloat16)


def per_device_general(
    alignment,
    pair_rep,
    align_mask,
    residue_mask,
    bias_weight,
    row_proj_weight,
    row_out_weight,
    column_proj_weight,
    column_out_weight,
    outer_factor_weight,
    outer_out,
):
    branch_count = lax.axis_size("branch")
    dap_count = lax.axis_size("dap")
    branch_index = lax.axis_index("branch")
    dap_index = lax.axis_index("dap")
    seq_dev = alignment.shape[0]
    res_dev = pair_rep.shape[0]
    quarter = pair_rep.shape[1]
    total_seqs = align_mask.shape[0]
    local_heads = ATTN_HEAD_COUNT // branch_count
    float_mask = align_mask.astype(jnp.float32)
    res_float = residue_mask.astype(jnp.float32)
    pair_normed = layer_normalize(pair_rep.astype(jnp.float32)).astype(jnp.bfloat16)
    bias_block = jnp.einsum(
        "ijc,ch->hij", pair_normed, bias_weight, preferred_element_type=jnp.float32
    ).astype(jnp.bfloat16)
    bias_wide = lax.all_gather(bias_block, "branch", axis=2, tiled=True)
    bias_full = lax.all_gather(bias_wide, "dap", axis=1, tiled=True)
    pair_score_bias = lax.dynamic_slice_in_dim(
        bias_full, branch_index * local_heads, local_heads, 0
    )
    sequence_row_mask = lax.dynamic_slice_in_dim(float_mask, dap_index * seq_dev, seq_dev, 0)
    row_alignment = attend_heads(
        alignment, sequence_row_mask, row_proj_weight, row_out_weight, pair_score_bias
    )
    send_mask = sequence_row_mask.astype(jnp.bfloat16)
    blocked_rows = row_alignment.reshape(seq_dev, dap_count, res_dev, row_alignment.shape[2])
    blocked_mask = send_mask.reshape(seq_dev, dap_count, res_dev)
    moved_rows = lax.all_to_all(blocked_rows, "dap", split_axis=1, concat_axis=0, tiled=True)
    moved_mask = lax.all_to_all(blocked_mask, "dap", split_axis=1, concat_axis=0, tiled=True)
    seq_total = moved_rows.shape[0]
    items = moved_rows.shape[2]
    flat_rows = moved_rows.reshape(seq_total, items, moved_rows.shape[3])
    flat_mask = moved_mask.reshape(seq_total, items)
    transposed_rows = jnp.swapaxes(flat_rows, 0, 1)
    key_mask = jnp.swapaxes(flat_mask, 0, 1).astype(jnp.float32)
    attended_rows = attend_heads(
        transposed_rows, key_mask, column_proj_weight, column_out_weight, None
    )
    column_alignment = jnp.swapaxes(attended_rows, 0, 1)
    outer_mean_normed = layer_normalize(column_alignment.astype(jnp.float32)).astype(jnp.bfloat16)
    projected = jnp.einsum(
        "src,ce->sre", outer_mean_normed, outer_factor_weight, preferred_element_type=jnp.float32
    )
    factor_pairs = (projected * flat_mask.astype(jnp.float32)[:, :, None]).astype(jnp.bfloat16)
    column_alignment, factor_pairs = (column_alignment, factor_pairs)
    blocked_out = column_alignment.reshape(seq_total, 1, items, column_alignment.shape[2])
    blocked_factors = factor_pairs.reshape(seq_total, 1, items, factor_pairs.shape[2])
    updated_alignment = blocked_out.reshape(total_seqs, res_dev, blocked_out.shape[3])
    factor_pairs = blocked_factors.reshape(total_seqs, res_dev, blocked_factors.shape[3])
    left_side = factor_pairs[:, :, :FACTOR_CHANNELS]
    right_local = factor_pairs[:, :, FACTOR_CHANNELS:]
    col_start = branch_index * quarter
    row_start = dap_index * res_dev
    mask_rows = lax.dynamic_slice_in_dim(align_mask, row_start, res_dev, 1).astype(jnp.bfloat16)
    mask_cols = lax.dynamic_slice_in_dim(align_mask, col_start, quarter, 1).astype(jnp.bfloat16)
    counts = jnp.einsum("si,sj->ij", mask_rows, mask_cols, preferred_element_type=jnp.float32)
    live_rows = lax.dynamic_slice_in_dim(res_float, row_start, res_dev, 0)
    live_cols = lax.dynamic_slice_in_dim(res_float, col_start, quarter, 0)
    outer_weight = outer_out.astype(jnp.float32)
    right_all = lax.all_gather(right_local, "dap", axis=1, tiled=True)
    right_mine = lax.dynamic_slice_in_dim(right_all, col_start, quarter, 1)
    outer_sums = jnp.einsum(
        "sic,sje->ijce", left_side, right_mine, preferred_element_type=jnp.float32
    )
    outer_sums = outer_sums.reshape(res_dev, quarter, FACTOR_CHANNELS * FACTOR_CHANNELS)
    update = jnp.einsum("ijf,fz->ijz", outer_sums, outer_weight, precision=lax.Precision.HIGHEST)
    live = live_rows[:, None] * live_cols[None, :]
    update = update / (counts[:, :, None] + count_eps) * live[:, :, None]
    pair_out = (pair_rep.astype(jnp.float32) + update).astype(jnp.bfloat16)
    return (updated_alignment, pair_out)


LANES = 128
LOG2E = math.log2(math.e)
LIVE_SCALE = 1.0 / 128.0
BF16 = jnp.bfloat16
F32 = jnp.float32
MIB = 1024 * 1024


def nt_dot(a, b):
    return lax.dot_general(a, b, (((1,), (1,)), ((), ())), preferred_element_type=F32)


def nn_dot(a, b):
    return jnp.dot(a, b, preferred_element_type=F32)


def full_spec(shape):
    zeros = (0,) * len(shape)
    return pl.BlockSpec(shape, lambda *_: zeros)


def params(mib):
    return pltpu.CompilerParams(vmem_limit_bytes=mib * MIB)


def tiled_scratch(rows, cols):
    return pltpu.VMEM((cols // LANES, rows, LANES), F32)


def store_strided(held, first, stride, values):
    rows = values.shape[0]
    for t in range(held.shape[0]):
        held[t, pl.ds(first, rows, stride=stride), :] = values[:, t * LANES : (t + 1) * LANES]


def load_strided(held, first, stride, rows):
    parts = [held[t, pl.ds(first, rows, stride=stride), :] for t in range(held.shape[0])]
    return jnp.concatenate(parts, axis=1)


def joined_tiles(held):
    return jnp.concatenate([held[t] for t in range(held.shape[0])], axis=1)


def in_hbm(*arrays):
    return [pltpu.with_memory_space_constraint(a, pltpu.HBM) for a in arrays]


def in_vmem(*arrays):
    return [pltpu.with_memory_space_constraint(a, pltpu.VMEM) for a in arrays]


def head_lanes(length):
    lane = lax.broadcasted_iota(jnp.int32, (length, LANES), 1) // HEAD_CHANNELS
    return [
        jnp.where(lane == t, 1.0, 0.0).astype(BF16) for t in range(LANES // HEAD_CHANNELS)
    ]


def one_hot(shape, dim, place, value=1.0):
    hit = lax.broadcasted_iota(jnp.int32, shape, dim) == place
    return jnp.where(hit, value, 0.0).astype(BF16)


def quotient(top, below):
    guess = pl.reciprocal(below, approx=True)
    return top * (guess * (2.0 - below * guess))


def attend_all(items, lanes, bias_of):
    per_tile = LANES // HEAD_CHANNELS
    rows, width = items[0][0].shape
    tasks = [(n, tile) for n in range(len(items)) for tile in range(width // LANES)]
    scores, raised, pieces = {}, {}, [[] for _ in items]

    def score(at):
        n, tile = tasks[at]
        cut = slice(tile * LANES, (tile + 1) * LANES)
        query, key = items[n][0][:, cut], items[n][1][:, cut]
        stacked = jnp.concatenate([query * lanes[t] for t in range(per_tile)], axis=0)
        scores[at] = nt_dot(stacked, key)

    def raise_scores(at):
        n, tile = tasks[at]
        stacked = scores.pop(at)
        parts = []
        for t in range(per_tile):
            part = stacked[t * rows : (t + 1) * rows]
            if bias_of is not None:
                part = part + bias_of(tile * per_tile + t)
            parts.append(jnp.exp2(part).astype(BF16))
        raised[at] = jnp.concatenate(parts, axis=1)

    def gather(at):
        n, tile = tasks[at]
        cut = slice(tile * LANES, (tile + 1) * LANES)
        live = items[n][3]
        value = items[n][2][:, cut] * live
        sides = [
            jnp.concatenate([value * lanes[t], live * lanes[t]], axis=1) for t in range(per_tile)
        ]
        total = nn_dot(raised.pop(at), jnp.concatenate(sides, axis=0))
        pieces[n].append(quotient(total[:, :LANES], total[:, LANES:]))

    for at in range(len(tasks) + 2):
        if at < len(tasks):
            score(at)
        if 0 <= at - 2:
            gather(at - 2)
        if 0 <= at - 1 < len(tasks):
            raise_scores(at - 1)
    return [jnp.concatenate(p, axis=1) for p in pieces]


def project(normed, weight_ref):
    scale = LOG2E / math.sqrt(HEAD_CHANNELS)
    query = (nn_dot(normed, weight_ref[0]) * scale).astype(BF16)
    key = nn_dot(normed, weight_ref[1]).astype(BF16)
    value = nn_dot(normed, weight_ref[2]).astype(BF16)
    gate = 0.5 * jnp.tanh(0.5 * nn_dot(normed, weight_ref[3])) + 0.5
    return query, key, value, gate


def bias_kernel(pair_ref, weight_ref, out_ref, held):
    rows, cols, width = pair_ref.shape
    normed = layer_normalize(pair_ref[...].astype(F32)).astype(BF16).reshape(rows * cols, width)
    bias = nt_dot(weight_ref[...], normed) * LOG2E
    for i in range(rows):
        store_strided(held, i, rows, bias[:, i * cols : (i + 1) * cols])
    out_ref[...] = joined_tiles(held).astype(BF16)


def pair_bias_block(pair_rep, bias_weight):
    rows, cols, width = pair_rep.shape
    out = jax.ShapeDtypeStruct((ATTN_HEAD_COUNT * rows, cols), BF16)
    weight = bias_weight.T
    return pl.pallas_call(
        bias_kernel,
        grid=(1,),
        in_specs=[full_spec(pair_rep.shape), full_spec(weight.shape)],
        out_specs=pl.BlockSpec(memory_space=pltpu.VMEM),
        out_shape=out,
        scratch_shapes=[tiled_scratch(*out.shape)],
        compiler_params=params(16),
        name="pair_bias",
    )(*in_hbm(pair_rep, weight))


def row_project_kernel(
    me_ref, x_ref, weight_ref, mask_ref, out_w_ref, q_ref, k_ref, v_ref, g_ref, own_ref, out_w_out
):
    step = x_ref.shape[0]
    seqs = own_ref.shape[0]

    @pl.when(pl.program_id(0) == 0)
    def _():
        rows = pl.ds(pl.multiple_of(me_ref[0] * seqs, seqs), seqs)
        own_ref[...] = mask_ref[rows, :].astype(F32)
        out_w_out[...] = out_w_ref[...]

    for s in range(step):
        at = pl.program_id(0) * step + s
        normed = layer_normalize(x_ref[s].astype(F32)).astype(BF16)
        q_ref[at], k_ref[at], v_ref[at], g_ref[s] = project(normed, weight_ref)


def row_project(me, alignment, weight, mask, out_weight):
    seqs, length, width = alignment.shape
    step = 2
    vmem = pl.BlockSpec(memory_space=pltpu.VMEM)
    block = pl.BlockSpec((step, length, width), lambda i: (i, 0, 0))
    return pl.pallas_call(
        row_project_kernel,
        grid=(seqs // step,),
        in_specs=[pl.BlockSpec(memory_space=pltpu.SMEM), block]
        + [full_spec(a.shape) for a in (weight, mask, out_weight)],
        out_specs=[vmem] * 3 + [block] + [vmem] * 2,
        out_shape=[pltpu.VMEM(alignment.shape, BF16)] * 3
        + [
            pltpu.HBM(alignment.shape, F32),
            pltpu.VMEM((seqs, mask.shape[1]), F32),
            pltpu.VMEM(out_weight.shape, BF16),
        ],
        compiler_params=params(24),
        name="row_project",
    )(me, *in_hbm(alignment, weight, mask, out_weight))


def row_attend_kernel(plan, me_ref, x_hbm, g_hbm, q_ref, k_ref, v_ref, own_ref, out_w_ref, *rest):
    bias_refs = rest[: len(plan)]
    out_ref, bias_all, x_ref, g_ref, sems = rest[len(plan) :]
    heads, length, _ = bias_all.shape
    seqs = q_ref.shape[0]
    parts = out_ref.shape[0]

    copies = [
        pltpu.make_async_copy(x_hbm, x_ref, sems.at[0]),
        pltpu.make_async_copy(g_hbm, g_ref, sems.at[1]),
    ]
    for copy in copies:
        copy.start()
    for bias_ref, offsets in zip(bias_refs, plan):
        for z, offset in enumerate(offsets):
            block = bias_ref[z].astype(F32).reshape(heads, -1, length)
            rows = block.shape[1]
            owner = me_ref[0] ^ offset
            bias_all[:, pl.ds(pl.multiple_of(owner * rows, rows), rows), :] = block

    lanes = head_lanes(length)
    own = own_ref[...].astype(BF16)
    items = []
    for s in range(seqs):
        spot = one_hot((seqs, LANES), 0, s, LIVE_SCALE)
        live = lax.dot_general(
            own, spot, (((0,), (0,)), ((), ())), preferred_element_type=F32
        ).astype(BF16)
        items.append((q_ref[s], k_ref[s], v_ref[s], live))
    attended = attend_all(items, lanes, lambda h: bias_all[h])
    for copy in copies:
        copy.wait()
    for pair in range(0, seqs, 2):
        results = []
        for s in (pair, pair + 1):
            gated = (attended[s] * g_ref[s]).astype(BF16)
            total = x_ref[s].astype(F32) + nn_dot(gated, out_w_ref[...])
            results.append(total.reshape(parts, 1, length // parts, total.shape[1]))
        joined = jnp.concatenate(results, axis=1)
        height = 2 * length // parts
        rows = slice(pair // 2 * height, (pair // 2 + 1) * height)
        out_ref[:, rows, :] = joined.reshape(parts, height, joined.shape[3]).astype(BF16)


def row_attend(me, alignment, gate, pinned, bias_parts, plan, parts):
    seqs, length, width = alignment.shape
    vmem = pl.BlockSpec(memory_space=pltpu.VMEM)
    hbm = pl.BlockSpec(memory_space=pltpu.HBM)
    held = in_vmem(*pinned, *bias_parts)
    return pl.pallas_call(
        functools.partial(row_attend_kernel, plan),
        in_specs=[pl.BlockSpec(memory_space=pltpu.SMEM), hbm, hbm] + [vmem] * len(held),
        out_specs=vmem,
        out_shape=jax.ShapeDtypeStruct((parts, seqs * length // parts, width), BF16),
        scratch_shapes=[
            pltpu.VMEM((ATTN_HEAD_COUNT, length, length), F32),
            pltpu.VMEM(alignment.shape, BF16),
            pltpu.VMEM(alignment.shape, F32),
            pltpu.SemaphoreType.DMA((2,)),
        ],
        compiler_params=params(44),
        name="row_attend",
    )(me, *in_hbm(alignment, gate), *held)


def column_kernel(
    items, me_ref, x_ref, mask_ref, weight_ref, out_w_ref, factor_ref,
    out_ref, left_ref, right_ref, held, right_held,
):
    total_rows = held.shape[1]
    length = total_rows // items
    for t in range(held.shape[0]):
        part = x_ref[:, :, t * LANES : (t + 1) * LANES].astype(F32)
        held[t] = part.reshape(total_rows, LANES)

    lanes = head_lanes(length)
    mask = mask_ref[...].astype(F32).astype(BF16)
    residues = mask.shape[1]
    place = me_ref[0] * items
    rows = [load_strided(held, n, items, length) for n in range(items)]
    inputs, gates, normed = [], [], {0: layer_normalize(rows[0]).astype(BF16)}
    for n in range(items):
        if n + 1 < items:
            normed[n + 1] = layer_normalize(rows[n + 1]).astype(BF16)
        query, key, value, gate = project(normed[n], weight_ref)
        live = nn_dot(mask, one_hot((residues, LANES), 0, place + n, LIVE_SCALE)).astype(BF16)
        inputs.append((query, key, value, live))
        gates.append(gate)
    heads = attend_all(inputs, lanes, None)
    feat = FACTOR_CHANNELS
    live_rows = nt_dot(
        one_hot((items, residues), 1, place + lax.broadcasted_iota(jnp.int32, (items, residues), 0)),
        mask,
    )
    updated = {}
    for at in range(items + 2):
        if at < items:
            heads_out = (heads[at] * gates[at]).astype(BF16)
            updated[at] = (rows[at] + nn_dot(heads_out, out_w_ref[...])).astype(BF16)
            out_ref[at] = updated[at]
        if 0 <= at - 2:
            n = at - 2
            factors = nt_dot(factor_ref[...], normed[n]) * live_rows[n : n + 1]
            left_ref[n * feat : (n + 1) * feat, :] = factors[:feat].astype(BF16)
            store_strided(right_held, n, items, factors[feat:])
        if 0 <= at - 1 < items:
            normed[at - 1] = layer_normalize(updated[at - 1].astype(F32)).astype(BF16)
    right_ref[...] = joined_tiles(right_held).astype(BF16)


def column_attend(me, moved, mask, weight, out_weight, factor_weight, items):
    width = moved.shape[2]
    total_rows = moved.shape[0] * moved.shape[1]
    length = total_rows // items
    side = (items * FACTOR_CHANNELS, length)
    left = right = jax.ShapeDtypeStruct(side, BF16)
    vmem = pl.BlockSpec(memory_space=pltpu.VMEM)
    operands = in_vmem(moved, mask, weight, out_weight, factor_weight.T)
    return pl.pallas_call(
        functools.partial(column_kernel, items),
        in_specs=[pl.BlockSpec(memory_space=pltpu.SMEM)] + [vmem] * len(operands),
        out_specs=[vmem] * 3,
        out_shape=[pltpu.VMEM((items, length, width), BF16), left, right],
        scratch_shapes=[tiled_scratch(total_rows, width), tiled_scratch(*side)],
        compiler_params=params(48),
        name="column_attend",
    )(me, *operands)


def interleave_kernel(rows_ref, out_ref, held):
    items, step = rows_ref.shape[0], out_ref.shape[0]
    at = pl.ds(pl.multiple_of(pl.program_id(0) * step, step), step)
    for item in range(items):
        store_strided(held, item, items, rows_ref[item, at, :].astype(F32))
    out_ref[...] = joined_tiles(held).reshape(out_ref.shape).astype(BF16)


def interleave(rows):
    items, length, width = rows.shape
    step = length // 4
    return pl.pallas_call(
        interleave_kernel,
        grid=(length // step,),
        in_specs=[pl.BlockSpec(memory_space=pltpu.VMEM)],
        out_specs=pl.BlockSpec((step, items, width), lambda i: (i, 0, 0)),
        out_shape=pltpu.HBM((length, items, width), BF16),
        scratch_shapes=[tiled_scratch(items * step, width)],
        compiler_params=params(16),
        name="interleave",
    )(*in_vmem(rows))


def spread_kernel(weight_ref, weight, weight_rows):
    feat = FACTOR_CHANNELS
    quad = LANES // feat
    width = weight_ref.shape[1]
    weight_rows[...] = weight_ref[...].astype(F32)
    weight[...] = jnp.zeros_like(weight)
    for e in range(feat):
        block = weight_rows[pl.ds(e, feat, stride=feat), :].astype(BF16)
        for i in range(quad):
            start = e * LANES + i * feat
            weight[start : start + feat, i * width : (i + 1) * width] = block


def spread_weight(outer_out):
    shape = (FACTOR_CHANNELS * LANES, LANES // FACTOR_CHANNELS * outer_out.shape[1])
    return pl.pallas_call(
        spread_kernel,
        grid=(1,),
        in_specs=[full_spec(outer_out.shape)],
        out_specs=pl.BlockSpec(memory_space=pltpu.VMEM),
        out_shape=pltpu.VMEM(shape, BF16),
        scratch_shapes=[pltpu.VMEM(outer_out.shape, F32)],
        compiler_params=params(8),
        name="spread_weight",
    )(*in_hbm(outer_out))


def outer_kernel(group, outer, items, *refs):
    lefts, rights = refs[:group], refs[group : group + outer]
    weight_ref = refs[group + outer]
    outs, held = refs[group + outer + 1 : -1], refs[-1]
    feat = FACTOR_CHANNELS
    quad = LANES // feat
    tiles = items * feat // LANES
    cols = outer * items
    width = weight_ref.shape[1] // quad

    right = jnp.concatenate([r[...] for r in rights], axis=0)
    def product(k):
        return nt_dot(right, lefts[k][...])

    later = product(0)
    for k in range(group):
        sums, later = later, product(k + 1) if k + 1 < group else None
        sums = sums.reshape(outer, feat, items, sums.shape[1])
        sums = jnp.transpose(sums, (1, 0, 2, 3)).reshape(feat, cols, sums.shape[3]).astype(BF16)
        for t in range(tiles):
            at = slice((k * tiles + t) * cols, (k * tiles + t + 1) * cols)
            for e in range(feat):
                held[at, e * LANES : (e + 1) * LANES] = sums[e, :, t * LANES : (t + 1) * LANES]
    update = nn_dot(held[...], weight_ref[...])
    for k in range(group):
        for t in range(tiles):
            rows = update[(k * tiles + t) * cols : (k * tiles + t + 1) * cols]
            for i in range(quad):
                outs[k][t * quad + i] = rows[:, i * width : (i + 1) * width].astype(BF16)


def outer_product(lefts, rights, weight, items):
    group, outer = len(lefts), len(rights)
    cols = outer * items
    tiles = items * FACTOR_CHANNELS // LANES
    width = weight.shape[1] * FACTOR_CHANNELS // LANES
    vmem = pl.BlockSpec(memory_space=pltpu.VMEM)
    return pl.pallas_call(
        functools.partial(outer_kernel, group, outer, items),
        in_specs=[vmem] * (group + outer + 1),
        out_shape=[jax.ShapeDtypeStruct((items, cols, width), BF16)] * group,
        scratch_shapes=[pltpu.VMEM((group * tiles * cols, weight.shape[0]), BF16)],
        compiler_params=params(28),
        name="outer_product",
    )(*lefts, *rights, *in_vmem(weight))


def finish_kernel(offsets, line, me_ref, pair_ref, scale_ref, *refs):
    parts, (out_ref, done, sems) = refs[:-3], refs[-3:]
    here = me_ref[0]
    items, cols, width = parts[0].shape
    outer = cols // items
    odd = (here & 1) == 1
    copies = []
    for i in range(items):
        for k, offset in enumerate(offsets):
            both = parts[k][i].astype(F32).reshape(outer // 2, 2, items, width)
            low, high = both[:, 0:1], both[:, 1:2]
            both = jnp.concatenate([jnp.where(odd, high, low), jnp.where(odd, low, high)], axis=1)
            both = both.reshape(outer // 2, 2 * items, width)
            for z in range(outer // 2):
                owner = here ^ (offset | line[z])
                start = pl.multiple_of((owner >> 1) * (2 * items), 2 * items)
                at = pl.ds(start, 2 * items)
                update = both[z] * scale_ref[at, i : i + 1]
                done[i, at, :] = (pair_ref[i, at, :].astype(F32) + update).astype(BF16)
        copies.append(pltpu.make_async_copy(done.at[i], out_ref.at[i], sems.at[i]))
        copies[i].start()
    for copy in copies:
        copy.wait()


def finish(me, pair_rep, scale, parts, offsets, line):
    vmem = pl.BlockSpec(memory_space=pltpu.VMEM)
    return pl.pallas_call(
        functools.partial(finish_kernel, offsets, line),
        in_specs=[pl.BlockSpec(memory_space=pltpu.SMEM)] + [vmem] * (2 + len(parts)),
        out_specs=pl.BlockSpec(memory_space=pltpu.HBM),
        out_shape=pltpu.HBM(pair_rep.shape, BF16),
        scratch_shapes=[
            pltpu.VMEM(pair_rep.shape, BF16),
            pltpu.SemaphoreType.DMA((pair_rep.shape[0],)),
        ],
        compiler_params=params(16),
        name="finish",
    )(me, pair_rep, scale, *parts)


def exchange(block, count, offset):
    if offset == 0:
        return block
    return lax.ppermute(block, "dap", [(i, i ^ offset) for i in range(count)])


def per_device_fast(
    alignment,
    pair_rep,
    align_mask,
    residue_mask,
    bias_weight,
    row_proj_weight,
    row_out_weight,
    column_proj_weight,
    column_out_weight,
    outer_factor_weight,
    outer_out,
):
    count = lax.axis_size("dap")
    dap_index = lax.axis_index("dap")
    me = jnp.reshape(dap_index, (1,)).astype(jnp.int32)
    plane, line = offset_groups(count)
    items = pair_rep.shape[0]

    bias = pair_bias_block(pair_rep, bias_weight)
    query, key, value, gate, own_mask, out_weight = row_project(
        me, alignment, row_proj_weight, align_mask, row_out_weight
    )
    column = [exchange(bias, count, z) for z in line]
    *column, gate = lax.optimization_barrier((*column, gate))
    column = jnp.stack(column)
    bias_parts = [exchange(column, count, k) for k in plane]
    plan = [[k | z for z in line] for k in plane]
    bias_parts += [exchange(part, count, 1) for part in bias_parts]
    plan += [[offset | 1 for offset in offsets] for offsets in plan]

    pinned = (query, key, value, own_mask, out_weight)
    rows = row_attend(me, alignment, gate, pinned, bias_parts, plan, count)
    rows, late_mask = lax.optimization_barrier((rows, align_mask))
    moved = lax.all_to_all(rows, "dap", split_axis=0, concat_axis=0, tiled=True)
    own_res = lax.dynamic_slice_in_dim(late_mask, dap_index * items, items, 1)
    counts = jnp.einsum(
        "si,sj->ji", own_res.astype(BF16), late_mask.astype(BF16), preferred_element_type=F32
    )
    res_float = residue_mask.astype(F32)
    live_rows = lax.dynamic_slice_in_dim(res_float, dap_index * items, items, 0)
    scale = live_rows[None, :] * res_float[:, None] / (counts + count_eps)
    updated, left, right = column_attend(
        me,
        moved,
        align_mask,
        column_proj_weight,
        column_out_weight,
        outer_factor_weight,
        items,
    )
    rights = [exchange(right, count, z) for z in line]
    rights[1], updated = lax.optimization_barrier((rights[1], updated))
    updated = interleave(updated)
    updated, outer_out = lax.optimization_barrier((updated, outer_out))
    spread = spread_weight(outer_out)
    *rights, updated, spread = lax.optimization_barrier((*rights, updated, spread))
    rights = [part for own in rights for part in (own, exchange(own, count, 1))]
    lefts = [exchange(left, count, k) for k in plane]
    sent = outer_product(lefts[1:], rights, spread, items)
    parts = [exchange(part, count, k) for part, k in zip(sent, plane[1:])]
    own = outer_product([left], rights, spread, items)
    parts = list(own) + parts
    pair_out = finish(me, pair_rep, scale, parts, plane, line)
    return updated, pair_out


def offset_groups(count):
    bits = count.bit_length() - 1
    near = (bits - 1) // 2
    plane = [k << 1 for k in sorted(range(1, 1 << near), key=lambda k: (-k.bit_count(), k))]
    plane = [0] + plane
    line = [z << (1 + near) for z in range(1 << (bits - 1 - near))]
    return plane, line


def solution(mesh):
    placed = (
        P("dap", None, None),
        P("dap", "branch", None),
        P(),
        P(),
        P(),
        P(None, None, "branch"),
        P(),
        P(None, None, "branch"),
        P(),
        P(),
        P(),
    )
    count = mesh.shape["dap"]
    whole_heads = mesh.shape["branch"] == 1 and count & (count - 1) == 0

    def per_device(*operands):
        alignment, pair_rep = operands[0], operands[1]
        tile = 8
        fits = whole_heads and alignment.shape[0] == tile and pair_rep.shape[0] == tile
        return (per_device_fast if fits else per_device_general)(*operands)

    return jax.shard_map(
        per_device,
        mesh=mesh,
        in_specs=placed,
        out_specs=(P(None, "dap", None), P("dap", "branch", None)),
        check_vma=False,
    )
```

```python
import functools
import math

import jax
import jax.numpy as jnp
from jax import lax
from jax.experimental import pallas as pl
from jax.experimental.pallas import tpu as pltpu
from jax.sharding import PartitionSpec as P

ATTN_HEAD_COUNT = 8
HEAD_CHANNELS = 32
FACTOR_CHANNELS = 32


norm_eps = 1e-05
count_eps = 0.001


def layer_normalize(values):
    centre = jnp.mean(values, axis=-1, keepdims=True)
    centred = values - centre
    spread = jnp.mean(centred * centred, axis=-1, keepdims=True)
    return centred * lax.rsqrt(spread + norm_eps)


def attend_heads(inputs, key_mask, proj_weight, out_weight, score_bias):
    batch = inputs.shape[0]
    length = inputs.shape[1]
    local_width = proj_weight.shape[2]
    local_heads = local_width // HEAD_CHANNELS
    normed = layer_normalize(inputs.astype(jnp.float32)).astype(jnp.bfloat16)
    projected = jnp.einsum("blc,kcd->kbld", normed, proj_weight, preferred_element_type=jnp.float32)
    triple = (
        projected[:3].astype(jnp.bfloat16).reshape(3, batch, length, local_heads, HEAD_CHANNELS)
    )
    gating = jax.nn.sigmoid(projected[3])

    def attend_one(operands):
        queries, key_rows, value_rows, mask_row = operands
        scores = jnp.einsum(
            "ihd,jhd->hij", queries, key_rows, preferred_element_type=jnp.float32
        ) / math.sqrt(HEAD_CHANNELS)
        if score_bias is not None:
            scores = scores + score_bias.astype(jnp.float32)
        raised = jnp.exp(scores) * mask_row[None, None, :]
        weights = (raised / jnp.sum(raised, axis=-1, keepdims=True)).astype(jnp.bfloat16)
        return jnp.einsum("hij,jhd->ihd", weights, value_rows, preferred_element_type=jnp.float32)

    attended_rows = lax.map(attend_one, (triple[0], triple[1], triple[2], key_mask))
    heads_out = (attended_rows.reshape(batch, length, local_width) * gating).astype(jnp.bfloat16)
    gathered = lax.all_gather(heads_out, "branch", axis=2, tiled=True)
    update = jnp.einsum("blf,fc->blc", gathered, out_weight, preferred_element_type=jnp.float32)
    return (inputs.astype(jnp.float32) + update).astype(jnp.bfloat16)


def per_device_general(
    alignment,
    pair_rep,
    align_mask,
    residue_mask,
    bias_weight,
    row_proj_weight,
    row_out_weight,
    column_proj_weight,
    column_out_weight,
    outer_factor_weight,
    outer_out,
):
    branch_count = lax.axis_size("branch")
    dap_count = lax.axis_size("dap")
    branch_index = lax.axis_index("branch")
    dap_index = lax.axis_index("dap")
    seq_dev = alignment.shape[0]
    res_dev = pair_rep.shape[0]
    quarter = pair_rep.shape[1]
    total_seqs = align_mask.shape[0]
    local_heads = ATTN_HEAD_COUNT // branch_count
    float_mask = align_mask.astype(jnp.float32)
    res_float = residue_mask.astype(jnp.float32)
    pair_normed = layer_normalize(pair_rep.astype(jnp.float32)).astype(jnp.bfloat16)
    bias_block = jnp.einsum(
        "ijc,ch->hij", pair_normed, bias_weight, preferred_element_type=jnp.float32
    ).astype(jnp.bfloat16)
    bias_wide = lax.all_gather(bias_block, "branch", axis=2, tiled=True)
    bias_full = lax.all_gather(bias_wide, "dap", axis=1, tiled=True)
    pair_score_bias = lax.dynamic_slice_in_dim(
        bias_full, branch_index * local_heads, local_heads, 0
    )
    sequence_row_mask = lax.dynamic_slice_in_dim(float_mask, dap_index * seq_dev, seq_dev, 0)
    row_alignment = attend_heads(
        alignment, sequence_row_mask, row_proj_weight, row_out_weight, pair_score_bias
    )
    send_mask = sequence_row_mask.astype(jnp.bfloat16)
    blocked_rows = row_alignment.reshape(seq_dev, dap_count, res_dev, row_alignment.shape[2])
    blocked_mask = send_mask.reshape(seq_dev, dap_count, res_dev)
    moved_rows = lax.all_to_all(blocked_rows, "dap", split_axis=1, concat_axis=0, tiled=True)
    moved_mask = lax.all_to_all(blocked_mask, "dap", split_axis=1, concat_axis=0, tiled=True)
    seq_total = moved_rows.shape[0]
    items = moved_rows.shape[2]
    flat_rows = moved_rows.reshape(seq_total, items, moved_rows.shape[3])
    flat_mask = moved_mask.reshape(seq_total, items)
    transposed_rows = jnp.swapaxes(flat_rows, 0, 1)
    key_mask = jnp.swapaxes(flat_mask, 0, 1).astype(jnp.float32)
    attended_rows = attend_heads(
        transposed_rows, key_mask, column_proj_weight, column_out_weight, None
    )
    column_alignment = jnp.swapaxes(attended_rows, 0, 1)
    outer_mean_normed = layer_normalize(column_alignment.astype(jnp.float32)).astype(jnp.bfloat16)
    projected = jnp.einsum(
        "src,ce->sre", outer_mean_normed, outer_factor_weight, preferred_element_type=jnp.float32
    )
    factor_pairs = (projected * flat_mask.astype(jnp.float32)[:, :, None]).astype(jnp.bfloat16)
    column_alignment, factor_pairs = (column_alignment, factor_pairs)
    blocked_out = column_alignment.reshape(seq_total, 1, items, column_alignment.shape[2])
    blocked_factors = factor_pairs.reshape(seq_total, 1, items, factor_pairs.shape[2])
    updated_alignment = blocked_out.reshape(total_seqs, res_dev, blocked_out.shape[3])
    factor_pairs = blocked_factors.reshape(total_seqs, res_dev, blocked_factors.shape[3])
    left_side = factor_pairs[:, :, :FACTOR_CHANNELS]
    right_local = factor_pairs[:, :, FACTOR_CHANNELS:]
    col_start = branch_index * quarter
    row_start = dap_index * res_dev
    mask_rows = lax.dynamic_slice_in_dim(align_mask, row_start, res_dev, 1).astype(jnp.bfloat16)
    mask_cols = lax.dynamic_slice_in_dim(align_mask, col_start, quarter, 1).astype(jnp.bfloat16)
    counts = jnp.einsum("si,sj->ij", mask_rows, mask_cols, preferred_element_type=jnp.float32)
    live_rows = lax.dynamic_slice_in_dim(res_float, row_start, res_dev, 0)
    live_cols = lax.dynamic_slice_in_dim(res_float, col_start, quarter, 0)
    outer_weight = outer_out.astype(jnp.float32)
    right_all = lax.all_gather(right_local, "dap", axis=1, tiled=True)
    right_mine = lax.dynamic_slice_in_dim(right_all, col_start, quarter, 1)
    outer_sums = jnp.einsum(
        "sic,sje->ijce", left_side, right_mine, preferred_element_type=jnp.float32
    )
    outer_sums = outer_sums.reshape(res_dev, quarter, FACTOR_CHANNELS * FACTOR_CHANNELS)
    update = jnp.einsum("ijf,fz->ijz", outer_sums, outer_weight, precision=lax.Precision.HIGHEST)
    live = live_rows[:, None] * live_cols[None, :]
    update = update / (counts[:, :, None] + count_eps) * live[:, :, None]
    pair_out = (pair_rep.astype(jnp.float32) + update).astype(jnp.bfloat16)
    return (updated_alignment, pair_out)


LANES = 128
LOG2E = math.log2(math.e)
LIVE_SCALE = 1.0 / 128.0
BF16 = jnp.bfloat16
F32 = jnp.float32
MIB = 1024 * 1024


def nt_dot(a, b):
    return lax.dot_general(a, b, (((1,), (1,)), ((), ())), preferred_element_type=F32)


def nn_dot(a, b):
    return jnp.dot(a, b, preferred_element_type=F32)


def full_spec(shape):
    zeros = (0,) * len(shape)
    return pl.BlockSpec(shape, lambda *_: zeros)


def params(mib):
    return pltpu.CompilerParams(vmem_limit_bytes=mib * MIB)


def tiled_scratch(rows, cols):
    return pltpu.VMEM((cols // LANES, rows, LANES), F32)


def store_strided(held, first, stride, values):
    rows = values.shape[0]
    for t in range(held.shape[0]):
        held[t, pl.ds(first, rows, stride=stride), :] = values[:, t * LANES : (t + 1) * LANES]


def load_strided(held, first, stride, rows):
    parts = [held[t, pl.ds(first, rows, stride=stride), :] for t in range(held.shape[0])]
    return jnp.concatenate(parts, axis=1)


def joined_tiles(held):
    return jnp.concatenate([held[t] for t in range(held.shape[0])], axis=1)


def in_hbm(*arrays):
    return [pltpu.with_memory_space_constraint(a, pltpu.HBM) for a in arrays]


def in_vmem(*arrays):
    return [pltpu.with_memory_space_constraint(a, pltpu.VMEM) for a in arrays]


def head_lanes(length):
    lane = lax.broadcasted_iota(jnp.int32, (length, LANES), 1) // HEAD_CHANNELS
    return [
        jnp.where(lane == t, 1.0, 0.0).astype(BF16) for t in range(LANES // HEAD_CHANNELS)
    ]


def one_hot(shape, dim, place, value=1.0):
    hit = lax.broadcasted_iota(jnp.int32, shape, dim) == place
    return jnp.where(hit, value, 0.0).astype(BF16)


def quotient(top, below):
    guess = pl.reciprocal(below, approx=True)
    return top * (guess * (2.0 - below * guess))


def attend_all(items, lanes, bias_of):
    per_tile = LANES // HEAD_CHANNELS
    rows, width = items[0][0].shape
    tasks = [(n, tile) for n in range(len(items)) for tile in range(width // LANES)]
    scores, raised, pieces = {}, {}, [[] for _ in items]

    def score(at):
        n, tile = tasks[at]
        cut = slice(tile * LANES, (tile + 1) * LANES)
        query, key = items[n][0][:, cut], items[n][1][:, cut]
        stacked = jnp.concatenate([query * lanes[t] for t in range(per_tile)], axis=0)
        scores[at] = nt_dot(stacked, key)

    def raise_scores(at):
        n, tile = tasks[at]
        stacked = scores.pop(at)
        parts = []
        for t in range(per_tile):
            part = stacked[t * rows : (t + 1) * rows]
            if bias_of is not None:
                part = part + bias_of(tile * per_tile + t)
            parts.append(jnp.exp2(part).astype(BF16))
        raised[at] = jnp.concatenate(parts, axis=1)

    def gather(at):
        n, tile = tasks[at]
        cut = slice(tile * LANES, (tile + 1) * LANES)
        live = items[n][3]
        value = items[n][2][:, cut] * live
        sides = [
            jnp.concatenate([value * lanes[t], live * lanes[t]], axis=1) for t in range(per_tile)
        ]
        total = nn_dot(raised.pop(at), jnp.concatenate(sides, axis=0))
        pieces[n].append(quotient(total[:, :LANES], total[:, LANES:]))

    for at in range(len(tasks) + 2):
        if at < len(tasks):
            score(at)
        if 0 <= at - 1 < len(tasks):
            raise_scores(at - 1)
        if 0 <= at - 2:
            gather(at - 2)
    return [jnp.concatenate(p, axis=1) for p in pieces]


def project(normed, weight_ref):
    scale = LOG2E / math.sqrt(HEAD_CHANNELS)
    query = (nn_dot(normed, weight_ref[0]) * scale).astype(BF16)
    key = nn_dot(normed, weight_ref[1]).astype(BF16)
    value = nn_dot(normed, weight_ref[2]).astype(BF16)
    gate = 0.5 * jnp.tanh(0.5 * nn_dot(normed, weight_ref[3])) + 0.5
    return query, key, value, gate


def bias_kernel(pair_ref, weight_ref, out_ref, held):
    rows, cols, width = pair_ref.shape
    normed = layer_normalize(pair_ref[...].astype(F32)).astype(BF16).reshape(rows * cols, width)
    bias = nt_dot(weight_ref[...], normed) * LOG2E
    for i in range(rows):
        store_strided(held, i, rows, bias[:, i * cols : (i + 1) * cols])
    out_ref[...] = joined_tiles(held).astype(BF16)


def pair_bias_block(pair_rep, bias_weight):
    rows, cols, width = pair_rep.shape
    out = jax.ShapeDtypeStruct((ATTN_HEAD_COUNT * rows, cols), BF16)
    weight = bias_weight.T
    return pl.pallas_call(
        bias_kernel,
        grid=(1,),
        in_specs=[full_spec(pair_rep.shape), full_spec(weight.shape)],
        out_specs=pl.BlockSpec(memory_space=pltpu.VMEM),
        out_shape=out,
        scratch_shapes=[tiled_scratch(*out.shape)],
        compiler_params=params(16),
        name="pair_bias",
    )(*in_hbm(pair_rep, weight))


def row_project_kernel(
    me_ref, x_ref, weight_ref, mask_ref, out_w_ref, q_ref, k_ref, v_ref, g_ref, own_ref, out_w_out
):
    step = x_ref.shape[0]
    seqs = own_ref.shape[0]

    @pl.when(pl.program_id(0) == 0)
    def _():
        rows = pl.ds(pl.multiple_of(me_ref[0] * seqs, seqs), seqs)
        own_ref[...] = mask_ref[rows, :].astype(F32)
        out_w_out[...] = out_w_ref[...]

    for s in range(step):
        at = pl.program_id(0) * step + s
        normed = layer_normalize(x_ref[s].astype(F32)).astype(BF16)
        q_ref[at], k_ref[at], v_ref[at], g_ref[s] = project(normed, weight_ref)


def row_project(me, alignment, weight, mask, out_weight):
    seqs, length, width = alignment.shape
    step = 2
    vmem = pl.BlockSpec(memory_space=pltpu.VMEM)
    block = pl.BlockSpec((step, length, width), lambda i: (i, 0, 0))
    return pl.pallas_call(
        row_project_kernel,
        grid=(seqs // step,),
        in_specs=[pl.BlockSpec(memory_space=pltpu.SMEM), block]
        + [full_spec(a.shape) for a in (weight, mask, out_weight)],
        out_specs=[vmem] * 3 + [block] + [vmem] * 2,
        out_shape=[pltpu.VMEM(alignment.shape, BF16)] * 3
        + [
            pltpu.HBM(alignment.shape, F32),
            pltpu.VMEM((seqs, mask.shape[1]), F32),
            pltpu.VMEM(out_weight.shape, BF16),
        ],
        compiler_params=params(24),
        name="row_project",
    )(me, *in_hbm(alignment, weight, mask, out_weight))


def row_attend_kernel(plan, me_ref, x_hbm, g_hbm, q_ref, k_ref, v_ref, own_ref, out_w_ref, *rest):
    bias_refs = rest[: len(plan)]
    out_ref, bias_all, x_ref, g_ref, sems = rest[len(plan) :]
    heads, length, _ = bias_all.shape
    seqs = q_ref.shape[0]
    parts = out_ref.shape[0]

    copies = [
        pltpu.make_async_copy(x_hbm, x_ref, sems.at[0]),
        pltpu.make_async_copy(g_hbm, g_ref, sems.at[1]),
    ]
    for copy in copies:
        copy.start()
    for bias_ref, offsets in zip(bias_refs, plan):
        for z, offset in enumerate(offsets):
            block = bias_ref[z].astype(F32).reshape(heads, -1, length)
            rows = block.shape[1]
            owner = me_ref[0] ^ offset
            bias_all[:, pl.ds(pl.multiple_of(owner * rows, rows), rows), :] = block

    lanes = head_lanes(length)
    own = own_ref[...].astype(BF16)
    items = []
    for s in range(seqs):
        spot = one_hot((seqs, LANES), 0, s, LIVE_SCALE)
        live = lax.dot_general(
            own, spot, (((0,), (0,)), ((), ())), preferred_element_type=F32
        ).astype(BF16)
        items.append((q_ref[s], k_ref[s], v_ref[s], live))
    attended = attend_all(items, lanes, lambda h: bias_all[h])
    for copy in copies:
        copy.wait()
    for pair in range(0, seqs, 2):
        results = []
        for s in (pair, pair + 1):
            gated = (attended[s] * g_ref[s]).astype(BF16)
            total = x_ref[s].astype(F32) + nn_dot(gated, out_w_ref[...])
            results.append(total.reshape(parts, 1, length // parts, total.shape[1]))
        joined = jnp.concatenate(results, axis=1)
        height = 2 * length // parts
        rows = slice(pair // 2 * height, (pair // 2 + 1) * height)
        out_ref[:, rows, :] = joined.reshape(parts, height, joined.shape[3]).astype(BF16)


def row_attend(me, alignment, gate, pinned, bias_parts, plan, parts):
    seqs, length, width = alignment.shape
    vmem = pl.BlockSpec(memory_space=pltpu.VMEM)
    hbm = pl.BlockSpec(memory_space=pltpu.HBM)
    held = in_vmem(*pinned, *bias_parts)
    return pl.pallas_call(
        functools.partial(row_attend_kernel, plan),
        in_specs=[pl.BlockSpec(memory_space=pltpu.SMEM), hbm, hbm] + [vmem] * len(held),
        out_specs=vmem,
        out_shape=jax.ShapeDtypeStruct((parts, seqs * length // parts, width), BF16),
        scratch_shapes=[
            pltpu.VMEM((ATTN_HEAD_COUNT, length, length), F32),
            pltpu.VMEM(alignment.shape, BF16),
            pltpu.VMEM(alignment.shape, F32),
            pltpu.SemaphoreType.DMA((2,)),
        ],
        compiler_params=params(44),
        name="row_attend",
    )(me, *in_hbm(alignment, gate), *held)


def column_kernel(
    items, me_ref, x_ref, mask_ref, weight_ref, out_w_ref, factor_ref,
    out_ref, left_ref, right_ref, held, right_held,
):
    total_rows = held.shape[1]
    length = total_rows // items
    for t in range(held.shape[0]):
        part = x_ref[:, :, t * LANES : (t + 1) * LANES].astype(F32)
        held[t] = part.reshape(total_rows, LANES)

    lanes = head_lanes(length)
    mask = mask_ref[...].astype(F32).astype(BF16)
    residues = mask.shape[1]
    place = me_ref[0] * items
    rows = [load_strided(held, n, items, length) for n in range(items)]
    inputs, gates, normed = [], [], {0: layer_normalize(rows[0]).astype(BF16)}
    for n in range(items):
        if n + 1 < items:
            normed[n + 1] = layer_normalize(rows[n + 1]).astype(BF16)
        query, key, value, gate = project(normed[n], weight_ref)
        live = nn_dot(mask, one_hot((residues, LANES), 0, place + n, LIVE_SCALE)).astype(BF16)
        inputs.append((query, key, value, live))
        gates.append(gate)
    heads = attend_all(inputs, lanes, None)
    feat = FACTOR_CHANNELS
    live_rows = nt_dot(
        one_hot((items, residues), 1, place + lax.broadcasted_iota(jnp.int32, (items, residues), 0)),
        mask,
    )
    updated = {}
    for at in range(items + 2):
        if at < items:
            heads_out = (heads[at] * gates[at]).astype(BF16)
            updated[at] = (rows[at] + nn_dot(heads_out, out_w_ref[...])).astype(BF16)
            out_ref[at] = updated[at]
        if 0 <= at - 2:
            n = at - 2
            factors = nt_dot(factor_ref[...], normed[n]) * live_rows[n : n + 1]
            left_ref[n * feat : (n + 1) * feat, :] = factors[:feat].astype(BF16)
            store_strided(right_held, n, items, factors[feat:])
        if 0 <= at - 1 < items:
            normed[at - 1] = layer_normalize(updated[at - 1].astype(F32)).astype(BF16)
    right_ref[...] = joined_tiles(right_held).astype(BF16)


def column_attend(me, moved, mask, weight, out_weight, factor_weight, items):
    width = moved.shape[2]
    total_rows = moved.shape[0] * moved.shape[1]
    length = total_rows // items
    side = (items * FACTOR_CHANNELS, length)
    left = right = jax.ShapeDtypeStruct(side, BF16)
    vmem = pl.BlockSpec(memory_space=pltpu.VMEM)
    operands = in_vmem(moved, mask, weight, out_weight, factor_weight.T)
    return pl.pallas_call(
        functools.partial(column_kernel, items),
        in_specs=[pl.BlockSpec(memory_space=pltpu.SMEM)] + [vmem] * len(operands),
        out_specs=[vmem] * 3,
        out_shape=[pltpu.VMEM((items, length, width), BF16), left, right],
        scratch_shapes=[tiled_scratch(total_rows, width), tiled_scratch(*side)],
        compiler_params=params(48),
        name="column_attend",
    )(me, *operands)


def interleave_kernel(rows_ref, out_ref, held):
    items, step = rows_ref.shape[0], out_ref.shape[0]
    at = pl.ds(pl.multiple_of(pl.program_id(0) * step, step), step)
    for item in range(items):
        store_strided(held, item, items, rows_ref[item, at, :].astype(F32))
    out_ref[...] = joined_tiles(held).reshape(out_ref.shape).astype(BF16)


def interleave(rows):
    items, length, width = rows.shape
    step = length // 4
    return pl.pallas_call(
        interleave_kernel,
        grid=(length // step,),
        in_specs=[pl.BlockSpec(memory_space=pltpu.VMEM)],
        out_specs=pl.BlockSpec((step, items, width), lambda i: (i, 0, 0)),
        out_shape=pltpu.HBM((length, items, width), BF16),
        scratch_shapes=[tiled_scratch(items * step, width)],
        compiler_params=params(16),
        name="interleave",
    )(*in_vmem(rows))


def outer_kernel(group, outer, items, *refs):
    lefts, rights = refs[:group], refs[group : group + outer]
    weight_ref = refs[group + outer]
    outs = refs[group + outer + 1 : -3]
    weight_rows, weight, held = refs[-3:]
    feat = FACTOR_CHANNELS
    quad = LANES // feat
    tiles = items * feat // LANES
    cols = outer * items
    width = weight_ref.shape[1]

    weight_rows[...] = weight_ref[...].astype(F32)
    weight[...] = jnp.zeros_like(weight)
    for e in range(feat):
        block = weight_rows[pl.ds(e, feat, stride=feat), :].astype(BF16)
        for i in range(quad):
            start = e * LANES + i * feat
            weight[start : start + feat, i * width : (i + 1) * width] = block

    right = jnp.concatenate([r[...] for r in rights], axis=0)
    def product(k):
        return nt_dot(right, lefts[k][...])

    later = product(0)
    for k in range(group):
        sums, later = later, product(k + 1) if k + 1 < group else None
        sums = sums.reshape(outer, feat, items, sums.shape[1])
        sums = jnp.transpose(sums, (1, 0, 2, 3)).reshape(feat, cols, sums.shape[3]).astype(BF16)
        for t in range(tiles):
            at = slice((k * tiles + t) * cols, (k * tiles + t + 1) * cols)
            for e in range(feat):
                held[at, e * LANES : (e + 1) * LANES] = sums[e, :, t * LANES : (t + 1) * LANES]
    update = nn_dot(held[...], weight[...])
    for k in range(group):
        for t in range(tiles):
            rows = update[(k * tiles + t) * cols : (k * tiles + t + 1) * cols]
            for i in range(quad):
                outs[k][t * quad + i] = rows[:, i * width : (i + 1) * width].astype(BF16)


def outer_product(lefts, rights, weight, items):
    group, outer = len(lefts), len(rights)
    cols = outer * items
    tiles = items * FACTOR_CHANNELS // LANES
    depth = FACTOR_CHANNELS * LANES
    width = weight.shape[1]
    return pl.pallas_call(
        functools.partial(outer_kernel, group, outer, items),
        out_shape=[jax.ShapeDtypeStruct((items, cols, width), BF16)] * group,
        scratch_shapes=[
            pltpu.VMEM(weight.shape, F32),
            pltpu.VMEM((depth, LANES // FACTOR_CHANNELS * width), BF16),
            pltpu.VMEM((group * tiles * cols, depth), BF16),
        ],
        compiler_params=params(28),
        name="outer_product",
    )(*lefts, *rights, weight)


def finish_kernel(offsets, line, me_ref, pair_ref, scale_ref, *refs):
    parts, (out_ref, done, sems) = refs[:-3], refs[-3:]
    here = me_ref[0]
    items, cols, width = parts[0].shape
    outer = cols // items
    odd = (here & 1) == 1
    copies = []
    for i in range(items):
        for k, offset in enumerate(offsets):
            both = parts[k][i].astype(F32).reshape(outer // 2, 2, items, width)
            low, high = both[:, 0:1], both[:, 1:2]
            both = jnp.concatenate([jnp.where(odd, high, low), jnp.where(odd, low, high)], axis=1)
            both = both.reshape(outer // 2, 2 * items, width)
            for z in range(outer // 2):
                owner = here ^ (offset | line[z])
                start = pl.multiple_of((owner >> 1) * (2 * items), 2 * items)
                at = pl.ds(start, 2 * items)
                update = both[z] * scale_ref[at, i : i + 1]
                done[i, at, :] = (pair_ref[i, at, :].astype(F32) + update).astype(BF16)
        copies.append(pltpu.make_async_copy(done.at[i], out_ref.at[i], sems.at[i]))
        copies[i].start()
    for copy in copies:
        copy.wait()


def finish(me, pair_rep, scale, parts, offsets, line):
    vmem = pl.BlockSpec(memory_space=pltpu.VMEM)
    return pl.pallas_call(
        functools.partial(finish_kernel, offsets, line),
        in_specs=[pl.BlockSpec(memory_space=pltpu.SMEM)] + [vmem] * (2 + len(parts)),
        out_specs=pl.BlockSpec(memory_space=pltpu.HBM),
        out_shape=pltpu.HBM(pair_rep.shape, BF16),
        scratch_shapes=[
            pltpu.VMEM(pair_rep.shape, BF16),
            pltpu.SemaphoreType.DMA((pair_rep.shape[0],)),
        ],
        compiler_params=params(16),
        name="finish",
    )(me, pair_rep, scale, *parts)


def exchange(block, count, offset):
    if offset == 0:
        return block
    return lax.ppermute(block, "dap", [(i, i ^ offset) for i in range(count)])


def per_device_fast(
    alignment,
    pair_rep,
    align_mask,
    residue_mask,
    bias_weight,
    row_proj_weight,
    row_out_weight,
    column_proj_weight,
    column_out_weight,
    outer_factor_weight,
    outer_out,
):
    count = lax.axis_size("dap")
    dap_index = lax.axis_index("dap")
    me = jnp.reshape(dap_index, (1,)).astype(jnp.int32)
    plane, line = offset_groups(count)
    items = pair_rep.shape[0]

    bias = pair_bias_block(pair_rep, bias_weight)
    query, key, value, gate, own_mask, out_weight = row_project(
        me, alignment, row_proj_weight, align_mask, row_out_weight
    )
    column = [exchange(bias, count, z) for z in line]
    *column, gate = lax.optimization_barrier((*column, gate))
    column = jnp.stack(column)
    bias_parts = [exchange(column, count, k) for k in plane]
    plan = [[k | z for z in line] for k in plane]
    bias_parts += [exchange(part, count, 1) for part in bias_parts]
    plan += [[offset | 1 for offset in offsets] for offsets in plan]

    pinned = (query, key, value, own_mask, out_weight)
    rows = row_attend(me, alignment, gate, pinned, bias_parts, plan, count)
    rows, late_mask = lax.optimization_barrier((rows, align_mask))
    moved = lax.all_to_all(rows, "dap", split_axis=0, concat_axis=0, tiled=True)
    own_res = lax.dynamic_slice_in_dim(late_mask, dap_index * items, items, 1)
    counts = jnp.einsum(
        "si,sj->ji", own_res.astype(BF16), late_mask.astype(BF16), preferred_element_type=F32
    )
    res_float = residue_mask.astype(F32)
    live_rows = lax.dynamic_slice_in_dim(res_float, dap_index * items, items, 0)
    scale = live_rows[None, :] * res_float[:, None] / (counts + count_eps)
    updated, left, right = column_attend(
        me,
        moved,
        align_mask,
        column_proj_weight,
        column_out_weight,
        outer_factor_weight,
        items,
    )
    rights = [exchange(right, count, z) for z in line]
    rights[1], updated = lax.optimization_barrier((rights[1], updated))
    updated = interleave(updated)
    *rights, updated = lax.optimization_barrier((*rights, updated))
    rights = [part for own in rights for part in (own, exchange(own, count, 1))]
    lefts = [exchange(left, count, k) for k in plane]
    sent = outer_product(lefts[1:], rights, outer_out, items)
    parts = [exchange(part, count, k) for part, k in zip(sent, plane[1:])]
    own = outer_product([left], rights, outer_out, items)
    parts = list(own) + parts
    pair_out = finish(me, pair_rep, scale, parts, plane, line)
    return updated, pair_out


def offset_groups(count):
    bits = count.bit_length() - 1
    near = (bits - 1) // 2
    plane = [k << 1 for k in range(1 << near)]
    line = [z << (1 + near) for z in range(1 << (bits - 1 - near))]
    return plane, line


def solution(mesh):
    placed = (
        P("dap", None, None),
        P("dap", "branch", None),
        P(),
        P(),
        P(),
        P(None, None, "branch"),
        P(),
        P(None, None, "branch"),
        P(),
        P(),
        P(),
    )
    count = mesh.shape["dap"]
    whole_heads = mesh.shape["branch"] == 1 and count & (count - 1) == 0

    def per_device(*operands):
        alignment, pair_rep = operands[0], operands[1]
        tile = 8
        fits = whole_heads and alignment.shape[0] == tile and pair_rep.shape[0] == tile
        return (per_device_fast if fits else per_device_general)(*operands)

    return jax.shard_map(
        per_device,
        mesh=mesh,
        in_specs=placed,
        out_specs=(P(None, "dap", None), P("dap", "branch", None)),
        check_vma=False,
    )
```
